32 devices in a mesh: site: 8 (over z, y), branch: 4 (over x, core).
Axes of the slice: x: 2, y: 2, z: 4, core: 2. Of those that a mesh axis runs over, the one named last changes fastest.
Arguments:
- states: int32 [256, 2048], P(None, 'site'), may hold values from 0 to 63, as said below
- gap_mask: int32 [256, 2048], P(None, 'site'), may hold values 0 or 1
- weights: int32 [2048], P('site'), may hold values from 1 to 9
- leaf_order: int32 [256], replicated, may hold values from 0 to 255, each once
- exchanges: float32 [64, 64], replicated, may hold values from 0.3 to 3
- codon_freq: float32 [64], replicated, may hold values from 0.3 to 3
- omega_ratio: float32 [8], replicated, may hold values from 0.1 to 2
- lengths: float32 [508], P('branch'), may hold values from 0.05 to 1.5
- classes: int32 [508], P('branch'), may hold values from 0 to 7
Outputs:
- grad_exch: float32 [64, 64], replicated
- grad_omega: float32 [8], replicated
- grad_length: float32 [508], P('branch')
- loglik: float32 [], replicated
The draws below stay inside these ranges and needn't reach their ends.
Inputs may be any that keep to these rules, and one draw needn't show every extreme that they name: `states`: every state is a sense codon: never 10, 11 or 14.
All inputs are finite; a program needn't handle non-finite values. No bound on the sum of `gap_mask` on one device may be relied on, other than what follows from the above.
Results may differ from the reference program's by a relative error of at most 0.0003.
Values sent between devices are 32-bit elements; how exact they have to be, the bound alone decides.
No kernel may reach another device: no remote copies, remote signals or barrier semaphores. Data moves between devices by JAX's collectives and lax.ppermute only.
A program may use at most 192 MiB of HBM per device.

```python
import math
import jax
import jax.numpy as jnp
import numpy as np
from jax import lax

LEVELS = 6
LEAF_DEV = 64
EDGES = 127
TAXA = 256
BRANCHES = 508
S_DEV = 256
SITES = 2048
CLASSES = 8
N_SITE = 8
N_BRANCH = 4


def draw_states(key, part):
    raw_state = jax.random.randint(key, (TAXA, SITES), 0, 61)
    return (raw_state + 2 * (raw_state >= 10).astype(jnp.int32) + (raw_state >= 12).astype(jnp.int32)).astype(jnp.int32)


def draw_weights(key, part):
    base_weight = jax.random.randint(key, (SITES,), 1, 4)
    position = jnp.arange(SITES, dtype=jnp.int32)
    tier_factor = 1 + 3 * position // SITES
    return (base_weight * tier_factor).astype(jnp.int32)


def with_ends(drawn, key, smallest, top_value):
    shape = drawn.shape
    place = [jax.random.randint(jax.random.fold_in(key, axis), (), 0, shape[axis]) for axis in range(len(shape))]
    drawn = drawn.at[tuple(place)].set(smallest)
    longest = shape.index(max(shape))
    place[longest] = (place[longest] + 1) % shape[longest]
    return drawn.at[tuple(place)].set(top_value)


def block_scale(own_key, shape, split, least, top_value):
    def one(axis_at, shards_of):
        draws = jax.random.uniform(jax.random.fold_in(jax.random.fold_in(own_key, 6), axis_at), (shards_of,), jnp.float32, least / len(split), top_value / len(split))
        return jnp.repeat(jnp.exp(draws), shape[axis_at] // shards_of).reshape((-1,) + (1,) * (len(shape) - axis_at - 1))

    loudness = one(*split[0])
    for cut in split[1:]:
        loudness = loudness * one(*cut)
    return loudness


def setup_inputs(seed: int = 0) -> dict:
    key_of = jax.random.split(jax.random.key(seed), 10)
    states = draw_states(jax.random.fold_in(key_of[9], 71), 0)
    gap_mask = with_ends((jax.random.randint(key_of[1], (TAXA, SITES), 0, 8) < 1).astype(jnp.int32), jax.random.fold_in(key_of[1], 1), 0, 1)
    weights = draw_weights(jax.random.fold_in(key_of[9], 71), 0)
    leaf_order = jax.random.permutation(key_of[3], TAXA).astype(jnp.int32)
    exchanges = jnp.clip(jnp.exp(jax.random.uniform(key_of[4], (64, 64), jnp.float32, math.log(0.3), math.log(3.0))), 0.3, 3.0)
    codon_freq = jnp.clip(jnp.exp(jax.random.uniform(key_of[5], (64,), jnp.float32, math.log(0.3), math.log(3.0))), 0.3, 3.0)
    omega_ratio = jnp.clip(jnp.exp(jax.random.uniform(key_of[6], (CLASSES,), jnp.float32, math.log(0.1), math.log(2.0))), 0.1, 2.0)
    lengths = jnp.clip(jnp.exp(math.log(1.5) - 3.4011974 * jax.random.uniform(key_of[7], (BRANCHES,), jnp.float32) ** block_scale(key_of[7], (BRANCHES,), ((0, 4),), -0.2, 0.2)), 0.05, 1.5)
    classes = with_ends(jax.random.randint(key_of[8], (BRANCHES,), 0, CLASSES), jax.random.fold_in(key_of[8], 1), 0, CLASSES - 1).astype(jnp.int32)
    return dict(states=states, gap_mask=gap_mask, weights=weights, leaf_order=leaf_order, exchanges=exchanges, codon_freq=codon_freq, omega_ratio=omega_ratio, lengths=lengths, classes=classes)


CODE_TABLE = 'FFLLSSSSYYXXCCXWLLLLPPPPHHQQRRRRIIIMTTTTNNKKSSRRVVVVAAAADDEEGGGG'

def codon_tables():
    amino_acid = np.array(list(CODE_TABLE))
    codon_index = np.arange(64)
    digits = np.stack([codon_index // 16, codon_index // 4 % 4, codon_index % 4], 1)
    differ = (digits[:, None, :] != digits[None, :, :]).sum(-1)
    is_sense = amino_acid != 'X'
    single = (differ == 1) & is_sense[:, None] & is_sense[None, :]
    nonsyn = single & (amino_acid[:, None] != amino_acid[None, :])
    return (is_sense.astype(np.float32), single.astype(np.float32), nonsyn.astype(np.float32))

def build_rates(exchanges, codon_freq, omega_ratio):
    is_sense, single, nonsyn = codon_tables()
    stationary = codon_freq * is_sense / jnp.sum(codon_freq * is_sense)
    symmetric = 0.5 * (exchanges + exchanges.T)
    factor = 1.0 + nonsyn[None, :, :] * (omega_ratio[:, None, None] - 1.0)
    off_diag = symmetric[None, :, :] * stationary[None, None, :] * factor * single[None, :, :]
    row_total = lax.optimization_barrier(jnp.sum(off_diag, axis=2))
    mean_rate = lax.optimization_barrier(jnp.sum(stationary[None, :] * row_total, axis=1))
    identity = jnp.eye(64, dtype=exchanges.dtype)
    rate_matrix = (off_diag - row_total[:, :, None] * identity[None]) / mean_rate[:, None, None]
    return (rate_matrix, stationary)

def product(left, right):
    return jnp.einsum('bij,bjk->bik', left, right, precision=lax.Precision.HIGHEST)

def expm_taylor(scaled):
    reduced = scaled / 16.0
    identity = jnp.eye(64, dtype=scaled.dtype)
    series = jnp.broadcast_to(identity, scaled.shape)
    for degree in range(8, 0, -1):
        series = identity + product(reduced, series) / degree
    for square_step in range(4):
        series = product(series, series)
    return series

def forward(probs, vectors):
    return jnp.einsum('bij,bjs->bis', probs, vectors, precision=lax.Precision.HIGHEST)

def carried(probs, vectors):
    return jnp.einsum('bji,bjs->bis', probs, vectors, precision=lax.Precision.HIGHEST)

def leaf_partials(leaf_states, gap_rows):
    codon_axis = jnp.arange(64, dtype=jnp.int32)
    indicator = (leaf_states[:, None, :] == codon_axis[None, :, None]).astype(jnp.float32)
    return jnp.where(gap_rows[:, None, :] > 0, jnp.float32(1.0), indicator)

def up_pass(probs, leaves):
    levels = [leaves]
    messages = []
    logscale = jnp.zeros(leaves.shape[2:], jnp.float32)
    current = leaves
    for height in range(LEVELS):
        amount = current.shape[0]
        offset = 2 * LEAF_DEV - 2 * amount
        message = forward(probs[offset:offset + amount], current)
        messages.append(message)
        raw_parent = message[0::2] * message[1::2]
        scaling = lax.optimization_barrier(jnp.sum(raw_parent, axis=1))
        current = raw_parent / scaling[:, None, :]
        logscale = logscale + lax.optimization_barrier(jnp.sum(jnp.log(scaling), axis=0))
        levels.append(current)
    messages.append(forward(probs[EDGES - 1:EDGES], current))
    return (levels, messages, logscale)

def root_terms(stationary, top_messages, top_logs):
    members = top_messages.shape[0]
    joint = stationary[:, None] * top_messages[0]
    for member in range(1, members):
        joint = joint * top_messages[member]
    site_ll = jnp.log(lax.optimization_barrier(jnp.sum(joint, axis=0))) + lax.optimization_barrier(jnp.sum(top_logs, axis=0))
    above_list = []
    for member in range(members):
        vector = jnp.broadcast_to(stationary[:, None], top_messages.shape[1:])
        for other in range(members):
            if other != member:
                vector = vector * top_messages[other]
        above_list.append(vector)
    return (site_ll, jnp.stack(above_list))

def down_pass(probs, levels, messages, above_top):
    a_list = [above_top]
    current = above_top
    for height in range(LEVELS, 0, -1):
        amount = levels[height].shape[0]
        offset = 2 * LEAF_DEV - 2 * amount
        down_part = carried(probs[offset:offset + amount], current)
        down_part = down_part / lax.optimization_barrier(jnp.sum(down_part, axis=1, keepdims=True))
        message = messages[height - 1]
        current = jnp.stack([down_part * message[1::2], down_part * message[0::2]], axis=1).reshape(message.shape)
        a_list.append(current)
    return a_list[::-1]

def weigh(a_list, messages, site_weight, total_sites):
    weighted = []
    for vector, message in zip(a_list, messages):
        likelihood = lax.optimization_barrier(jnp.sum(vector * message, axis=1))
        weighted.append(vector * (site_weight / (likelihood * total_sites))[:, None, :])
    return weighted

def reference(states, gap_mask, weights, leaf_order, exchanges, codon_freq, omega_ratio, lengths, classes):
    rate_matrix, stationary = build_rates(exchanges, codon_freq, omega_ratio)
    class_pick = (classes[:, None] == jnp.arange(CLASSES, dtype=jnp.int32)[None, :]).astype(jnp.float32)
    branch_rates = jnp.einsum('bc,cij->bij', class_pick, rate_matrix, precision=lax.Precision.HIGHEST)
    scaled = branch_rates * lengths[:, None, None]
    probs_all, pullback = jax.vjp(expm_taylor, scaled)
    probs_tree = probs_all.reshape(N_BRANCH, EDGES, 64, 64)
    state_blocks = states.reshape(TAXA, N_SITE, S_DEV).transpose(1, 0, 2)
    gap_blocks = gap_mask.reshape(TAXA, N_SITE, S_DEV).transpose(1, 0, 2)
    weight_blocks = weights.reshape(N_SITE, S_DEV).astype(jnp.float32)

    def block_step(carry, inputs):
        counts_sum, log_sum = carry
        block_states, block_gaps, site_weight = inputs
        level_sets = []
        message_sets = []
        top_list = []
        log_list = []
        for member in range(N_BRANCH):
            taxon_rows = leaf_order[member * LEAF_DEV:(member + 1) * LEAF_DEV]
            leaves = leaf_partials(jnp.take(block_states, taxon_rows, axis=0), jnp.take(block_gaps, taxon_rows, axis=0))
            levels, messages, logscale = up_pass(probs_tree[member], leaves)
            level_sets.append(levels)
            message_sets.append(messages)
            top_list.append(messages[-1])
            log_list.append(logscale)
        top_messages = jnp.concatenate(top_list, axis=0)
        top_logs = jnp.stack(log_list)
        site_ll, above_all = root_terms(stationary, top_messages, top_logs)
        block_counts = []
        for member in range(N_BRANCH):
            a_list = down_pass(probs_tree[member], level_sets[member], message_sets[member], above_all[member:member + 1])
            weighted = weigh(a_list, message_sets[member], site_weight, SITES)
            for vector, partial_value in zip(weighted, level_sets[member]):
                block_counts.append(jnp.einsum('bis,bjs->bij', vector, partial_value, precision=lax.Precision.HIGHEST))
        new_counts = counts_sum + jnp.concatenate(block_counts, axis=0)
        return ((new_counts, log_sum + jnp.sum(site_weight * site_ll)), None)
    start_carry = (jnp.zeros((N_BRANCH * EDGES, 64, 64), jnp.float32), jnp.float32(0.0))
    (counts, log_total), unused = lax.scan(block_step, start_carry, (state_blocks, gap_blocks, weight_blocks))
    d_scaled = pullback(counts)[0]
    grad_length = lax.optimization_barrier(jnp.sum(d_scaled * branch_rates, axis=(1, 2)))
    d_rates = jnp.einsum('bc,bij->cij', class_pick, d_scaled * lengths[:, None, None], precision=lax.Precision.HIGHEST)
    unused_rates, pull_rates = jax.vjp(lambda table, ratio: build_rates(table, codon_freq, ratio)[0], exchanges, omega_ratio)
    grad_exch, grad_omega = pull_rates(d_rates)
    loglik = log_total / SITES / TAXA
    return (grad_exch, grad_omega, grad_length, loglik)
```

```python
import functools
import jax
import jax.numpy as jnp
import numpy as np
from jax import lax
from jax.experimental import pallas as pl
from jax.experimental.pallas import tpu as pltpu
from jax.sharding import PartitionSpec as P

LEAF_DEV = 64
EDGES = 127
PAIRS = 64
CLASSES = 8
ORDER = 8
BF = jnp.bfloat16
F32 = jnp.float32

CODE_TABLE = "FFLLSSSSYYXXCCXWLLLLPPPPHHQQRRRRIIIMTTTTNNKKSSRRVVVVAAAADDEEGGGG"


def codon_tables():
    amino_acid = np.array(list(CODE_TABLE))
    codon_index = np.arange(64)
    digits = np.stack([codon_index // 16, codon_index // 4 % 4, codon_index % 4], 1)
    differ = (digits[:, None, :] != digits[None, :, :]).sum(-1)
    is_sense = amino_acid != "X"
    single = (differ == 1) & is_sense[:, None] & is_sense[None, :]
    nonsyn = single & (amino_acid[:, None] != amino_acid[None, :])
    return (is_sense.astype(np.float32), single.astype(np.float32), nonsyn.astype(np.float32))


def low_half():
    return lax.broadcasted_iota(jnp.int32, (64, 128), 1) < 64


def split(x):
    high = x.astype(BF)
    low = (x - high.astype(F32)).astype(BF)
    return high, low


def spread(x):
    mask = low_half()
    zero = jnp.zeros_like(x)
    return jnp.concatenate([jnp.where(mask, x, zero), jnp.where(mask, zero, x)], axis=0)


def mxu(left, right):
    return jnp.dot(left, right, preferred_element_type=F32)


def mxu_nt(left, right):
    return lax.dot_general(left, right, (((1,), (1,)), ((), ())), preferred_element_type=F32)


def exact(left, right):
    return jnp.dot(left, right, preferred_element_type=F32, precision=lax.Precision.HIGHEST)


def exact_tn(left, right):
    return lax.dot_general(
        left, right, (((0,), (0,)), ((), ())), preferred_element_type=F32,
        precision=lax.Precision.HIGHEST,
    )


def pair_products(*terms):
    lefts, rights = [], []
    for left, right in terms:
        left_high, left_low = split(left)
        right_high, right_low = split(right)
        wide_high, wide_low = spread(right_high), spread(right_low)
        lefts += [left_high, left_high, left_low]
        rights += [wide_high, wide_low, wide_high]
    return mxu(jnp.concatenate(lefts, axis=1), jnp.concatenate(rights, axis=0))


def per_pair_messages(matrix, high, low):
    matrix_high, matrix_low = split(matrix)
    wide_high, wide_low = spread(matrix_high), spread(matrix_low)
    if low is None:
        return mxu(
            jnp.concatenate([wide_high, wide_low], axis=1), jnp.concatenate([high, high], axis=0)
        )
    return mxu(
        jnp.concatenate([wide_high, wide_high, wide_low], axis=1),
        jnp.concatenate([high, low, high], axis=0),
    )


def frequencies(freq_ref, sense_ref):
    row = lax.broadcasted_iota(jnp.int32, (64, 128), 0)
    lane = lax.broadcasted_iota(jnp.int32, (64, 128), 1)
    twice = (row == lane % 64).astype(F32)
    sense2 = sense_ref[...]
    freq2 = exact(jnp.broadcast_to(freq_ref[...], (8, 64)), twice)[0:1] * sense2
    total = 0.5 * jnp.sum(freq2, axis=1, keepdims=True)
    pi_row = freq2 / total
    pi_col = 0.5 * jnp.sum(twice * pi_row, axis=1, keepdims=True)
    sense_col = 0.5 * jnp.sum(twice * sense2, axis=1, keepdims=True)
    root_row = jnp.sqrt(jnp.where(sense2 > 0, pi_row, 1.0))
    root_col = jnp.sqrt(jnp.where(sense_col > 0, pi_col, 1.0))
    return twice, pi_row, pi_col, root_row, root_col


def symmetric_table(ex_ref, single_ref, twice):
    ex = ex_ref[...]
    return 0.5 * (exact(ex, twice) + exact_tn(ex, twice)) * single_ref[...]


def class_pair(table, nonsyn, omega_ref, pair, twice, pi_row, pi_col):
    mask = low_half()
    omega = jnp.where(mask, omega_ref[2 * pair], omega_ref[2 * pair + 1])
    factor = 1.0 + nonsyn * (omega - 1.0)
    flux = table * factor
    off = flux * pi_row
    row0 = jnp.sum(jnp.where(mask, off, 0.0), axis=1, keepdims=True)
    row1 = jnp.sum(jnp.where(mask, 0.0, off), axis=1, keepdims=True)
    mean0 = jnp.sum(pi_col * row0, axis=0, keepdims=True)
    mean1 = jnp.sum(pi_col * row1, axis=0, keepdims=True)
    rows = jnp.where(mask, row0, row1)
    mean = jnp.where(mask, mean0, mean1)
    return factor, off, rows, mean


def up_kernel(
    states_ref, gap_ref, order_ref, ex_ref, freq_ref, omega_ref, len_ref, cls_ref,
    sense_ref, single_ref, nonsyn_ref,
    top_ref, chain_ref, slope_ref, power_ref, message_ref, high_ref, low_ref, leaf_ref,
    scale_ref, inverse_ref, dup_ref,
):
    subtree = lax.axis_index("branch")
    mask = low_half()
    twice, pi_row, pi_col, root_row, root_col = frequencies(freq_ref, sense_ref)
    table = symmetric_table(ex_ref, single_ref, twice)
    nonsyn = nonsyn_ref[...]

    powers = []
    for pair in range(CLASSES // 2):
        factor, off, rows, mean = class_pair(
            table, nonsyn, omega_ref, pair, twice, pi_row, pi_col
        )
        powers.append([(table * factor * root_col * root_row - twice * rows) / mean])
    for left, right in ((0, 0), (1, 0), (1, 1), (3, 0), (3, 1), (3, 2), (3, 3)):
        for pair in range(CLASSES // 2):
            powers[pair].append(pair_products((powers[pair][left], powers[pair][right])))
    for pair in range(CLASSES // 2):
        for k in range(ORDER):
            value = powers[pair][k]
            swapped = pltpu.roll(value, 64, 1)
            dup_ref[2 * pair, k] = jnp.where(mask, value, swapped)
            dup_ref[2 * pair + 1, k] = jnp.where(mask, swapped, value)
            if k < 4:
                power_ref[pair, k] = value

    def exponentials(step, carry):
        held = []
        for j in range(8):
            p = step * 8 + j
            odd = jnp.minimum(2 * p + 1, EDGES - 1)
            y0 = len_ref[2 * p] * 0.0625
            y1 = jnp.where(2 * p + 1 < EDGES, len_ref[odd] * 0.0625, 0.0)
            c0, c1 = cls_ref[2 * p], cls_ref[odd]
            y = jnp.where(lax.broadcasted_iota(jnp.int32, (8, 128), 1) < 64, y0, y1)
            slope_coef = jnp.ones_like(y)
            value = slope = None
            for k in range(ORDER):
                coef = slope_coef * y * (1.0 / (k + 1))
                matrix = jnp.where(mask, dup_ref[c0, k], dup_ref[c1, k])
                first, second = matrix * coef[0:1], matrix * slope_coef[0:1]
                value = first if k == 0 else value + first
                slope = second if k == 0 else slope + second
                slope_coef = coef
            chain_ref[0, p] = value
            slope_ref[p] = slope
            held.append(value)
        for level in range(4):
            for j in range(8):
                held[j] = 2.0 * held[j] + pair_products((held[j], held[j]))
                chain_ref[level + 1, step * 8 + j] = held[j]
        return carry

    lax.fori_loop(0, PAIRS // 8, exponentials, 0)

    eye2 = twice
    inverse_root_col = 1.0 / root_col

    def transition(p):
        return inverse_root_col * (chain_ref[4, p] + eye2) * root_row

    def finish(p, message):
        message_ref[p] = message
        raw = message[0:64] * message[64:128]
        scaling = jnp.sum(raw, axis=0, keepdims=True)
        inverse = 1.0 / scaling
        scale_ref[pl.ds(p, 1), :] = scaling
        inverse_ref[pl.ds(p, 1), :] = inverse
        high, low = split(raw * inverse)
        high_ref[p] = high
        low_ref[p] = low

    sites = states_ref.shape[1]
    codon = lax.broadcasted_iota(jnp.int32, (64, sites), 0)

    def leaf_level(step, carry):
        for j in range(4):
            p = step * 4 + j
            both = []
            for e in range(2):
                taxon = order_ref[subtree * LEAF_DEV + 2 * p + e]
                state = jnp.where(
                    gap_ref[pl.ds(taxon, 1), :] > 0, -1, states_ref[pl.ds(taxon, 1), :]
                )
                hit = (codon == state) | (state < 0)
                both.append(jnp.where(hit, 1.0, 0.0).astype(BF))
            leaves = jnp.concatenate(both, axis=0)
            leaf_ref[p] = leaves
            finish(p, per_pair_messages(transition(p), leaves, None))
        return carry

    lax.fori_loop(0, LEAF_DEV // 8, leaf_level, 0)

    def inner(p):
        child = 2 * p - 64
        high = jnp.concatenate([high_ref[child], high_ref[child + 1]], axis=0)
        low = jnp.concatenate([low_ref[child], low_ref[child + 1]], axis=0)
        return per_pair_messages(transition(p), high, low)

    def second_level(step, carry):
        for j in range(4):
            finish(32 + step * 4 + j, inner(32 + step * 4 + j))
        return carry

    lax.fori_loop(0, 4, second_level, 0)
    for p in range(48, 63):
        finish(p, inner(p))
    high_ref[63] = jnp.zeros((64, sites), BF)
    low_ref[63] = jnp.zeros((64, sites), BF)
    scale_ref[63:64, :] = jnp.ones((1, sites), F32)
    inverse_ref[63:64, :] = jnp.ones((1, sites), F32)
    top = inner(63)
    message_ref[63] = top
    top_ref[...] = top[0:64]


def down_kernel(
    total_sites,
    tops_ref, chain_ref, slope_ref, power_ref, message_ref, high_ref, low_ref, leaf_ref,
    scale_ref, inverse_ref, weights_ref, ex_ref, freq_ref, omega_ref, len_ref, cls_ref,
    sense_ref, single_ref, nonsyn_ref,
    out_ref,
    a_high_ref, a_low_ref, count_ref, bins_ref, dot_ref,
):
    subtree = lax.axis_index("branch")
    members = lax.axis_size("branch")
    mask = low_half()
    twice, pi_row, pi_col, root_row, root_col = frequencies(freq_ref, sense_ref)
    inverse_root_row, inverse_root_col = 1.0 / root_row, 1.0 / root_col
    sites = weights_ref.shape[1]
    weight = weights_ref[...].astype(F32)

    above = jnp.broadcast_to(pi_col, (64, sites))
    own = jnp.zeros((64, sites), F32)
    for member in range(members):
        message = tops_ref[member * 64 : member * 64 + 64, :]
        above = jnp.where(subtree == member, above, above * message)
        own = jnp.where(subtree == member, message, own)
    likelihood = jnp.sum(above * own, axis=0, keepdims=True)
    logs = jnp.sum(jnp.log(scale_ref[...]), axis=0, keepdims=True)
    logs = logs + jnp.where(subtree == 0, jnp.log(likelihood), 0.0)
    log_part = jnp.sum(weight * logs, axis=1, keepdims=True)
    high, low = split(above * (weight / (likelihood * total_sites)))
    a_high_ref[31, 0:64, :] = high
    a_low_ref[31, 0:64, :] = low
    a_high_ref[31, 64:128, :] = jnp.zeros((64, sites), BF)
    a_low_ref[31, 64:128, :] = jnp.zeros((64, sites), BF)

    eye2 = twice

    def store_counts(p, square):
        counts = jnp.where(mask, square[0:64], square[64:128])
        count_ref[p] = inverse_root_col * counts * root_row

    def descend(r):
        a_high, a_low = a_high_ref[r - 32], a_low_ref[r - 32]
        child = 2 * r - 64
        u_high = jnp.concatenate([high_ref[child], high_ref[child + 1]], axis=0)
        u_low = jnp.concatenate([low_ref[child], low_ref[child + 1]], axis=0)
        first = mxu_nt(a_high, jnp.concatenate([u_high, u_low], axis=0))
        second = mxu_nt(a_low, u_high)
        store_counts(r, first[:, 0:128] + first[:, 128:256] + second)
        matrix = root_col * (chain_ref[4, r] + eye2) * inverse_root_row
        return per_pair_messages(matrix, a_high, a_low)

    def children(down, e, p):
        vector = down[64 * e : 64 * e + 64]
        inverse = inverse_ref[pl.ds(p, 1), :]
        message = message_ref[p]
        pair = jnp.concatenate(
            [vector * message[64:128] * inverse, vector * message[0:64] * inverse], axis=0
        )
        return split(pair)

    def inner(r):
        down = descend(r)
        for e in range(2):
            p = 2 * r + e - 64
            if isinstance(p, int) and p == 63:
                continue
            high, low = children(down, e, p)
            a_high_ref[p - 32] = high
            a_low_ref[p - 32] = low

    for r in range(63, 47, -1):
        inner(r)

    def leaf_level(step, carry):
        for j in range(2):
            r = 32 + step * 2 + j
            down = descend(r)
            for e in range(2):
                p = 2 * r + e - 64
                high, low = children(down, e, p)
                square = mxu_nt(jnp.concatenate([high, low], axis=0), leaf_ref[p])
                store_counts(p, square[0:128] + square[128:256])
        return carry

    lax.fori_loop(0, 8, leaf_level, 0)

    bins_ref[...] = jnp.zeros_like(bins_ref)

    def adjoint(step, carry):
        held = [count_ref[step * 8 + j] for j in range(8)]
        for level in range(3, -1, -1):
            for j in range(8):
                matrix = chain_ref[level, step * 8 + j]
                held[j] = 2.0 * held[j] + pair_products((held[j], matrix), (matrix, held[j]))
        for j in range(8):
            p = step * 8 + j
            odd = jnp.minimum(2 * p + 1, EDGES - 1)
            y0 = len_ref[2 * p] * 0.0625
            y1 = jnp.where(2 * p + 1 < EDGES, len_ref[odd] * 0.0625, 0.0)
            c0, c1 = cls_ref[2 * p], cls_ref[odd]
            y = jnp.where(lax.broadcasted_iota(jnp.int32, (8, 128), 1) < 64, y0, y1)
            dot_ref[p] = jnp.sum((held[j] * slope_ref[p]).reshape(8, 8, 128), axis=0)
            even = jnp.where(mask, held[j], 0.0)
            other = jnp.where(mask, 0.0, held[j])
            coef = jnp.ones_like(y)
            for k in range(ORDER):
                coef = coef * y * (1.0 / (k + 1))
                bins_ref[c0, k] += even * coef[0:1]
                bins_ref[c1, k] += other * coef[0:1]
        return carry

    lax.fori_loop(0, PAIRS // 8, adjoint, 0)

    table = symmetric_table(ex_ref, single_ref, twice)
    nonsyn = nonsyn_ref[...]
    row = lax.broadcasted_iota(jnp.int32, (64, 128), 0)
    lane = lax.broadcasted_iota(jnp.int32, (64, 128), 1)
    table_grad = jnp.zeros((64, 128), F32)
    omega_row = jnp.zeros((1, 128), F32)
    lane_row = lax.broadcasted_iota(jnp.int32, (1, 128), 1)
    for pair in range(CLASSES // 2):
        grads = []
        for k in range(ORDER):
            first, second = bins_ref[2 * pair, k], bins_ref[2 * pair + 1, k]
            first = first + pltpu.roll(first, 64, 1)
            second = second + pltpu.roll(second, 64, 1)
            grads.append(jnp.where(mask, first, second))
        g1, g2, g3, g4, g5, g6, g7, g8 = grads
        a1, a2, a3, a4 = [power_ref[pair, k] for k in range(4)]
        g4 = g4 + pair_products((g8, a4), (a4, g8), (g7, a3), (g6, a2), (g5, a1))
        g3 = g3 + pair_products((a4, g7))
        g2 = g2 + pair_products((a4, g6))
        g1 = g1 + pair_products((a4, g5))
        g2 = g2 + pair_products((g4, a2), (a2, g4), (g3, a1))
        g1 = g1 + pair_products((a2, g3))
        g1 = g1 + pair_products((g2, a1), (a1, g2))
        factor, off, rows, mean = class_pair(
            table, nonsyn, omega_ref, pair, twice, pi_row, pi_col
        )
        d_rate = root_col * g1 * inverse_root_row
        rate = (off - twice * rows) / mean
        weighted = d_rate * rate
        diagonal = d_rate * twice
        total0 = jnp.sum(jnp.where(mask, weighted, 0.0), axis=1, keepdims=True)
        total1 = jnp.sum(jnp.where(mask, 0.0, weighted), axis=1, keepdims=True)
        total0 = jnp.sum(total0, axis=0, keepdims=True)
        total1 = jnp.sum(total1, axis=0, keepdims=True)
        diag0 = jnp.sum(jnp.where(mask, diagonal, 0.0), axis=1, keepdims=True)
        diag1 = jnp.sum(jnp.where(mask, 0.0, diagonal), axis=1, keepdims=True)
        row_grad = jnp.where(mask, diag0 + pi_col * total0, diag1 + pi_col * total1)
        flux_grad = (d_rate - row_grad) * pi_row / mean
        table_grad = table_grad + flux_grad * factor * single_ref[...]
        ratio = flux_grad * table * nonsyn
        ratio0 = jnp.sum(jnp.where(mask, ratio, 0.0), axis=1, keepdims=True)
        ratio1 = jnp.sum(jnp.where(mask, 0.0, ratio), axis=1, keepdims=True)
        ratio0 = jnp.sum(ratio0, axis=0, keepdims=True)
        ratio1 = jnp.sum(ratio1, axis=0, keepdims=True)
        omega_row = jnp.where(lane_row == 2 * pair, ratio0, omega_row)
        omega_row = jnp.where(lane_row == 2 * pair + 1, ratio1, omega_row)
    table_grad = table_grad + pltpu.roll(table_grad, 64, 1)
    one = table_grad[:, 0:64]
    out_ref[0:64, :] = 0.5 * (exact(one, twice) + exact_tn(one, twice))

    slopes = jnp.sum(dot_ref[...], axis=1) * 0.0625
    even = jnp.sum(jnp.where(mask, slopes, 0.0), axis=1, keepdims=True)
    other = jnp.sum(jnp.where(mask, 0.0, slopes), axis=1, keepdims=True)
    placed = jnp.where(lane == 2 * row, even, 0.0) + jnp.where(lane == 2 * row + 1, other, 0.0)
    length_row = jnp.sum(placed, axis=0, keepdims=True)
    line = lax.broadcasted_iota(jnp.int32, (8, 128), 0)
    tail = jnp.where(line == subtree, length_row, 0.0)
    tail = tail + jnp.where(line == members, omega_row, 0.0)
    tail = tail + jnp.where(line == members + 1, log_part, 0.0)
    out_ref[64:72, :] = tail


def body(
    total_sites, states, gap_mask, weights, leaf_order, exchanges, codon_freq, omega_ratio,
    lengths, classes,
):
    sites = states.shape[1]
    members = lax.axis_size("branch")
    sense, single, nonsyn = codon_tables()
    sense2 = jnp.asarray(np.tile(sense[None, :], (1, 2)))
    single2 = jnp.asarray(np.tile(single, (1, 2)))
    nonsyn2 = jnp.asarray(np.tile(nonsyn, (1, 2)))
    freq = codon_freq.reshape(1, 64)
    vmem = pl.BlockSpec(memory_space=pltpu.VMEM)
    smem = pl.BlockSpec(memory_space=pltpu.SMEM)
    shape = jax.ShapeDtypeStruct
    top, *kept = pl.pallas_call(
        up_kernel,
        out_shape=[
            shape((64, sites), F32),
            shape((5, PAIRS, 64, 128), F32),
            shape((PAIRS, 64, 128), F32),
            shape((CLASSES // 2, 4, 64, 128), F32),
            shape((PAIRS, 128, sites), F32),
            shape((64, 64, sites), BF),
            shape((64, 64, sites), BF),
            shape((32, 128, sites), BF),
            shape((64, sites), F32),
            shape((64, sites), F32),
        ],
        in_specs=[vmem, vmem, smem, vmem, vmem, smem, smem, smem, vmem, vmem, vmem],
        out_specs=[vmem] * 10,
        scratch_shapes=[pltpu.VMEM((CLASSES, ORDER, 64, 128), F32)],
        compiler_params=pltpu.CompilerParams(vmem_limit_bytes=56 * 2**20),
        name="up",
    )(
        states, gap_mask, leaf_order, exchanges, freq, omega_ratio, lengths, classes,
        sense2, single2, nonsyn2,
    )
    tops = lax.all_gather(top, "branch", axis=0, tiled=True)
    part = pl.pallas_call(
        functools.partial(down_kernel, total_sites),
        out_shape=shape((72, 128), F32),
        in_specs=[vmem] * 13 + [smem] * 3 + [vmem] * 3,
        out_specs=vmem,
        scratch_shapes=[
            pltpu.VMEM((32, 128, sites), BF),
            pltpu.VMEM((32, 128, sites), BF),
            pltpu.VMEM((PAIRS, 64, 128), F32),
            pltpu.VMEM((CLASSES, ORDER, 64, 128), F32),
            pltpu.VMEM((PAIRS, 8, 128), F32),
        ],
        compiler_params=pltpu.CompilerParams(vmem_limit_bytes=56 * 2**20),
        name="down",
    )(
        tops, *kept, weights.reshape(1, sites), exchanges, freq, omega_ratio, lengths, classes,
        sense2, single2, nonsyn2,
    )
    total = lax.psum(part, ("site", "branch"))
    length_out = lax.dynamic_slice_in_dim(total, 64 + lax.axis_index("branch"), 1, 0)[0, :EDGES]
    loglik = total[64 + members + 1, 0] / total_sites / (LEAF_DEV * members)
    return (total[0:64, 0:64], total[64 + members, 0:CLASSES], length_out, loglik)


def solution(mesh):
    def whole(states, *rest):
        total_sites = states.shape[1]
        return jax.shard_map(
            functools.partial(body, total_sites),
            mesh=mesh,
            in_specs=(
                P(None, "site"),
                P(None, "site"),
                P("site"),
                P(),
                P(),
                P(),
                P(),
                P("branch"),
                P("branch"),
            ),
            out_specs=(P(), P(), P("branch"), P()),
            check_vma=False,
        )(states, *rest)

    return whole
```

```python
import functools
import jax
import jax.numpy as jnp
import numpy as np
from jax import lax
from jax.experimental import pallas as pl
from jax.experimental.pallas import tpu as pltpu
from jax.sharding import PartitionSpec as P

LEAF_DEV = 64
EDGES = 127
PAIRS = 64
CLASSES = 8
ORDER = 8
BF = jnp.bfloat16
F32 = jnp.float32

CODE_TABLE = "FFLLSSSSYYXXCCXWLLLLPPPPHHQQRRRRIIIMTTTTNNKKSSRRVVVVAAAADDEEGGGG"


def codon_tables():
    amino_acid = np.array(list(CODE_TABLE))
    codon_index = np.arange(64)
    digits = np.stack([codon_index // 16, codon_index // 4 % 4, codon_index % 4], 1)
    differ = (digits[:, None, :] != digits[None, :, :]).sum(-1)
    is_sense = amino_acid != "X"
    single = (differ == 1) & is_sense[:, None] & is_sense[None, :]
    nonsyn = single & (amino_acid[:, None] != amino_acid[None, :])
    return (is_sense.astype(np.float32), single.astype(np.float32), nonsyn.astype(np.float32))


def low_half():
    return lax.broadcasted_iota(jnp.int32, (64, 128), 1) < 64


def split(x):
    high = x.astype(BF)
    low = (x - high.astype(F32)).astype(BF)
    return high, low


def spread(x):
    mask = low_half()
    zero = jnp.zeros_like(x)
    return jnp.concatenate([jnp.where(mask, x, zero), jnp.where(mask, zero, x)], axis=0)


def mxu(left, right):
    return jnp.dot(left, right, preferred_element_type=F32)


def mxu_nt(left, right):
    return lax.dot_general(left, right, (((1,), (1,)), ((), ())), preferred_element_type=F32)


def exact(left, right):
    return jnp.dot(left, right, preferred_element_type=F32, precision=lax.Precision.HIGHEST)


def exact_tn(left, right):
    return lax.dot_general(
        left, right, (((0,), (0,)), ((), ())), preferred_element_type=F32,
        precision=lax.Precision.HIGHEST,
    )


def pair_products(*terms):
    lefts, rights = [], []
    for left, right in terms:
        left_high, left_low = split(left)
        right_high, right_low = split(right)
        wide_high, wide_low = spread(right_high), spread(right_low)
        lefts += [left_high, left_high, left_low]
        rights += [wide_high, wide_low, wide_high]
    return mxu(jnp.concatenate(lefts, axis=1), jnp.concatenate(rights, axis=0))


def per_pair_messages(matrix, high, low):
    matrix_high, matrix_low = split(matrix)
    wide_high, wide_low = spread(matrix_high), spread(matrix_low)
    if low is None:
        return mxu(
            jnp.concatenate([wide_high, wide_low], axis=1), jnp.concatenate([high, high], axis=0)
        )
    return mxu(
        jnp.concatenate([wide_high, wide_high, wide_low], axis=1),
        jnp.concatenate([high, low, high], axis=0),
    )


def frequencies(freq_ref, sense_ref):
    row = lax.broadcasted_iota(jnp.int32, (64, 128), 0)
    lane = lax.broadcasted_iota(jnp.int32, (64, 128), 1)
    twice = (row == lane % 64).astype(F32)
    sense2 = sense_ref[...]
    freq2 = exact(jnp.broadcast_to(freq_ref[...], (8, 64)), twice)[0:1] * sense2
    total = 0.5 * jnp.sum(freq2, axis=1, keepdims=True)
    pi_row = freq2 / total
    pi_col = 0.5 * jnp.sum(twice * pi_row, axis=1, keepdims=True)
    sense_col = 0.5 * jnp.sum(twice * sense2, axis=1, keepdims=True)
    root_row = jnp.sqrt(jnp.where(sense2 > 0, pi_row, 1.0))
    root_col = jnp.sqrt(jnp.where(sense_col > 0, pi_col, 1.0))
    return twice, pi_row, pi_col, root_row, root_col


def symmetric_table(ex_ref, single_ref, twice):
    ex = ex_ref[...]
    return 0.5 * (exact(ex, twice) + exact_tn(ex, twice)) * single_ref[...]


def class_pair(table, nonsyn, omega_ref, pair, twice, pi_row, pi_col):
    mask = low_half()
    omega = jnp.where(mask, omega_ref[2 * pair], omega_ref[2 * pair + 1])
    factor = 1.0 + nonsyn * (omega - 1.0)
    flux = table * factor
    off = flux * pi_row
    row0 = jnp.sum(jnp.where(mask, off, 0.0), axis=1, keepdims=True)
    row1 = jnp.sum(jnp.where(mask, 0.0, off), axis=1, keepdims=True)
    mean0 = jnp.sum(pi_col * row0, axis=0, keepdims=True)
    mean1 = jnp.sum(pi_col * row1, axis=0, keepdims=True)
    rows = jnp.where(mask, row0, row1)
    mean = jnp.where(mask, mean0, mean1)
    return factor, off, rows, mean


def neighbours():
    row = lax.broadcasted_iota(jnp.int32, (64, 128), 0)
    lane = lax.broadcasted_iota(jnp.int32, (64, 128), 1) % 64
    masks = [
        row % 16 == lane % 16,
        (row // 16 == lane // 16) & (row % 4 == lane % 4),
        row // 4 == lane // 4,
    ]
    codon = lax.broadcasted_iota(jnp.int32, (64, 16), 0)
    column = lax.broadcasted_iota(jnp.int32, (64, 16), 1)
    digits = [codon // 16, codon // 4 % 4, codon % 4]
    picks = [(column == 4 * p + digits[p]).astype(F32) for p in range(3)]
    return masks, picks


def up_kernel(
    states_ref, gap_ref, order_ref, ex_ref, freq_ref, omega_ref, len_ref, cls_ref,
    sense_ref, single_ref, nonsyn_ref,
    top_ref, chain_ref, slope_ref, power_ref, message_ref, high_ref, low_ref, leaf_ref,
    scale_ref, inverse_ref, dup_ref,
):
    subtree = lax.axis_index("branch")
    mask = low_half()
    twice, pi_row, pi_col, root_row, root_col = frequencies(freq_ref, sense_ref)
    table = symmetric_table(ex_ref, single_ref, twice)
    nonsyn = nonsyn_ref[...]

    powers = []
    for pair in range(CLASSES // 2):
        factor, off, rows, mean = class_pair(
            table, nonsyn, omega_ref, pair, twice, pi_row, pi_col
        )
        powers.append([(table * factor * root_col * root_row - twice * rows) / mean])
    for left, right in ((0, 0), (1, 0), (1, 1), (3, 0), (3, 1), (3, 2), (3, 3)):
        for pair in range(CLASSES // 2):
            powers[pair].append(pair_products((powers[pair][left], powers[pair][right])))
    for pair in range(CLASSES // 2):
        for k in range(ORDER):
            value = powers[pair][k]
            swapped = pltpu.roll(value, 64, 1)
            dup_ref[2 * pair, k] = jnp.where(mask, value, swapped)
            dup_ref[2 * pair + 1, k] = jnp.where(mask, swapped, value)
            if k < 4:
                power_ref[pair, k] = value

    def exponentials(step, carry):
        held = []
        for j in range(8):
            p = step * 8 + j
            odd = jnp.minimum(2 * p + 1, EDGES - 1)
            y0 = len_ref[2 * p] * 0.0625
            y1 = jnp.where(2 * p + 1 < EDGES, len_ref[odd] * 0.0625, 0.0)
            c0, c1 = cls_ref[2 * p], cls_ref[odd]
            y = jnp.where(lax.broadcasted_iota(jnp.int32, (8, 128), 1) < 64, y0, y1)
            slope_coef = jnp.ones_like(y)
            value = slope = None
            for k in range(ORDER):
                coef = slope_coef * y * (1.0 / (k + 1))
                matrix = jnp.where(mask, dup_ref[c0, k], dup_ref[c1, k])
                first, second = matrix * coef[0:1], matrix * slope_coef[0:1]
                value = first if k == 0 else value + first
                slope = second if k == 0 else slope + second
                slope_coef = coef
            chain_ref[0, p] = value
            slope_ref[p] = slope
            held.append(value)
        for level in range(4):
            for j in range(8):
                held[j] = 2.0 * held[j] + pair_products((held[j], held[j]))
                chain_ref[level + 1, step * 8 + j] = held[j]
        return carry

    lax.fori_loop(0, PAIRS // 8, exponentials, 0)

    eye2 = twice
    inverse_root_col = 1.0 / root_col

    def transition(p):
        return inverse_root_col * (chain_ref[4, p] + eye2) * root_row

    def finish(p, message):
        message_ref[p] = message
        raw = message[0:64] * message[64:128]
        scaling = jnp.sum(raw, axis=0, keepdims=True)
        inverse = 1.0 / scaling
        scale_ref[pl.ds(p, 1), :] = scaling
        inverse_ref[pl.ds(p, 1), :] = inverse
        high, low = split(raw * inverse)
        high_ref[p] = high
        low_ref[p] = low

    sites = states_ref.shape[1]
    codon = lax.broadcasted_iota(jnp.int32, (64, sites), 0)

    def leaf_level(step, carry):
        for j in range(4):
            p = step * 4 + j
            both = []
            for e in range(2):
                taxon = order_ref[subtree * LEAF_DEV + 2 * p + e]
                state = jnp.where(
                    gap_ref[pl.ds(taxon, 1), :] > 0, -1, states_ref[pl.ds(taxon, 1), :]
                )
                hit = (codon == state) | (state < 0)
                both.append(jnp.where(hit, 1.0, 0.0).astype(BF))
            leaves = jnp.concatenate(both, axis=0)
            leaf_ref[p] = leaves
            finish(p, per_pair_messages(transition(p), leaves, None))
        return carry

    lax.fori_loop(0, LEAF_DEV // 8, leaf_level, 0)

    def inner(p):
        child = 2 * p - 64
        high = jnp.concatenate([high_ref[child], high_ref[child + 1]], axis=0)
        low = jnp.concatenate([low_ref[child], low_ref[child + 1]], axis=0)
        return per_pair_messages(transition(p), high, low)

    def second_level(step, carry):
        for j in range(4):
            finish(32 + step * 4 + j, inner(32 + step * 4 + j))
        return carry

    lax.fori_loop(0, 4, second_level, 0)
    for p in range(48, 63):
        finish(p, inner(p))
    high_ref[63] = jnp.zeros((64, sites), BF)
    low_ref[63] = jnp.zeros((64, sites), BF)
    scale_ref[63:64, :] = jnp.ones((1, sites), F32)
    inverse_ref[63:64, :] = jnp.ones((1, sites), F32)
    top = inner(63)
    message_ref[63] = top
    top_ref[...] = top[0:64]


def down_kernel(
    total_sites,
    tops_ref, chain_ref, slope_ref, power_ref, message_ref, high_ref, low_ref, leaf_ref,
    scale_ref, inverse_ref, weights_ref, ex_ref, freq_ref, omega_ref, len_ref, cls_ref,
    sense_ref, single_ref, nonsyn_ref,
    out_ref,
    a_high_ref, a_low_ref, count_ref, bins_ref, dot_ref,
):
    subtree = lax.axis_index("branch")
    members = lax.axis_size("branch")
    mask = low_half()
    twice, pi_row, pi_col, root_row, root_col = frequencies(freq_ref, sense_ref)
    inverse_root_row, inverse_root_col = 1.0 / root_row, 1.0 / root_col
    sites = weights_ref.shape[1]
    weight = weights_ref[...].astype(F32)

    above = jnp.broadcast_to(pi_col, (64, sites))
    own = jnp.zeros((64, sites), F32)
    for member in range(members):
        message = tops_ref[member * 64 : member * 64 + 64, :]
        above = jnp.where(subtree == member, above, above * message)
        own = jnp.where(subtree == member, message, own)
    likelihood = jnp.sum(above * own, axis=0, keepdims=True)
    logs = jnp.sum(jnp.log(scale_ref[...]), axis=0, keepdims=True)
    logs = logs + jnp.where(subtree == 0, jnp.log(likelihood), 0.0)
    log_part = jnp.sum(weight * logs, axis=1, keepdims=True)
    high, low = split(above * (weight / (likelihood * total_sites)))
    a_high_ref[31, 0:64, :] = high
    a_low_ref[31, 0:64, :] = low
    a_high_ref[31, 64:128, :] = jnp.zeros((64, sites), BF)
    a_low_ref[31, 64:128, :] = jnp.zeros((64, sites), BF)

    eye2 = twice

    def store_counts(p, square):
        counts = jnp.where(mask, square[0:64], square[64:128])
        count_ref[p] = inverse_root_col * counts * root_row

    def descend(r):
        a_high, a_low = a_high_ref[r - 32], a_low_ref[r - 32]
        child = 2 * r - 64
        u_high = jnp.concatenate([high_ref[child], high_ref[child + 1]], axis=0)
        u_low = jnp.concatenate([low_ref[child], low_ref[child + 1]], axis=0)
        first = mxu_nt(a_high, jnp.concatenate([u_high, u_low], axis=0))
        second = mxu_nt(a_low, u_high)
        store_counts(r, first[:, 0:128] + first[:, 128:256] + second)
        matrix = root_col * (chain_ref[4, r] + eye2) * inverse_root_row
        return per_pair_messages(matrix, a_high, a_low)

    def children(down, e, p):
        vector = down[64 * e : 64 * e + 64]
        inverse = inverse_ref[pl.ds(p, 1), :]
        message = message_ref[p]
        pair = jnp.concatenate(
            [vector * message[64:128] * inverse, vector * message[0:64] * inverse], axis=0
        )
        return split(pair)

    def inner(r):
        down = descend(r)
        for e in range(2):
            p = 2 * r + e - 64
            if isinstance(p, int) and p == 63:
                continue
            high, low = children(down, e, p)
            a_high_ref[p - 32] = high
            a_low_ref[p - 32] = low

    for r in range(63, 47, -1):
        inner(r)

    def leaf_level(step, carry):
        for j in range(2):
            r = 32 + step * 2 + j
            down = descend(r)
            for e in range(2):
                p = 2 * r + e - 64
                high, low = children(down, e, p)
                square = mxu_nt(jnp.concatenate([high, low], axis=0), leaf_ref[p])
                store_counts(p, square[0:128] + square[128:256])
        return carry

    lax.fori_loop(0, 8, leaf_level, 0)

    bins_ref[...] = jnp.zeros_like(bins_ref)

    def adjoint(step, carry):
        held = [count_ref[step * 8 + j] for j in range(8)]
        for level in range(3, -1, -1):
            for j in range(8):
                matrix = chain_ref[level, step * 8 + j]
                held[j] = 2.0 * held[j] + pair_products((held[j], matrix), (matrix, held[j]))
        for j in range(8):
            p = step * 8 + j
            odd = jnp.minimum(2 * p + 1, EDGES - 1)
            y0 = len_ref[2 * p] * 0.0625
            y1 = jnp.where(2 * p + 1 < EDGES, len_ref[odd] * 0.0625, 0.0)
            c0, c1 = cls_ref[2 * p], cls_ref[odd]
            y = jnp.where(lax.broadcasted_iota(jnp.int32, (8, 128), 1) < 64, y0, y1)
            dot_ref[p] = jnp.sum((held[j] * slope_ref[p]).reshape(8, 8, 128), axis=0)
            even = jnp.where(mask, held[j], 0.0)
            other = jnp.where(mask, 0.0, held[j])
            coef = jnp.ones_like(y)
            for k in range(ORDER):
                coef = coef * y * (1.0 / (k + 1))
                bins_ref[c0, k] += even * coef[0:1]
                bins_ref[c1, k] += other * coef[0:1]
        return carry

    lax.fori_loop(0, PAIRS // 8, adjoint, 0)

    table = symmetric_table(ex_ref, single_ref, twice)
    nonsyn = nonsyn_ref[...]
    row = lax.broadcasted_iota(jnp.int32, (64, 128), 0)
    lane = lax.broadcasted_iota(jnp.int32, (64, 128), 1)
    table_grad = jnp.zeros((64, 128), F32)
    omega_row = jnp.zeros((1, 128), F32)
    lane_row = lax.broadcasted_iota(jnp.int32, (1, 128), 1)
    for pair in range(CLASSES // 2):
        grads = []
        for k in range(ORDER):
            first, second = bins_ref[2 * pair, k], bins_ref[2 * pair + 1, k]
            first = first + pltpu.roll(first, 64, 1)
            second = second + pltpu.roll(second, 64, 1)
            grads.append(jnp.where(mask, first, second))
        g1, g2, g3, g4, g5, g6, g7, g8 = grads
        a1, a2, a3, a4 = [power_ref[pair, k] for k in range(4)]
        g4 = g4 + pair_products((g8, a4), (a4, g8), (g7, a3), (g6, a2), (g5, a1))
        g3 = g3 + pair_products((a4, g7))
        g2 = g2 + pair_products((a4, g6))
        g1 = g1 + pair_products((a4, g5))
        g2 = g2 + pair_products((g4, a2), (a2, g4), (g3, a1))
        g1 = g1 + pair_products((a2, g3))
        g1 = g1 + pair_products((g2, a1), (a1, g2))
        factor, off, rows, mean = class_pair(
            table, nonsyn, omega_ref, pair, twice, pi_row, pi_col
        )
        d_rate = root_col * g1 * inverse_root_row
        rate = (off - twice * rows) / mean
        weighted = d_rate * rate
        diagonal = d_rate * twice
        total0 = jnp.sum(jnp.where(mask, weighted, 0.0), axis=1, keepdims=True)
        total1 = jnp.sum(jnp.where(mask, 0.0, weighted), axis=1, keepdims=True)
        total0 = jnp.sum(total0, axis=0, keepdims=True)
        total1 = jnp.sum(total1, axis=0, keepdims=True)
        diag0 = jnp.sum(jnp.where(mask, diagonal, 0.0), axis=1, keepdims=True)
        diag1 = jnp.sum(jnp.where(mask, 0.0, diagonal), axis=1, keepdims=True)
        row_grad = jnp.where(mask, diag0 + pi_col * total0, diag1 + pi_col * total1)
        flux_grad = (d_rate - row_grad) * pi_row / mean
        table_grad = table_grad + flux_grad * factor * single_ref[...]
        ratio = flux_grad * table * nonsyn
        ratio0 = jnp.sum(jnp.where(mask, ratio, 0.0), axis=1, keepdims=True)
        ratio1 = jnp.sum(jnp.where(mask, 0.0, ratio), axis=1, keepdims=True)
        ratio0 = jnp.sum(ratio0, axis=0, keepdims=True)
        ratio1 = jnp.sum(ratio1, axis=0, keepdims=True)
        omega_row = jnp.where(lane_row == 2 * pair, ratio0, omega_row)
        omega_row = jnp.where(lane_row == 2 * pair + 1, ratio1, omega_row)
    table_grad = table_grad + pltpu.roll(table_grad, 64, 1)
    one = table_grad[:, 0:64]
    both = 0.5 * (exact(one, twice) + exact_tn(one, twice))
    masks, picks = neighbours()
    packed = jnp.zeros((16, 128), F32)
    for at_position, pick in zip(masks, picks):
        packed = packed + exact_tn(pick, jnp.where(at_position, both, 0.0))
    packed = jnp.where(lax.broadcasted_iota(jnp.int32, (16, 128), 1) < 64, packed, 0.0)

    slopes = jnp.sum(dot_ref[...], axis=1) * 0.0625
    even = jnp.sum(jnp.where(mask, slopes, 0.0), axis=1, keepdims=True)
    other = jnp.sum(jnp.where(mask, 0.0, slopes), axis=1, keepdims=True)
    placed = jnp.where(lane == 2 * row, even, 0.0) + jnp.where(lane == 2 * row + 1, other, 0.0)
    length_row = jnp.sum(placed, axis=0, keepdims=True)
    line = lax.broadcasted_iota(jnp.int32, out_ref.shape, 0)
    omega_row = jnp.where(lane_row == CLASSES, log_part, omega_row)
    omega_row = pltpu.roll(jnp.broadcast_to(omega_row, (8, 128)), 64, 1)[0:1]
    packed = packed + jnp.where(line == 0, omega_row, 0.0)
    out_ref[...] = packed + jnp.where(line == 12 + subtree, length_row, 0.0)


def last_kernel(total_sites, parts_ref, exch_ref, omega_ref, length_ref, log_ref):
    members = lax.axis_size("branch")
    subtree = lax.axis_index("branch")
    devices = parts_ref.shape[0]
    total = parts_ref[0]
    for device in range(1, devices):
        total = total + parts_ref[device]
    masks, picks = neighbours()
    table = jnp.zeros((64, 128), F32)
    for at_position, pick in zip(masks, picks):
        table = table + jnp.where(at_position, exact(pick, total), 0.0)
    exch_ref[...] = table[:, 0:64]
    moved = pltpu.roll(total[0:8], 64, 1)
    omega_ref[...] = moved[0:1, 0:CLASSES]
    line = lax.broadcasted_iota(jnp.int32, total.shape, 0)
    lengths = jnp.sum(jnp.where(line == 12 + subtree, total, 0.0), axis=0, keepdims=True)
    length_ref[...] = lengths[:, 0:EDGES]
    log_ref[...] = moved[0:1, CLASSES : CLASSES + 1] / total_sites / (LEAF_DEV * members)


def body(
    total_sites, states, gap_mask, weights, leaf_order, exchanges, codon_freq, omega_ratio,
    lengths, classes,
):
    sites = states.shape[1]
    members = lax.axis_size("branch")
    sense, single, nonsyn = codon_tables()
    sense2 = jnp.asarray(np.tile(sense[None, :], (1, 2)))
    single2 = jnp.asarray(np.tile(single, (1, 2)))
    nonsyn2 = jnp.asarray(np.tile(nonsyn, (1, 2)))
    freq = codon_freq.reshape(1, 64)
    vmem = pl.BlockSpec(memory_space=pltpu.VMEM)
    smem = pl.BlockSpec(memory_space=pltpu.SMEM)
    shape = jax.ShapeDtypeStruct
    held = pltpu.VMEM
    top, *kept = pl.pallas_call(
        up_kernel,
        out_shape=[
            shape((64, sites), F32),
            held((5, PAIRS, 64, 128), F32),
            held((PAIRS, 64, 128), F32),
            held((CLASSES // 2, 4, 64, 128), F32),
            held((PAIRS, 128, sites), F32),
            held((64, 64, sites), BF),
            held((64, 64, sites), BF),
            held((32, 128, sites), BF),
            held((64, sites), F32),
            held((64, sites), F32),
        ],
        in_specs=[vmem, vmem, smem, vmem, vmem, smem, smem, smem, vmem, vmem, vmem],
        out_specs=[vmem] * 10,
        scratch_shapes=[pltpu.VMEM((CLASSES, ORDER, 64, 128), F32)],
        compiler_params=pltpu.CompilerParams(vmem_limit_bytes=28 * 2**20),
        name="up",
    )(
        states, gap_mask, leaf_order, exchanges, freq, omega_ratio, lengths, classes,
        sense2, single2, nonsyn2,
    )
    kept = [pltpu.with_memory_space_constraint(x, pltpu.VMEM) for x in kept]
    tops = lax.all_gather(top, "branch", axis=0, tiled=True)
    part = pl.pallas_call(
        functools.partial(down_kernel, total_sites),
        out_shape=shape((16, 128), F32),
        in_specs=[vmem] * 13 + [smem] * 3 + [vmem] * 3,
        out_specs=vmem,
        scratch_shapes=[
            pltpu.VMEM((32, 128, sites), BF),
            pltpu.VMEM((32, 128, sites), BF),
            pltpu.VMEM((PAIRS, 64, 128), F32),
            pltpu.VMEM((CLASSES, ORDER, 64, 128), F32),
            pltpu.VMEM((PAIRS, 8, 128), F32),
        ],
        compiler_params=pltpu.CompilerParams(vmem_limit_bytes=28 * 2**20),
        name="down",
    )(
        tops, *kept, weights.reshape(1, sites), exchanges, freq, omega_ratio, lengths, classes,
        sense2, single2, nonsyn2,
    )
    parts = lax.all_gather(part, ("site", "branch"), axis=0)
    exch, omega, length, loglik = pl.pallas_call(
        functools.partial(last_kernel, total_sites),
        out_shape=[shape((64, 64), F32), shape((1, CLASSES), F32), shape((1, EDGES), F32), shape((1, 1), F32)],
        in_specs=[vmem],
        out_specs=[vmem] * 4,
        compiler_params=pltpu.CompilerParams(vmem_limit_bytes=24 * 2**20),
        name="last",
    )(parts)
    return (exch, omega.reshape(CLASSES), length.reshape(EDGES), loglik.reshape(()))


def solution(mesh):
    def whole(states, *rest):
        total_sites = states.shape[1]
        return jax.shard_map(
            functools.partial(body, total_sites),
            mesh=mesh,
            in_specs=(
                P(None, "site"),
                P(None, "site"),
                P("site"),
                P(),
                P(),
                P(),
                P(),
                P("branch"),
                P("branch"),
            ),
            out_specs=(P(), P(), P("branch"), P()),
            check_vma=False,
        )(states, *rest)

    return whole
```

```python
import functools
import jax
import jax.numpy as jnp
import numpy as np
from jax import lax
from jax.experimental import pallas as pl
from jax.experimental.pallas import tpu as pltpu
from jax.sharding import PartitionSpec as P

LEAF_DEV = 64
EDGES = 127
PAIRS = 64
CLASSES = 8
ORDER = 8
BF = jnp.bfloat16
F32 = jnp.float32

CODE_TABLE = "FFLLSSSSYYXXCCXWLLLLPPPPHHQQRRRRIIIMTTTTNNKKSSRRVVVVAAAADDEEGGGG"


def codon_tables():
    amino_acid = np.array(list(CODE_TABLE))
    codon_index = np.arange(64)
    digits = np.stack([codon_index // 16, codon_index // 4 % 4, codon_index % 4], 1)
    differ = (digits[:, None, :] != digits[None, :, :]).sum(-1)
    is_sense = amino_acid != "X"
    single = (differ == 1) & is_sense[:, None] & is_sense[None, :]
    nonsyn = single & (amino_acid[:, None] != amino_acid[None, :])
    return (is_sense.astype(np.float32), single.astype(np.float32), nonsyn.astype(np.float32))


def low_half():
    return lax.broadcasted_iota(jnp.int32, (64, 128), 1) < 64


def split(x):
    high = x.astype(BF)
    low = (x - high.astype(F32)).astype(BF)
    return high, low


def spread(x):
    mask = low_half()
    zero = jnp.zeros_like(x)
    return jnp.concatenate([jnp.where(mask, x, zero), jnp.where(mask, zero, x)], axis=0)


def mxu(left, right):
    return jnp.dot(left, right, preferred_element_type=F32)


def mxu_nt(left, right):
    return lax.dot_general(left, right, (((1,), (1,)), ((), ())), preferred_element_type=F32)


def exact(left, right):
    return jnp.dot(left, right, preferred_element_type=F32, precision=lax.Precision.HIGHEST)


def exact_tn(left, right):
    return lax.dot_general(
        left, right, (((0,), (0,)), ((), ())), preferred_element_type=F32,
        precision=lax.Precision.HIGHEST,
    )


def pair_products(*terms):
    lefts, rights = [], []
    for left, right in terms:
        left_high, left_low = split(left)
        right_high, right_low = split(right)
        wide_high, wide_low = spread(right_high), spread(right_low)
        lefts += [left_high, left_high, left_low]
        rights += [wide_high, wide_low, wide_high]
    return mxu(jnp.concatenate(lefts, axis=1), jnp.concatenate(rights, axis=0))


def per_pair_messages(matrix, high, low):
    matrix_high, matrix_low = split(matrix)
    wide_high, wide_low = spread(matrix_high), spread(matrix_low)
    if low is None:
        return mxu(
            jnp.concatenate([wide_high, wide_low], axis=1), jnp.concatenate([high, high], axis=0)
        )
    return mxu(
        jnp.concatenate([wide_high, wide_high, wide_low], axis=1),
        jnp.concatenate([high, low, high], axis=0),
    )


def frequencies(freq_ref, sense_ref):
    row = lax.broadcasted_iota(jnp.int32, (64, 128), 0)
    lane = lax.broadcasted_iota(jnp.int32, (64, 128), 1)
    twice = (row == lane % 64).astype(F32)
    sense2 = sense_ref[...]
    freq2 = exact(jnp.broadcast_to(freq_ref[...], (8, 64)), twice)[0:1] * sense2
    total = 0.5 * jnp.sum(freq2, axis=1, keepdims=True)
    pi_row = freq2 / total
    pi_col = 0.5 * jnp.sum(twice * pi_row, axis=1, keepdims=True)
    sense_col = 0.5 * jnp.sum(twice * sense2, axis=1, keepdims=True)
    root_row = jnp.sqrt(jnp.where(sense2 > 0, pi_row, 1.0))
    root_col = jnp.sqrt(jnp.where(sense_col > 0, pi_col, 1.0))
    return twice, pi_row, pi_col, root_row, root_col


def symmetric_table(ex_ref, single_ref, twice):
    ex = ex_ref[...]
    return 0.5 * (exact(ex, twice) + exact_tn(ex, twice)) * single_ref[...]


def class_pair(table, nonsyn, omega_ref, pair, twice, pi_row, pi_col):
    mask = low_half()
    omega = jnp.where(mask, omega_ref[2 * pair], omega_ref[2 * pair + 1])
    factor = 1.0 + nonsyn * (omega - 1.0)
    flux = table * factor
    off = flux * pi_row
    row0 = jnp.sum(jnp.where(mask, off, 0.0), axis=1, keepdims=True)
    row1 = jnp.sum(jnp.where(mask, 0.0, off), axis=1, keepdims=True)
    mean0 = jnp.sum(pi_col * row0, axis=0, keepdims=True)
    mean1 = jnp.sum(pi_col * row1, axis=0, keepdims=True)
    rows = jnp.where(mask, row0, row1)
    mean = jnp.where(mask, mean0, mean1)
    return factor, off, rows, mean


def neighbours():
    row = lax.broadcasted_iota(jnp.int32, (64, 128), 0)
    lane = lax.broadcasted_iota(jnp.int32, (64, 128), 1) % 64
    masks = [
        row % 16 == lane % 16,
        (row // 16 == lane // 16) & (row % 4 == lane % 4),
        row // 4 == lane // 4,
    ]
    codon = lax.broadcasted_iota(jnp.int32, (64, 16), 0)
    column = lax.broadcasted_iota(jnp.int32, (64, 16), 1)
    digits = [codon // 16, codon // 4 % 4, codon % 4]
    picks = [(column == 4 * p + digits[p]).astype(F32) for p in range(3)]
    return masks, picks


def up_kernel(
    states_ref, gap_ref, order_ref, ex_ref, freq_ref, omega_ref, len_ref, cls_ref,
    sense_ref, single_ref, nonsyn_ref,
    top_ref, chain_ref, slope_ref, power_ref, message_ref, high_ref, low_ref, leaf_ref,
    scale_ref, inverse_ref, dup_ref,
):
    subtree = lax.axis_index("branch")
    mask = low_half()
    twice, pi_row, pi_col, root_row, root_col = frequencies(freq_ref, sense_ref)
    table = symmetric_table(ex_ref, single_ref, twice)
    nonsyn = nonsyn_ref[...]

    powers = []
    for pair in range(CLASSES // 2):
        factor, off, rows, mean = class_pair(
            table, nonsyn, omega_ref, pair, twice, pi_row, pi_col
        )
        powers.append([(table * factor * root_col * root_row - twice * rows) / mean])
    for left, right in ((0, 0), (1, 0), (1, 1), (3, 0), (3, 1), (3, 2), (3, 3)):
        for pair in range(CLASSES // 2):
            powers[pair].append(pair_products((powers[pair][left], powers[pair][right])))
    for pair in range(CLASSES // 2):
        for k in range(ORDER):
            value = powers[pair][k]
            swapped = pltpu.roll(value, 64, 1)
            dup_ref[2 * pair, k] = jnp.where(mask, value, swapped)
            dup_ref[2 * pair + 1, k] = jnp.where(mask, swapped, value)
            if k < 4:
                power_ref[pair, k] = value

    def exponentials(step, carry):
        held = []
        for j in range(8):
            p = step * 8 + j
            odd = jnp.minimum(2 * p + 1, EDGES - 1)
            y0 = len_ref[2 * p] * 0.0625
            y1 = jnp.where(2 * p + 1 < EDGES, len_ref[odd] * 0.0625, 0.0)
            c0, c1 = cls_ref[2 * p], cls_ref[odd]
            y = jnp.where(lax.broadcasted_iota(jnp.int32, (8, 128), 1) < 64, y0, y1)
            slope_coef = jnp.ones_like(y)
            value = slope = None
            for k in range(ORDER):
                coef = slope_coef * y * (1.0 / (k + 1))
                matrix = jnp.where(mask, dup_ref[c0, k], dup_ref[c1, k])
                first, second = matrix * coef[0:1], matrix * slope_coef[0:1]
                value = first if k == 0 else value + first
                slope = second if k == 0 else slope + second
                slope_coef = coef
            chain_ref[0, p] = value
            slope_ref[p] = slope
            held.append(value)
        for level in range(4):
            for j in range(8):
                held[j] = 2.0 * held[j] + pair_products((held[j], held[j]))
                chain_ref[level + 1, step * 8 + j] = held[j]
        return carry

    lax.fori_loop(0, PAIRS // 8, exponentials, 0)

    eye2 = twice
    inverse_root_col = 1.0 / root_col

    def transition(p):
        return inverse_root_col * (chain_ref[4, p] + eye2) * root_row

    def finish(p, message):
        message_ref[p] = message
        raw = message[0:64] * message[64:128]
        scaling = jnp.sum(raw, axis=0, keepdims=True)
        inverse = 1.0 / scaling
        scale_ref[pl.ds(p, 1), :] = scaling
        inverse_ref[pl.ds(p, 1), :] = inverse
        high, low = split(raw * inverse)
        high_ref[p] = high
        low_ref[p] = low

    sites = states_ref.shape[1]
    codon = lax.broadcasted_iota(jnp.int32, (64, sites), 0)

    def leaf_level(step, carry):
        for j in range(4):
            p = step * 4 + j
            both = []
            for e in range(2):
                taxon = order_ref[subtree * LEAF_DEV + 2 * p + e]
                state = jnp.where(
                    gap_ref[pl.ds(taxon, 1), :] > 0, -1, states_ref[pl.ds(taxon, 1), :]
                )
                hit = (codon == state) | (state < 0)
                both.append(jnp.where(hit, 1.0, 0.0).astype(BF))
            leaves = jnp.concatenate(both, axis=0)
            leaf_ref[p] = leaves
            finish(p, per_pair_messages(transition(p), leaves, None))
        return carry

    lax.fori_loop(0, LEAF_DEV // 8, leaf_level, 0)

    def inner(p):
        child = 2 * p - 64
        high = jnp.concatenate([high_ref[child], high_ref[child + 1]], axis=0)
        low = jnp.concatenate([low_ref[child], low_ref[child + 1]], axis=0)
        return per_pair_messages(transition(p), high, low)

    def second_level(step, carry):
        for j in range(4):
            finish(32 + step * 4 + j, inner(32 + step * 4 + j))
        return carry

    lax.fori_loop(0, 4, second_level, 0)
    for p in range(48, 63):
        finish(p, inner(p))
    high_ref[63] = jnp.zeros((64, sites), BF)
    low_ref[63] = jnp.zeros((64, sites), BF)
    scale_ref[63:64, :] = jnp.ones((1, sites), F32)
    inverse_ref[63:64, :] = jnp.ones((1, sites), F32)
    top = inner(63)
    message_ref[63] = top
    top_ref[...] = top[0:64]


def down_kernel(total_sites, members, *refs):
    tops, refs = refs[:members], refs[members:]
    (
        chain_ref, slope_ref, power_ref, message_ref, high_ref, low_ref, leaf_ref,
    scale_ref, inverse_ref, weights_ref, ex_ref, freq_ref, omega_ref, len_ref, cls_ref,
    sense_ref, single_ref, nonsyn_ref,
    out_ref,
    a_high_ref, a_low_ref, count_ref, bins_ref, dot_ref,
    ) = refs
    subtree = lax.axis_index("branch")
    mask = low_half()
    twice, pi_row, pi_col, root_row, root_col = frequencies(freq_ref, sense_ref)
    inverse_root_row, inverse_root_col = 1.0 / root_row, 1.0 / root_col
    sites = weights_ref.shape[1]
    weight = weights_ref[...].astype(F32)

    above = jnp.broadcast_to(pi_col, (64, sites))
    for other in tops[1:]:
        above = above * other[...]
    own = tops[0][...]
    likelihood = jnp.sum(above * own, axis=0, keepdims=True)
    logs = jnp.sum(jnp.log(scale_ref[...]), axis=0, keepdims=True)
    logs = logs + jnp.where(subtree == 0, jnp.log(likelihood), 0.0)
    log_part = jnp.sum(weight * logs, axis=1, keepdims=True)
    high, low = split(above * (weight / (likelihood * total_sites)))
    a_high_ref[31, 0:64, :] = high
    a_low_ref[31, 0:64, :] = low
    a_high_ref[31, 64:128, :] = jnp.zeros((64, sites), BF)
    a_low_ref[31, 64:128, :] = jnp.zeros((64, sites), BF)

    eye2 = twice

    def store_counts(p, square):
        counts = jnp.where(mask, square[0:64], square[64:128])
        count_ref[p] = inverse_root_col * counts * root_row

    def descend(r):
        a_high, a_low = a_high_ref[r - 32], a_low_ref[r - 32]
        child = 2 * r - 64
        u_high = jnp.concatenate([high_ref[child], high_ref[child + 1]], axis=0)
        u_low = jnp.concatenate([low_ref[child], low_ref[child + 1]], axis=0)
        first = mxu_nt(a_high, jnp.concatenate([u_high, u_low], axis=0))
        second = mxu_nt(a_low, u_high)
        store_counts(r, first[:, 0:128] + first[:, 128:256] + second)
        matrix = root_col * (chain_ref[4, r] + eye2) * inverse_root_row
        return per_pair_messages(matrix, a_high, a_low)

    def children(down, e, p):
        vector = down[64 * e : 64 * e + 64]
        inverse = inverse_ref[pl.ds(p, 1), :]
        message = message_ref[p]
        pair = jnp.concatenate(
            [vector * message[64:128] * inverse, vector * message[0:64] * inverse], axis=0
        )
        return split(pair)

    def inner(r):
        down = descend(r)
        for e in range(2):
            p = 2 * r + e - 64
            if isinstance(p, int) and p == 63:
                continue
            high, low = children(down, e, p)
            a_high_ref[p - 32] = high
            a_low_ref[p - 32] = low

    for r in range(63, 47, -1):
        inner(r)

    def leaf_level(step, carry):
        for j in range(2):
            r = 32 + step * 2 + j
            down = descend(r)
            for e in range(2):
                p = 2 * r + e - 64
                high, low = children(down, e, p)
                square = mxu_nt(jnp.concatenate([high, low], axis=0), leaf_ref[p])
                store_counts(p, square[0:128] + square[128:256])
        return carry

    lax.fori_loop(0, 8, leaf_level, 0)

    bins_ref[...] = jnp.zeros_like(bins_ref)

    def adjoint(step, carry):
        held = [count_ref[step * 8 + j] for j in range(8)]
        for level in range(3, -1, -1):
            for j in range(8):
                matrix = chain_ref[level, step * 8 + j]
                held[j] = 2.0 * held[j] + pair_products((held[j], matrix), (matrix, held[j]))
        for j in range(8):
            p = step * 8 + j
            odd = jnp.minimum(2 * p + 1, EDGES - 1)
            y0 = len_ref[2 * p] * 0.0625
            y1 = jnp.where(2 * p + 1 < EDGES, len_ref[odd] * 0.0625, 0.0)
            c0, c1 = cls_ref[2 * p], cls_ref[odd]
            y = jnp.where(lax.broadcasted_iota(jnp.int32, (8, 128), 1) < 64, y0, y1)
            dot_ref[p] = jnp.sum((held[j] * slope_ref[p]).reshape(8, 8, 128), axis=0)
            even = jnp.where(mask, held[j], 0.0)
            other = jnp.where(mask, 0.0, held[j])
            coef = jnp.ones_like(y)
            for k in range(ORDER):
                coef = coef * y * (1.0 / (k + 1))
                bins_ref[c0, k] += even * coef[0:1]
                bins_ref[c1, k] += other * coef[0:1]
        return carry

    lax.fori_loop(0, PAIRS // 8, adjoint, 0)

    table = symmetric_table(ex_ref, single_ref, twice)
    nonsyn = nonsyn_ref[...]
    row = lax.broadcasted_iota(jnp.int32, (64, 128), 0)
    lane = lax.broadcasted_iota(jnp.int32, (64, 128), 1)
    table_grad = jnp.zeros((64, 128), F32)
    omega_row = jnp.zeros((1, 128), F32)
    lane_row = lax.broadcasted_iota(jnp.int32, (1, 128), 1)
    for pair in range(CLASSES // 2):
        grads = []
        for k in range(ORDER):
            first, second = bins_ref[2 * pair, k], bins_ref[2 * pair + 1, k]
            first = first + pltpu.roll(first, 64, 1)
            second = second + pltpu.roll(second, 64, 1)
            grads.append(jnp.where(mask, first, second))
        g1, g2, g3, g4, g5, g6, g7, g8 = grads
        a1, a2, a3, a4 = [power_ref[pair, k] for k in range(4)]
        g4 = g4 + pair_products((g8, a4), (a4, g8), (g7, a3), (g6, a2), (g5, a1))
        g3 = g3 + pair_products((a4, g7))
        g2 = g2 + pair_products((a4, g6))
        g1 = g1 + pair_products((a4, g5))
        g2 = g2 + pair_products((g4, a2), (a2, g4), (g3, a1))
        g1 = g1 + pair_products((a2, g3))
        g1 = g1 + pair_products((g2, a1), (a1, g2))
        factor, off, rows, mean = class_pair(
            table, nonsyn, omega_ref, pair, twice, pi_row, pi_col
        )
        d_rate = root_col * g1 * inverse_root_row
        rate = (off - twice * rows) / mean
        weighted = d_rate * rate
        diagonal = d_rate * twice
        total0 = jnp.sum(jnp.where(mask, weighted, 0.0), axis=1, keepdims=True)
        total1 = jnp.sum(jnp.where(mask, 0.0, weighted), axis=1, keepdims=True)
        total0 = jnp.sum(total0, axis=0, keepdims=True)
        total1 = jnp.sum(total1, axis=0, keepdims=True)
        diag0 = jnp.sum(jnp.where(mask, diagonal, 0.0), axis=1, keepdims=True)
        diag1 = jnp.sum(jnp.where(mask, 0.0, diagonal), axis=1, keepdims=True)
        row_grad = jnp.where(mask, diag0 + pi_col * total0, diag1 + pi_col * total1)
        flux_grad = (d_rate - row_grad) * pi_row / mean
        table_grad = table_grad + flux_grad * factor * single_ref[...]
        ratio = flux_grad * table * nonsyn
        ratio0 = jnp.sum(jnp.where(mask, ratio, 0.0), axis=1, keepdims=True)
        ratio1 = jnp.sum(jnp.where(mask, 0.0, ratio), axis=1, keepdims=True)
        ratio0 = jnp.sum(ratio0, axis=0, keepdims=True)
        ratio1 = jnp.sum(ratio1, axis=0, keepdims=True)
        omega_row = jnp.where(lane_row == 2 * pair, ratio0, omega_row)
        omega_row = jnp.where(lane_row == 2 * pair + 1, ratio1, omega_row)
    table_grad = table_grad + pltpu.roll(table_grad, 64, 1)
    one = table_grad[:, 0:64]
    both = 0.5 * (exact(one, twice) + exact_tn(one, twice))
    masks, picks = neighbours()
    packed = jnp.zeros((16, 128), F32)
    for at_position, pick in zip(masks, picks):
        packed = packed + exact_tn(pick, jnp.where(at_position, both, 0.0))
    packed = jnp.where(lax.broadcasted_iota(jnp.int32, (16, 128), 1) < 64, packed, 0.0)

    slopes = jnp.sum(dot_ref[...], axis=1) * 0.0625
    even = jnp.sum(jnp.where(mask, slopes, 0.0), axis=1, keepdims=True)
    other = jnp.sum(jnp.where(mask, 0.0, slopes), axis=1, keepdims=True)
    placed = jnp.where(lane == 2 * row, even, 0.0) + jnp.where(lane == 2 * row + 1, other, 0.0)
    length_row = jnp.sum(placed, axis=0, keepdims=True)
    line = lax.broadcasted_iota(jnp.int32, out_ref.shape, 0)
    omega_row = jnp.where(lane_row == CLASSES, log_part, omega_row)
    omega_row = pltpu.roll(jnp.broadcast_to(omega_row, (8, 128)), 64, 1)[0:1]
    packed = packed + jnp.where(line == 0, omega_row, 0.0)
    out_ref[...] = packed + jnp.where(line == 12 + subtree, length_row, 0.0)


def last_kernel(total_sites, count, *refs):
    members = lax.axis_size("branch")
    subtree = lax.axis_index("branch")
    exch_ref, omega_ref, length_ref, log_ref = refs[count:]
    total = tree_sum([ref[...] for ref in refs[:count]])
    masks, picks = neighbours()
    table = jnp.zeros((64, 128), F32)
    for at_position, pick in zip(masks, picks):
        table = table + jnp.where(at_position, exact(pick, total), 0.0)
    exch_ref[...] = table[:, 0:64]
    moved = pltpu.roll(total[0:8], 64, 1)
    omega_ref[...] = moved[0:1, 0:CLASSES]
    line = lax.broadcasted_iota(jnp.int32, total.shape, 0)
    lengths = jnp.sum(jnp.where(line == 12 + subtree, total, 0.0), axis=0, keepdims=True)
    length_ref[...] = lengths[:, 0:EDGES]
    log_ref[...] = moved[0:1, CLASSES : CLASSES + 1] / total_sites / (LEAF_DEV * members)


def partners(x, axis, start, radix):
    size = lax.axis_size(axis)
    others = [
        lax.ppermute(x, axis, [(i, i ^ (step * start)) for i in range(size)])
        for step in range(1, radix)
    ]
    return [x] + others


def tree_sum(parts):
    while len(parts) > 1:
        parts = [parts[i] + parts[i + 1] for i in range(0, len(parts), 2)]
    return parts[0]


def axis_steps(axis):
    size, start, steps = lax.axis_size(axis), 1, []
    while start < size:
        radix = min(8, size // start)
        steps.append((axis, start, radix))
        start *= radix
    return steps


def body(
    total_sites, states, gap_mask, weights, leaf_order, exchanges, codon_freq, omega_ratio,
    lengths, classes,
):
    sites = states.shape[1]
    members = lax.axis_size("branch")
    sense, single, nonsyn = codon_tables()
    sense2 = jnp.asarray(np.tile(sense[None, :], (1, 2)))
    single2 = jnp.asarray(np.tile(single, (1, 2)))
    nonsyn2 = jnp.asarray(np.tile(nonsyn, (1, 2)))
    freq = codon_freq.reshape(1, 64)
    vmem = pl.BlockSpec(memory_space=pltpu.VMEM)
    smem = pl.BlockSpec(memory_space=pltpu.SMEM)
    shape = jax.ShapeDtypeStruct
    held = pltpu.VMEM
    top, *kept = pl.pallas_call(
        up_kernel,
        out_shape=[
            shape((64, sites), F32),
            held((5, PAIRS, 64, 128), F32),
            held((PAIRS, 64, 128), F32),
            held((CLASSES // 2, 4, 64, 128), F32),
            held((PAIRS, 128, sites), F32),
            held((64, 64, sites), BF),
            held((64, 64, sites), BF),
            held((32, 128, sites), BF),
            held((64, sites), F32),
            held((64, sites), F32),
        ],
        in_specs=[vmem, vmem, smem, vmem, vmem, smem, smem, smem, vmem, vmem, vmem],
        out_specs=[vmem] * 10,
        scratch_shapes=[pltpu.VMEM((CLASSES, ORDER, 64, 128), F32)],
        compiler_params=pltpu.CompilerParams(vmem_limit_bytes=28 * 2**20),
        name="up",
    )(
        states, gap_mask, leaf_order, exchanges, freq, omega_ratio, lengths, classes,
        sense2, single2, nonsyn2,
    )
    kept = [pltpu.with_memory_space_constraint(x, pltpu.VMEM) for x in kept]
    tops = partners(top, "branch", 1, members)
    part = pl.pallas_call(
        functools.partial(down_kernel, total_sites, members),
        out_shape=shape((16, 128), F32),
        in_specs=[vmem] * (12 + members) + [smem] * 3 + [vmem] * 3,
        out_specs=vmem,
        scratch_shapes=[
            pltpu.VMEM((32, 128, sites), BF),
            pltpu.VMEM((32, 128, sites), BF),
            pltpu.VMEM((PAIRS, 64, 128), F32),
            pltpu.VMEM((CLASSES, ORDER, 64, 128), F32),
            pltpu.VMEM((PAIRS, 8, 128), F32),
        ],
        compiler_params=pltpu.CompilerParams(vmem_limit_bytes=28 * 2**20),
        name="down",
    )(
        *tops, *kept, weights.reshape(1, sites), exchanges, freq, omega_ratio, lengths, classes,
        sense2, single2, nonsyn2,
    )
    steps = axis_steps("branch") + axis_steps("site")
    for step in steps[:-1]:
        part = tree_sum(partners(part, *step))
    parts = partners(part, *steps[-1])
    exch, omega, length, loglik = pl.pallas_call(
        functools.partial(last_kernel, total_sites, len(parts)),
        out_shape=[shape((64, 64), F32), shape((1, CLASSES), F32), shape((1, EDGES), F32), shape((1, 1), F32)],
        in_specs=[vmem] * len(parts),
        out_specs=[vmem] * 4,
        compiler_params=pltpu.CompilerParams(vmem_limit_bytes=24 * 2**20),
        name="last",
    )(*parts)
    return (exch, omega.reshape(CLASSES), length.reshape(EDGES), loglik.reshape(()))


def solution(mesh):
    def whole(states, *rest):
        total_sites = states.shape[1]
        return jax.shard_map(
            functools.partial(body, total_sites),
            mesh=mesh,
            in_specs=(
                P(None, "site"),
                P(None, "site"),
                P("site"),
                P(),
                P(),
                P(),
                P(),
                P("branch"),
                P("branch"),
            ),
            out_specs=(P(), P(), P("branch"), P()),
            check_vma=False,
        )(states, *rest)

    return whole
```

```python
import functools
import jax
import jax.numpy as jnp
import numpy as np
from jax import lax
from jax.experimental import pallas as pl
from jax.experimental.pallas import tpu as pltpu
from jax.sharding import PartitionSpec as P

LEAF_DEV = 64
EDGES = 127
PAIRS = 64
CLASSES = 8
ORDER = 8
BF = jnp.bfloat16
F32 = jnp.float32

CODE_TABLE = "FFLLSSSSYYXXCCXWLLLLPPPPHHQQRRRRIIIMTTTTNNKKSSRRVVVVAAAADDEEGGGG"


def codon_tables():
    amino_acid = np.array(list(CODE_TABLE))
    codon_index = np.arange(64)
    digits = np.stack([codon_index // 16, codon_index // 4 % 4, codon_index % 4], 1)
    differ = (digits[:, None, :] != digits[None, :, :]).sum(-1)
    is_sense = amino_acid != "X"
    single = (differ == 1) & is_sense[:, None] & is_sense[None, :]
    nonsyn = single & (amino_acid[:, None] != amino_acid[None, :])
    return (is_sense.astype(np.float32), single.astype(np.float32), nonsyn.astype(np.float32))


def low_half():
    return lax.broadcasted_iota(jnp.int32, (64, 128), 1) < 64


def split(x):
    high = x.astype(BF)
    low = (x - high.astype(F32)).astype(BF)
    return high, low


def spread(x):
    mask = low_half()
    zero = jnp.zeros_like(x)
    return jnp.concatenate([jnp.where(mask, x, zero), jnp.where(mask, zero, x)], axis=0)


def mxu(left, right):
    return jnp.dot(left, right, preferred_element_type=F32)


def mxu_nt(left, right):
    return lax.dot_general(left, right, (((1,), (1,)), ((), ())), preferred_element_type=F32)


def exact(left, right):
    return jnp.dot(left, right, preferred_element_type=F32, precision=lax.Precision.HIGHEST)


def exact_tn(left, right):
    return lax.dot_general(
        left, right, (((0,), (0,)), ((), ())), preferred_element_type=F32,
        precision=lax.Precision.HIGHEST,
    )


def pair_products(*terms):
    lefts, rights = [], []
    for left, right in terms:
        left_high, left_low = split(left)
        right_high, right_low = split(right)
        wide_high, wide_low = spread(right_high), spread(right_low)
        lefts += [left_high, left_high, left_low]
        rights += [wide_high, wide_low, wide_high]
    return mxu(jnp.concatenate(lefts, axis=1), jnp.concatenate(rights, axis=0))


def per_pair_messages(matrix, high, low):
    matrix_high, matrix_low = split(matrix)
    wide_high, wide_low = spread(matrix_high), spread(matrix_low)
    if low is None:
        return mxu(
            jnp.concatenate([wide_high, wide_low], axis=1), jnp.concatenate([high, high], axis=0)
        )
    return mxu(
        jnp.concatenate([wide_high, wide_high, wide_low], axis=1),
        jnp.concatenate([high, low, high], axis=0),
    )


def frequencies(freq_ref, sense_ref):
    row = lax.broadcasted_iota(jnp.int32, (64, 128), 0)
    lane = lax.broadcasted_iota(jnp.int32, (64, 128), 1)
    twice = (row == lane % 64).astype(F32)
    sense2 = sense_ref[...]
    freq2 = exact(jnp.broadcast_to(freq_ref[...], (8, 64)), twice)[0:1] * sense2
    total = 0.5 * jnp.sum(freq2, axis=1, keepdims=True)
    pi_row = freq2 / total
    pi_col = 0.5 * jnp.sum(twice * pi_row, axis=1, keepdims=True)
    sense_col = 0.5 * jnp.sum(twice * sense2, axis=1, keepdims=True)
    root_row = jnp.sqrt(jnp.where(sense2 > 0, pi_row, 1.0))
    root_col = jnp.sqrt(jnp.where(sense_col > 0, pi_col, 1.0))
    return twice, pi_row, pi_col, root_row, root_col


def symmetric_table(ex_ref, single_ref, twice):
    ex = ex_ref[...]
    return 0.5 * (exact(ex, twice) + exact_tn(ex, twice)) * single_ref[...]


def class_pair(table, nonsyn, omega_ref, pair, twice, pi_row, pi_col):
    mask = low_half()
    omega = jnp.where(mask, omega_ref[2 * pair], omega_ref[2 * pair + 1])
    factor = 1.0 + nonsyn * (omega - 1.0)
    flux = table * factor
    off = flux * pi_row
    row0 = jnp.sum(jnp.where(mask, off, 0.0), axis=1, keepdims=True)
    row1 = jnp.sum(jnp.where(mask, 0.0, off), axis=1, keepdims=True)
    mean0 = jnp.sum(pi_col * row0, axis=0, keepdims=True)
    mean1 = jnp.sum(pi_col * row1, axis=0, keepdims=True)
    rows = jnp.where(mask, row0, row1)
    mean = jnp.where(mask, mean0, mean1)
    return factor, off, rows, mean


def neighbours():
    row = lax.broadcasted_iota(jnp.int32, (64, 128), 0)
    lane = lax.broadcasted_iota(jnp.int32, (64, 128), 1) % 64
    masks = [
        row % 16 == lane % 16,
        (row // 16 == lane // 16) & (row % 4 == lane % 4),
        row // 4 == lane // 4,
    ]
    codon = lax.broadcasted_iota(jnp.int32, (64, 16), 0)
    column = lax.broadcasted_iota(jnp.int32, (64, 16), 1)
    digits = [codon // 16, codon // 4 % 4, codon % 4]
    picks = [(column == 4 * p + digits[p]).astype(F32) for p in range(3)]
    return masks, picks


def up_kernel(
    states_ref, gap_ref, order_ref, ex_ref, freq_ref, omega_ref, len_ref, cls_ref,
    sense_ref, single_ref, nonsyn_ref,
    top_ref, chain_ref, slope_ref, power_ref, message_ref, high_ref, low_ref, leaf_ref,
    scale_ref, inverse_ref, dup_ref,
):
    subtree = lax.axis_index("branch")
    mask = low_half()
    twice, pi_row, pi_col, root_row, root_col = frequencies(freq_ref, sense_ref)
    table = symmetric_table(ex_ref, single_ref, twice)
    nonsyn = nonsyn_ref[...]

    powers = []
    for pair in range(CLASSES // 2):
        factor, off, rows, mean = class_pair(
            table, nonsyn, omega_ref, pair, twice, pi_row, pi_col
        )
        powers.append([(table * factor * root_col * root_row - twice * rows) / mean])
    for left, right in ((0, 0), (1, 0), (1, 1), (3, 0), (3, 1), (3, 2), (3, 3)):
        for pair in range(CLASSES // 2):
            powers[pair].append(pair_products((powers[pair][left], powers[pair][right])))
    for pair in range(CLASSES // 2):
        for k in range(ORDER):
            value = powers[pair][k]
            swapped = pltpu.roll(value, 64, 1)
            dup_ref[2 * pair, k] = jnp.where(mask, value, swapped)
            dup_ref[2 * pair + 1, k] = jnp.where(mask, swapped, value)
            if k < 4:
                power_ref[pair, k] = value

    def exponentials(step, carry):
        held = []
        for j in range(8):
            p = step * 8 + j
            odd = jnp.minimum(2 * p + 1, EDGES - 1)
            y0 = len_ref[2 * p] * 0.0625
            y1 = jnp.where(2 * p + 1 < EDGES, len_ref[odd] * 0.0625, 0.0)
            c0, c1 = cls_ref[2 * p], cls_ref[odd]
            y = jnp.where(lax.broadcasted_iota(jnp.int32, (8, 128), 1) < 64, y0, y1)
            slope_coef = jnp.ones_like(y)
            value = slope = None
            for k in range(ORDER):
                coef = slope_coef * y * (1.0 / (k + 1))
                matrix = jnp.where(mask, dup_ref[c0, k], dup_ref[c1, k])
                first, second = matrix * coef[0:1], matrix * slope_coef[0:1]
                value = first if k == 0 else value + first
                slope = second if k == 0 else slope + second
                slope_coef = coef
            chain_ref[0, p] = value
            slope_ref[p] = slope
            held.append(value)
        for level in range(4):
            for j in range(8):
                held[j] = 2.0 * held[j] + pair_products((held[j], held[j]))
                chain_ref[level + 1, step * 8 + j] = held[j]
        return carry

    lax.fori_loop(0, PAIRS // 8, exponentials, 0)

    eye2 = twice
    inverse_root_col = 1.0 / root_col

    def transition(p):
        return inverse_root_col * (chain_ref[4, p] + eye2) * root_row

    def finish(p, message):
        message_ref[p] = message
        raw = message[0:64] * message[64:128]
        scaling = jnp.sum(raw, axis=0, keepdims=True)
        inverse = 1.0 / scaling
        scale_ref[pl.ds(p, 1), :] = scaling
        inverse_ref[pl.ds(p, 1), :] = inverse
        high, low = split(raw * inverse)
        high_ref[p] = high
        low_ref[p] = low

    sites = states_ref.shape[1]
    codon = lax.broadcasted_iota(jnp.int32, (64, sites), 0)

    def leaf_level(step, carry):
        for j in range(4):
            p = step * 4 + j
            both = []
            for e in range(2):
                taxon = order_ref[subtree * LEAF_DEV + 2 * p + e]
                state = jnp.where(
                    gap_ref[pl.ds(taxon, 1), :] > 0, -1, states_ref[pl.ds(taxon, 1), :]
                )
                hit = (codon == state) | (state < 0)
                both.append(jnp.where(hit, 1.0, 0.0).astype(BF))
            leaves = jnp.concatenate(both, axis=0)
            leaf_ref[p] = leaves
            finish(p, per_pair_messages(transition(p), leaves, None))
        return carry

    lax.fori_loop(0, LEAF_DEV // 8, leaf_level, 0)

    def inner(p):
        child = 2 * p - 64
        high = jnp.concatenate([high_ref[child], high_ref[child + 1]], axis=0)
        low = jnp.concatenate([low_ref[child], low_ref[child + 1]], axis=0)
        return per_pair_messages(transition(p), high, low)

    def second_level(step, carry):
        for j in range(4):
            finish(32 + step * 4 + j, inner(32 + step * 4 + j))
        return carry

    lax.fori_loop(0, 4, second_level, 0)
    for p in range(48, 63):
        finish(p, inner(p))
    high_ref[63] = jnp.zeros((64, sites), BF)
    low_ref[63] = jnp.zeros((64, sites), BF)
    scale_ref[63:64, :] = jnp.ones((1, sites), F32)
    inverse_ref[63:64, :] = jnp.ones((1, sites), F32)
    top = inner(63)
    message_ref[63] = top
    for member in range(top_ref.shape[0]):
        top_ref[member] = top[0:64]


def down_kernel(
    total_sites,
    tops_ref, chain_ref, slope_ref, power_ref, message_ref, high_ref, low_ref, leaf_ref,
    scale_ref, inverse_ref, weights_ref, ex_ref, freq_ref, omega_ref, len_ref, cls_ref,
    sense_ref, single_ref, nonsyn_ref,
    out_ref,
    a_high_ref, a_low_ref, count_ref, bins_ref, dot_ref,
):
    subtree = lax.axis_index("branch")
    mask = low_half()
    twice, pi_row, pi_col, root_row, root_col = frequencies(freq_ref, sense_ref)
    inverse_root_row, inverse_root_col = 1.0 / root_row, 1.0 / root_col
    sites = weights_ref.shape[1]
    weight = weights_ref[...].astype(F32)

    above = jnp.broadcast_to(pi_col, (64, sites))
    own = jnp.zeros((64, sites), F32)
    for member in range(tops_ref.shape[0]):
        message = tops_ref[member]
        above = jnp.where(subtree == member, above, above * message)
        own = jnp.where(subtree == member, message, own)
    likelihood = jnp.sum(above * own, axis=0, keepdims=True)
    logs = jnp.sum(jnp.log(scale_ref[...]), axis=0, keepdims=True)
    logs = logs + jnp.where(subtree == 0, jnp.log(likelihood), 0.0)
    log_part = jnp.sum(weight * logs, axis=1, keepdims=True)
    high, low = split(above * (weight / (likelihood * total_sites)))
    a_high_ref[31, 0:64, :] = high
    a_low_ref[31, 0:64, :] = low
    a_high_ref[31, 64:128, :] = jnp.zeros((64, sites), BF)
    a_low_ref[31, 64:128, :] = jnp.zeros((64, sites), BF)

    eye2 = twice

    def store_counts(p, square):
        counts = jnp.where(mask, square[0:64], square[64:128])
        count_ref[p] = inverse_root_col * counts * root_row

    def descend(r):
        a_high, a_low = a_high_ref[r - 32], a_low_ref[r - 32]
        child = 2 * r - 64
        u_high = jnp.concatenate([high_ref[child], high_ref[child + 1]], axis=0)
        u_low = jnp.concatenate([low_ref[child], low_ref[child + 1]], axis=0)
        first = mxu_nt(a_high, jnp.concatenate([u_high, u_low], axis=0))
        second = mxu_nt(a_low, u_high)
        store_counts(r, first[:, 0:128] + first[:, 128:256] + second)
        matrix = root_col * (chain_ref[4, r] + eye2) * inverse_root_row
        return per_pair_messages(matrix, a_high, a_low)

    def children(down, e, p):
        vector = down[64 * e : 64 * e + 64]
        inverse = inverse_ref[pl.ds(p, 1), :]
        message = message_ref[p]
        pair = jnp.concatenate(
            [vector * message[64:128] * inverse, vector * message[0:64] * inverse], axis=0
        )
        return split(pair)

    def inner(r):
        down = descend(r)
        for e in range(2):
            p = 2 * r + e - 64
            if isinstance(p, int) and p == 63:
                continue
            high, low = children(down, e, p)
            a_high_ref[p - 32] = high
            a_low_ref[p - 32] = low

    for r in range(63, 47, -1):
        inner(r)

    def leaf_level(step, carry):
        for j in range(2):
            r = 32 + step * 2 + j
            down = descend(r)
            for e in range(2):
                p = 2 * r + e - 64
                high, low = children(down, e, p)
                square = mxu_nt(jnp.concatenate([high, low], axis=0), leaf_ref[p])
                store_counts(p, square[0:128] + square[128:256])
        return carry

    lax.fori_loop(0, 8, leaf_level, 0)

    bins_ref[...] = jnp.zeros_like(bins_ref)

    def adjoint(step, carry):
        held = [count_ref[step * 8 + j] for j in range(8)]
        for level in range(3, -1, -1):
            for j in range(8):
                matrix = chain_ref[level, step * 8 + j]
                held[j] = 2.0 * held[j] + pair_products((held[j], matrix), (matrix, held[j]))
        for j in range(8):
            p = step * 8 + j
            odd = jnp.minimum(2 * p + 1, EDGES - 1)
            y0 = len_ref[2 * p] * 0.0625
            y1 = jnp.where(2 * p + 1 < EDGES, len_ref[odd] * 0.0625, 0.0)
            c0, c1 = cls_ref[2 * p], cls_ref[odd]
            y = jnp.where(lax.broadcasted_iota(jnp.int32, (8, 128), 1) < 64, y0, y1)
            dot_ref[p] = jnp.sum((held[j] * slope_ref[p]).reshape(8, 8, 128), axis=0)
            even = jnp.where(mask, held[j], 0.0)
            other = jnp.where(mask, 0.0, held[j])
            coef = jnp.ones_like(y)
            for k in range(ORDER):
                coef = coef * y * (1.0 / (k + 1))
                bins_ref[c0, k] += even * coef[0:1]
                bins_ref[c1, k] += other * coef[0:1]
        return carry

    lax.fori_loop(0, PAIRS // 8, adjoint, 0)

    table = symmetric_table(ex_ref, single_ref, twice)
    nonsyn = nonsyn_ref[...]
    row = lax.broadcasted_iota(jnp.int32, (64, 128), 0)
    lane = lax.broadcasted_iota(jnp.int32, (64, 128), 1)
    table_grad = jnp.zeros((64, 128), F32)
    omega_row = jnp.zeros((1, 128), F32)
    lane_row = lax.broadcasted_iota(jnp.int32, (1, 128), 1)
    for pair in range(CLASSES // 2):
        grads = []
        for k in range(ORDER):
            first, second = bins_ref[2 * pair, k], bins_ref[2 * pair + 1, k]
            first = first + pltpu.roll(first, 64, 1)
            second = second + pltpu.roll(second, 64, 1)
            grads.append(jnp.where(mask, first, second))
        g1, g2, g3, g4, g5, g6, g7, g8 = grads
        a1, a2, a3, a4 = [power_ref[pair, k] for k in range(4)]
        g4 = g4 + pair_products((g8, a4), (a4, g8), (g7, a3), (g6, a2), (g5, a1))
        g3 = g3 + pair_products((a4, g7))
        g2 = g2 + pair_products((a4, g6))
        g1 = g1 + pair_products((a4, g5))
        g2 = g2 + pair_products((g4, a2), (a2, g4), (g3, a1))
        g1 = g1 + pair_products((a2, g3))
        g1 = g1 + pair_products((g2, a1), (a1, g2))
        factor, off, rows, mean = class_pair(
            table, nonsyn, omega_ref, pair, twice, pi_row, pi_col
        )
        d_rate = root_col * g1 * inverse_root_row
        rate = (off - twice * rows) / mean
        weighted = d_rate * rate
        diagonal = d_rate * twice
        total0 = jnp.sum(jnp.where(mask, weighted, 0.0), axis=1, keepdims=True)
        total1 = jnp.sum(jnp.where(mask, 0.0, weighted), axis=1, keepdims=True)
        total0 = jnp.sum(total0, axis=0, keepdims=True)
        total1 = jnp.sum(total1, axis=0, keepdims=True)
        diag0 = jnp.sum(jnp.where(mask, diagonal, 0.0), axis=1, keepdims=True)
        diag1 = jnp.sum(jnp.where(mask, 0.0, diagonal), axis=1, keepdims=True)
        row_grad = jnp.where(mask, diag0 + pi_col * total0, diag1 + pi_col * total1)
        flux_grad = (d_rate - row_grad) * pi_row / mean
        table_grad = table_grad + flux_grad * factor * single_ref[...]
        ratio = flux_grad * table * nonsyn
        ratio0 = jnp.sum(jnp.where(mask, ratio, 0.0), axis=1, keepdims=True)
        ratio1 = jnp.sum(jnp.where(mask, 0.0, ratio), axis=1, keepdims=True)
        ratio0 = jnp.sum(ratio0, axis=0, keepdims=True)
        ratio1 = jnp.sum(ratio1, axis=0, keepdims=True)
        omega_row = jnp.where(lane_row == 2 * pair, ratio0, omega_row)
        omega_row = jnp.where(lane_row == 2 * pair + 1, ratio1, omega_row)
    table_grad = table_grad + pltpu.roll(table_grad, 64, 1)
    one = table_grad[:, 0:64]
    both = 0.5 * (exact(one, twice) + exact_tn(one, twice))
    masks, picks = neighbours()
    packed = jnp.zeros((16, 128), F32)
    for at_position, pick in zip(masks, picks):
        packed = packed + exact_tn(pick, jnp.where(at_position, both, 0.0))
    packed = jnp.where(lax.broadcasted_iota(jnp.int32, (16, 128), 1) < 64, packed, 0.0)

    slopes = jnp.sum(dot_ref[...], axis=1) * 0.0625
    even = jnp.sum(jnp.where(mask, slopes, 0.0), axis=1, keepdims=True)
    other = jnp.sum(jnp.where(mask, 0.0, slopes), axis=1, keepdims=True)
    placed = jnp.where(lane == 2 * row, even, 0.0) + jnp.where(lane == 2 * row + 1, other, 0.0)
    length_row = jnp.sum(placed, axis=0, keepdims=True)
    line = lax.broadcasted_iota(jnp.int32, packed.shape, 0)
    omega_row = jnp.where(lane_row == CLASSES, log_part, omega_row)
    omega_row = pltpu.roll(jnp.broadcast_to(omega_row, (8, 128)), 64, 1)[0:1]
    packed = packed + jnp.where(line == 0, omega_row, 0.0)
    packed = packed + jnp.where(line == 12 + subtree, length_row, 0.0)
    for device in range(out_ref.shape[0]):
        out_ref[device] = packed


def last_kernel(total_sites, parts_ref, exch_ref, omega_ref, length_ref, log_ref):
    members = lax.axis_size("branch")
    subtree = lax.axis_index("branch")
    total = tree_sum([parts_ref[device] for device in range(parts_ref.shape[0])])
    masks, picks = neighbours()
    table = jnp.zeros((64, 128), F32)
    for at_position, pick in zip(masks, picks):
        table = table + jnp.where(at_position, exact(pick, total), 0.0)
    exch_ref[...] = table[:, 0:64]
    moved = pltpu.roll(total[0:8], 64, 1)
    omega_ref[...] = moved[0:1, 0:CLASSES]
    line = lax.broadcasted_iota(jnp.int32, total.shape, 0)
    lengths = jnp.sum(jnp.where(line == 12 + subtree, total, 0.0), axis=0, keepdims=True)
    length_ref[...] = lengths[:, 0:EDGES]
    log_ref[...] = moved[0:1, CLASSES : CLASSES + 1] / total_sites / (LEAF_DEV * members)


def tree_sum(parts):
    while len(parts) > 1:
        parts = [parts[i] + parts[i + 1] for i in range(0, len(parts), 2)]
    return parts[0]


def body(
    total_sites, states, gap_mask, weights, leaf_order, exchanges, codon_freq, omega_ratio,
    lengths, classes,
):
    sites = states.shape[1]
    members = lax.axis_size("branch")
    devices = members * lax.axis_size("site")
    sense, single, nonsyn = codon_tables()
    sense2 = jnp.asarray(np.tile(sense[None, :], (1, 2)))
    single2 = jnp.asarray(np.tile(single, (1, 2)))
    nonsyn2 = jnp.asarray(np.tile(nonsyn, (1, 2)))
    freq = codon_freq.reshape(1, 64)
    vmem = pl.BlockSpec(memory_space=pltpu.VMEM)
    smem = pl.BlockSpec(memory_space=pltpu.SMEM)
    shape = jax.ShapeDtypeStruct
    held = pltpu.VMEM
    top, *kept = pl.pallas_call(
        up_kernel,
        out_shape=[
            shape((members, 64, sites), F32),
            held((5, PAIRS, 64, 128), F32),
            held((PAIRS, 64, 128), F32),
            held((CLASSES // 2, 4, 64, 128), F32),
            held((PAIRS, 128, sites), F32),
            held((64, 64, sites), BF),
            held((64, 64, sites), BF),
            held((32, 128, sites), BF),
            held((64, sites), F32),
            held((64, sites), F32),
        ],
        in_specs=[vmem, vmem, smem, vmem, vmem, smem, smem, smem, vmem, vmem, vmem],
        out_specs=[vmem] * 10,
        scratch_shapes=[pltpu.VMEM((CLASSES, ORDER, 64, 128), F32)],
        compiler_params=pltpu.CompilerParams(vmem_limit_bytes=28 * 2**20),
        name="up",
    )(
        states, gap_mask, leaf_order, exchanges, freq, omega_ratio, lengths, classes,
        sense2, single2, nonsyn2,
    )
    kept = [pltpu.with_memory_space_constraint(x, pltpu.VMEM) for x in kept]
    tops = lax.all_to_all(top, "branch", 0, 0, tiled=True)
    part = pl.pallas_call(
        functools.partial(down_kernel, total_sites),
        out_shape=shape((devices, 16, 128), F32),
        in_specs=[vmem] * 13 + [smem] * 3 + [vmem] * 3,
        out_specs=vmem,
        scratch_shapes=[
            pltpu.VMEM((32, 128, sites), BF),
            pltpu.VMEM((32, 128, sites), BF),
            pltpu.VMEM((PAIRS, 64, 128), F32),
            pltpu.VMEM((CLASSES, ORDER, 64, 128), F32),
            pltpu.VMEM((PAIRS, 8, 128), F32),
        ],
        compiler_params=pltpu.CompilerParams(vmem_limit_bytes=28 * 2**20),
        name="down",
    )(
        tops, *kept, weights.reshape(1, sites), exchanges, freq, omega_ratio, lengths, classes,
        sense2, single2, nonsyn2,
    )
    parts = lax.all_to_all(part, ("site", "branch"), 0, 0, tiled=True)
    exch, omega, length, loglik = pl.pallas_call(
        functools.partial(last_kernel, total_sites),
        out_shape=[shape((64, 64), F32), shape((1, CLASSES), F32), shape((1, EDGES), F32), shape((1, 1), F32)],
        in_specs=[vmem],
        out_specs=[vmem] * 4,
        compiler_params=pltpu.CompilerParams(vmem_limit_bytes=24 * 2**20),
        name="last",
    )(parts)
    return (exch, omega.reshape(CLASSES), length.reshape(EDGES), loglik.reshape(()))


def solution(mesh):
    def whole(states, *rest):
        total_sites = states.shape[1]
        return jax.shard_map(
            functools.partial(body, total_sites),
            mesh=mesh,
            in_specs=(
                P(None, "site"),
                P(None, "site"),
                P("site"),
                P(),
                P(),
                P(),
                P(),
                P("branch"),
                P("branch"),
            ),
            out_specs=(P(), P(), P("branch"), P()),
            check_vma=False,
        )(states, *rest)

    return whole
```

```python
import functools
import jax
import jax.numpy as jnp
import numpy as np
from jax import lax
from jax.experimental import pallas as pl
from jax.experimental.pallas import tpu as pltpu
from jax.sharding import PartitionSpec as P

LEAF_DEV = 64
EDGES = 127
PAIRS = 64
CLASSES = 8
ORDER = 8
BF = jnp.bfloat16
F32 = jnp.float32

CODE_TABLE = "FFLLSSSSYYXXCCXWLLLLPPPPHHQQRRRRIIIMTTTTNNKKSSRRVVVVAAAADDEEGGGG"


def codon_tables():
    amino_acid = np.array(list(CODE_TABLE))
    codon_index = np.arange(64)
    digits = np.stack([codon_index // 16, codon_index // 4 % 4, codon_index % 4], 1)
    differ = (digits[:, None, :] != digits[None, :, :]).sum(-1)
    is_sense = amino_acid != "X"
    single = (differ == 1) & is_sense[:, None] & is_sense[None, :]
    nonsyn = single & (amino_acid[:, None] != amino_acid[None, :])
    return (is_sense.astype(np.float32), single.astype(np.float32), nonsyn.astype(np.float32))


def low_half():
    return lax.broadcasted_iota(jnp.int32, (64, 128), 1) < 64


def split(x):
    high = x.astype(BF)
    low = (x - high.astype(F32)).astype(BF)
    return high, low


def spread(x):
    mask = low_half()
    zero = jnp.zeros_like(x)
    return jnp.concatenate([jnp.where(mask, x, zero), jnp.where(mask, zero, x)], axis=0)


def mxu(left, right):
    return jnp.dot(left, right, preferred_element_type=F32)


def mxu_nt(left, right):
    return lax.dot_general(left, right, (((1,), (1,)), ((), ())), preferred_element_type=F32)


def exact(left, right):
    return jnp.dot(left, right, preferred_element_type=F32, precision=lax.Precision.HIGHEST)


def exact_tn(left, right):
    return lax.dot_general(
        left, right, (((0,), (0,)), ((), ())), preferred_element_type=F32,
        precision=lax.Precision.HIGHEST,
    )


def pair_products(*terms):
    lefts, rights = [], []
    for left, right in terms:
        left_high, left_low = split(left)
        right_high, right_low = split(right)
        wide_high, wide_low = spread(right_high), spread(right_low)
        lefts += [left_high, left_high, left_low]
        rights += [wide_high, wide_low, wide_high]
    return mxu(jnp.concatenate(lefts, axis=1), jnp.concatenate(rights, axis=0))


def per_pair_messages(matrix, high, low):
    matrix_high, matrix_low = split(matrix)
    wide_high, wide_low = spread(matrix_high), spread(matrix_low)
    if low is None:
        return mxu(
            jnp.concatenate([wide_high, wide_low], axis=1), jnp.concatenate([high, high], axis=0)
        )
    return mxu(
        jnp.concatenate([wide_high, wide_high, wide_low], axis=1),
        jnp.concatenate([high, low, high], axis=0),
    )


def frequencies(freq_ref, sense_ref):
    row = lax.broadcasted_iota(jnp.int32, (64, 128), 0)
    lane = lax.broadcasted_iota(jnp.int32, (64, 128), 1)
    twice = (row == lane % 64).astype(F32)
    sense2 = sense_ref[...]
    freq2 = exact(jnp.broadcast_to(freq_ref[...], (8, 64)), twice)[0:1] * sense2
    total = 0.5 * jnp.sum(freq2, axis=1, keepdims=True)
    pi_row = freq2 / total
    pi_col = 0.5 * jnp.sum(twice * pi_row, axis=1, keepdims=True)
    sense_col = 0.5 * jnp.sum(twice * sense2, axis=1, keepdims=True)
    root_row = jnp.sqrt(jnp.where(sense2 > 0, pi_row, 1.0))
    root_col = jnp.sqrt(jnp.where(sense_col > 0, pi_col, 1.0))
    return twice, pi_row, pi_col, root_row, root_col


def symmetric_table(ex_ref, single_ref, twice):
    ex = ex_ref[...]
    return 0.5 * (exact(ex, twice) + exact_tn(ex, twice)) * single_ref[...]


def class_pair(table, nonsyn, omega_ref, pair, twice, pi_row, pi_col):
    mask = low_half()
    omega = jnp.where(mask, omega_ref[2 * pair], omega_ref[2 * pair + 1])
    factor = 1.0 + nonsyn * (omega - 1.0)
    flux = table * factor
    off = flux * pi_row
    row0 = jnp.sum(jnp.where(mask, off, 0.0), axis=1, keepdims=True)
    row1 = jnp.sum(jnp.where(mask, 0.0, off), axis=1, keepdims=True)
    mean0 = jnp.sum(pi_col * row0, axis=0, keepdims=True)
    mean1 = jnp.sum(pi_col * row1, axis=0, keepdims=True)
    rows = jnp.where(mask, row0, row1)
    mean = jnp.where(mask, mean0, mean1)
    return factor, off, rows, mean


def neighbours():
    row = lax.broadcasted_iota(jnp.int32, (64, 128), 0)
    lane = lax.broadcasted_iota(jnp.int32, (64, 128), 1) % 64
    masks = [
        row % 16 == lane % 16,
        (row // 16 == lane // 16) & (row % 4 == lane % 4),
        row // 4 == lane // 4,
    ]
    codon = lax.broadcasted_iota(jnp.int32, (64, 16), 0)
    column = lax.broadcasted_iota(jnp.int32, (64, 16), 1)
    digits = [codon // 16, codon // 4 % 4, codon % 4]
    picks = [(column == 4 * p + digits[p]).astype(F32) for p in range(3)]
    return masks, picks


def coefficients(len_ref, cls_ref):
    lane = lax.broadcasted_iota(jnp.int32, (PAIRS, EDGES), 1)
    row = lax.broadcasted_iota(jnp.int32, (PAIRS, EDGES), 0)
    lengths = len_ref[...] * 0.0625
    classes = cls_ref[...].astype(F32)

    def column(values, odd):
        return jnp.sum(jnp.where(lane == 2 * row + odd, values, 0.0), axis=1, keepdims=True)

    mask = low_half()
    y = jnp.where(mask, column(lengths, 0), column(lengths, 1))
    owner = jnp.where(mask, column(classes, 0), column(classes, 1))
    place = lax.broadcasted_iota(jnp.int32, (PAIRS, 128), 1) % 64
    current = jnp.ones((PAIRS, 128), F32)
    series = slopes = jnp.zeros((PAIRS, 128), F32)
    for k in range(ORDER):
        slopes = jnp.where(place // CLASSES == k, current, slopes)
        current = current * y * (1.0 / (k + 1))
        series = jnp.where(place // CLASSES == k, current, series)
    member = (place % CLASSES).astype(F32) == owner
    return jnp.where(member, series, 0.0), jnp.where(member, slopes, 0.0)


def thrice_left(x):
    high, low = split(x)
    return jnp.concatenate([high, high, low], axis=1)


def thrice_right(x):
    high, low = split(x)
    return jnp.concatenate([high, low, high], axis=0)


def spread_thrice(x):
    high, low = split(x)
    wide_high, wide_low = spread(high), spread(low)
    return jnp.concatenate([wide_high, wide_low, wide_high], axis=0)


def rows_of(step, width):
    return pl.ds(pl.multiple_of(step * width, width), width)


def up_kernel(
    states_ref, gap_ref, order_ref, ex_ref, freq_ref, omega_ref, len_ref, cls_ref,
    sense_ref, single_ref, nonsyn_ref,
    top_ref, chain_ref, last_ref, power_ref, message_ref, high_ref, low_ref, leaf_ref,
    scale_ref, inverse_ref, dup_ref,
    first_ref,
):
    subtree = lax.axis_index("branch")
    mask = low_half()
    twice, pi_row, pi_col, root_row, root_col = frequencies(freq_ref, sense_ref)
    table = symmetric_table(ex_ref, single_ref, twice)
    nonsyn = nonsyn_ref[...]

    powers = []
    for pair in range(CLASSES // 2):
        factor, off, rows, mean = class_pair(
            table, nonsyn, omega_ref, pair, twice, pi_row, pi_col
        )
        powers.append([(table * factor * root_col * root_row - twice * rows) / mean])
    for left, right in ((0, 0), (1, 0), (1, 1), (3, 0), (3, 1), (3, 2), (3, 3)):
        for pair in range(CLASSES // 2):
            powers[pair].append(pair_products((powers[pair][left], powers[pair][right])))
    for pair in range(CLASSES // 2):
        for k in range(ORDER):
            value = powers[pair][k]
            swapped = pltpu.roll(value, 64, 1)
            at = CLASSES * k + 2 * pair
            dup_ref[pl.ds(at, 64, stride=64), :] = jnp.where(mask, value, swapped)
            dup_ref[pl.ds(at + 1, 64, stride=64), :] = jnp.where(mask, swapped, value)
            if k < 4:
                power_ref[pair, k] = value

    series, slopes = coefficients(len_ref, cls_ref)
    left = thrice_left(series)

    def expansions(step, carry):
        for j in range(8):
            i = step * 8 + j
            first_ref[rows_of(i, 64), :] = mxu(left, spread_thrice(dup_ref[rows_of(i, 64), :]))
        return carry

    lax.fori_loop(0, 8, expansions, 0)

    def squarings(step, carry):
        held = [first_ref[pl.ds(step * 8 + j, 64, stride=64), :] for j in range(8)]
        for level in range(4):
            for j in range(8):
                chain_ref[level, step * 8 + j] = held[j]
                held[j] = 2.0 * held[j] + pair_products((held[j], held[j]))
        for j in range(8):
            last_ref[step * 8 + j] = held[j]
        return carry

    lax.fori_loop(0, PAIRS // 8, squarings, 0)

    eye2 = twice
    inverse_root_col = 1.0 / root_col

    def transition(p):
        return inverse_root_col * (last_ref[p] + eye2) * root_row

    def finish(p, message):
        message_ref[p] = message
        raw = message[0:64] * message[64:128]
        scaling = jnp.sum(raw, axis=0, keepdims=True)
        inverse = 1.0 / scaling
        scale_ref[pl.ds(p, 1), :] = scaling
        inverse_ref[pl.ds(p, 1), :] = inverse
        high, low = split(raw * inverse)
        high_ref[p] = high
        low_ref[p] = low

    sites = states_ref.shape[1]
    codon = lax.broadcasted_iota(jnp.int32, (64, sites), 0)

    def leaf_level(step, carry):
        for j in range(4):
            p = step * 4 + j
            both = []
            for e in range(2):
                taxon = order_ref[subtree * LEAF_DEV + 2 * p + e]
                state = jnp.where(
                    gap_ref[pl.ds(taxon, 1), :] > 0, -1, states_ref[pl.ds(taxon, 1), :]
                )
                hit = (codon == state) | (state < 0)
                both.append(jnp.where(hit, 1.0, 0.0).astype(BF))
            leaves = jnp.concatenate(both, axis=0)
            leaf_ref[p] = leaves
            finish(p, per_pair_messages(transition(p), leaves, None))
        return carry

    lax.fori_loop(0, LEAF_DEV // 8, leaf_level, 0)

    def inner(p):
        child = 2 * p - 64
        high = jnp.concatenate([high_ref[child], high_ref[child + 1]], axis=0)
        low = jnp.concatenate([low_ref[child], low_ref[child + 1]], axis=0)
        return per_pair_messages(transition(p), high, low)

    def second_level(step, carry):
        for j in range(4):
            finish(32 + step * 4 + j, inner(32 + step * 4 + j))
        return carry

    lax.fori_loop(0, 4, second_level, 0)
    for p in range(48, 63):
        finish(p, inner(p))
    high_ref[63] = jnp.zeros((64, sites), BF)
    low_ref[63] = jnp.zeros((64, sites), BF)
    scale_ref[63:64, :] = jnp.ones((1, sites), F32)
    inverse_ref[63:64, :] = jnp.ones((1, sites), F32)
    top = inner(63)
    message_ref[63] = top
    top_ref[...] = top[0:64]


def side_kernel(
    dup_ref, last_ref, len_ref, cls_ref, freq_ref, sense_ref, slope_ref, matrix_ref, turned_ref,
):
    twice, pi_row, pi_col, root_row, root_col = frequencies(freq_ref, sense_ref)
    series, slopes = coefficients(len_ref, cls_ref)
    left = thrice_left(slopes)

    def expansions(step, carry):
        for j in range(8):
            i = step * 8 + j
            slope_ref[rows_of(i, 64), :] = mxu(left, spread_thrice(dup_ref[rows_of(i, 64), :]))
        return carry

    lax.fori_loop(0, 8, expansions, 0)
    turned_ref[...] = exact_tn(series, twice[:, 0:64])
    inverse_root_row = 1.0 / root_row

    def matrices(step, carry):
        for j in range(8):
            r = step * 8 + j
            high, low = split(root_col * (last_ref[32 + r] + twice) * inverse_root_row)
            matrix_ref[0, r] = high
            matrix_ref[1, r] = low
        return carry

    lax.fori_loop(0, 4, matrices, 0)


def down_kernel(total_sites, members, *refs):
    tops, refs = refs[:members], refs[members:]
    (
        chain_ref, matrix_ref, turned_ref, slope_ref, power_ref, message_ref, high_ref, low_ref, leaf_ref,
    scale_ref, inverse_ref, weights_ref, ex_ref, freq_ref, omega_ref,
    sense_ref, single_ref, nonsyn_ref,
    out_ref,
    a_high_ref, a_low_ref, count_ref, back_ref, bins_ref,
    ) = refs
    subtree = lax.axis_index("branch")
    mask = low_half()
    twice, pi_row, pi_col, root_row, root_col = frequencies(freq_ref, sense_ref)
    inverse_root_row, inverse_root_col = 1.0 / root_row, 1.0 / root_col
    sites = weights_ref.shape[1]
    weight = weights_ref[...].astype(F32)

    above = jnp.broadcast_to(pi_col, (64, sites))
    for other in tops[1:]:
        above = above * other[...]
    own = tops[0][...]
    likelihood = jnp.sum(above * own, axis=0, keepdims=True)
    logs = jnp.sum(jnp.log(scale_ref[...]), axis=0, keepdims=True)
    logs = logs + jnp.where(subtree == 0, jnp.log(likelihood), 0.0)
    log_part = jnp.sum(weight * logs, axis=1, keepdims=True)
    high, low = split(above * (weight / (likelihood * total_sites)))
    a_high_ref[31, 0:64, :] = high
    a_low_ref[31, 0:64, :] = low
    a_high_ref[31, 64:128, :] = jnp.zeros((64, sites), BF)
    a_low_ref[31, 64:128, :] = jnp.zeros((64, sites), BF)

    def store_counts(p, square):
        counts = jnp.where(mask, square[0:64], square[64:128])
        count_ref[p] = inverse_root_col * counts * root_row

    def descend(r):
        a_high, a_low = a_high_ref[r - 32], a_low_ref[r - 32]
        child = 2 * r - 64
        u_high = jnp.concatenate([high_ref[child], high_ref[child + 1]], axis=0)
        u_low = jnp.concatenate([low_ref[child], low_ref[child + 1]], axis=0)
        first = mxu_nt(a_high, jnp.concatenate([u_high, u_low], axis=0))
        second = mxu_nt(a_low, u_high)
        store_counts(r, first[:, 0:128] + first[:, 128:256] + second)
        wide_high, wide_low = spread(matrix_ref[0, r - 32]), spread(matrix_ref[1, r - 32])
        return mxu(
            jnp.concatenate([wide_high, wide_high, wide_low], axis=1),
            jnp.concatenate([a_high, a_low, a_high], axis=0),
        )

    def children(down, e, p):
        vector = down[64 * e : 64 * e + 64]
        inverse = inverse_ref[pl.ds(p, 1), :]
        message = message_ref[p]
        pair = jnp.concatenate(
            [vector * message[64:128] * inverse, vector * message[0:64] * inverse], axis=0
        )
        return split(pair)

    def inner(r):
        down = descend(r)
        for e in range(2):
            p = 2 * r + e - 64
            if isinstance(p, int) and p == 63:
                continue
            high, low = children(down, e, p)
            a_high_ref[p - 32] = high
            a_low_ref[p - 32] = low

    for r in range(63, 47, -1):
        inner(r)

    def leaf_level(step, carry):
        for j in range(2):
            r = 32 + step * 2 + j
            down = descend(r)
            for e in range(2):
                p = 2 * r + e - 64
                high, low = children(down, e, p)
                square = mxu_nt(jnp.concatenate([high, low], axis=0), leaf_ref[p])
                store_counts(p, square[0:128] + square[128:256])
        return carry

    lax.fori_loop(0, 8, leaf_level, 0)

    def adjoint(step, carry):
        held = [count_ref[step * 8 + j] for j in range(8)]
        for level in range(3, -1, -1):
            for j in range(8):
                matrix = chain_ref[level, step * 8 + j]
                held[j] = 2.0 * held[j] + pair_products((held[j], matrix), (matrix, held[j]))
        for j in range(8):
            back_ref[pl.ds(step * 8 + j, 64, stride=64), :] = held[j]
        return carry

    lax.fori_loop(0, PAIRS // 8, adjoint, 0)

    left = thrice_left(turned_ref[...])

    def sums(step, total):
        for j in range(8):
            at = rows_of(step * 8 + j, 64)
            value = back_ref[at, :]
            total = total + value * slope_ref[at, :]
            both = mxu(left, thrice_right(value))
            bins_ref[at, :] = jnp.where(mask, both[0:64], both[64:128])
        return total

    slopes = lax.fori_loop(0, 8, sums, jnp.zeros((64, 128), F32)) * 0.0625

    table = symmetric_table(ex_ref, single_ref, twice)
    nonsyn = nonsyn_ref[...]
    row = lax.broadcasted_iota(jnp.int32, (64, 128), 0)
    lane = lax.broadcasted_iota(jnp.int32, (64, 128), 1)
    table_grad = jnp.zeros((64, 128), F32)
    omega_row = jnp.zeros((1, 128), F32)
    lane_row = lax.broadcasted_iota(jnp.int32, (1, 128), 1)
    for pair in range(CLASSES // 2):
        grads = []
        for k in range(ORDER):
            at = CLASSES * k + 2 * pair
            first = bins_ref[pl.ds(at, 64, stride=64), :]
            second = bins_ref[pl.ds(at + 1, 64, stride=64), :]
            first = first + pltpu.roll(first, 64, 1)
            second = second + pltpu.roll(second, 64, 1)
            grads.append(jnp.where(mask, first, second))
        g1, g2, g3, g4, g5, g6, g7, g8 = grads
        a1, a2, a3, a4 = [power_ref[pair, k] for k in range(4)]
        g4 = g4 + pair_products((g8, a4), (a4, g8), (g7, a3), (g6, a2), (g5, a1))
        g3 = g3 + pair_products((a4, g7))
        g2 = g2 + pair_products((a4, g6))
        g1 = g1 + pair_products((a4, g5))
        g2 = g2 + pair_products((g4, a2), (a2, g4), (g3, a1))
        g1 = g1 + pair_products((a2, g3))
        g1 = g1 + pair_products((g2, a1), (a1, g2))
        factor, off, rows, mean = class_pair(
            table, nonsyn, omega_ref, pair, twice, pi_row, pi_col
        )
        d_rate = root_col * g1 * inverse_root_row
        rate = (off - twice * rows) / mean
        weighted = d_rate * rate
        diagonal = d_rate * twice
        total0 = jnp.sum(jnp.where(mask, weighted, 0.0), axis=1, keepdims=True)
        total1 = jnp.sum(jnp.where(mask, 0.0, weighted), axis=1, keepdims=True)
        total0 = jnp.sum(total0, axis=0, keepdims=True)
        total1 = jnp.sum(total1, axis=0, keepdims=True)
        diag0 = jnp.sum(jnp.where(mask, diagonal, 0.0), axis=1, keepdims=True)
        diag1 = jnp.sum(jnp.where(mask, 0.0, diagonal), axis=1, keepdims=True)
        row_grad = jnp.where(mask, diag0 + pi_col * total0, diag1 + pi_col * total1)
        flux_grad = (d_rate - row_grad) * pi_row / mean
        table_grad = table_grad + flux_grad * factor * single_ref[...]
        ratio = flux_grad * table * nonsyn
        ratio0 = jnp.sum(jnp.where(mask, ratio, 0.0), axis=1, keepdims=True)
        ratio1 = jnp.sum(jnp.where(mask, 0.0, ratio), axis=1, keepdims=True)
        ratio0 = jnp.sum(ratio0, axis=0, keepdims=True)
        ratio1 = jnp.sum(ratio1, axis=0, keepdims=True)
        omega_row = jnp.where(lane_row == 2 * pair, ratio0, omega_row)
        omega_row = jnp.where(lane_row == 2 * pair + 1, ratio1, omega_row)
    table_grad = table_grad + pltpu.roll(table_grad, 64, 1)
    one = table_grad[:, 0:64]
    both = 0.5 * (exact(one, twice) + exact_tn(one, twice))
    masks, picks = neighbours()
    packed = jnp.zeros((16, 128), F32)
    for at_position, pick in zip(masks, picks):
        packed = packed + exact_tn(pick, jnp.where(at_position, both, 0.0))
    packed = jnp.where(lax.broadcasted_iota(jnp.int32, (16, 128), 1) < 64, packed, 0.0)

    even = jnp.sum(jnp.where(mask, slopes, 0.0), axis=1, keepdims=True)
    other = jnp.sum(jnp.where(mask, 0.0, slopes), axis=1, keepdims=True)
    placed = jnp.where(lane == 2 * row, even, 0.0) + jnp.where(lane == 2 * row + 1, other, 0.0)
    length_row = jnp.sum(placed, axis=0, keepdims=True)
    line = lax.broadcasted_iota(jnp.int32, out_ref.shape, 0)
    omega_row = jnp.where(lane_row == CLASSES, log_part, omega_row)
    omega_row = pltpu.roll(jnp.broadcast_to(omega_row, (8, 128)), 64, 1)[0:1]
    packed = packed + jnp.where(line == 0, omega_row, 0.0)
    out_ref[...] = packed + jnp.where(line == 12 + subtree, length_row, 0.0)


def last_kernel(total_sites, count, *refs):
    members = lax.axis_size("branch")
    subtree = lax.axis_index("branch")
    exch_ref, omega_ref, length_ref, log_ref = refs[count:]
    total = tree_sum([ref[...] for ref in refs[:count]])
    masks, picks = neighbours()
    table = jnp.zeros((64, 128), F32)
    for at_position, pick in zip(masks, picks):
        table = table + jnp.where(at_position, exact(pick, total), 0.0)
    exch_ref[...] = table[:, 0:64]
    moved = pltpu.roll(total[0:8], 64, 1)
    omega_ref[...] = moved[0:1, 0:CLASSES]
    line = lax.broadcasted_iota(jnp.int32, total.shape, 0)
    lengths = jnp.sum(jnp.where(line == 12 + subtree, total, 0.0), axis=0, keepdims=True)
    length_ref[...] = lengths[:, 0:EDGES]
    log_ref[...] = moved[0:1, CLASSES : CLASSES + 1] / total_sites / (LEAF_DEV * members)


def partners(x, axis, start, radix):
    size = lax.axis_size(axis)
    others = [
        lax.ppermute(x, axis, [(i, i ^ (step * start)) for i in range(size)])
        for step in range(1, radix)
    ]
    return [x] + others


def tree_sum(parts):
    while len(parts) > 1:
        parts = [parts[i] + parts[i + 1] for i in range(0, len(parts), 2)]
    return parts[0]


def axis_steps(axis):
    size, start, steps = lax.axis_size(axis), 1, []
    while start < size:
        radix = min(4, size // start)
        steps.append((axis, start, radix))
        start *= radix
    return steps


def body(
    total_sites, states, gap_mask, weights, leaf_order, exchanges, codon_freq, omega_ratio,
    lengths, classes,
):
    sites = states.shape[1]
    members = lax.axis_size("branch")
    sense, single, nonsyn = codon_tables()
    sense2 = jnp.asarray(np.tile(sense[None, :], (1, 2)))
    single2 = jnp.asarray(np.tile(single, (1, 2)))
    nonsyn2 = jnp.asarray(np.tile(nonsyn, (1, 2)))
    freq = codon_freq.reshape(1, 64)
    span, owner = lengths.reshape(1, EDGES), classes.reshape(1, EDGES)
    vmem = pl.BlockSpec(memory_space=pltpu.VMEM)
    smem = pl.BlockSpec(memory_space=pltpu.SMEM)
    shape = jax.ShapeDtypeStruct
    held = pltpu.VMEM
    top, *kept = pl.pallas_call(
        up_kernel,
        out_shape=[
            shape((64, sites), F32),
            held((4, PAIRS, 64, 128), F32),
            held((PAIRS, 64, 128), F32),
            held((CLASSES // 2, 4, 64, 128), F32),
            held((PAIRS, 128, sites), F32),
            held((64, 64, sites), BF),
            held((64, 64, sites), BF),
            held((32, 128, sites), BF),
            held((64, sites), F32),
            held((64, sites), F32),
            held((ORDER * CLASSES * 64, 128), F32),
        ],
        in_specs=[vmem, vmem, smem, vmem, vmem, smem, vmem, vmem, vmem, vmem, vmem],
        out_specs=[vmem] * 11,
        scratch_shapes=[pltpu.VMEM((PAIRS * 64, 128), F32)],
        compiler_params=pltpu.CompilerParams(vmem_limit_bytes=20 * 2**20),
        name="up",
    )(
        states, gap_mask, leaf_order, exchanges, freq, omega_ratio, span, owner,
        sense2, single2, nonsyn2,
    )
    tops = partners(top, "branch", 1, members)
    chain, last, powers, message, high, low, leaf, scale, inverse, dup = [
        pltpu.with_memory_space_constraint(x, pltpu.VMEM) for x in kept
    ]
    side = pl.pallas_call(
        side_kernel,
        out_shape=[
            held((PAIRS * 64, 128), F32),
            held((2, 32, 64, 128), BF),
            held((128, 64), F32),
        ],
        in_specs=[vmem] * 6,
        out_specs=[vmem] * 3,
        compiler_params=pltpu.CompilerParams(vmem_limit_bytes=20 * 2**20),
        name="side",
    )(dup, last, span, owner, freq, sense2)
    slope, matrix, turned = [
        pltpu.with_memory_space_constraint(x, pltpu.VMEM) for x in side
    ]
    part = pl.pallas_call(
        functools.partial(down_kernel, total_sites, members),
        out_shape=shape((16, 128), F32),
        in_specs=[vmem] * (14 + members) + [smem] + [vmem] * 3,
        out_specs=vmem,
        scratch_shapes=[
            pltpu.VMEM((32, 128, sites), BF),
            pltpu.VMEM((32, 128, sites), BF),
            pltpu.VMEM((PAIRS, 64, 128), F32),
            pltpu.VMEM((PAIRS * 64, 128), F32),
            pltpu.VMEM((64 * 64, 128), F32),
        ],
        compiler_params=pltpu.CompilerParams(vmem_limit_bytes=20 * 2**20),
        name="down",
    )(
        *tops, chain, matrix, turned, slope, powers, message, high, low, leaf, scale, inverse,
        weights.reshape(1, sites), exchanges, freq, omega_ratio, sense2, single2, nonsyn2,
    )
    steps = axis_steps("branch") + axis_steps("site")
    for step in steps[:-1]:
        part = tree_sum(partners(part, *step))
    parts = partners(part, *steps[-1])
    exch, omega, length, loglik = pl.pallas_call(
        functools.partial(last_kernel, total_sites, len(parts)),
        out_shape=[shape((64, 64), F32), shape((1, CLASSES), F32), shape((1, EDGES), F32), shape((1, 1), F32)],
        in_specs=[vmem] * len(parts),
        out_specs=[vmem] * 4,
        compiler_params=pltpu.CompilerParams(vmem_limit_bytes=20 * 2**20),
        name="last",
    )(*parts)
    return (exch, omega.reshape(CLASSES), length.reshape(EDGES), loglik.reshape(()))


def solution(mesh):
    def whole(states, *rest):
        total_sites = states.shape[1]
        return jax.shard_map(
            functools.partial(body, total_sites),
            mesh=mesh,
            in_specs=(
                P(None, "site"),
                P(None, "site"),
                P("site"),
                P(),
                P(),
                P(),
                P(),
                P("branch"),
                P("branch"),
            ),
            out_specs=(P(), P(), P("branch"), P()),
            check_vma=False,
        )(states, *rest)

    return whole
```

```python
import functools
import jax
import jax.numpy as jnp
import numpy as np
from jax import lax
from jax.experimental import pallas as pl
from jax.experimental.pallas import tpu as pltpu
from jax.sharding import PartitionSpec as P

LEAF_DEV = 64
EDGES = 127
PAIRS = 64
CLASSES = 8
ORDER = 8
BF = jnp.bfloat16
F32 = jnp.float32

CODE_TABLE = "FFLLSSSSYYXXCCXWLLLLPPPPHHQQRRRRIIIMTTTTNNKKSSRRVVVVAAAADDEEGGGG"


def codon_tables():
    amino_acid = np.array(list(CODE_TABLE))
    codon_index = np.arange(64)
    digits = np.stack([codon_index // 16, codon_index // 4 % 4, codon_index % 4], 1)
    differ = (digits[:, None, :] != digits[None, :, :]).sum(-1)
    is_sense = amino_acid != "X"
    single = (differ == 1) & is_sense[:, None] & is_sense[None, :]
    nonsyn = single & (amino_acid[:, None] != amino_acid[None, :])
    return (is_sense.astype(np.float32), single.astype(np.float32), nonsyn.astype(np.float32))


def low_half():
    return lax.broadcasted_iota(jnp.int32, (64, 128), 1) < 64


def split(x):
    high = x.astype(BF)
    low = (x - high.astype(F32)).astype(BF)
    return high, low


def spread(x):
    mask = low_half()
    low = jnp.where(mask, 1.0, 0.0).astype(x.dtype)
    high = jnp.where(mask, 0.0, 1.0).astype(x.dtype)
    return jnp.concatenate([x * low, x * high], axis=0)


def mxu(left, right):
    return jnp.dot(left, right, preferred_element_type=F32)


def mxu_nt(left, right):
    return lax.dot_general(left, right, (((1,), (1,)), ((), ())), preferred_element_type=F32)


def exact(left, right):
    return jnp.dot(left, right, preferred_element_type=F32, precision=lax.Precision.HIGHEST)


def exact_tn(left, right):
    return lax.dot_general(
        left, right, (((0,), (0,)), ((), ())), preferred_element_type=F32,
        precision=lax.Precision.HIGHEST,
    )


def pair_products(*terms):
    lefts, rights = [], []
    for left, right in terms:
        left_high, left_low = split(left)
        right_high, right_low = split(right)
        wide_high, wide_low = spread(right_high), spread(right_low)
        lefts += [left_high, left_high, left_low]
        rights += [wide_high, wide_low, wide_high]
    return mxu(jnp.concatenate(lefts, axis=1), jnp.concatenate(rights, axis=0))


def pair_messages(ref, at, high, low):
    wide_high, wide_low = spread(ref[0, at]), spread(ref[1, at])
    if low is None:
        return mxu(
            jnp.concatenate([wide_high, wide_low], axis=1), jnp.concatenate([high, high], axis=0)
        )
    return mxu(
        jnp.concatenate([wide_high, wide_high, wide_low], axis=1),
        jnp.concatenate([high, low, high], axis=0),
    )


def frequencies(freq_ref, sense_ref):
    row = lax.broadcasted_iota(jnp.int32, (64, 128), 0)
    lane = lax.broadcasted_iota(jnp.int32, (64, 128), 1)
    twice = (row == lane % 64).astype(F32)
    sense2 = sense_ref[...]
    freq2 = exact(jnp.broadcast_to(freq_ref[...], (8, 64)), twice)[0:1] * sense2
    total = 0.5 * jnp.sum(freq2, axis=1, keepdims=True)
    pi_row = freq2 / total
    pi_col = 0.5 * jnp.sum(twice * pi_row, axis=1, keepdims=True)
    sense_col = 0.5 * jnp.sum(twice * sense2, axis=1, keepdims=True)
    root_row = jnp.sqrt(jnp.where(sense2 > 0, pi_row, 1.0))
    root_col = jnp.sqrt(jnp.where(sense_col > 0, pi_col, 1.0))
    return twice, pi_row, pi_col, root_row, root_col


def symmetric_table(ex_ref, single_ref, twice):
    ex = ex_ref[...]
    return 0.5 * (exact(ex, twice) + exact_tn(ex, twice)) * single_ref[...]


def class_pair(table, nonsyn, omega_ref, pair, twice, pi_row, pi_col):
    mask = low_half()
    omega = jnp.where(mask, omega_ref[2 * pair], omega_ref[2 * pair + 1])
    factor = 1.0 + nonsyn * (omega - 1.0)
    flux = table * factor
    off = flux * pi_row
    row0 = jnp.sum(jnp.where(mask, off, 0.0), axis=1, keepdims=True)
    row1 = jnp.sum(jnp.where(mask, 0.0, off), axis=1, keepdims=True)
    mean0 = jnp.sum(pi_col * row0, axis=0, keepdims=True)
    mean1 = jnp.sum(pi_col * row1, axis=0, keepdims=True)
    rows = jnp.where(mask, row0, row1)
    mean = jnp.where(mask, mean0, mean1)
    return factor, off, rows, mean


def neighbours():
    row = lax.broadcasted_iota(jnp.int32, (64, 128), 0)
    lane = lax.broadcasted_iota(jnp.int32, (64, 128), 1) % 64
    masks = [
        row % 16 == lane % 16,
        (row // 16 == lane // 16) & (row % 4 == lane % 4),
        row // 4 == lane // 4,
    ]
    codon = lax.broadcasted_iota(jnp.int32, (64, 16), 0)
    column = lax.broadcasted_iota(jnp.int32, (64, 16), 1)
    digits = [codon // 16, codon // 4 % 4, codon % 4]
    picks = [(column == 4 * p + digits[p]).astype(F32) for p in range(3)]
    return masks, picks


def coefficients(len_ref, cls_ref):
    lane = lax.broadcasted_iota(jnp.int32, (PAIRS, EDGES), 1)
    row = lax.broadcasted_iota(jnp.int32, (PAIRS, EDGES), 0)
    lengths = len_ref[...] * 0.0625
    classes = cls_ref[...].astype(F32)

    def column(values, odd):
        return jnp.sum(jnp.where(lane == 2 * row + odd, values, 0.0), axis=1, keepdims=True)

    mask = low_half()
    y = jnp.where(mask, column(lengths, 0), column(lengths, 1))
    owner = jnp.where(mask, column(classes, 0), column(classes, 1))
    place = lax.broadcasted_iota(jnp.int32, (PAIRS, 128), 1) % 64
    current = jnp.ones((PAIRS, 128), F32)
    series = slopes = jnp.zeros((PAIRS, 128), F32)
    for k in range(ORDER):
        slopes = jnp.where(place // CLASSES == k, current, slopes)
        current = current * y * (1.0 / (k + 1))
        series = jnp.where(place // CLASSES == k, current, series)
    member = (place % CLASSES).astype(F32) == owner
    return jnp.where(member, series, 0.0), jnp.where(member, slopes, 0.0)


def thrice_left(x):
    high, low = split(x)
    return jnp.concatenate([high, high, low], axis=1)


def thrice_right(x):
    high, low = split(x)
    return jnp.concatenate([high, low, high], axis=0)


def spread_thrice(x):
    high, low = split(x)
    wide_high, wide_low = spread(high), spread(low)
    return jnp.concatenate([wide_high, wide_low, wide_high], axis=0)


def rows_of(step, width):
    return pl.ds(pl.multiple_of(step * width, width), width)


def matrix_kernel(
    ex_ref, freq_ref, omega_ref, len_ref, cls_ref, sense_ref, single_ref, nonsyn_ref,
    chain_ref, last_ref, up_ref, power_ref, dup_ref,
    first_ref,
):
    mask = low_half()
    twice, pi_row, pi_col, root_row, root_col = frequencies(freq_ref, sense_ref)
    table = symmetric_table(ex_ref, single_ref, twice)
    nonsyn = nonsyn_ref[...]

    powers = []
    for pair in range(CLASSES // 2):
        factor, off, rows, mean = class_pair(
            table, nonsyn, omega_ref, pair, twice, pi_row, pi_col
        )
        powers.append([(table * factor * root_col * root_row - twice * rows) / mean])
    for left, right in ((0, 0), (1, 0), (1, 1), (3, 0), (3, 1), (3, 2), (3, 3)):
        for pair in range(CLASSES // 2):
            powers[pair].append(pair_products((powers[pair][left], powers[pair][right])))
    for pair in range(CLASSES // 2):
        for k in range(ORDER):
            value = powers[pair][k]
            swapped = pltpu.roll(value, 64, 1)
            at = CLASSES * k + 2 * pair
            dup_ref[pl.ds(at, 64, stride=64), :] = jnp.where(mask, value, swapped)
            dup_ref[pl.ds(at + 1, 64, stride=64), :] = jnp.where(mask, swapped, value)
            if k < 4:
                power_ref[pair, k] = value

    series, slopes = coefficients(len_ref, cls_ref)
    left = thrice_left(series)

    def expansions(step, carry):
        for j in range(8):
            i = step * 8 + j
            first_ref[rows_of(i, 64), :] = mxu(left, spread_thrice(dup_ref[rows_of(i, 64), :]))
        return carry

    lax.fori_loop(0, 8, expansions, 0)

    def squarings(step, carry):
        held = [first_ref[pl.ds(step * 8 + j, 64, stride=64), :] for j in range(8)]
        for level in range(4):
            for j in range(8):
                chain_ref[level, step * 8 + j] = held[j]
                held[j] = 2.0 * held[j] + pair_products((held[j], held[j]))
        for j in range(8):
            p = step * 8 + j
            last_ref[p] = held[j]
            high, low = split(inverse_root_col * (held[j] + twice) * root_row)
            up_ref[0, p] = high
            up_ref[1, p] = low
        return carry

    inverse_root_col = 1.0 / root_col
    lax.fori_loop(0, PAIRS // 8, squarings, 0)


def up_kernel(
    states_ref, gap_ref, order_ref, up_ref,
    top_ref, message_ref, high_ref, low_ref, leaf_ref, scale_ref, inverse_ref,
):
    subtree = lax.axis_index("branch")

    def finish(p, message):
        message_ref[p] = message
        raw = message[0:64] * message[64:128]
        scaling = jnp.sum(raw, axis=0, keepdims=True)
        inverse = 1.0 / scaling
        scale_ref[pl.ds(p, 1), :] = scaling
        inverse_ref[pl.ds(p, 1), :] = inverse
        high, low = split(raw * inverse)
        high_ref[p] = high
        low_ref[p] = low

    sites = states_ref.shape[1]
    codon = lax.broadcasted_iota(jnp.int32, (64, sites), 0)

    def leaf_level(step, carry):
        for j in range(4):
            p = step * 4 + j
            both = []
            for e in range(2):
                taxon = order_ref[subtree * LEAF_DEV + 2 * p + e]
                state = jnp.where(
                    gap_ref[pl.ds(taxon, 1), :] > 0, -1, states_ref[pl.ds(taxon, 1), :]
                )
                hit = (codon == state) | (state < 0)
                both.append(jnp.where(hit, 1.0, 0.0).astype(BF))
            leaves = jnp.concatenate(both, axis=0)
            leaf_ref[p] = leaves
            finish(p, pair_messages(up_ref, p, leaves, None))
        return carry

    lax.fori_loop(0, LEAF_DEV // 8, leaf_level, 0)

    def inner(p):
        child = 2 * p - 64
        high = jnp.concatenate([high_ref[child], high_ref[child + 1]], axis=0)
        low = jnp.concatenate([low_ref[child], low_ref[child + 1]], axis=0)
        return pair_messages(up_ref, p, high, low)

    def second_level(step, carry):
        for j in range(4):
            finish(32 + step * 4 + j, inner(32 + step * 4 + j))
        return carry

    lax.fori_loop(0, 4, second_level, 0)
    for p in range(48, 63):
        finish(p, inner(p))
    high_ref[63] = jnp.zeros((64, sites), BF)
    low_ref[63] = jnp.zeros((64, sites), BF)
    scale_ref[63:64, :] = jnp.ones((1, sites), F32)
    inverse_ref[63:64, :] = jnp.ones((1, sites), F32)
    top = inner(63)
    message_ref[63] = top
    top_ref[...] = top[0:64]


def side_kernel(
    dup_ref, last_ref, len_ref, cls_ref, freq_ref, sense_ref, slope_ref, matrix_ref, turned_ref,
):
    twice, pi_row, pi_col, root_row, root_col = frequencies(freq_ref, sense_ref)
    series, slopes = coefficients(len_ref, cls_ref)
    left = thrice_left(slopes)

    def expansions(step, carry):
        for j in range(8):
            i = step * 8 + j
            slope_ref[rows_of(i, 64), :] = mxu(left, spread_thrice(dup_ref[rows_of(i, 64), :]))
        return carry

    lax.fori_loop(0, 8, expansions, 0)
    turned_ref[...] = exact_tn(series, twice[:, 0:64])
    inverse_root_row = 1.0 / root_row

    def matrices(step, carry):
        for j in range(8):
            r = step * 8 + j
            high, low = split(root_col * (last_ref[32 + r] + twice) * inverse_root_row)
            matrix_ref[0, r] = high
            matrix_ref[1, r] = low
        return carry

    lax.fori_loop(0, 4, matrices, 0)


def down_kernel(total_sites, members, *refs):
    tops = refs[:members]
    (
        matrix_ref, message_ref, high_ref, low_ref, leaf_ref, scale_ref, inverse_ref,
        weights_ref, freq_ref, sense_ref,
        count_ref, log_ref,
        a_high_ref, a_low_ref,
    ) = refs[members:]
    subtree = lax.axis_index("branch")
    mask = low_half()
    twice, pi_row, pi_col, root_row, root_col = frequencies(freq_ref, sense_ref)
    inverse_root_row, inverse_root_col = 1.0 / root_row, 1.0 / root_col
    sites = weights_ref.shape[1]
    weight = weights_ref[...].astype(F32)

    above = jnp.broadcast_to(pi_col, (64, sites))
    for other in tops[1:]:
        above = above * other[...]
    own = tops[0][...]
    likelihood = jnp.sum(above * own, axis=0, keepdims=True)
    logs = jnp.sum(jnp.log(scale_ref[...]), axis=0, keepdims=True)
    logs = logs + jnp.where(subtree == 0, jnp.log(likelihood), 0.0)
    log_ref[...] = jnp.broadcast_to(jnp.sum(weight * logs, axis=1, keepdims=True), (8, 128))
    high, low = split(above * (weight / (likelihood * total_sites)))
    a_high_ref[31, 0:64, :] = high
    a_low_ref[31, 0:64, :] = low
    a_high_ref[31, 64:128, :] = jnp.zeros((64, sites), BF)
    a_low_ref[31, 64:128, :] = jnp.zeros((64, sites), BF)

    def store_counts(p, square):
        counts = jnp.where(mask, square[0:64], square[64:128])
        count_ref[p] = inverse_root_col * counts * root_row

    def descend(r):
        a_high, a_low = a_high_ref[r - 32], a_low_ref[r - 32]
        child = 2 * r - 64
        u_high = jnp.concatenate([high_ref[child], high_ref[child + 1]], axis=0)
        u_low = jnp.concatenate([low_ref[child], low_ref[child + 1]], axis=0)
        first = mxu_nt(a_high, jnp.concatenate([u_high, u_low], axis=0))
        second = mxu_nt(a_low, u_high)
        store_counts(r, first[:, 0:128] + first[:, 128:256] + second)
        return pair_messages(matrix_ref, r - 32, a_high, a_low)

    def children(down, e, p):
        vector = down[64 * e : 64 * e + 64]
        inverse = inverse_ref[pl.ds(p, 1), :]
        message = message_ref[p]
        pair = jnp.concatenate(
            [vector * message[64:128] * inverse, vector * message[0:64] * inverse], axis=0
        )
        return split(pair)

    def inner(r):
        down = descend(r)
        for e in range(2):
            p = 2 * r + e - 64
            if isinstance(p, int) and p == 63:
                continue
            high, low = children(down, e, p)
            a_high_ref[p - 32] = high
            a_low_ref[p - 32] = low

    for r in range(63, 47, -1):
        inner(r)

    def leaf_level(step, carry):
        for j in range(2):
            r = 32 + step * 2 + j
            down = descend(r)
            for e in range(2):
                p = 2 * r + e - 64
                high, low = children(down, e, p)
                square = mxu_nt(jnp.concatenate([high, low], axis=0), leaf_ref[p])
                store_counts(p, square[0:128] + square[128:256])
        return carry

    lax.fori_loop(0, 8, leaf_level, 0)


def adjoint_kernel(
    members,
    chain_ref, turned_ref, slope_ref, power_ref, count_ref, log_ref, ex_ref, freq_ref, omega_ref,
    sense_ref, single_ref, nonsyn_ref,
    out_ref,
    back_ref, bins_ref,
):
    subtree = lax.axis_index("branch")
    mask = low_half()
    twice, pi_row, pi_col, root_row, root_col = frequencies(freq_ref, sense_ref)
    inverse_root_row = 1.0 / root_row

    def adjoint(step, carry):
        held = [count_ref[step * 8 + j] for j in range(8)]
        for level in range(3, -1, -1):
            for j in range(8):
                matrix = chain_ref[level, step * 8 + j]
                held[j] = 2.0 * held[j] + pair_products((held[j], matrix), (matrix, held[j]))
        for j in range(8):
            back_ref[pl.ds(step * 8 + j, 64, stride=64), :] = held[j]
        return carry

    lax.fori_loop(0, PAIRS // 8, adjoint, 0)

    left = thrice_left(turned_ref[...])

    def sums(step, total):
        for j in range(8):
            at = rows_of(step * 8 + j, 64)
            value = back_ref[at, :]
            total = total + value * slope_ref[at, :]
            both = mxu(left, thrice_right(value))
            bins_ref[at, :] = jnp.where(mask, both[0:64], both[64:128])
        return total

    slopes = lax.fori_loop(0, 8, sums, jnp.zeros((64, 128), F32)) * 0.0625

    table = symmetric_table(ex_ref, single_ref, twice)
    nonsyn = nonsyn_ref[...]
    row = lax.broadcasted_iota(jnp.int32, (64, 128), 0)
    lane = lax.broadcasted_iota(jnp.int32, (64, 128), 1)
    table_grad = jnp.zeros((64, 128), F32)
    omega_row = jnp.zeros((1, 128), F32)
    lane_row = lax.broadcasted_iota(jnp.int32, (1, 128), 1)
    for pair in range(CLASSES // 2):
        grads = []
        for k in range(ORDER):
            at = CLASSES * k + 2 * pair
            first = bins_ref[pl.ds(at, 64, stride=64), :]
            second = bins_ref[pl.ds(at + 1, 64, stride=64), :]
            first = first + pltpu.roll(first, 64, 1)
            second = second + pltpu.roll(second, 64, 1)
            grads.append(jnp.where(mask, first, second))
        g1, g2, g3, g4, g5, g6, g7, g8 = grads
        a1, a2, a3, a4 = [power_ref[pair, k] for k in range(4)]
        g4 = g4 + pair_products((g8, a4), (a4, g8), (g7, a3), (g6, a2), (g5, a1))
        g3 = g3 + pair_products((a4, g7))
        g2 = g2 + pair_products((a4, g6))
        g1 = g1 + pair_products((a4, g5))
        g2 = g2 + pair_products((g4, a2), (a2, g4), (g3, a1))
        g1 = g1 + pair_products((a2, g3))
        g1 = g1 + pair_products((g2, a1), (a1, g2))
        factor, off, rows, mean = class_pair(
            table, nonsyn, omega_ref, pair, twice, pi_row, pi_col
        )
        d_rate = root_col * g1 * inverse_root_row
        rate = (off - twice * rows) / mean
        weighted = d_rate * rate
        diagonal = d_rate * twice
        total0 = jnp.sum(jnp.where(mask, weighted, 0.0), axis=1, keepdims=True)
        total1 = jnp.sum(jnp.where(mask, 0.0, weighted), axis=1, keepdims=True)
        total0 = jnp.sum(total0, axis=0, keepdims=True)
        total1 = jnp.sum(total1, axis=0, keepdims=True)
        diag0 = jnp.sum(jnp.where(mask, diagonal, 0.0), axis=1, keepdims=True)
        diag1 = jnp.sum(jnp.where(mask, 0.0, diagonal), axis=1, keepdims=True)
        row_grad = jnp.where(mask, diag0 + pi_col * total0, diag1 + pi_col * total1)
        flux_grad = (d_rate - row_grad) * pi_row / mean
        table_grad = table_grad + flux_grad * factor * single_ref[...]
        ratio = flux_grad * table * nonsyn
        ratio0 = jnp.sum(jnp.where(mask, ratio, 0.0), axis=1, keepdims=True)
        ratio1 = jnp.sum(jnp.where(mask, 0.0, ratio), axis=1, keepdims=True)
        ratio0 = jnp.sum(ratio0, axis=0, keepdims=True)
        ratio1 = jnp.sum(ratio1, axis=0, keepdims=True)
        omega_row = jnp.where(lane_row == 2 * pair, ratio0, omega_row)
        omega_row = jnp.where(lane_row == 2 * pair + 1, ratio1, omega_row)
    table_grad = table_grad + pltpu.roll(table_grad, 64, 1)
    one = table_grad[:, 0:64]
    both = 0.5 * (exact(one, twice) + exact_tn(one, twice))
    masks, picks = neighbours()
    packed = jnp.zeros((16, 128), F32)
    for at_position, pick in zip(masks, picks):
        packed = packed + exact_tn(pick, jnp.where(at_position, both, 0.0))
    packed = jnp.where(lax.broadcasted_iota(jnp.int32, (16, 128), 1) < 64, packed, 0.0)

    even = jnp.sum(jnp.where(mask, slopes, 0.0), axis=1, keepdims=True)
    other = jnp.sum(jnp.where(mask, 0.0, slopes), axis=1, keepdims=True)
    placed = jnp.where(lane == 2 * row, even, 0.0) + jnp.where(lane == 2 * row + 1, other, 0.0)
    length_row = jnp.sum(placed, axis=0, keepdims=True)
    line = lax.broadcasted_iota(jnp.int32, out_ref.shape, 0)
    omega_row = jnp.where(lane_row == CLASSES, log_ref[0:1, :], omega_row)
    omega_row = pltpu.roll(jnp.broadcast_to(omega_row, (8, 128)), 64, 1)[0:1]
    packed = packed + jnp.where(line == 0, omega_row, 0.0)
    out_ref[...] = packed + jnp.where(line == 12 + subtree, length_row, 0.0)


def last_kernel(total_sites, count, *refs):
    members = lax.axis_size("branch")
    subtree = lax.axis_index("branch")
    exch_ref, omega_ref, length_ref, log_ref = refs[count:]
    total = tree_sum([ref[...] for ref in refs[:count]])
    masks, picks = neighbours()
    table = jnp.zeros((64, 128), F32)
    for at_position, pick in zip(masks, picks):
        table = table + jnp.where(at_position, exact(pick, total), 0.0)
    exch_ref[...] = table[:, 0:64]
    moved = pltpu.roll(total[0:8], 64, 1)
    omega_ref[...] = moved[0:1, 0:CLASSES]
    line = lax.broadcasted_iota(jnp.int32, total.shape, 0)
    lengths = jnp.sum(jnp.where(line == 12 + subtree, total, 0.0), axis=0, keepdims=True)
    length_ref[...] = lengths[:, 0:EDGES]
    log_ref[...] = moved[0:1, CLASSES : CLASSES + 1] / total_sites / (LEAF_DEV * members)


def partners(x, axis, start, radix):
    size = lax.axis_size(axis)
    others = [
        lax.ppermute(x, axis, [(i, i ^ (step * start)) for i in range(size)])
        for step in range(1, radix)
    ]
    return [x] + others


def tree_sum(parts):
    while len(parts) > 1:
        parts = [parts[i] + parts[i + 1] for i in range(0, len(parts), 2)]
    return parts[0]


def axis_steps(axis):
    size, start, steps = lax.axis_size(axis), 1, []
    while start < size:
        radix = min(4, size // start)
        steps.append((axis, start, radix))
        start *= radix
    return steps


def body(
    total_sites, states, gap_mask, weights, leaf_order, exchanges, codon_freq, omega_ratio,
    lengths, classes,
):
    sites = states.shape[1]
    members = lax.axis_size("branch")
    sense, single, nonsyn = codon_tables()
    vmem = pl.BlockSpec(memory_space=pltpu.VMEM)
    smem = pl.BlockSpec(memory_space=pltpu.SMEM)
    shape = jax.ShapeDtypeStruct
    held = pltpu.VMEM
    limit = pltpu.CompilerParams(vmem_limit_bytes=20 * 2**20)

    def outside(x):
        return pltpu.with_memory_space_constraint(x, pltpu.HBM)

    def inside(xs):
        return [pltpu.with_memory_space_constraint(x, pltpu.VMEM) for x in xs]

    sense2 = outside(jnp.asarray(np.tile(sense[None, :], (1, 2))))
    single2 = outside(jnp.asarray(np.tile(single, (1, 2))))
    nonsyn2 = outside(jnp.asarray(np.tile(nonsyn, (1, 2))))
    freq = outside(codon_freq.reshape(1, 64))
    span, owner = outside(lengths.reshape(1, EDGES)), outside(classes.reshape(1, EDGES))
    table, omega = outside(exchanges), outside(omega_ratio)

    chain, last, up, powers, dup = inside(pl.pallas_call(
        matrix_kernel,
        out_shape=[
            held((4, PAIRS, 64, 128), F32),
            held((PAIRS, 64, 128), F32),
            held((2, PAIRS, 64, 128), BF),
            held((CLASSES // 2, 4, 64, 128), F32),
            held((ORDER * CLASSES * 64, 128), F32),
        ],
        in_specs=[vmem, vmem, smem] + [vmem] * 5,
        out_specs=[vmem] * 5,
        scratch_shapes=[pltpu.VMEM((PAIRS * 64, 128), F32)],
        compiler_params=limit,
        name="matrices",
    )(table, freq, omega, span, owner, sense2, single2, nonsyn2))
    top, *kept = pl.pallas_call(
        up_kernel,
        out_shape=[
            shape((64, sites), F32),
            held((PAIRS, 128, sites), F32),
            held((64, 64, sites), BF),
            held((64, 64, sites), BF),
            held((32, 128, sites), BF),
            held((64, sites), F32),
            held((64, sites), F32),
        ],
        in_specs=[vmem, vmem, smem, vmem],
        out_specs=[vmem] * 7,
        compiler_params=limit,
        name="up",
    )(outside(states), outside(gap_mask), outside(leaf_order), up)
    message, high, low, leaf, scale, inverse = inside(kept)
    tops = partners(top, "branch", 1, members)
    slope, matrix, turned = inside(pl.pallas_call(
        side_kernel,
        out_shape=[
            held((PAIRS * 64, 128), F32),
            held((2, 32, 64, 128), BF),
            held((128, 64), F32),
        ],
        in_specs=[vmem] * 6,
        out_specs=[vmem] * 3,
        compiler_params=limit,
        name="side",
    )(dup, last, span, owner, freq, sense2))
    counts, logs = inside(pl.pallas_call(
        functools.partial(down_kernel, total_sites, members),
        out_shape=[held((PAIRS, 64, 128), F32), held((8, 128), F32)],
        in_specs=[vmem] * (10 + members),
        out_specs=[vmem] * 2,
        scratch_shapes=[
            pltpu.VMEM((32, 128, sites), BF),
            pltpu.VMEM((32, 128, sites), BF),
        ],
        compiler_params=limit,
        name="down",
    )(
        *tops, matrix, message, high, low, leaf, scale, inverse,
        outside(weights.reshape(1, sites)), freq, sense2,
    ))
    part = pl.pallas_call(
        functools.partial(adjoint_kernel, members),
        out_shape=shape((16, 128), F32),
        in_specs=[vmem] * 8 + [smem] + [vmem] * 3,
        out_specs=vmem,
        scratch_shapes=[
            pltpu.VMEM((PAIRS * 64, 128), F32),
            pltpu.VMEM((64 * 64, 128), F32),
        ],
        compiler_params=limit,
        name="adjoint",
    )(
        chain, turned, slope, powers, counts, logs, table, freq, omega,
        sense2, single2, nonsyn2,
    )
    steps = axis_steps("branch") + axis_steps("site")
    for step in steps[:-1]:
        part = tree_sum(partners(part, *step))
    parts = partners(part, *steps[-1])
    exch, ratio, length, loglik = pl.pallas_call(
        functools.partial(last_kernel, total_sites, len(parts)),
        out_shape=[shape((64, 64), F32), shape((1, CLASSES), F32), shape((1, EDGES), F32), shape((1, 1), F32)],
        in_specs=[vmem] * len(parts),
        out_specs=[vmem] * 4,
        compiler_params=limit,
        name="last",
    )(*parts)
    return (exch, ratio.reshape(CLASSES), length.reshape(EDGES), loglik.reshape(()))


def solution(mesh):
    def whole(states, *rest):
        total_sites = states.shape[1]
        return jax.shard_map(
            functools.partial(body, total_sites),
            mesh=mesh,
            in_specs=(
                P(None, "site"),
                P(None, "site"),
                P("site"),
                P(),
                P(),
                P(),
                P(),
                P("branch"),
                P("branch"),
            ),
            out_specs=(P(), P(), P("branch"), P()),
            check_vma=False,
        )(states, *rest)

    return whole
```

```python
import functools
import jax
import jax.numpy as jnp
import numpy as np
from jax import lax
from jax.experimental import pallas as pl
from jax.experimental.pallas import tpu as pltpu
from jax.sharding import PartitionSpec as P

LEAF_DEV = 64
EDGES = 127
PAIRS = 64
CLASSES = 8
ORDER = 8
BF = jnp.bfloat16
F32 = jnp.float32

CODE_TABLE = "FFLLSSSSYYXXCCXWLLLLPPPPHHQQRRRRIIIMTTTTNNKKSSRRVVVVAAAADDEEGGGG"


def codon_tables():
    amino_acid = np.array(list(CODE_TABLE))
    codon_index = np.arange(64)
    digits = np.stack([codon_index // 16, codon_index // 4 % 4, codon_index % 4], 1)
    differ = (digits[:, None, :] != digits[None, :, :]).sum(-1)
    is_sense = amino_acid != "X"
    single = (differ == 1) & is_sense[:, None] & is_sense[None, :]
    nonsyn = single & (amino_acid[:, None] != amino_acid[None, :])
    return (is_sense.astype(np.float32), single.astype(np.float32), nonsyn.astype(np.float32))


def low_half():
    return lax.broadcasted_iota(jnp.int32, (64, 128), 1) < 64


def split(x):
    high = x.astype(BF)
    low = (x - high.astype(F32)).astype(BF)
    return high, low


def spread(x, scale=1.0):
    mask = low_half()
    low = jnp.where(mask, scale, 0.0).astype(x.dtype)
    high = jnp.where(mask, 0.0, scale).astype(x.dtype)
    return jnp.concatenate([x * low, x * high], axis=0)


def mxu(left, right):
    return jnp.dot(left, right, preferred_element_type=F32)


def mxu_nt(left, right):
    return lax.dot_general(left, right, (((1,), (1,)), ((), ())), preferred_element_type=F32)


def exact(left, right):
    return jnp.dot(left, right, preferred_element_type=F32, precision=lax.Precision.HIGHEST)


def exact_tn(left, right):
    return lax.dot_general(
        left, right, (((0,), (0,)), ((), ())), preferred_element_type=F32,
        precision=lax.Precision.HIGHEST,
    )


def pair_products(*terms):
    lefts, rights = [], []
    for left, right in terms:
        left_high, left_low = split(left)
        right_high, right_low = split(right)
        wide_high, wide_low = spread(right_high), spread(right_low)
        lefts += [left_high, left_high, left_low]
        rights += [wide_high, wide_low, wide_high]
    return mxu(jnp.concatenate(lefts, axis=1), jnp.concatenate(rights, axis=0))


def messages(matrix, high, low):
    return mxu(matrix, jnp.concatenate([high, low, high, low], axis=0))


def double(ref, p, x):
    mask = low_half()
    swapped = pltpu.roll(x, 64, 1)
    for e, both in enumerate((jnp.where(mask, x, swapped), jnp.where(mask, swapped, x))):
        high, low = split(both)
        ref[2 * p + e] = jnp.concatenate([high, low], axis=1)


def transposes(first, second):
    mask = low_half()
    turned = jnp.concatenate([first, second], axis=0).T
    top, bottom = turned[0:64], turned[64:128]
    return (
        jnp.where(mask, top, pltpu.roll(bottom, 64, 1)),
        jnp.where(mask, pltpu.roll(top, 64, 1), bottom),
    )


def frequencies(freq_ref, sense_ref):
    row = lax.broadcasted_iota(jnp.int32, (64, 128), 0)
    lane = lax.broadcasted_iota(jnp.int32, (64, 128), 1)
    twice = (row == lane % 64).astype(F32)
    sense2 = sense_ref[...]
    freq2 = exact(jnp.broadcast_to(freq_ref[...], (8, 64)), twice)[0:1] * sense2
    total = 0.5 * jnp.sum(freq2, axis=1, keepdims=True)
    pi_row = freq2 / total
    pi_col = 0.5 * jnp.sum(twice * pi_row, axis=1, keepdims=True)
    sense_col = 0.5 * jnp.sum(twice * sense2, axis=1, keepdims=True)
    root_row = jnp.sqrt(jnp.where(sense2 > 0, pi_row, 1.0))
    root_col = jnp.sqrt(jnp.where(sense_col > 0, pi_col, 1.0))
    return twice, pi_row, pi_col, root_row, root_col


def symmetric_table(ex_ref, single_ref, twice):
    ex = ex_ref[...]
    return 0.5 * (exact(ex, twice) + exact_tn(ex, twice)) * single_ref[...]


def class_pair(table, nonsyn, omega_ref, pair, twice, pi_row, pi_col):
    mask = low_half()
    omega = jnp.where(mask, omega_ref[2 * pair], omega_ref[2 * pair + 1])
    factor = 1.0 + nonsyn * (omega - 1.0)
    flux = table * factor
    off = flux * pi_row
    row0 = jnp.sum(jnp.where(mask, off, 0.0), axis=1, keepdims=True)
    row1 = jnp.sum(jnp.where(mask, 0.0, off), axis=1, keepdims=True)
    mean0 = jnp.sum(pi_col * row0, axis=0, keepdims=True)
    mean1 = jnp.sum(pi_col * row1, axis=0, keepdims=True)
    rows = jnp.where(mask, row0, row1)
    mean = jnp.where(mask, mean0, mean1)
    return factor, off, rows, mean


def neighbours():
    row = lax.broadcasted_iota(jnp.int32, (64, 128), 0)
    lane = lax.broadcasted_iota(jnp.int32, (64, 128), 1) % 64
    masks = [
        row % 16 == lane % 16,
        (row // 16 == lane // 16) & (row % 4 == lane % 4),
        row // 4 == lane // 4,
    ]
    codon = lax.broadcasted_iota(jnp.int32, (64, 16), 0)
    column = lax.broadcasted_iota(jnp.int32, (64, 16), 1)
    digits = [codon // 16, codon // 4 % 4, codon % 4]
    picks = [(column == 4 * p + digits[p]).astype(F32) for p in range(3)]
    return masks, picks


def coefficients(len_ref, cls_ref, slope):
    lane = lax.broadcasted_iota(jnp.int32, (PAIRS, EDGES), 1)
    row = lax.broadcasted_iota(jnp.int32, (PAIRS, EDGES), 0)
    lengths = len_ref[...] * 0.0625
    classes = cls_ref[...].astype(F32)
    place = lax.broadcasted_iota(jnp.int32, (PAIRS, 128), 1) % 64
    found = []
    for odd in range(2):
        here = lane == 2 * row + odd
        y = jnp.sum(jnp.where(here, lengths, 0.0), axis=1, keepdims=True)
        owner = jnp.sum(jnp.where(here, classes, 0.0), axis=1, keepdims=True)
        current = jnp.ones((PAIRS, 128), F32)
        series = jnp.zeros((PAIRS, 128), F32)
        for k in range(ORDER):
            following = current * y * (1.0 / (k + 1))
            series = jnp.where(place // CLASSES == k, current if slope else following, series)
            current = following
        found.append(jnp.where((place % CLASSES).astype(F32) == owner, series, 0.0))
    return found


def four_left(x):
    high, low = split(x)
    return jnp.concatenate([high, low], axis=1)


def four_right(x):
    high, low = split(x)
    return jnp.concatenate([high, low, high, low], axis=0)


def expand(left, dup_ref, store):
    mask = low_half()

    def some(step, carry):
        for j in range(2):
            i = step * 4 + 2 * j
            rows = jnp.concatenate(
                [dup_ref[rows_of(i, 64), :], dup_ref[rows_of(i + 1, 64), :]], axis=1
            )
            both = mxu(left, four_right(rows))
            for t in range(2):
                even, odd = both[0:64, 128 * t : 128 * t + 128], both[64:128, 128 * t : 128 * t + 128]
                store(i + t, jnp.where(mask, even, pltpu.roll(odd, 64, 1)))
                store(i + t + 32, jnp.where(mask, pltpu.roll(even, 64, 1), odd))
        return carry

    lax.fori_loop(0, 8, some, 0)


def rows_of(step, width):
    return pl.ds(pl.multiple_of(step * width, width), width)


def matrix_kernel(
    ex_ref, freq_ref, omega_ref, len_ref, cls_ref, sense_ref, single_ref, nonsyn_ref,
    chain_ref, last_ref, up_ref, power_ref, dup_ref,
    first_ref,
):
    mask = low_half()
    twice, pi_row, pi_col, root_row, root_col = frequencies(freq_ref, sense_ref)
    table = symmetric_table(ex_ref, single_ref, twice)
    nonsyn = nonsyn_ref[...]

    powers = []
    for pair in range(CLASSES // 2):
        factor, off, rows, mean = class_pair(
            table, nonsyn, omega_ref, pair, twice, pi_row, pi_col
        )
        powers.append([(table * factor * root_col * root_row - twice * rows) / mean])
    for left, right in ((0, 0), (1, 0), (1, 1), (3, 0), (3, 1), (3, 2), (3, 3)):
        for pair in range(CLASSES // 2):
            powers[pair].append(pair_products((powers[pair][left], powers[pair][right])))
    for pair in range(CLASSES // 2):
        for k in range(ORDER):
            value = powers[pair][k]
            swapped = pltpu.roll(value, 64, 1)
            at = CLASSES * k + 2 * pair
            top, half = value[0:32], low_half()[0:32]
            dup_ref[pl.ds(at, 32, stride=64), :] = jnp.where(half, top, swapped[32:64])
            dup_ref[pl.ds(at + 1, 32, stride=64), :] = jnp.where(half, swapped[0:32], value[32:64])
            if k < 4:
                power_ref[pair, k] = value

    even, odd = coefficients(len_ref, cls_ref, False)

    def store(i, value):
        first_ref[rows_of(i, 64), :] = value

    expand(four_left(jnp.concatenate([even, odd], axis=0)), dup_ref, store)

    def squarings(step, carry):
        held = [first_ref[pl.ds(step * 8 + j, 64, stride=64), :] for j in range(8)]
        for level in range(4):
            parts = []
            for j in range(8):
                high, low = split(held[j])
                chain_ref[level, 0, step * 8 + j] = high
                chain_ref[level, 1, step * 8 + j] = low
                parts.append(mxu(
                    jnp.concatenate([high, high], axis=1),
                    jnp.concatenate([spread(high, 0.5), spread(low)], axis=0),
                ))
            for j in range(0, 8, 2):
                turned = transposes(parts[j], parts[j + 1])
                for t in range(2):
                    held[j + t] = 2.0 * held[j + t] + parts[j + t] + turned[t]
        for j in range(8):
            p = step * 8 + j
            last_ref[p] = held[j]
            double(up_ref, p, inverse_root_col * (held[j] + twice) * root_row)
        return carry

    inverse_root_col = 1.0 / root_col
    lax.fori_loop(0, PAIRS // 8, squarings, 0)


def up_kernel(
    states_ref, gap_ref, order_ref, up_ref,
    top_ref, message_ref, high_ref, low_ref, leaf_ref, scale_ref, inverse_ref,
):
    subtree = lax.axis_index("branch")

    def finish(p, message):
        message_ref[p] = jnp.concatenate(message, axis=0)
        raw = message[0] * message[1]
        scaling = jnp.sum(raw, axis=0, keepdims=True)
        inverse = 1.0 / scaling
        scale_ref[pl.ds(p, 1), :] = scaling
        inverse_ref[pl.ds(p, 1), :] = inverse
        high, low = split(raw * inverse)
        high_ref[p] = high
        low_ref[p] = low

    sites = states_ref.shape[1]
    codon = lax.broadcasted_iota(jnp.int32, (64, sites), 0)

    def leaf_level(step, carry):
        for j in range(4):
            p = step * 4 + j
            both = []
            for e in range(2):
                taxon = order_ref[subtree * LEAF_DEV + 2 * p + e]
                state = jnp.where(
                    gap_ref[pl.ds(taxon, 1), :] > 0, -1, states_ref[pl.ds(taxon, 1), :]
                )
                hit = (codon == state) | (state < 0)
                both.append(jnp.where(hit, 1.0, 0.0).astype(BF))
            leaf_ref[p] = jnp.concatenate(both, axis=0)
            nothing = jnp.zeros_like(both[0])
            finish(p, [messages(up_ref[2 * p + e], both[e], nothing) for e in range(2)])
        return carry

    lax.fori_loop(0, LEAF_DEV // 8, leaf_level, 0)

    def inner(p):
        child = 2 * p - 64
        return [
            messages(up_ref[2 * p + e], high_ref[child + e], low_ref[child + e]) for e in range(2)
        ]

    def second_level(step, carry):
        for j in range(4):
            finish(32 + step * 4 + j, inner(32 + step * 4 + j))
        return carry

    lax.fori_loop(0, 4, second_level, 0)
    for p in range(48, 63):
        finish(p, inner(p))
    high_ref[63] = jnp.zeros((64, sites), BF)
    low_ref[63] = jnp.zeros((64, sites), BF)
    scale_ref[63:64, :] = jnp.ones((1, sites), F32)
    inverse_ref[63:64, :] = jnp.ones((1, sites), F32)
    top = inner(63)
    message_ref[63] = jnp.concatenate(top, axis=0)
    top_ref[...] = top[0]


def side_kernel(
    dup_ref, last_ref, len_ref, cls_ref, freq_ref, sense_ref, slope_ref, matrix_ref, turned_ref,
):
    twice, pi_row, pi_col, root_row, root_col = frequencies(freq_ref, sense_ref)
    even, odd = coefficients(len_ref, cls_ref, True)

    def store(i, value):
        slope_ref[rows_of(i, 64), :] = value

    expand(four_left(jnp.concatenate([even, odd], axis=0)), dup_ref, store)
    even, odd = coefficients(len_ref, cls_ref, False)
    turned_ref[...] = exact_tn(jnp.where(low_half(), even, odd), twice)
    inverse_root_row = 1.0 / root_row

    def matrices(step, carry):
        for j in range(8):
            r = step * 8 + j
            double(matrix_ref, r, root_col * (last_ref[32 + r] + twice) * inverse_root_row)
        return carry

    lax.fori_loop(0, 4, matrices, 0)


def down_kernel(total_sites, members, *refs):
    tops = refs[:members]
    (
        matrix_ref, message_ref, high_ref, low_ref, leaf_ref, scale_ref, inverse_ref,
        weights_ref, freq_ref, sense_ref,
        count_ref, log_ref,
        a_high_ref, a_low_ref,
    ) = refs[members:]
    subtree = lax.axis_index("branch")
    mask = low_half()
    twice, pi_row, pi_col, root_row, root_col = frequencies(freq_ref, sense_ref)
    inverse_root_row, inverse_root_col = 1.0 / root_row, 1.0 / root_col
    sites = weights_ref.shape[1]
    weight = weights_ref[...].astype(F32)

    above = jnp.broadcast_to(pi_col, (64, sites))
    for other in tops[1:]:
        above = above * other[...]
    own = tops[0][...]
    likelihood = jnp.sum(above * own, axis=0, keepdims=True)
    logs = jnp.sum(jnp.log(scale_ref[...]), axis=0, keepdims=True)
    logs = logs + jnp.where(subtree == 0, jnp.log(likelihood), 0.0)
    log_ref[...] = jnp.broadcast_to(jnp.sum(weight * logs, axis=1, keepdims=True), (8, 128))
    high, low = split(above * (weight / (likelihood * total_sites)))
    a_high_ref[31, 0:64, :] = high
    a_low_ref[31, 0:64, :] = low
    a_high_ref[31, 64:128, :] = jnp.zeros((64, sites), BF)
    a_low_ref[31, 64:128, :] = jnp.zeros((64, sites), BF)

    def store_counts(p, square):
        counts = jnp.where(mask, square[0:64], square[64:128])
        count_ref[p] = root_col * counts * inverse_root_row

    def descend(r):
        a_high, a_low = a_high_ref[r - 32], a_low_ref[r - 32]
        child = 2 * r - 64
        u_high = jnp.concatenate([high_ref[child], high_ref[child + 1]], axis=0)
        u_low = jnp.concatenate([low_ref[child], low_ref[child + 1]], axis=0)
        first = mxu_nt(u_high, jnp.concatenate([a_high, a_low], axis=0))
        second = mxu_nt(u_low, a_high)
        store_counts(r, first[:, 0:128] + first[:, 128:256] + second)
        return [
            messages(
                matrix_ref[2 * (r - 32) + e], a_high[64 * e : 64 * e + 64], a_low[64 * e : 64 * e + 64]
            )
            for e in range(2)
        ]

    def children(down, e, p):
        vector = down[e]
        inverse = inverse_ref[pl.ds(p, 1), :]
        message = message_ref[p]
        pair = jnp.concatenate(
            [vector * message[64:128] * inverse, vector * message[0:64] * inverse], axis=0
        )
        return split(pair)

    def inner(r):
        down = descend(r)
        for e in range(2):
            p = 2 * r + e - 64
            if isinstance(p, int) and p == 63:
                continue
            high, low = children(down, e, p)
            a_high_ref[p - 32] = high
            a_low_ref[p - 32] = low

    for r in range(63, 47, -1):
        inner(r)

    def leaf_level(step, carry):
        for j in range(2):
            r = 32 + step * 2 + j
            down = descend(r)
            for e in range(2):
                p = 2 * r + e - 64
                high, low = children(down, e, p)
                square = mxu_nt(leaf_ref[p], jnp.concatenate([high, low], axis=0))
                store_counts(p, square[:, 0:128] + square[:, 128:256])
        return carry

    lax.fori_loop(0, 8, leaf_level, 0)


def adjoint_kernel(
    members,
    chain_ref, turned_ref, slope_ref, power_ref, count_ref, log_ref, ex_ref, freq_ref, omega_ref,
    sense_ref, single_ref, nonsyn_ref,
    out_ref,
    back_ref, bins_ref,
):
    subtree = lax.axis_index("branch")
    mask = low_half()
    twice, pi_row, pi_col, root_row, root_col = frequencies(freq_ref, sense_ref)
    inverse_root_row = 1.0 / root_row

    def adjoint(step, carry):
        held = []
        for j in range(0, 8, 2):
            here = [count_ref[step * 8 + j + t] for t in range(2)]
            turned = transposes(*here)
            held += [0.5 * (here[t] + turned[t]) for t in range(2)]
        zero = jnp.zeros((128, 128), BF)
        for level in range(3, -1, -1):
            for j in range(0, 8, 2):
                parts, highs, lows = [], [], []
                for t in range(2):
                    high, low = split(held[j + t])
                    wide = spread(chain_ref[level, 0, step * 8 + j + t])
                    lows.append(spread(chain_ref[level, 1, step * 8 + j + t]))
                    highs.append(high)
                    parts.append(mxu(
                        jnp.concatenate([high, low], axis=1),
                        jnp.concatenate([wide, wide], axis=0),
                    ))
                rest = mxu(
                    jnp.concatenate(highs, axis=1),
                    jnp.concatenate([
                        jnp.concatenate([lows[0], zero], axis=1),
                        jnp.concatenate([zero, lows[1]], axis=1),
                    ], axis=0),
                )
                parts = [parts[t] + rest[:, 128 * t : 128 * t + 128] for t in range(2)]
                turned = transposes(*parts)
                for t in range(2):
                    held[j + t] = 2.0 * held[j + t] + parts[t] + turned[t]
        for j in range(8):
            back_ref[pl.ds(step * 8 + j, 64, stride=64), :] = held[j]
        return carry

    lax.fori_loop(0, PAIRS // 8, adjoint, 0)

    left = four_left(turned_ref[...])

    def sums(step, total):
        for j in range(4):
            ats = [rows_of(step * 8 + 2 * j + t, 64) for t in range(2)]
            values = [back_ref[at, :] for at in ats]
            both = mxu(left, four_right(jnp.concatenate(values, axis=1)))
            for t in range(2):
                total = total + values[t] * slope_ref[ats[t], :]
                here = both[:, 128 * t : 128 * t + 128]
                bins_ref[ats[t], :] = jnp.where(mask, here[0:64], here[64:128])
        return total

    slopes = lax.fori_loop(0, 8, sums, jnp.zeros((64, 128), F32)) * 0.0625

    table = symmetric_table(ex_ref, single_ref, twice)
    nonsyn = nonsyn_ref[...]
    row = lax.broadcasted_iota(jnp.int32, (64, 128), 0)
    lane = lax.broadcasted_iota(jnp.int32, (64, 128), 1)
    table_grad = jnp.zeros((64, 128), F32)
    omega_row = jnp.zeros((1, 128), F32)
    lane_row = lax.broadcasted_iota(jnp.int32, (1, 128), 1)
    for pair in range(CLASSES // 2):
        grads = []
        for k in range(ORDER):
            at = CLASSES * k + 2 * pair
            first = bins_ref[pl.ds(at, 64, stride=64), :]
            second = bins_ref[pl.ds(at + 1, 64, stride=64), :]
            first = first + pltpu.roll(first, 64, 1)
            second = second + pltpu.roll(second, 64, 1)
            grads.append(jnp.where(mask, first, second))
        g1, g2, g3, g4, g5, g6, g7, g8 = grads
        a1, a2, a3, a4 = [power_ref[pair, k] for k in range(4)]
        g4 = g4 + pair_products((g8, a4), (a4, g8), (g7, a3), (g6, a2), (g5, a1))
        g3 = g3 + pair_products((a4, g7))
        g2 = g2 + pair_products((a4, g6))
        g1 = g1 + pair_products((a4, g5))
        g2 = g2 + pair_products((g4, a2), (a2, g4), (g3, a1))
        g1 = g1 + pair_products((a2, g3))
        g1 = g1 + pair_products((g2, a1), (a1, g2))
        factor, off, rows, mean = class_pair(
            table, nonsyn, omega_ref, pair, twice, pi_row, pi_col
        )
        d_rate = root_col * g1 * inverse_root_row
        rate = (off - twice * rows) / mean
        weighted = d_rate * rate
        diagonal = d_rate * twice
        total0 = jnp.sum(jnp.where(mask, weighted, 0.0), axis=1, keepdims=True)
        total1 = jnp.sum(jnp.where(mask, 0.0, weighted), axis=1, keepdims=True)
        total0 = jnp.sum(total0, axis=0, keepdims=True)
        total1 = jnp.sum(total1, axis=0, keepdims=True)
        diag0 = jnp.sum(jnp.where(mask, diagonal, 0.0), axis=1, keepdims=True)
        diag1 = jnp.sum(jnp.where(mask, 0.0, diagonal), axis=1, keepdims=True)
        row_grad = jnp.where(mask, diag0 + pi_col * total0, diag1 + pi_col * total1)
        flux_grad = (d_rate - row_grad) * pi_row / mean
        table_grad = table_grad + flux_grad * factor * single_ref[...]
        ratio = flux_grad * table * nonsyn
        ratio0 = jnp.sum(jnp.where(mask, ratio, 0.0), axis=1, keepdims=True)
        ratio1 = jnp.sum(jnp.where(mask, 0.0, ratio), axis=1, keepdims=True)
        ratio0 = jnp.sum(ratio0, axis=0, keepdims=True)
        ratio1 = jnp.sum(ratio1, axis=0, keepdims=True)
        omega_row = jnp.where(lane_row == 2 * pair, ratio0, omega_row)
        omega_row = jnp.where(lane_row == 2 * pair + 1, ratio1, omega_row)
    table_grad = table_grad + pltpu.roll(table_grad, 64, 1)
    one = table_grad[:, 0:64]
    both = 0.5 * (exact(one, twice) + exact_tn(one, twice))
    masks, picks = neighbours()
    packed = jnp.zeros((16, 128), F32)
    for at_position, pick in zip(masks, picks):
        packed = packed + exact_tn(pick, jnp.where(at_position, both, 0.0))
    packed = jnp.where(lax.broadcasted_iota(jnp.int32, (16, 128), 1) < 64, packed, 0.0)

    even = jnp.sum(jnp.where(mask, slopes, 0.0), axis=1, keepdims=True)
    other = jnp.sum(jnp.where(mask, 0.0, slopes), axis=1, keepdims=True)
    placed = jnp.where(lane == 2 * row, even, 0.0) + jnp.where(lane == 2 * row + 1, other, 0.0)
    length_row = jnp.sum(placed, axis=0, keepdims=True)
    line = lax.broadcasted_iota(jnp.int32, out_ref.shape, 0)
    omega_row = jnp.where(lane_row == CLASSES, log_ref[0:1, :], omega_row)
    omega_row = pltpu.roll(jnp.broadcast_to(omega_row, (8, 128)), 64, 1)[0:1]
    packed = packed + jnp.where(line == 0, omega_row, 0.0)
    out_ref[...] = packed + jnp.where(line == 12 + subtree, length_row, 0.0)


def last_kernel(total_sites, count, *refs):
    members = lax.axis_size("branch")
    subtree = lax.axis_index("branch")
    exch_ref, omega_ref, length_ref, log_ref = refs[count:]
    total = tree_sum([ref[...] for ref in refs[:count]])
    masks, picks = neighbours()
    table = jnp.zeros((64, 128), F32)
    for at_position, pick in zip(masks, picks):
        table = table + jnp.where(at_position, exact(pick, total), 0.0)
    exch_ref[...] = table[:, 0:64]
    moved = pltpu.roll(total[0:8], 64, 1)
    omega_ref[...] = moved[0:1, 0:CLASSES]
    line = lax.broadcasted_iota(jnp.int32, total.shape, 0)
    lengths = jnp.sum(jnp.where(line == 12 + subtree, total, 0.0), axis=0, keepdims=True)
    length_ref[...] = lengths[:, 0:EDGES]
    log_ref[...] = moved[0:1, CLASSES : CLASSES + 1] / total_sites / (LEAF_DEV * members)


def partners(x, axis, start, radix):
    size = lax.axis_size(axis)
    others = [
        lax.ppermute(x, axis, [(i, i ^ (step * start)) for i in range(size)])
        for step in range(1, radix)
    ]
    return [x] + others


def tree_sum(parts):
    while len(parts) > 1:
        parts = [parts[i] + parts[i + 1] for i in range(0, len(parts), 2)]
    return parts[0]


def axis_steps(axis):
    size, start, steps = lax.axis_size(axis), 1, []
    while start < size:
        radix = min(4, size // start)
        steps.append((axis, start, radix))
        start *= radix
    return steps


def body(
    total_sites, states, gap_mask, weights, leaf_order, exchanges, codon_freq, omega_ratio,
    lengths, classes,
):
    sites = states.shape[1]
    members = lax.axis_size("branch")
    sense, single, nonsyn = codon_tables()
    vmem = pl.BlockSpec(memory_space=pltpu.VMEM)
    smem = pl.BlockSpec(memory_space=pltpu.SMEM)
    shape = jax.ShapeDtypeStruct
    held = pltpu.VMEM
    limit = pltpu.CompilerParams(vmem_limit_bytes=20 * 2**20)

    def outside(x):
        return pltpu.with_memory_space_constraint(x, pltpu.HBM)

    def inside(xs):
        return [pltpu.with_memory_space_constraint(x, pltpu.VMEM) for x in xs]

    sense2 = outside(jnp.asarray(np.tile(sense[None, :], (1, 2))))
    single2 = outside(jnp.asarray(np.tile(single, (1, 2))))
    nonsyn2 = outside(jnp.asarray(np.tile(nonsyn, (1, 2))))
    freq = outside(codon_freq.reshape(1, 64))
    span, owner = outside(lengths.reshape(1, EDGES)), outside(classes.reshape(1, EDGES))
    table, omega = outside(exchanges), outside(omega_ratio)

    chain, last, up, powers, dup = inside(pl.pallas_call(
        matrix_kernel,
        out_shape=[
            held((4, 2, PAIRS, 64, 128), BF),
            held((PAIRS, 64, 128), F32),
            held((2 * PAIRS, 64, 256), BF),
            held((CLASSES // 2, 4, 64, 128), F32),
            held((ORDER * CLASSES * 32, 128), F32),
        ],
        in_specs=[vmem, vmem, smem] + [vmem] * 5,
        out_specs=[vmem] * 5,
        scratch_shapes=[pltpu.VMEM((PAIRS * 64, 128), F32)],
        compiler_params=limit,
        name="matrices",
    )(table, freq, omega, span, owner, sense2, single2, nonsyn2))
    top, *kept = pl.pallas_call(
        up_kernel,
        out_shape=[
            shape((64, sites), F32),
            held((PAIRS, 128, sites), F32),
            held((64, 64, sites), BF),
            held((64, 64, sites), BF),
            held((32, 128, sites), BF),
            held((64, sites), F32),
            held((64, sites), F32),
        ],
        in_specs=[vmem, vmem, smem, vmem],
        out_specs=[vmem] * 7,
        compiler_params=limit,
        name="up",
    )(outside(states), outside(gap_mask), outside(leaf_order), up)
    message, high, low, leaf, scale, inverse = inside(kept)
    tops = partners(top, "branch", 1, members)
    slope, matrix, turned = inside(pl.pallas_call(
        side_kernel,
        out_shape=[
            held((PAIRS * 64, 128), F32),
            held((64, 64, 256), BF),
            held((128, 128), F32),
        ],
        in_specs=[vmem] * 6,
        out_specs=[vmem] * 3,
        compiler_params=limit,
        name="side",
    )(dup, last, span, owner, freq, sense2))
    counts, logs = inside(pl.pallas_call(
        functools.partial(down_kernel, total_sites, members),
        out_shape=[held((PAIRS, 64, 128), F32), held((8, 128), F32)],
        in_specs=[vmem] * (10 + members),
        out_specs=[vmem] * 2,
        scratch_shapes=[
            pltpu.VMEM((32, 128, sites), BF),
            pltpu.VMEM((32, 128, sites), BF),
        ],
        compiler_params=limit,
        name="down",
    )(
        *tops, matrix, message, high, low, leaf, scale, inverse,
        outside(weights.reshape(1, sites)), freq, sense2,
    ))
    part = pl.pallas_call(
        functools.partial(adjoint_kernel, members),
        out_shape=shape((16, 128), F32),
        in_specs=[vmem] * 8 + [smem] + [vmem] * 3,
        out_specs=vmem,
        scratch_shapes=[
            pltpu.VMEM((PAIRS * 64, 128), F32),
            pltpu.VMEM((64 * 64, 128), F32),
        ],
        compiler_params=limit,
        name="adjoint",
    )(
        chain, turned, slope, powers, counts, logs, table, freq, omega,
        sense2, single2, nonsyn2,
    )
    steps = axis_steps("branch") + axis_steps("site")
    for step in steps[:-1]:
        part = tree_sum(partners(part, *step))
    parts = partners(part, *steps[-1])
    exch, ratio, length, loglik = pl.pallas_call(
        functools.partial(last_kernel, total_sites, len(parts)),
        out_shape=[shape((64, 64), F32), shape((1, CLASSES), F32), shape((1, EDGES), F32), shape((1, 1), F32)],
        in_specs=[vmem] * len(parts),
        out_specs=[vmem] * 4,
        compiler_params=limit,
        name="last",
    )(*parts)
    return (exch, ratio.reshape(CLASSES), length.reshape(EDGES), loglik.reshape(()))


def solution(mesh):
    def whole(states, *rest):
        total_sites = states.shape[1]
        return jax.shard_map(
            functools.partial(body, total_sites),
            mesh=mesh,
            in_specs=(
                P(None, "site"),
                P(None, "site"),
                P("site"),
                P(),
                P(),
                P(),
                P(),
                P("branch"),
                P("branch"),
            ),
            out_specs=(P(), P(), P("branch"), P()),
            check_vma=False,
        )(states, *rest)

    return whole
```

```python
import functools
import jax
import jax.numpy as jnp
import numpy as np
from jax import lax
from jax.experimental import pallas as pl
from jax.experimental.pallas import tpu as pltpu
from jax.sharding import PartitionSpec as P

LEAF_DEV = 64
EDGES = 127
PAIRS = 64
CLASSES = 8
ORDER = 8
BF = jnp.bfloat16
F32 = jnp.float32

CODE_TABLE = "FFLLSSSSYYXXCCXWLLLLPPPPHHQQRRRRIIIMTTTTNNKKSSRRVVVVAAAADDEEGGGG"


def codon_tables():
    amino_acid = np.array(list(CODE_TABLE))
    codon_index = np.arange(64)
    digits = np.stack([codon_index // 16, codon_index // 4 % 4, codon_index % 4], 1)
    differ = (digits[:, None, :] != digits[None, :, :]).sum(-1)
    is_sense = amino_acid != "X"
    single = (differ == 1) & is_sense[:, None] & is_sense[None, :]
    nonsyn = single & (amino_acid[:, None] != amino_acid[None, :])
    return (is_sense.astype(np.float32), single.astype(np.float32), nonsyn.astype(np.float32))


def low_half():
    return lax.broadcasted_iota(jnp.int32, (64, 128), 1) < 64


def split(x):
    high = x.astype(BF)
    low = (x - high.astype(F32)).astype(BF)
    return high, low


def spread(x, scale=1.0):
    mask = low_half()
    low = jnp.where(mask, scale, 0.0).astype(x.dtype)
    high = jnp.where(mask, 0.0, scale).astype(x.dtype)
    return jnp.concatenate([x * low, x * high], axis=0)


def two_blocks(pairs, zero):
    return jnp.concatenate([
        jnp.concatenate([spread(pairs[0]), zero], axis=1),
        jnp.concatenate([zero, spread(pairs[1])], axis=1),
    ], axis=0)


def mxu(left, right):
    return jnp.dot(left, right, preferred_element_type=F32)


def mxu_nt(left, right):
    return lax.dot_general(left, right, (((1,), (1,)), ((), ())), preferred_element_type=F32)


def exact(left, right):
    return jnp.dot(left, right, preferred_element_type=F32, precision=lax.Precision.HIGHEST)


def exact_tn(left, right):
    return lax.dot_general(
        left, right, (((0,), (0,)), ((), ())), preferred_element_type=F32,
        precision=lax.Precision.HIGHEST,
    )


def pair_products(*terms):
    lefts, rights = [], []
    for left, right in terms:
        left_high, left_low = split(left)
        right_high, right_low = split(right)
        wide_high, wide_low = spread(right_high), spread(right_low)
        lefts += [left_high, left_high, left_low]
        rights += [wide_high, wide_low, wide_high]
    return mxu(jnp.concatenate(lefts, axis=1), jnp.concatenate(rights, axis=0))


def messages(matrix, high, low):
    return mxu(matrix, jnp.concatenate([high, low, high, low], axis=0))


def double(ref, p, x):
    mask = low_half()
    swapped = pltpu.roll(x, 64, 1)
    for e, both in enumerate((jnp.where(mask, x, swapped), jnp.where(mask, swapped, x))):
        high, low = split(both)
        ref[2 * p + e] = jnp.concatenate([high, low], axis=1)


def frequencies(freq_ref, sense_ref):
    row = lax.broadcasted_iota(jnp.int32, (64, 128), 0)
    lane = lax.broadcasted_iota(jnp.int32, (64, 128), 1)
    twice = (row == lane % 64).astype(F32)
    sense2 = sense_ref[...]
    freq2 = exact(jnp.broadcast_to(freq_ref[...], (8, 64)), twice)[0:1] * sense2
    total = 0.5 * jnp.sum(freq2, axis=1, keepdims=True)
    pi_row = freq2 / total
    pi_col = 0.5 * jnp.sum(twice * pi_row, axis=1, keepdims=True)
    sense_col = 0.5 * jnp.sum(twice * sense2, axis=1, keepdims=True)
    root_row = jnp.sqrt(jnp.where(sense2 > 0, pi_row, 1.0))
    root_col = jnp.sqrt(jnp.where(sense_col > 0, pi_col, 1.0))
    return twice, pi_row, pi_col, root_row, root_col


def symmetric_table(ex_ref, single_ref, twice):
    ex = ex_ref[...]
    return 0.5 * (exact(ex, twice) + exact_tn(ex, twice)) * single_ref[...]


def class_pair(table, nonsyn, omega_ref, pair, twice, pi_row, pi_col):
    mask = low_half()
    omega = jnp.where(mask, omega_ref[2 * pair], omega_ref[2 * pair + 1])
    factor = 1.0 + nonsyn * (omega - 1.0)
    flux = table * factor
    off = flux * pi_row
    row0 = jnp.sum(jnp.where(mask, off, 0.0), axis=1, keepdims=True)
    row1 = jnp.sum(jnp.where(mask, 0.0, off), axis=1, keepdims=True)
    mean0 = jnp.sum(pi_col * row0, axis=0, keepdims=True)
    mean1 = jnp.sum(pi_col * row1, axis=0, keepdims=True)
    rows = jnp.where(mask, row0, row1)
    mean = jnp.where(mask, mean0, mean1)
    return factor, off, rows, mean


def neighbours():
    row = lax.broadcasted_iota(jnp.int32, (64, 128), 0)
    lane = lax.broadcasted_iota(jnp.int32, (64, 128), 1) % 64
    masks = [
        row % 16 == lane % 16,
        (row // 16 == lane // 16) & (row % 4 == lane % 4),
        row // 4 == lane // 4,
    ]
    codon = lax.broadcasted_iota(jnp.int32, (64, 16), 0)
    column = lax.broadcasted_iota(jnp.int32, (64, 16), 1)
    digits = [codon // 16, codon // 4 % 4, codon % 4]
    picks = [(column == 4 * p + digits[p]).astype(F32) for p in range(3)]
    return masks, picks


def coefficients(len_ref, cls_ref, slope):
    lane = lax.broadcasted_iota(jnp.int32, (PAIRS, EDGES), 1)
    row = lax.broadcasted_iota(jnp.int32, (PAIRS, EDGES), 0)
    lengths = len_ref[...] * 0.0625
    classes = cls_ref[...].astype(F32)
    place = lax.broadcasted_iota(jnp.int32, (PAIRS, 128), 1) % 64
    found = []
    for odd in range(2):
        here = lane == 2 * row + odd
        y = jnp.sum(jnp.where(here, lengths, 0.0), axis=1, keepdims=True)
        owner = jnp.sum(jnp.where(here, classes, 0.0), axis=1, keepdims=True)
        current = jnp.ones((PAIRS, 128), F32)
        series = jnp.zeros((PAIRS, 128), F32)
        for k in range(ORDER):
            following = current * y * (1.0 / (k + 1))
            series = jnp.where(place // CLASSES == k, current if slope else following, series)
            current = following
        found.append(jnp.where((place % CLASSES).astype(F32) == owner, series, 0.0))
    return found


def four_left(x):
    high, low = split(x)
    return jnp.concatenate([high, low], axis=1)


def four_right(x):
    high, low = split(x)
    return jnp.concatenate([high, low, high, low], axis=0)


def expand(coefs, dup_ref, store):
    high, low = split(coefs)
    left = jnp.concatenate(
        [jnp.concatenate([high, high], axis=1), jnp.concatenate([low, low], axis=1)], axis=0
    )

    def some(step, carry):
        for j in range(4):
            i = step * 8 + 2 * j
            parts = [split(dup_ref[rows_of(i + t, 64), :]) for t in range(2)]
            right = jnp.concatenate([
                jnp.concatenate([spread(parts[0][h]), spread(parts[1][h])], axis=1)
                for h in range(2)
            ], axis=0)
            both = mxu(left, right)
            both = both[0:64] + both[64:128]
            for t in range(2):
                store(i + t, both[:, 128 * t : 128 * t + 128])
        return carry

    lax.fori_loop(0, 8, some, 0)


def rows_of(step, width):
    return pl.ds(pl.multiple_of(step * width, width), width)


def matrix_kernel(
    ex_ref, freq_ref, omega_ref, len_ref, cls_ref, sense_ref, single_ref, nonsyn_ref,
    chain_ref, last_ref, up_ref, power_ref, dup_ref,
    first_ref,
):
    mask = low_half()
    twice, pi_row, pi_col, root_row, root_col = frequencies(freq_ref, sense_ref)
    table = symmetric_table(ex_ref, single_ref, twice)
    nonsyn = nonsyn_ref[...]

    powers = []
    for pair in range(CLASSES // 2):
        factor, off, rows, mean = class_pair(
            table, nonsyn, omega_ref, pair, twice, pi_row, pi_col
        )
        powers.append([(table * factor * root_col * root_row - twice * rows) / mean])
    for left, right in ((0, 0), (1, 0), (1, 1), (3, 0), (3, 1), (3, 2), (3, 3)):
        for pair in range(CLASSES // 2):
            powers[pair].append(pair_products((powers[pair][left], powers[pair][right])))
    for pair in range(CLASSES // 2):
        for k in range(ORDER):
            value = powers[pair][k]
            swapped = pltpu.roll(value, 64, 1)
            at = CLASSES * k + 2 * pair
            dup_ref[pl.ds(at, 64, stride=64), :] = jnp.where(mask, value, swapped)
            dup_ref[pl.ds(at + 1, 64, stride=64), :] = jnp.where(mask, swapped, value)
            if k < 4:
                power_ref[pair, k] = value

    even, odd = coefficients(len_ref, cls_ref, False)

    def store(i, value):
        first_ref[rows_of(i, 64), :] = value

    expand(jnp.where(low_half(), even, odd), dup_ref, store)

    def squarings(step, carry):
        held = [first_ref[pl.ds(step * 8 + j, 64, stride=64), :] for j in range(8)]
        zero = jnp.zeros((128, 128), BF)
        for level in range(4):
            for j in range(0, 8, 2):
                highs, lows = [], []
                for t in range(2):
                    high, low = split(held[j + t])
                    chain_ref[level, 0, step * 8 + j + t] = high
                    chain_ref[level, 1, step * 8 + j + t] = low
                    highs.append(high)
                    lows.append(low)
                upper, lower = jnp.concatenate(highs, axis=1), jnp.concatenate(lows, axis=1)
                one = mxu(jnp.concatenate([upper, lower], axis=0), two_blocks(highs, zero))
                two = mxu(upper, two_blocks(lows, zero))
                both = one[0:64] + one[64:128] + two
                for t in range(2):
                    held[j + t] = 2.0 * held[j + t] + both[:, 128 * t : 128 * t + 128]
        for j in range(8):
            p = step * 8 + j
            last_ref[p] = held[j]
            double(up_ref, p, inverse_root_col * (held[j] + twice) * root_row)
        return carry

    inverse_root_col = 1.0 / root_col
    lax.fori_loop(0, PAIRS // 8, squarings, 0)


def up_kernel(
    states_ref, gap_ref, order_ref, up_ref,
    top_ref, message_ref, high_ref, low_ref, leaf_ref, scale_ref, inverse_ref,
):
    subtree = lax.axis_index("branch")

    def finish(p, message):
        message_ref[p] = jnp.concatenate(message, axis=0)
        raw = message[0] * message[1]
        scaling = jnp.sum(raw, axis=0, keepdims=True)
        inverse = 1.0 / scaling
        scale_ref[pl.ds(p, 1), :] = scaling
        inverse_ref[pl.ds(p, 1), :] = inverse
        high, low = split(raw * inverse)
        high_ref[p] = high
        low_ref[p] = low

    sites = states_ref.shape[1]
    codon = lax.broadcasted_iota(jnp.int32, (64, sites), 0)

    def leaf_level(step, carry):
        for j in range(4):
            p = step * 4 + j
            both = []
            for e in range(2):
                taxon = order_ref[subtree * LEAF_DEV + 2 * p + e]
                state = jnp.where(
                    gap_ref[pl.ds(taxon, 1), :] > 0, -1, states_ref[pl.ds(taxon, 1), :]
                )
                hit = (codon == state) | (state < 0)
                both.append(jnp.where(hit, 1.0, 0.0).astype(BF))
            leaf_ref[p] = jnp.concatenate(both, axis=0)
            nothing = jnp.zeros_like(both[0])
            finish(p, [messages(up_ref[2 * p + e], both[e], nothing) for e in range(2)])
        return carry

    lax.fori_loop(0, LEAF_DEV // 8, leaf_level, 0)

    def inner(p):
        child = 2 * p - 64
        return [
            messages(up_ref[2 * p + e], high_ref[child + e], low_ref[child + e]) for e in range(2)
        ]

    def second_level(step, carry):
        for j in range(4):
            finish(32 + step * 4 + j, inner(32 + step * 4 + j))
        return carry

    lax.fori_loop(0, 4, second_level, 0)
    for p in range(48, 63):
        finish(p, inner(p))
    high_ref[63] = jnp.zeros((64, sites), BF)
    low_ref[63] = jnp.zeros((64, sites), BF)
    scale_ref[63:64, :] = jnp.ones((1, sites), F32)
    inverse_ref[63:64, :] = jnp.ones((1, sites), F32)
    top = inner(63)
    message_ref[63] = jnp.concatenate(top, axis=0)
    top_ref[...] = top[0]


def side_kernel(
    dup_ref, last_ref, len_ref, cls_ref, freq_ref, sense_ref, slope_ref, matrix_ref, turned_ref,
):
    twice, pi_row, pi_col, root_row, root_col = frequencies(freq_ref, sense_ref)
    even, odd = coefficients(len_ref, cls_ref, True)

    def store(i, value):
        slope_ref[rows_of(i, 64), :] = value

    expand(jnp.where(low_half(), even, odd), dup_ref, store)
    even, odd = coefficients(len_ref, cls_ref, False)
    turned_ref[...] = exact_tn(jnp.where(low_half(), even, odd), twice)
    inverse_root_row = 1.0 / root_row

    def matrices(step, carry):
        for j in range(8):
            r = step * 8 + j
            double(matrix_ref, r, root_col * (last_ref[32 + r] + twice) * inverse_root_row)
        return carry

    lax.fori_loop(0, 4, matrices, 0)


def down_kernel(total_sites, members, *refs):
    tops = refs[:members]
    (
        matrix_ref, message_ref, high_ref, low_ref, leaf_ref, scale_ref, inverse_ref,
        weights_ref, freq_ref, sense_ref,
        count_ref, log_ref,
        a_high_ref, a_low_ref,
    ) = refs[members:]
    subtree = lax.axis_index("branch")
    mask = low_half()
    twice, pi_row, pi_col, root_row, root_col = frequencies(freq_ref, sense_ref)
    inverse_root_row, inverse_root_col = 1.0 / root_row, 1.0 / root_col
    sites = weights_ref.shape[1]
    weight = weights_ref[...].astype(F32)

    above = jnp.broadcast_to(pi_col, (64, sites))
    for other in tops[1:]:
        above = above * other[...]
    own = tops[0][...]
    likelihood = jnp.sum(above * own, axis=0, keepdims=True)
    logs = jnp.sum(jnp.log(scale_ref[...]), axis=0, keepdims=True)
    logs = logs + jnp.where(subtree == 0, jnp.log(likelihood), 0.0)
    log_ref[...] = jnp.broadcast_to(jnp.sum(weight * logs, axis=1, keepdims=True), (8, 128))
    high, low = split(above * (weight / (likelihood * total_sites)))
    a_high_ref[31, 0:64, :] = high
    a_low_ref[31, 0:64, :] = low
    a_high_ref[31, 64:128, :] = jnp.zeros((64, sites), BF)
    a_low_ref[31, 64:128, :] = jnp.zeros((64, sites), BF)

    def store_counts(p, square):
        counts = jnp.where(mask, square[0:64], square[64:128])
        count_ref[p] = root_col * counts * inverse_root_row

    def descend(r):
        a_high, a_low = a_high_ref[r - 32], a_low_ref[r - 32]
        child = 2 * r - 64
        u_high = jnp.concatenate([high_ref[child], high_ref[child + 1]], axis=0)
        u_low = jnp.concatenate([low_ref[child], low_ref[child + 1]], axis=0)
        first = mxu_nt(u_high, jnp.concatenate([a_high, a_low], axis=0))
        second = mxu_nt(u_low, a_high)
        store_counts(r, first[:, 0:128] + first[:, 128:256] + second)
        return [
            messages(
                matrix_ref[2 * (r - 32) + e], a_high[64 * e : 64 * e + 64], a_low[64 * e : 64 * e + 64]
            )
            for e in range(2)
        ]

    def children(down, e, p):
        vector = down[e]
        inverse = inverse_ref[pl.ds(p, 1), :]
        message = message_ref[p]
        pair = jnp.concatenate(
            [vector * message[64:128] * inverse, vector * message[0:64] * inverse], axis=0
        )
        return split(pair)

    def inner(r):
        down = descend(r)
        for e in range(2):
            p = 2 * r + e - 64
            if isinstance(p, int) and p == 63:
                continue
            high, low = children(down, e, p)
            a_high_ref[p - 32] = high
            a_low_ref[p - 32] = low

    for r in range(63, 47, -1):
        inner(r)

    def leaf_level(step, carry):
        for j in range(2):
            r = 32 + step * 2 + j
            down = descend(r)
            for e in range(2):
                p = 2 * r + e - 64
                high, low = children(down, e, p)
                square = mxu_nt(leaf_ref[p], jnp.concatenate([high, low], axis=0))
                store_counts(p, square[:, 0:128] + square[:, 128:256])
        return carry

    lax.fori_loop(0, 8, leaf_level, 0)


def adjoint_kernel(
    members,
    chain_ref, turned_ref, slope_ref, power_ref, count_ref, log_ref, ex_ref, freq_ref, omega_ref,
    sense_ref, single_ref, nonsyn_ref,
    out_ref,
    back_ref, bins_ref,
):
    subtree = lax.axis_index("branch")
    mask = low_half()
    twice, pi_row, pi_col, root_row, root_col = frequencies(freq_ref, sense_ref)
    inverse_root_row = 1.0 / root_row

    def adjoint(step, carry):
        held = [count_ref[step * 8 + j] for j in range(8)]
        for level in range(3, -1, -1):
            for j in range(8):
                high, low = split(held[j])
                e_high, e_low = chain_ref[level, 0, step * 8 + j], chain_ref[level, 1, step * 8 + j]
                left = jnp.concatenate([
                    jnp.concatenate([high, e_high], axis=1),
                    jnp.concatenate([low, e_low], axis=1),
                ], axis=0)
                right = jnp.concatenate([
                    jnp.concatenate([spread(e_high), spread(e_low)], axis=1),
                    jnp.concatenate([spread(high), spread(low)], axis=1),
                ], axis=0)
                four = mxu(left, right)
                four = four[0:64] + four[64:128]
                held[j] = 2.0 * held[j] + four[:, 0:128] + four[:, 128:256]
        for j in range(8):
            back_ref[pl.ds(step * 8 + j, 64, stride=64), :] = held[j]
        return carry

    lax.fori_loop(0, PAIRS // 8, adjoint, 0)

    left = four_left(turned_ref[...])

    def sums(step, total):
        for j in range(4):
            ats = [rows_of(step * 8 + 2 * j + t, 64) for t in range(2)]
            values = [back_ref[at, :] for at in ats]
            both = mxu(left, four_right(jnp.concatenate(values, axis=1)))
            for t in range(2):
                total = total + values[t] * slope_ref[ats[t], :]
                here = both[:, 128 * t : 128 * t + 128]
                bins_ref[ats[t], :] = jnp.where(mask, here[0:64], here[64:128])
        return total

    slopes = lax.fori_loop(0, 8, sums, jnp.zeros((64, 128), F32)) * 0.0625

    table = symmetric_table(ex_ref, single_ref, twice)
    nonsyn = nonsyn_ref[...]
    row = lax.broadcasted_iota(jnp.int32, (64, 128), 0)
    lane = lax.broadcasted_iota(jnp.int32, (64, 128), 1)
    table_grad = jnp.zeros((64, 128), F32)
    omega_row = jnp.zeros((1, 128), F32)
    lane_row = lax.broadcasted_iota(jnp.int32, (1, 128), 1)
    for pair in range(CLASSES // 2):
        grads = []
        for k in range(ORDER):
            at = CLASSES * k + 2 * pair
            first = bins_ref[pl.ds(at, 64, stride=64), :]
            second = bins_ref[pl.ds(at + 1, 64, stride=64), :]
            first = first + pltpu.roll(first, 64, 1)
            second = second + pltpu.roll(second, 64, 1)
            grads.append(jnp.where(mask, first, second))
        g1, g2, g3, g4, g5, g6, g7, g8 = grads
        a1, a2, a3, a4 = [power_ref[pair, k] for k in range(4)]
        g4 = g4 + pair_products((g8, a4), (a4, g8), (g7, a3), (g6, a2), (g5, a1))
        g3 = g3 + pair_products((a4, g7))
        g2 = g2 + pair_products((a4, g6))
        g1 = g1 + pair_products((a4, g5))
        g2 = g2 + pair_products((g4, a2), (a2, g4), (g3, a1))
        g1 = g1 + pair_products((a2, g3))
        g1 = g1 + pair_products((g2, a1), (a1, g2))
        factor, off, rows, mean = class_pair(
            table, nonsyn, omega_ref, pair, twice, pi_row, pi_col
        )
        d_rate = root_col * g1 * inverse_root_row
        rate = (off - twice * rows) / mean
        weighted = d_rate * rate
        diagonal = d_rate * twice
        total0 = jnp.sum(jnp.where(mask, weighted, 0.0), axis=1, keepdims=True)
        total1 = jnp.sum(jnp.where(mask, 0.0, weighted), axis=1, keepdims=True)
        total0 = jnp.sum(total0, axis=0, keepdims=True)
        total1 = jnp.sum(total1, axis=0, keepdims=True)
        diag0 = jnp.sum(jnp.where(mask, diagonal, 0.0), axis=1, keepdims=True)
        diag1 = jnp.sum(jnp.where(mask, 0.0, diagonal), axis=1, keepdims=True)
        row_grad = jnp.where(mask, diag0 + pi_col * total0, diag1 + pi_col * total1)
        flux_grad = (d_rate - row_grad) * pi_row / mean
        table_grad = table_grad + flux_grad * factor * single_ref[...]
        ratio = flux_grad * table * nonsyn
        ratio0 = jnp.sum(jnp.where(mask, ratio, 0.0), axis=1, keepdims=True)
        ratio1 = jnp.sum(jnp.where(mask, 0.0, ratio), axis=1, keepdims=True)
        ratio0 = jnp.sum(ratio0, axis=0, keepdims=True)
        ratio1 = jnp.sum(ratio1, axis=0, keepdims=True)
        omega_row = jnp.where(lane_row == 2 * pair, ratio0, omega_row)
        omega_row = jnp.where(lane_row == 2 * pair + 1, ratio1, omega_row)
    table_grad = table_grad + pltpu.roll(table_grad, 64, 1)
    one = table_grad[:, 0:64]
    both = 0.5 * (exact(one, twice) + exact_tn(one, twice))
    masks, picks = neighbours()
    packed = jnp.zeros((16, 128), F32)
    for at_position, pick in zip(masks, picks):
        packed = packed + exact_tn(pick, jnp.where(at_position, both, 0.0))
    packed = jnp.where(lax.broadcasted_iota(jnp.int32, (16, 128), 1) < 64, packed, 0.0)

    even = jnp.sum(jnp.where(mask, slopes, 0.0), axis=1, keepdims=True)
    other = jnp.sum(jnp.where(mask, 0.0, slopes), axis=1, keepdims=True)
    placed = jnp.where(lane == 2 * row, even, 0.0) + jnp.where(lane == 2 * row + 1, other, 0.0)
    length_row = jnp.sum(placed, axis=0, keepdims=True)
    line = lax.broadcasted_iota(jnp.int32, out_ref.shape, 0)
    omega_row = jnp.where(lane_row == CLASSES, log_ref[0:1, :], omega_row)
    omega_row = pltpu.roll(jnp.broadcast_to(omega_row, (8, 128)), 64, 1)[0:1]
    packed = packed + jnp.where(line == 0, omega_row, 0.0)
    out_ref[...] = packed + jnp.where(line == 12 + subtree, length_row, 0.0)


def last_kernel(total_sites, count, *refs):
    members = lax.axis_size("branch")
    subtree = lax.axis_index("branch")
    exch_ref, omega_ref, length_ref, log_ref = refs[count:]
    total = tree_sum([ref[...] for ref in refs[:count]])
    masks, picks = neighbours()
    table = jnp.zeros((64, 128), F32)
    for at_position, pick in zip(masks, picks):
        table = table + jnp.where(at_position, exact(pick, total), 0.0)
    exch_ref[...] = table[:, 0:64]
    moved = pltpu.roll(total[0:8], 64, 1)
    omega_ref[...] = moved[0:1, 0:CLASSES]
    line = lax.broadcasted_iota(jnp.int32, total.shape, 0)
    lengths = jnp.sum(jnp.where(line == 12 + subtree, total, 0.0), axis=0, keepdims=True)
    length_ref[...] = lengths[:, 0:EDGES]
    log_ref[...] = moved[0:1, CLASSES : CLASSES + 1] / total_sites / (LEAF_DEV * members)


def partners(x, axis, start, radix):
    size = lax.axis_size(axis)
    others = [
        lax.ppermute(x, axis, [(i, i ^ (step * start)) for i in range(size)])
        for step in range(1, radix)
    ]
    return [x] + others


def tree_sum(parts):
    while len(parts) > 1:
        parts = [parts[i] + parts[i + 1] for i in range(0, len(parts), 2)]
    return parts[0]


def axis_steps(axis):
    size, start, steps = lax.axis_size(axis), 1, []
    while start < size:
        radix = min(4, size // start)
        steps.append((axis, start, radix))
        start *= radix
    return steps


def body(
    total_sites, states, gap_mask, weights, leaf_order, exchanges, codon_freq, omega_ratio,
    lengths, classes,
):
    sites = states.shape[1]
    members = lax.axis_size("branch")
    sense, single, nonsyn = codon_tables()
    vmem = pl.BlockSpec(memory_space=pltpu.VMEM)
    smem = pl.BlockSpec(memory_space=pltpu.SMEM)
    shape = jax.ShapeDtypeStruct
    held = pltpu.VMEM
    limit = pltpu.CompilerParams(vmem_limit_bytes=20 * 2**20)

    def outside(x):
        return pltpu.with_memory_space_constraint(x, pltpu.HBM)

    def inside(xs):
        return [pltpu.with_memory_space_constraint(x, pltpu.VMEM) for x in xs]

    sense2 = outside(jnp.asarray(np.tile(sense[None, :], (1, 2))))
    single2 = outside(jnp.asarray(np.tile(single, (1, 2))))
    nonsyn2 = outside(jnp.asarray(np.tile(nonsyn, (1, 2))))
    freq = outside(codon_freq.reshape(1, 64))
    span, owner = outside(lengths.reshape(1, EDGES)), outside(classes.reshape(1, EDGES))
    table, omega = outside(exchanges), outside(omega_ratio)

    chain, last, up, powers, dup = inside(pl.pallas_call(
        matrix_kernel,
        out_shape=[
            held((4, 2, PAIRS, 64, 128), BF),
            held((PAIRS, 64, 128), F32),
            held((2 * PAIRS, 64, 256), BF),
            held((CLASSES // 2, 4, 64, 128), F32),
            held((ORDER * CLASSES * 64, 128), F32),
        ],
        in_specs=[vmem, vmem, smem] + [vmem] * 5,
        out_specs=[vmem] * 5,
        scratch_shapes=[pltpu.VMEM((PAIRS * 64, 128), F32)],
        compiler_params=limit,
        name="matrices",
    )(table, freq, omega, span, owner, sense2, single2, nonsyn2))
    top, *kept = pl.pallas_call(
        up_kernel,
        out_shape=[
            shape((64, sites), F32),
            held((PAIRS, 128, sites), F32),
            held((64, 64, sites), BF),
            held((64, 64, sites), BF),
            held((32, 128, sites), BF),
            held((64, sites), F32),
            held((64, sites), F32),
        ],
        in_specs=[vmem, vmem, smem, vmem],
        out_specs=[vmem] * 7,
        compiler_params=limit,
        name="up",
    )(outside(states), outside(gap_mask), outside(leaf_order), up)
    message, high, low, leaf, scale, inverse = inside(kept)
    tops = partners(top, "branch", 1, members)
    slope, matrix, turned = inside(pl.pallas_call(
        side_kernel,
        out_shape=[
            held((PAIRS * 64, 128), F32),
            held((64, 64, 256), BF),
            held((128, 128), F32),
        ],
        in_specs=[vmem] * 6,
        out_specs=[vmem] * 3,
        compiler_params=limit,
        name="side",
    )(dup, last, span, owner, freq, sense2))
    counts, logs = inside(pl.pallas_call(
        functools.partial(down_kernel, total_sites, members),
        out_shape=[held((PAIRS, 64, 128), F32), held((8, 128), F32)],
        in_specs=[vmem] * (10 + members),
        out_specs=[vmem] * 2,
        scratch_shapes=[
            pltpu.VMEM((32, 128, sites), BF),
            pltpu.VMEM((32, 128, sites), BF),
        ],
        compiler_params=limit,
        name="down",
    )(
        *tops, matrix, message, high, low, leaf, scale, inverse,
        outside(weights.reshape(1, sites)), freq, sense2,
    ))
    part = pl.pallas_call(
        functools.partial(adjoint_kernel, members),
        out_shape=shape((16, 128), F32),
        in_specs=[vmem] * 8 + [smem] + [vmem] * 3,
        out_specs=vmem,
        scratch_shapes=[
            pltpu.VMEM((PAIRS * 64, 128), F32),
            pltpu.VMEM((64 * 64, 128), F32),
        ],
        compiler_params=limit,
        name="adjoint",
    )(
        chain, turned, slope, powers, counts, logs, table, freq, omega,
        sense2, single2, nonsyn2,
    )
    steps = axis_steps("branch") + axis_steps("site")
    for step in steps[:-1]:
        part = tree_sum(partners(part, *step))
    parts = partners(part, *steps[-1])
    exch, ratio, length, loglik = pl.pallas_call(
        functools.partial(last_kernel, total_sites, len(parts)),
        out_shape=[shape((64, 64), F32), shape((1, CLASSES), F32), shape((1, EDGES), F32), shape((1, 1), F32)],
        in_specs=[vmem] * len(parts),
        out_specs=[vmem] * 4,
        compiler_params=limit,
        name="last",
    )(*parts)
    return (exch, ratio.reshape(CLASSES), length.reshape(EDGES), loglik.reshape(()))


def solution(mesh):
    def whole(states, *rest):
        total_sites = states.shape[1]
        return jax.shard_map(
            functools.partial(body, total_sites),
            mesh=mesh,
            in_specs=(
                P(None, "site"),
                P(None, "site"),
                P("site"),
                P(),
                P(),
                P(),
                P(),
                P("branch"),
                P("branch"),
            ),
            out_specs=(P(), P(), P("branch"), P()),
            check_vma=False,
        )(states, *rest)

    return whole
```

```python
import functools
import jax
import jax.numpy as jnp
import numpy as np
from jax import lax
from jax.experimental import pallas as pl
from jax.experimental.pallas import tpu as pltpu
from jax.sharding import PartitionSpec as P

LEAF_DEV = 64
EDGES = 127
PAIRS = 64
CLASSES = 8
ORDER = 8
BF = jnp.bfloat16
F32 = jnp.float32

CODE_TABLE = "FFLLSSSSYYXXCCXWLLLLPPPPHHQQRRRRIIIMTTTTNNKKSSRRVVVVAAAADDEEGGGG"


def codon_tables():
    amino_acid = np.array(list(CODE_TABLE))
    codon_index = np.arange(64)
    digits = np.stack([codon_index // 16, codon_index // 4 % 4, codon_index % 4], 1)
    differ = (digits[:, None, :] != digits[None, :, :]).sum(-1)
    is_sense = amino_acid != "X"
    single = (differ == 1) & is_sense[:, None] & is_sense[None, :]
    nonsyn = single & (amino_acid[:, None] != amino_acid[None, :])
    return (is_sense.astype(np.float32), single.astype(np.float32), nonsyn.astype(np.float32))


def low_half():
    return lax.broadcasted_iota(jnp.int32, (64, 128), 1) < 64


def split(x):
    high = x.astype(BF)
    low = (x - high.astype(F32)).astype(BF)
    return high, low


def spread(x, scale=1.0):
    mask = low_half()
    low = jnp.where(mask, scale, 0.0).astype(x.dtype)
    high = jnp.where(mask, 0.0, scale).astype(x.dtype)
    return jnp.concatenate([x * low, x * high], axis=0)


def mxu(left, right):
    return jnp.dot(left, right, preferred_element_type=F32)


def mxu_nt(left, right):
    return lax.dot_general(left, right, (((1,), (1,)), ((), ())), preferred_element_type=F32)


def exact(left, right):
    return jnp.dot(left, right, preferred_element_type=F32, precision=lax.Precision.HIGHEST)


def exact_tn(left, right):
    return lax.dot_general(
        left, right, (((0,), (0,)), ((), ())), preferred_element_type=F32,
        precision=lax.Precision.HIGHEST,
    )


def pair_products(*terms):
    lefts, rights = [], []
    for left, right in terms:
        left_high, left_low = split(left)
        right_high, right_low = split(right)
        wide_high, wide_low = spread(right_high), spread(right_low)
        lefts += [left_high, left_high, left_low]
        rights += [wide_high, wide_low, wide_high]
    return mxu(jnp.concatenate(lefts, axis=1), jnp.concatenate(rights, axis=0))


def messages(matrix, high, low):
    return mxu(matrix, jnp.concatenate([high, low, high, low], axis=0))


def double(ref, p, x):
    mask = low_half()
    swapped = pltpu.roll(x, 64, 1)
    for e, both in enumerate((jnp.where(mask, x, swapped), jnp.where(mask, swapped, x))):
        high, low = split(both)
        ref[2 * p + e] = jnp.concatenate([high, low], axis=1)


def frequencies(freq_ref, sense_ref):
    row = lax.broadcasted_iota(jnp.int32, (64, 128), 0)
    lane = lax.broadcasted_iota(jnp.int32, (64, 128), 1)
    twice = (row == lane % 64).astype(F32)
    sense2 = sense_ref[...]
    freq2 = exact(jnp.broadcast_to(freq_ref[...], (8, 64)), twice)[0:1] * sense2
    total = 0.5 * jnp.sum(freq2, axis=1, keepdims=True)
    pi_row = freq2 / total
    pi_col = 0.5 * jnp.sum(twice * pi_row, axis=1, keepdims=True)
    sense_col = 0.5 * jnp.sum(twice * sense2, axis=1, keepdims=True)
    root_row = jnp.sqrt(jnp.where(sense2 > 0, pi_row, 1.0))
    root_col = jnp.sqrt(jnp.where(sense_col > 0, pi_col, 1.0))
    return twice, pi_row, pi_col, root_row, root_col


def symmetric_table(ex_ref, single_ref, twice):
    ex = ex_ref[...]
    return 0.5 * (exact(ex, twice) + exact_tn(ex, twice)) * single_ref[...]


def class_pair(table, nonsyn, omega_ref, pair, twice, pi_row, pi_col):
    mask = low_half()
    omega = jnp.where(mask, omega_ref[2 * pair], omega_ref[2 * pair + 1])
    factor = 1.0 + nonsyn * (omega - 1.0)
    flux = table * factor
    off = flux * pi_row
    row0 = jnp.sum(jnp.where(mask, off, 0.0), axis=1, keepdims=True)
    row1 = jnp.sum(jnp.where(mask, 0.0, off), axis=1, keepdims=True)
    mean0 = jnp.sum(pi_col * row0, axis=0, keepdims=True)
    mean1 = jnp.sum(pi_col * row1, axis=0, keepdims=True)
    rows = jnp.where(mask, row0, row1)
    mean = jnp.where(mask, mean0, mean1)
    return factor, off, rows, mean


def neighbours():
    row = lax.broadcasted_iota(jnp.int32, (64, 128), 0)
    lane = lax.broadcasted_iota(jnp.int32, (64, 128), 1) % 64
    masks = [
        row % 16 == lane % 16,
        (row // 16 == lane // 16) & (row % 4 == lane % 4),
        row // 4 == lane // 4,
    ]
    codon = lax.broadcasted_iota(jnp.int32, (64, 16), 0)
    column = lax.broadcasted_iota(jnp.int32, (64, 16), 1)
    digits = [codon // 16, codon // 4 % 4, codon % 4]
    picks = [(column == 4 * p + digits[p]).astype(F32) for p in range(3)]
    return masks, picks


def coefficients(len_ref, cls_ref, slope):
    lane = lax.broadcasted_iota(jnp.int32, (PAIRS, EDGES), 1)
    row = lax.broadcasted_iota(jnp.int32, (PAIRS, EDGES), 0)
    lengths = len_ref[...] * 0.0625
    classes = cls_ref[...].astype(F32)
    place = lax.broadcasted_iota(jnp.int32, (PAIRS, 128), 1) % 64
    found = []
    for odd in range(2):
        here = lane == 2 * row + odd
        y = jnp.sum(jnp.where(here, lengths, 0.0), axis=1, keepdims=True)
        owner = jnp.sum(jnp.where(here, classes, 0.0), axis=1, keepdims=True)
        current = jnp.ones((PAIRS, 128), F32)
        series = jnp.zeros((PAIRS, 128), F32)
        for k in range(ORDER):
            following = current * y * (1.0 / (k + 1))
            series = jnp.where(place // CLASSES == k, current if slope else following, series)
            current = following
        found.append(jnp.where((place % CLASSES).astype(F32) == owner, series, 0.0))
    return found


def four_left(x):
    high, low = split(x)
    return jnp.concatenate([high, low], axis=1)


def four_right(x):
    high, low = split(x)
    return jnp.concatenate([high, low, high, low], axis=0)


def expand(coefs, dup_ref, store):
    high, low = split(coefs)
    left = jnp.concatenate(
        [jnp.concatenate([high, high], axis=1), jnp.concatenate([low, low], axis=1)], axis=0
    )

    def some(step, carry):
        for j in range(4):
            i = step * 8 + 2 * j
            parts = [split(dup_ref[rows_of(i + t, 64), :]) for t in range(2)]
            right = jnp.concatenate([
                jnp.concatenate([spread(parts[0][h]), spread(parts[1][h])], axis=1)
                for h in range(2)
            ], axis=0)
            both = mxu(left, right)
            both = both[0:64] + both[64:128]
            for t in range(2):
                store(i + t, both[:, 128 * t : 128 * t + 128])
        return carry

    lax.fori_loop(0, 8, some, 0)


def rows_of(step, width):
    return pl.ds(pl.multiple_of(step * width, width), width)


def matrix_kernel(
    ex_ref, freq_ref, omega_ref, len_ref, cls_ref, sense_ref, single_ref, nonsyn_ref,
    chain_ref, last_ref, up_ref, power_ref, dup_ref,
    first_ref,
):
    mask = low_half()
    twice, pi_row, pi_col, root_row, root_col = frequencies(freq_ref, sense_ref)
    table = symmetric_table(ex_ref, single_ref, twice)
    nonsyn = nonsyn_ref[...]

    powers = []
    for pair in range(CLASSES // 2):
        factor, off, rows, mean = class_pair(
            table, nonsyn, omega_ref, pair, twice, pi_row, pi_col
        )
        powers.append([(table * factor * root_col * root_row - twice * rows) / mean])
    for left, right in ((0, 0), (1, 0), (1, 1), (3, 0), (3, 1), (3, 2), (3, 3)):
        for pair in range(CLASSES // 2):
            powers[pair].append(pair_products((powers[pair][left], powers[pair][right])))
    for pair in range(CLASSES // 2):
        for k in range(ORDER):
            value = powers[pair][k]
            swapped = pltpu.roll(value, 64, 1)
            at = CLASSES * k + 2 * pair
            dup_ref[pl.ds(at, 64, stride=64), :] = jnp.where(mask, value, swapped)
            dup_ref[pl.ds(at + 1, 64, stride=64), :] = jnp.where(mask, swapped, value)
            if k < 4:
                power_ref[pair, k] = value

    even, odd = coefficients(len_ref, cls_ref, False)

    def store(i, value):
        first_ref[rows_of(i, 64), :] = value

    expand(jnp.where(low_half(), even, odd), dup_ref, store)

    def squarings(step, carry):
        width = 16
        held = [first_ref[pl.ds(step * width + j, 64, stride=64), :] for j in range(width)]
        for level in range(4):
            for j in range(width):
                high, low = split(held[j])
                chain_ref[level, 0, step * width + j] = high
                chain_ref[level, 1, step * width + j] = low
                wide_high, wide_low = spread(high), spread(low)
                held[j] = 2.0 * held[j] + mxu(
                    jnp.concatenate([high, high, low], axis=1),
                    jnp.concatenate([wide_high, wide_low, wide_high], axis=0),
                )
        for j in range(width):
            p = step * width + j
            last_ref[p] = held[j]
            double(up_ref, p, inverse_root_col * (held[j] + twice) * root_row)
        return carry

    inverse_root_col = 1.0 / root_col
    lax.fori_loop(0, PAIRS // 16, squarings, 0)


def up_kernel(
    states_ref, gap_ref, order_ref, up_ref,
    top_ref, message_ref, high_ref, low_ref, leaf_ref, scale_ref, inverse_ref,
):
    subtree = lax.axis_index("branch")

    def finish(p, message):
        message_ref[p] = jnp.concatenate(message, axis=0)
        raw = message[0] * message[1]
        scaling = jnp.sum(raw, axis=0, keepdims=True)
        inverse = 1.0 / scaling
        scale_ref[pl.ds(p, 1), :] = scaling
        inverse_ref[pl.ds(p, 1), :] = inverse
        high, low = split(raw * inverse)
        high_ref[p] = high
        low_ref[p] = low

    sites = states_ref.shape[1]
    codon = lax.broadcasted_iota(jnp.int32, (64, sites), 0)

    def leaf_level(step, carry):
        for j in range(8):
            p = step * 8 + j
            both = []
            for e in range(2):
                taxon = order_ref[subtree * LEAF_DEV + 2 * p + e]
                state = jnp.where(
                    gap_ref[pl.ds(taxon, 1), :] > 0, -1, states_ref[pl.ds(taxon, 1), :]
                )
                hit = (codon == state) | (state < 0)
                both.append(jnp.where(hit, 1.0, 0.0).astype(BF))
            leaf_ref[p] = jnp.concatenate(both, axis=0)
            nothing = jnp.zeros_like(both[0])
            finish(p, [messages(up_ref[2 * p + e], both[e], nothing) for e in range(2)])
        return carry

    lax.fori_loop(0, LEAF_DEV // 16, leaf_level, 0)

    def inner(p):
        child = 2 * p - 64
        return [
            messages(up_ref[2 * p + e], high_ref[child + e], low_ref[child + e]) for e in range(2)
        ]

    for p in range(32, 48):
        finish(p, inner(p))
    for p in range(48, 63):
        finish(p, inner(p))
    high_ref[63] = jnp.zeros((64, sites), BF)
    low_ref[63] = jnp.zeros((64, sites), BF)
    scale_ref[63:64, :] = jnp.ones((1, sites), F32)
    inverse_ref[63:64, :] = jnp.ones((1, sites), F32)
    top = inner(63)
    message_ref[63] = jnp.concatenate(top, axis=0)
    top_ref[...] = top[0]


def side_kernel(
    dup_ref, last_ref, len_ref, cls_ref, freq_ref, sense_ref, slope_ref, matrix_ref, turned_ref,
):
    twice, pi_row, pi_col, root_row, root_col = frequencies(freq_ref, sense_ref)
    even, odd = coefficients(len_ref, cls_ref, True)

    def store(i, value):
        slope_ref[rows_of(i, 64), :] = value

    expand(jnp.where(low_half(), even, odd), dup_ref, store)
    even, odd = coefficients(len_ref, cls_ref, False)
    turned_ref[...] = exact_tn(jnp.where(low_half(), even, odd), twice)
    inverse_root_row = 1.0 / root_row

    def matrices(step, carry):
        for j in range(8):
            r = step * 8 + j
            double(matrix_ref, r, root_col * (last_ref[32 + r] + twice) * inverse_root_row)
        return carry

    lax.fori_loop(0, 4, matrices, 0)


def down_kernel(total_sites, members, *refs):
    tops = refs[:members]
    (
        matrix_ref, message_ref, high_ref, low_ref, leaf_ref, scale_ref, inverse_ref,
        weights_ref, freq_ref, sense_ref,
        count_ref, log_ref,
        a_high_ref, a_low_ref,
    ) = refs[members:]
    subtree = lax.axis_index("branch")
    mask = low_half()
    twice, pi_row, pi_col, root_row, root_col = frequencies(freq_ref, sense_ref)
    inverse_root_row, inverse_root_col = 1.0 / root_row, 1.0 / root_col
    sites = weights_ref.shape[1]
    weight = weights_ref[...].astype(F32)

    above = jnp.broadcast_to(pi_col, (64, sites))
    for other in tops[1:]:
        above = above * other[...]
    own = tops[0][...]
    likelihood = jnp.sum(above * own, axis=0, keepdims=True)
    logs = jnp.sum(jnp.log(scale_ref[...]), axis=0, keepdims=True)
    logs = logs + jnp.where(subtree == 0, jnp.log(likelihood), 0.0)
    log_ref[...] = jnp.broadcast_to(jnp.sum(weight * logs, axis=1, keepdims=True), (8, 128))
    high, low = split(above * (weight / (likelihood * total_sites)))
    a_high_ref[31, 0:64, :] = high
    a_low_ref[31, 0:64, :] = low
    a_high_ref[31, 64:128, :] = jnp.zeros((64, sites), BF)
    a_low_ref[31, 64:128, :] = jnp.zeros((64, sites), BF)

    def store_counts(p, square):
        counts = jnp.where(mask, square[0:64], square[64:128])
        count_ref[p] = root_col * counts * inverse_root_row

    def descend(r):
        a_high, a_low = a_high_ref[r - 32], a_low_ref[r - 32]
        child = 2 * r - 64
        u_high = jnp.concatenate([high_ref[child], high_ref[child + 1]], axis=0)
        u_low = jnp.concatenate([low_ref[child], low_ref[child + 1]], axis=0)
        first = mxu_nt(u_high, jnp.concatenate([a_high, a_low], axis=0))
        second = mxu_nt(u_low, a_high)
        store_counts(r, first[:, 0:128] + first[:, 128:256] + second)
        return [
            messages(
                matrix_ref[2 * (r - 32) + e], a_high[64 * e : 64 * e + 64], a_low[64 * e : 64 * e + 64]
            )
            for e in range(2)
        ]

    def children(down, e, p):
        vector = down[e]
        inverse = inverse_ref[pl.ds(p, 1), :]
        message = message_ref[p]
        pair = jnp.concatenate(
            [vector * message[64:128] * inverse, vector * message[0:64] * inverse], axis=0
        )
        return split(pair)

    def inner(r):
        down = descend(r)
        for e in range(2):
            p = 2 * r + e - 64
            if isinstance(p, int) and p == 63:
                continue
            high, low = children(down, e, p)
            a_high_ref[p - 32] = high
            a_low_ref[p - 32] = low

    for r in range(63, 47, -1):
        inner(r)

    def leaf_level(step, carry):
        for j in range(4):
            r = 32 + step * 4 + j
            down = descend(r)
            for e in range(2):
                p = 2 * r + e - 64
                high, low = children(down, e, p)
                square = mxu_nt(leaf_ref[p], jnp.concatenate([high, low], axis=0))
                store_counts(p, square[:, 0:128] + square[:, 128:256])
        return carry

    lax.fori_loop(0, 4, leaf_level, 0)


def adjoint_kernel(
    members,
    chain_ref, turned_ref, slope_ref, power_ref, count_ref, log_ref, ex_ref, freq_ref, omega_ref,
    sense_ref, single_ref, nonsyn_ref,
    out_ref,
    back_ref, bins_ref,
):
    subtree = lax.axis_index("branch")
    mask = low_half()
    twice, pi_row, pi_col, root_row, root_col = frequencies(freq_ref, sense_ref)
    inverse_root_row = 1.0 / root_row

    def adjoint(step, carry):
        held = [count_ref[step * 16 + j] for j in range(16)]
        for level in range(3, -1, -1):
            for j in range(16):
                high, low = split(held[j])
                e_high, e_low = chain_ref[level, 0, step * 16 + j], chain_ref[level, 1, step * 16 + j]
                left = jnp.concatenate([
                    jnp.concatenate([high, e_high], axis=1),
                    jnp.concatenate([low, e_low], axis=1),
                ], axis=0)
                right = jnp.concatenate([
                    jnp.concatenate([spread(e_high), spread(e_low)], axis=1),
                    jnp.concatenate([spread(high), spread(low)], axis=1),
                ], axis=0)
                four = mxu(left, right)
                four = four[0:64] + four[64:128]
                held[j] = 2.0 * held[j] + four[:, 0:128] + four[:, 128:256]
        for j in range(16):
            back_ref[pl.ds(step * 16 + j, 64, stride=64), :] = held[j]
        return carry

    lax.fori_loop(0, PAIRS // 16, adjoint, 0)

    left = four_left(turned_ref[...])

    def sums(step, total):
        for j in range(4):
            ats = [rows_of(step * 8 + 2 * j + t, 64) for t in range(2)]
            values = [back_ref[at, :] for at in ats]
            both = mxu(left, four_right(jnp.concatenate(values, axis=1)))
            for t in range(2):
                total = total + values[t] * slope_ref[ats[t], :]
                here = both[:, 128 * t : 128 * t + 128]
                bins_ref[ats[t], :] = jnp.where(mask, here[0:64], here[64:128])
        return total

    slopes = lax.fori_loop(0, 8, sums, jnp.zeros((64, 128), F32)) * 0.0625

    table = symmetric_table(ex_ref, single_ref, twice)
    nonsyn = nonsyn_ref[...]
    row = lax.broadcasted_iota(jnp.int32, (64, 128), 0)
    lane = lax.broadcasted_iota(jnp.int32, (64, 128), 1)
    table_grad = jnp.zeros((64, 128), F32)
    omega_row = jnp.zeros((1, 128), F32)
    lane_row = lax.broadcasted_iota(jnp.int32, (1, 128), 1)
    for pair in range(CLASSES // 2):
        grads = []
        for k in range(ORDER):
            at = CLASSES * k + 2 * pair
            first = bins_ref[pl.ds(at, 64, stride=64), :]
            second = bins_ref[pl.ds(at + 1, 64, stride=64), :]
            first = first + pltpu.roll(first, 64, 1)
            second = second + pltpu.roll(second, 64, 1)
            grads.append(jnp.where(mask, first, second))
        g1, g2, g3, g4, g5, g6, g7, g8 = grads
        a1, a2, a3, a4 = [power_ref[pair, k] for k in range(4)]
        g4 = g4 + pair_products((g8, a4), (a4, g8), (g7, a3), (g6, a2), (g5, a1))
        g3 = g3 + pair_products((a4, g7))
        g2 = g2 + pair_products((a4, g6))
        g1 = g1 + pair_products((a4, g5))
        g2 = g2 + pair_products((g4, a2), (a2, g4), (g3, a1))
        g1 = g1 + pair_products((a2, g3))
        g1 = g1 + pair_products((g2, a1), (a1, g2))
        factor, off, rows, mean = class_pair(
            table, nonsyn, omega_ref, pair, twice, pi_row, pi_col
        )
        d_rate = root_col * g1 * inverse_root_row
        rate = (off - twice * rows) / mean
        weighted = d_rate * rate
        diagonal = d_rate * twice
        total0 = jnp.sum(jnp.where(mask, weighted, 0.0), axis=1, keepdims=True)
        total1 = jnp.sum(jnp.where(mask, 0.0, weighted), axis=1, keepdims=True)
        total0 = jnp.sum(total0, axis=0, keepdims=True)
        total1 = jnp.sum(total1, axis=0, keepdims=True)
        diag0 = jnp.sum(jnp.where(mask, diagonal, 0.0), axis=1, keepdims=True)
        diag1 = jnp.sum(jnp.where(mask, 0.0, diagonal), axis=1, keepdims=True)
        row_grad = jnp.where(mask, diag0 + pi_col * total0, diag1 + pi_col * total1)
        flux_grad = (d_rate - row_grad) * pi_row / mean
        table_grad = table_grad + flux_grad * factor * single_ref[...]
        ratio = flux_grad * table * nonsyn
        ratio0 = jnp.sum(jnp.where(mask, ratio, 0.0), axis=1, keepdims=True)
        ratio1 = jnp.sum(jnp.where(mask, 0.0, ratio), axis=1, keepdims=True)
        ratio0 = jnp.sum(ratio0, axis=0, keepdims=True)
        ratio1 = jnp.sum(ratio1, axis=0, keepdims=True)
        omega_row = jnp.where(lane_row == 2 * pair, ratio0, omega_row)
        omega_row = jnp.where(lane_row == 2 * pair + 1, ratio1, omega_row)
    table_grad = table_grad + pltpu.roll(table_grad, 64, 1)
    one = table_grad[:, 0:64]
    both = 0.5 * (exact(one, twice) + exact_tn(one, twice))
    masks, picks = neighbours()
    packed = jnp.zeros((16, 128), F32)
    for at_position, pick in zip(masks, picks):
        packed = packed + exact_tn(pick, jnp.where(at_position, both, 0.0))
    packed = jnp.where(lax.broadcasted_iota(jnp.int32, (16, 128), 1) < 64, packed, 0.0)

    even = jnp.sum(jnp.where(mask, slopes, 0.0), axis=1, keepdims=True)
    other = jnp.sum(jnp.where(mask, 0.0, slopes), axis=1, keepdims=True)
    placed = jnp.where(lane == 2 * row, even, 0.0) + jnp.where(lane == 2 * row + 1, other, 0.0)
    length_row = jnp.sum(placed, axis=0, keepdims=True)
    line = lax.broadcasted_iota(jnp.int32, out_ref.shape, 0)
    omega_row = jnp.where(lane_row == CLASSES, log_ref[0:1, :], omega_row)
    omega_row = pltpu.roll(jnp.broadcast_to(omega_row, (8, 128)), 64, 1)[0:1]
    packed = packed + jnp.where(line == 0, omega_row, 0.0)
    out_ref[...] = packed + jnp.where(line == 12 + subtree, length_row, 0.0)


def last_kernel(total_sites, count, *refs):
    members = lax.axis_size("branch")
    subtree = lax.axis_index("branch")
    exch_ref, omega_ref, length_ref, log_ref = refs[count:]
    total = tree_sum([ref[...] for ref in refs[:count]])
    masks, picks = neighbours()
    table = jnp.zeros((64, 128), F32)
    for at_position, pick in zip(masks, picks):
        table = table + jnp.where(at_position, exact(pick, total), 0.0)
    exch_ref[...] = table[:, 0:64]
    moved = pltpu.roll(total[0:8], 64, 1)
    omega_ref[...] = moved[0:1, 0:CLASSES]
    line = lax.broadcasted_iota(jnp.int32, total.shape, 0)
    lengths = jnp.sum(jnp.where(line == 12 + subtree, total, 0.0), axis=0, keepdims=True)
    length_ref[...] = lengths[:, 0:EDGES]
    log_ref[...] = moved[0:1, CLASSES : CLASSES + 1] / total_sites / (LEAF_DEV * members)


def partners(x, axis, start, radix):
    size = lax.axis_size(axis)
    others = [
        lax.ppermute(x, axis, [(i, i ^ (step * start)) for i in range(size)])
        for step in range(1, radix)
    ]
    return [x] + others


def tree_sum(parts):
    while len(parts) > 1:
        parts = [parts[i] + parts[i + 1] for i in range(0, len(parts), 2)]
    return parts[0]


def axis_steps(axis):
    size, start, steps = lax.axis_size(axis), 1, []
    while start < size:
        radix = min(4, size // start)
        steps.append((axis, start, radix))
        start *= radix
    return steps


def body(
    total_sites, states, gap_mask, weights, leaf_order, exchanges, codon_freq, omega_ratio,
    lengths, classes,
):
    sites = states.shape[1]
    members = lax.axis_size("branch")
    sense, single, nonsyn = codon_tables()
    vmem = pl.BlockSpec(memory_space=pltpu.VMEM)
    smem = pl.BlockSpec(memory_space=pltpu.SMEM)
    shape = jax.ShapeDtypeStruct
    held = pltpu.VMEM
    limit = pltpu.CompilerParams(vmem_limit_bytes=20 * 2**20)

    def outside(x):
        return pltpu.with_memory_space_constraint(x, pltpu.HBM)

    def inside(xs):
        return [pltpu.with_memory_space_constraint(x, pltpu.VMEM) for x in xs]

    sense2 = outside(jnp.asarray(np.tile(sense[None, :], (1, 2))))
    single2 = outside(jnp.asarray(np.tile(single, (1, 2))))
    nonsyn2 = outside(jnp.asarray(np.tile(nonsyn, (1, 2))))
    freq = outside(codon_freq.reshape(1, 64))
    span, owner = outside(lengths.reshape(1, EDGES)), outside(classes.reshape(1, EDGES))
    table, omega = outside(exchanges), outside(omega_ratio)

    chain, last, up, powers, dup = inside(pl.pallas_call(
        matrix_kernel,
        out_shape=[
            held((4, 2, PAIRS, 64, 128), BF),
            held((PAIRS, 64, 128), F32),
            held((2 * PAIRS, 64, 256), BF),
            held((CLASSES // 2, 4, 64, 128), F32),
            held((ORDER * CLASSES * 64, 128), F32),
        ],
        in_specs=[vmem, vmem, smem] + [vmem] * 5,
        out_specs=[vmem] * 5,
        scratch_shapes=[pltpu.VMEM((PAIRS * 64, 128), F32)],
        compiler_params=limit,
        name="matrices",
    )(table, freq, omega, span, owner, sense2, single2, nonsyn2))
    top, *kept = pl.pallas_call(
        up_kernel,
        out_shape=[
            shape((64, sites), F32),
            held((PAIRS, 128, sites), F32),
            held((64, 64, sites), BF),
            held((64, 64, sites), BF),
            held((32, 128, sites), BF),
            held((64, sites), F32),
            held((64, sites), F32),
        ],
        in_specs=[vmem, vmem, smem, vmem],
        out_specs=[vmem] * 7,
        compiler_params=limit,
        name="up",
    )(outside(states), outside(gap_mask), outside(leaf_order), up)
    message, high, low, leaf, scale, inverse = inside(kept)
    tops = partners(top, "branch", 1, members)
    slope, matrix, turned = inside(pl.pallas_call(
        side_kernel,
        out_shape=[
            held((PAIRS * 64, 128), F32),
            held((64, 64, 256), BF),
            held((128, 128), F32),
        ],
        in_specs=[vmem] * 6,
        out_specs=[vmem] * 3,
        compiler_params=limit,
        name="side",
    )(dup, last, span, owner, freq, sense2))
    counts, logs = inside(pl.pallas_call(
        functools.partial(down_kernel, total_sites, members),
        out_shape=[held((PAIRS, 64, 128), F32), held((8, 128), F32)],
        in_specs=[vmem] * (10 + members),
        out_specs=[vmem] * 2,
        scratch_shapes=[
            pltpu.VMEM((32, 128, sites), BF),
            pltpu.VMEM((32, 128, sites), BF),
        ],
        compiler_params=limit,
        name="down",
    )(
        *tops, matrix, message, high, low, leaf, scale, inverse,
        outside(weights.reshape(1, sites)), freq, sense2,
    ))
    part = pl.pallas_call(
        functools.partial(adjoint_kernel, members),
        out_shape=shape((16, 128), F32),
        in_specs=[vmem] * 8 + [smem] + [vmem] * 3,
        out_specs=vmem,
        scratch_shapes=[
            pltpu.VMEM((PAIRS * 64, 128), F32),
            pltpu.VMEM((64 * 64, 128), F32),
        ],
        compiler_params=limit,
        name="adjoint",
    )(
        chain, turned, slope, powers, counts, logs, table, freq, omega,
        sense2, single2, nonsyn2,
    )
    steps = axis_steps("branch") + axis_steps("site")
    for step in steps[:-1]:
        part = tree_sum(partners(part, *step))
    parts = partners(part, *steps[-1])
    exch, ratio, length, loglik = pl.pallas_call(
        functools.partial(last_kernel, total_sites, len(parts)),
        out_shape=[shape((64, 64), F32), shape((1, CLASSES), F32), shape((1, EDGES), F32), shape((1, 1), F32)],
        in_specs=[vmem] * len(parts),
        out_specs=[vmem] * 4,
        compiler_params=limit,
        name="last",
    )(*parts)
    return (exch, ratio.reshape(CLASSES), length.reshape(EDGES), loglik.reshape(()))


def solution(mesh):
    def whole(states, *rest):
        total_sites = states.shape[1]
        return jax.shard_map(
            functools.partial(body, total_sites),
            mesh=mesh,
            in_specs=(
                P(None, "site"),
                P(None, "site"),
                P("site"),
                P(),
                P(),
                P(),
                P(),
                P("branch"),
                P("branch"),
            ),
            out_specs=(P(), P(), P("branch"), P()),
            check_vma=False,
        )(states, *rest)

    return whole
```

```python
import functools
import jax
import jax.numpy as jnp
import numpy as np
from jax import lax
from jax.experimental import pallas as pl
from jax.experimental.pallas import tpu as pltpu
from jax.sharding import PartitionSpec as P

LEAF_DEV = 64
EDGES = 127
PAIRS = 64
CLASSES = 8
ORDER = 8
BF = jnp.bfloat16
F32 = jnp.float32

CODE_TABLE = "FFLLSSSSYYXXCCXWLLLLPPPPHHQQRRRRIIIMTTTTNNKKSSRRVVVVAAAADDEEGGGG"


def codon_tables():
    amino_acid = np.array(list(CODE_TABLE))
    codon_index = np.arange(64)
    digits = np.stack([codon_index // 16, codon_index // 4 % 4, codon_index % 4], 1)
    differ = (digits[:, None, :] != digits[None, :, :]).sum(-1)
    is_sense = amino_acid != "X"
    single = (differ == 1) & is_sense[:, None] & is_sense[None, :]
    nonsyn = single & (amino_acid[:, None] != amino_acid[None, :])
    return (is_sense.astype(np.float32), single.astype(np.float32), nonsyn.astype(np.float32))


def low_half():
    return lax.broadcasted_iota(jnp.int32, (64, 128), 1) < 64


def split(x):
    high = x.astype(BF)
    low = (x - high.astype(F32)).astype(BF)
    return high, low


def spread(x, scale=1.0):
    mask = low_half()
    low = jnp.where(mask, scale, 0.0).astype(x.dtype)
    high = jnp.where(mask, 0.0, scale).astype(x.dtype)
    return jnp.concatenate([x * low, x * high], axis=0)


def mxu(left, right):
    return jnp.dot(left, right, preferred_element_type=F32)


def mxu_nt(left, right):
    return lax.dot_general(left, right, (((1,), (1,)), ((), ())), preferred_element_type=F32)


def exact(left, right):
    return jnp.dot(left, right, preferred_element_type=F32, precision=lax.Precision.HIGHEST)


def exact_tn(left, right):
    return lax.dot_general(
        left, right, (((0,), (0,)), ((), ())), preferred_element_type=F32,
        precision=lax.Precision.HIGHEST,
    )


def pair_products(*terms):
    lefts, rights = [], []
    for left, right in terms:
        left_high, left_low = split(left)
        right_high, right_low = split(right)
        wide_high, wide_low = spread(right_high), spread(right_low)
        lefts += [left_high, left_high, left_low]
        rights += [wide_high, wide_low, wide_high]
    return mxu(jnp.concatenate(lefts, axis=1), jnp.concatenate(rights, axis=0))


def messages(matrix, high, low):
    return mxu(matrix, jnp.concatenate([high, low, high, low], axis=0))


def double(ref, p, x):
    mask = low_half()
    swapped = pltpu.roll(x, 64, 1)
    for e, both in enumerate((jnp.where(mask, x, swapped), jnp.where(mask, swapped, x))):
        high, low = split(both)
        ref[2 * p + e] = jnp.concatenate([high, low], axis=1)


def identity_twice():
    row = lax.broadcasted_iota(jnp.int32, (64, 128), 0)
    lane = lax.broadcasted_iota(jnp.int32, (64, 128), 1)
    return (row == lane % 64).astype(F32)


def frequencies(freq_ref, sense_ref):
    twice = identity_twice()
    sense2 = sense_ref[...]
    freq2 = exact(jnp.broadcast_to(freq_ref[...], (8, 64)), twice)[0:1] * sense2
    total = 0.5 * jnp.sum(freq2, axis=1, keepdims=True)
    pi_row = freq2 / total
    pi_col = 0.5 * jnp.sum(twice * pi_row, axis=1, keepdims=True)
    sense_col = 0.5 * jnp.sum(twice * sense2, axis=1, keepdims=True)
    root_row = jnp.sqrt(jnp.where(sense2 > 0, pi_row, 1.0))
    root_col = jnp.sqrt(jnp.where(sense_col > 0, pi_col, 1.0))
    return twice, pi_row, pi_col, root_row, root_col


def symmetric_table(ex_ref, single_ref, twice):
    ex = ex_ref[...]
    return 0.5 * (exact(ex, twice) + exact_tn(ex, twice)) * single_ref[...]


def class_pair(table, nonsyn, omega_ref, pair, twice, pi_row, pi_col):
    mask = low_half()
    omega = jnp.where(mask, omega_ref[2 * pair], omega_ref[2 * pair + 1])
    factor = 1.0 + nonsyn * (omega - 1.0)
    flux = table * factor
    off = flux * pi_row
    row0 = jnp.sum(jnp.where(mask, off, 0.0), axis=1, keepdims=True)
    row1 = jnp.sum(jnp.where(mask, 0.0, off), axis=1, keepdims=True)
    mean0 = jnp.sum(pi_col * row0, axis=0, keepdims=True)
    mean1 = jnp.sum(pi_col * row1, axis=0, keepdims=True)
    rows = jnp.where(mask, row0, row1)
    mean = jnp.where(mask, mean0, mean1)
    return factor, off, rows, mean


def neighbours():
    row = lax.broadcasted_iota(jnp.int32, (64, 128), 0)
    lane = lax.broadcasted_iota(jnp.int32, (64, 128), 1) % 64
    masks = [
        row % 16 == lane % 16,
        (row // 16 == lane // 16) & (row % 4 == lane % 4),
        row // 4 == lane // 4,
    ]
    codon = lax.broadcasted_iota(jnp.int32, (64, 16), 0)
    column = lax.broadcasted_iota(jnp.int32, (64, 16), 1)
    digits = [codon // 16, codon // 4 % 4, codon % 4]
    picks = [(column == 4 * p + digits[p]).astype(F32) for p in range(3)]
    return masks, picks


def coefficients(len_ref, cls_ref, slope):
    lane = lax.broadcasted_iota(jnp.int32, (PAIRS, EDGES), 1)
    row = lax.broadcasted_iota(jnp.int32, (PAIRS, EDGES), 0)
    lengths = len_ref[...] * 0.0625
    classes = cls_ref[...].astype(F32)
    place = lax.broadcasted_iota(jnp.int32, (PAIRS, 128), 1) % 64
    found = []
    for odd in range(2):
        here = lane == 2 * row + odd
        y = jnp.sum(jnp.where(here, lengths, 0.0), axis=1, keepdims=True)
        owner = jnp.sum(jnp.where(here, classes, 0.0), axis=1, keepdims=True)
        current = jnp.ones((PAIRS, 128), F32)
        series = jnp.zeros((PAIRS, 128), F32)
        for k in range(ORDER):
            following = current * y * (1.0 / (k + 1))
            series = jnp.where(place // CLASSES == k, current if slope else following, series)
            current = following
        found.append(jnp.where((place % CLASSES).astype(F32) == owner, series, 0.0))
    return found


def four_left(x):
    high, low = split(x)
    return jnp.concatenate([high, low], axis=1)


def four_right(x):
    high, low = split(x)
    return jnp.concatenate([high, low, high, low], axis=0)


def expand(coefs, dup_ref, store):
    high, low = split(coefs)
    left = jnp.concatenate(
        [jnp.concatenate([high, high], axis=1), jnp.concatenate([low, low], axis=1)], axis=0
    )

    def some(step, carry):
        for j in range(16):
            i = step * 32 + 2 * j
            parts = [split(dup_ref[rows_of(i + t, 64), :]) for t in range(2)]
            right = jnp.concatenate([
                jnp.concatenate([spread(parts[0][h]), spread(parts[1][h])], axis=1)
                for h in range(2)
            ], axis=0)
            both = mxu(left, right)
            both = both[0:64] + both[64:128]
            for t in range(2):
                store(i + t, both[:, 128 * t : 128 * t + 128])
        return carry

    lax.fori_loop(0, 2, some, 0)


def rows_of(step, width):
    return pl.ds(pl.multiple_of(step * width, width), width)


def up_kernel(
    states_ref, gap_ref, order_ref,
    ex_ref, freq_ref, omega_ref, len_ref, cls_ref, sense_ref, single_ref, nonsyn_ref,
    top_ref, chain_ref, last_ref, power_ref, dup_ref, fixed_ref,
    message_ref, high_ref, low_ref, leaf_ref, scale_ref, inverse_ref,
    first_ref, up_ref,
):
    subtree = lax.axis_index("branch")
    mask = low_half()
    twice, pi_row, pi_col, root_row, root_col = frequencies(freq_ref, sense_ref)
    table = symmetric_table(ex_ref, single_ref, twice)
    nonsyn = nonsyn_ref[...]
    for at, value in enumerate(
        (pi_row, pi_col, root_row, root_col, 1.0 / root_row, 1.0 / root_col, table)
    ):
        fixed_ref[at] = jnp.broadcast_to(value, (64, 128))

    powers = []
    for pair in range(CLASSES // 2):
        factor, off, rows, mean = class_pair(
            table, nonsyn, omega_ref, pair, twice, pi_row, pi_col
        )
        powers.append([(table * factor * root_col * root_row - twice * rows) / mean])
    for left, right in ((0, 0), (1, 0), (1, 1), (3, 0), (3, 1), (3, 2), (3, 3)):
        for pair in range(CLASSES // 2):
            powers[pair].append(pair_products((powers[pair][left], powers[pair][right])))
    for pair in range(CLASSES // 2):
        for k in range(ORDER):
            value = powers[pair][k]
            swapped = pltpu.roll(value, 64, 1)
            at = CLASSES * k + 2 * pair
            dup_ref[pl.ds(at, 64, stride=64), :] = jnp.where(mask, value, swapped)
            dup_ref[pl.ds(at + 1, 64, stride=64), :] = jnp.where(mask, swapped, value)
            if k < 4:
                power_ref[pair, k] = value

    even, odd = coefficients(len_ref, cls_ref, False)

    def store(i, value):
        first_ref[rows_of(i, 64), :] = value

    expand(jnp.where(low_half(), even, odd), dup_ref, store)

    def squarings(step, carry):
        width = 16
        held = [first_ref[pl.ds(step * width + j, 64, stride=64), :] for j in range(width)]
        for level in range(4):
            for j in range(width):
                high, low = split(held[j])
                chain_ref[level, 0, step * width + j] = high
                chain_ref[level, 1, step * width + j] = low
                wide_high, wide_low = spread(high), spread(low)
                held[j] = 2.0 * held[j] + mxu(
                    jnp.concatenate([high, high, low], axis=1),
                    jnp.concatenate([wide_high, wide_low, wide_high], axis=0),
                )
        for j in range(width):
            p = step * width + j
            last_ref[p] = held[j]
            double(up_ref, p, inverse_root_col * (held[j] + twice) * root_row)
        return carry

    inverse_root_col = 1.0 / root_col
    lax.fori_loop(0, PAIRS // 16, squarings, 0)

    def finish(p, message):
        message_ref[p] = jnp.concatenate(message, axis=0)
        raw = message[0] * message[1]
        scaling = jnp.sum(raw, axis=0, keepdims=True)
        inverse = 1.0 / scaling
        scale_ref[pl.ds(p, 1), :] = scaling
        inverse_ref[pl.ds(p, 1), :] = inverse
        high, low = split(raw * inverse)
        high_ref[p] = high
        low_ref[p] = low

    sites = states_ref.shape[1]
    codon = lax.broadcasted_iota(jnp.int32, (64, sites), 0)

    def leaf_level(step, carry):
        for j in range(8):
            p = step * 8 + j
            both = []
            for e in range(2):
                taxon = order_ref[subtree * LEAF_DEV + 2 * p + e]
                state = jnp.where(
                    gap_ref[pl.ds(taxon, 1), :] > 0, -1, states_ref[pl.ds(taxon, 1), :]
                )
                hit = (codon == state) | (state < 0)
                both.append(jnp.where(hit, 1.0, 0.0).astype(BF))
            leaf_ref[p] = jnp.concatenate(both, axis=0)
            nothing = jnp.zeros_like(both[0])
            finish(p, [messages(up_ref[2 * p + e], both[e], nothing) for e in range(2)])
        return carry

    lax.fori_loop(0, LEAF_DEV // 16, leaf_level, 0)

    def inner(p):
        child = 2 * p - 64
        return [
            messages(up_ref[2 * p + e], high_ref[child + e], low_ref[child + e]) for e in range(2)
        ]

    for p in range(32, 48):
        finish(p, inner(p))
    for p in range(48, 63):
        finish(p, inner(p))
    high_ref[63] = jnp.zeros((64, sites), BF)
    low_ref[63] = jnp.zeros((64, sites), BF)
    scale_ref[63:64, :] = jnp.ones((1, sites), F32)
    inverse_ref[63:64, :] = jnp.ones((1, sites), F32)
    top = inner(63)
    message_ref[63] = jnp.concatenate(top, axis=0)
    top_ref[...] = top[0]


def side_kernel(
    dup_ref, last_ref, len_ref, cls_ref, fixed_ref, slope_ref, matrix_ref, turned_ref,
):
    twice = identity_twice()
    even, odd = coefficients(len_ref, cls_ref, True)

    def store(i, value):
        slope_ref[rows_of(i, 64), :] = value

    expand(jnp.where(low_half(), even, odd), dup_ref, store)
    even, odd = coefficients(len_ref, cls_ref, False)
    turned_ref[...] = exact_tn(jnp.where(low_half(), even, odd), twice)
    root_col, inverse_root_row = fixed_ref[3], fixed_ref[4]

    def matrices(step, carry):
        for j in range(8):
            r = step * 8 + j
            double(matrix_ref, r, root_col * (last_ref[32 + r] + twice) * inverse_root_row)
        return carry

    lax.fori_loop(0, 4, matrices, 0)


def down_kernel(total_sites, members, *refs):
    tops = refs[:members]
    (
        matrix_ref, message_ref, high_ref, low_ref, leaf_ref, scale_ref, inverse_ref,
        chain_ref, turned_ref, slope_ref, power_ref, fixed_ref,
        weights_ref, omega_ref, single_ref, nonsyn_ref,
        out_ref,
        a_high_ref, a_low_ref, count_ref, back_ref, bins_ref,
    ) = refs[members:]
    subtree = lax.axis_index("branch")
    mask = low_half()
    twice = identity_twice()
    pi_row, pi_col, root_col, inverse_root_row = [fixed_ref[at] for at in (0, 1, 3, 4)]
    sites = weights_ref.shape[1]
    weight = weights_ref[...].astype(F32)

    above = jnp.broadcast_to(pi_col[:, 0:1], (64, sites))
    for other in tops[1:]:
        above = above * other[...]
    own = tops[0][...]
    likelihood = jnp.sum(above * own, axis=0, keepdims=True)
    logs = jnp.sum(jnp.log(scale_ref[...]), axis=0, keepdims=True)
    logs = logs + jnp.where(subtree == 0, jnp.log(likelihood), 0.0)
    log_part = jnp.sum(weight * logs, axis=1, keepdims=True)
    high, low = split(above * (weight / (likelihood * total_sites)))
    a_high_ref[31, 0:64, :] = high
    a_low_ref[31, 0:64, :] = low
    a_high_ref[31, 64:128, :] = jnp.zeros((64, sites), BF)
    a_low_ref[31, 64:128, :] = jnp.zeros((64, sites), BF)

    def store_counts(p, square):
        counts = jnp.where(mask, square[0:64], square[64:128])
        count_ref[p] = root_col * counts * inverse_root_row

    def descend(r):
        a_high, a_low = a_high_ref[r - 32], a_low_ref[r - 32]
        child = 2 * r - 64
        u_high = jnp.concatenate([high_ref[child], high_ref[child + 1]], axis=0)
        u_low = jnp.concatenate([low_ref[child], low_ref[child + 1]], axis=0)
        first = mxu_nt(u_high, jnp.concatenate([a_high, a_low], axis=0))
        second = mxu_nt(u_low, a_high)
        store_counts(r, first[:, 0:128] + first[:, 128:256] + second)
        return [
            messages(
                matrix_ref[2 * (r - 32) + e], a_high[64 * e : 64 * e + 64], a_low[64 * e : 64 * e + 64]
            )
            for e in range(2)
        ]

    def children(down, e, p):
        vector = down[e]
        inverse = inverse_ref[pl.ds(p, 1), :]
        message = message_ref[p]
        pair = jnp.concatenate(
            [vector * message[64:128] * inverse, vector * message[0:64] * inverse], axis=0
        )
        return split(pair)

    def inner(r):
        down = descend(r)
        for e in range(2):
            p = 2 * r + e - 64
            if isinstance(p, int) and p == 63:
                continue
            high, low = children(down, e, p)
            a_high_ref[p - 32] = high
            a_low_ref[p - 32] = low

    for r in range(63, 47, -1):
        inner(r)

    def leaf_level(step, carry):
        for j in range(4):
            r = 32 + step * 4 + j
            down = descend(r)
            for e in range(2):
                p = 2 * r + e - 64
                high, low = children(down, e, p)
                square = mxu_nt(leaf_ref[p], jnp.concatenate([high, low], axis=0))
                store_counts(p, square[:, 0:128] + square[:, 128:256])
        return carry

    lax.fori_loop(0, 4, leaf_level, 0)


    def adjoint(step, carry):
        held = [count_ref[step * 16 + j] for j in range(16)]
        for level in range(3, -1, -1):
            for j in range(16):
                high, low = split(held[j])
                e_high, e_low = chain_ref[level, 0, step * 16 + j], chain_ref[level, 1, step * 16 + j]
                left = jnp.concatenate([
                    jnp.concatenate([high, e_high], axis=1),
                    jnp.concatenate([low, e_low], axis=1),
                ], axis=0)
                right = jnp.concatenate([
                    jnp.concatenate([spread(e_high), spread(e_low)], axis=1),
                    jnp.concatenate([spread(high), spread(low)], axis=1),
                ], axis=0)
                four = mxu(left, right)
                four = four[0:64] + four[64:128]
                held[j] = 2.0 * held[j] + four[:, 0:128] + four[:, 128:256]
        for j in range(16):
            back_ref[pl.ds(step * 16 + j, 64, stride=64), :] = held[j]
        return carry

    lax.fori_loop(0, PAIRS // 16, adjoint, 0)

    left = four_left(turned_ref[...])

    def sums(step, total):
        for j in range(16):
            ats = [rows_of(step * 32 + 2 * j + t, 64) for t in range(2)]
            values = [back_ref[at, :] for at in ats]
            both = mxu(left, four_right(jnp.concatenate(values, axis=1)))
            for t in range(2):
                total = total + values[t] * slope_ref[ats[t], :]
                here = both[:, 128 * t : 128 * t + 128]
                bins_ref[ats[t], :] = jnp.where(mask, here[0:64], here[64:128])
        return total

    slopes = lax.fori_loop(0, 2, sums, jnp.zeros((64, 128), F32)) * 0.0625

    table, nonsyn = fixed_ref[6], nonsyn_ref[...]
    row = lax.broadcasted_iota(jnp.int32, (64, 128), 0)
    lane = lax.broadcasted_iota(jnp.int32, (64, 128), 1)
    table_grad = jnp.zeros((64, 128), F32)
    omega_row = jnp.zeros((1, 128), F32)
    lane_row = lax.broadcasted_iota(jnp.int32, (1, 128), 1)
    for pair in range(CLASSES // 2):
        grads = []
        for k in range(ORDER):
            at = CLASSES * k + 2 * pair
            first = bins_ref[pl.ds(at, 64, stride=64), :]
            second = bins_ref[pl.ds(at + 1, 64, stride=64), :]
            first = first + pltpu.roll(first, 64, 1)
            second = second + pltpu.roll(second, 64, 1)
            grads.append(jnp.where(mask, first, second))
        g1, g2, g3, g4, g5, g6, g7, g8 = grads
        a1, a2, a3, a4 = [power_ref[pair, k] for k in range(4)]
        g4 = g4 + pair_products((g8, a4), (a4, g8), (g7, a3), (g6, a2), (g5, a1))
        g3 = g3 + pair_products((a4, g7))
        g2 = g2 + pair_products((a4, g6))
        g1 = g1 + pair_products((a4, g5))
        g2 = g2 + pair_products((g4, a2), (a2, g4), (g3, a1))
        g1 = g1 + pair_products((a2, g3))
        g1 = g1 + pair_products((g2, a1), (a1, g2))
        factor, off, rows, mean = class_pair(
            table, nonsyn, omega_ref, pair, twice, pi_row, pi_col
        )
        d_rate = root_col * g1 * inverse_root_row
        rate = (off - twice * rows) / mean
        weighted = d_rate * rate
        diagonal = d_rate * twice
        total0 = jnp.sum(jnp.where(mask, weighted, 0.0), axis=1, keepdims=True)
        total1 = jnp.sum(jnp.where(mask, 0.0, weighted), axis=1, keepdims=True)
        total0 = jnp.sum(total0, axis=0, keepdims=True)
        total1 = jnp.sum(total1, axis=0, keepdims=True)
        diag0 = jnp.sum(jnp.where(mask, diagonal, 0.0), axis=1, keepdims=True)
        diag1 = jnp.sum(jnp.where(mask, 0.0, diagonal), axis=1, keepdims=True)
        row_grad = jnp.where(mask, diag0 + pi_col * total0, diag1 + pi_col * total1)
        flux_grad = (d_rate - row_grad) * pi_row / mean
        table_grad = table_grad + flux_grad * factor * single_ref[...]
        ratio = flux_grad * table * nonsyn
        ratio0 = jnp.sum(jnp.where(mask, ratio, 0.0), axis=1, keepdims=True)
        ratio1 = jnp.sum(jnp.where(mask, 0.0, ratio), axis=1, keepdims=True)
        ratio0 = jnp.sum(ratio0, axis=0, keepdims=True)
        ratio1 = jnp.sum(ratio1, axis=0, keepdims=True)
        omega_row = jnp.where(lane_row == 2 * pair, ratio0, omega_row)
        omega_row = jnp.where(lane_row == 2 * pair + 1, ratio1, omega_row)
    table_grad = table_grad + pltpu.roll(table_grad, 64, 1)
    masks, picks = neighbours()
    packed = jnp.zeros((16, 128), F32)
    for at_position, pick in zip(masks, picks):
        some = jnp.where(at_position, 0.5 * table_grad, 0.0)
        packed = packed + exact_tn(pick, some) + exact_tn(pick, exact_tn(some[:, 0:64], twice))
    packed = jnp.where(lax.broadcasted_iota(jnp.int32, (16, 128), 1) < 64, packed, 0.0)

    even = jnp.sum(jnp.where(mask, slopes, 0.0), axis=1, keepdims=True)
    other = jnp.sum(jnp.where(mask, 0.0, slopes), axis=1, keepdims=True)
    placed = jnp.where(lane == 2 * row, even, 0.0) + jnp.where(lane == 2 * row + 1, other, 0.0)
    length_row = jnp.sum(placed, axis=0, keepdims=True)
    line = lax.broadcasted_iota(jnp.int32, out_ref.shape, 0)
    omega_row = jnp.where(lane_row == CLASSES, log_part, omega_row)
    omega_row = pltpu.roll(jnp.broadcast_to(omega_row, (8, 128)), 64, 1)[0:1]
    packed = packed + jnp.where(line == 0, omega_row, 0.0)
    out_ref[...] = packed + jnp.where(line == 12 + subtree, length_row, 0.0)


def last_kernel(total_sites, count, *refs):
    members = lax.axis_size("branch")
    subtree = lax.axis_index("branch")
    exch_ref, omega_ref, length_ref, log_ref = refs[count:]
    total = tree_sum([ref[...] for ref in refs[:count]])
    masks, picks = neighbours()
    table = jnp.zeros((64, 128), F32)
    for at_position, pick in zip(masks, picks):
        table = table + jnp.where(at_position, exact(pick, total), 0.0)
    exch_ref[...] = table[:, 0:64]
    moved = pltpu.roll(total[0:8], 64, 1)
    omega_ref[...] = moved[0:1, 0:CLASSES]
    line = lax.broadcasted_iota(jnp.int32, total.shape, 0)
    lengths = jnp.sum(jnp.where(line == 12 + subtree, total, 0.0), axis=0, keepdims=True)
    length_ref[...] = lengths[:, 0:EDGES]
    log_ref[...] = moved[0:1, CLASSES : CLASSES + 1] / total_sites / (LEAF_DEV * members)


def partners(x, axis, start, radix):
    size = lax.axis_size(axis)
    others = [
        lax.ppermute(x, axis, [(i, i ^ (step * start)) for i in range(size)])
        for step in range(1, radix)
    ]
    return [x] + others


def tree_sum(parts):
    while len(parts) > 1:
        parts = [parts[i] + parts[i + 1] for i in range(0, len(parts), 2)]
    return parts[0]


def axis_steps(axis):
    size, start, steps = lax.axis_size(axis), 1, []
    while start < size:
        radix = 2 if size // start in (2, 8) else 4
        steps.append((axis, start, radix))
        start *= radix
    return steps[::-1]


def body(
    total_sites, states, gap_mask, weights, leaf_order, exchanges, codon_freq, omega_ratio,
    lengths, classes,
):
    sites = states.shape[1]
    members = lax.axis_size("branch")
    sense, single, nonsyn = codon_tables()
    vmem = pl.BlockSpec(memory_space=pltpu.VMEM)
    smem = pl.BlockSpec(memory_space=pltpu.SMEM)
    shape = jax.ShapeDtypeStruct
    held = pltpu.VMEM
    limit = pltpu.CompilerParams(vmem_limit_bytes=20 * 2**20)

    def outside(x):
        return pltpu.with_memory_space_constraint(x, pltpu.HBM)

    def inside(xs):
        return [pltpu.with_memory_space_constraint(x, pltpu.VMEM) for x in xs]

    sense2 = outside(jnp.asarray(np.tile(sense[None, :], (1, 2))))
    single2 = outside(jnp.asarray(np.tile(single, (1, 2))))
    nonsyn2 = outside(jnp.asarray(np.tile(nonsyn, (1, 2))))
    freq = outside(codon_freq.reshape(1, 64))
    span, owner = outside(lengths.reshape(1, EDGES)), outside(classes.reshape(1, EDGES))
    table, omega = outside(exchanges), outside(omega_ratio)

    top, *kept = pl.pallas_call(
        up_kernel,
        out_shape=[
            shape((64, sites), F32),
            held((4, 2, PAIRS, 64, 128), BF),
            held((PAIRS, 64, 128), F32),
            held((CLASSES // 2, 4, 64, 128), F32),
            held((ORDER * CLASSES * 64, 128), F32),
            held((7, 64, 128), F32),
            held((PAIRS, 128, sites), F32),
            held((64, 64, sites), BF),
            held((64, 64, sites), BF),
            held((32, 128, sites), BF),
            held((64, sites), F32),
            held((64, sites), F32),
        ],
        in_specs=[vmem, vmem, smem, vmem, vmem, smem] + [vmem] * 5,
        out_specs=[vmem] * 12,
        scratch_shapes=[
            pltpu.VMEM((PAIRS * 64, 128), F32),
            pltpu.VMEM((2 * PAIRS, 64, 256), BF),
        ],
        compiler_params=limit,
        name="up",
    )(
        outside(states), outside(gap_mask), outside(leaf_order),
        table, freq, omega, span, owner, sense2, single2, nonsyn2,
    )
    (
        chain, last, powers, dup, fixed, message, high, low, leaf, scale, inverse,
    ) = inside(kept)
    tops = partners(top, "branch", 1, members)
    slope, matrix, turned = inside(pl.pallas_call(
        side_kernel,
        out_shape=[
            held((PAIRS * 64, 128), F32),
            held((64, 64, 256), BF),
            held((128, 128), F32),
        ],
        in_specs=[vmem] * 5,
        out_specs=[vmem] * 3,
        compiler_params=limit,
        name="side",
    )(dup, last, span, owner, fixed))
    part = pl.pallas_call(
        functools.partial(down_kernel, total_sites, members),
        out_shape=shape((16, 128), F32),
        in_specs=[vmem] * (13 + members) + [smem, vmem, vmem],
        out_specs=vmem,
        scratch_shapes=[
            pltpu.VMEM((32, 128, sites), BF),
            pltpu.VMEM((32, 128, sites), BF),
            pltpu.VMEM((PAIRS, 64, 128), F32),
            pltpu.VMEM((PAIRS * 64, 128), F32),
            pltpu.VMEM((64 * 64, 128), F32),
        ],
        compiler_params=limit,
        name="down",
    )(
        *tops, matrix, message, high, low, leaf, scale, inverse,
        chain, turned, slope, powers, fixed,
        outside(weights.reshape(1, sites)), omega, single2, nonsyn2,
    )
    steps = axis_steps("branch") + axis_steps("site")
    for step in steps[:-1]:
        part = tree_sum(partners(part, *step))
    parts = partners(part, *steps[-1])
    exch, ratio, length, loglik = pl.pallas_call(
        functools.partial(last_kernel, total_sites, len(parts)),
        out_shape=[shape((64, 64), F32), shape((1, CLASSES), F32), shape((1, EDGES), F32), shape((1, 1), F32)],
        in_specs=[vmem] * len(parts),
        out_specs=[vmem] * 4,
        compiler_params=limit,
        name="last",
    )(*parts)
    return (exch, ratio.reshape(CLASSES), length.reshape(EDGES), loglik.reshape(()))


def solution(mesh):
    def whole(states, *rest):
        total_sites = states.shape[1]
        return jax.shard_map(
            functools.partial(body, total_sites),
            mesh=mesh,
            in_specs=(
                P(None, "site"),
                P(None, "site"),
                P("site"),
                P(),
                P(),
                P(),
                P(),
                P("branch"),
                P("branch"),
            ),
            out_specs=(P(), P(), P("branch"), P()),
            check_vma=False,
        )(states, *rest)

    return whole
```

```python
import functools
import jax
import jax.numpy as jnp
import numpy as np
from jax import lax
from jax.experimental import pallas as pl
from jax.experimental.pallas import tpu as pltpu
from jax.sharding import PartitionSpec as P

LEAF_DEV = 64
EDGES = 127
PAIRS = 64
CLASSES = 8
ORDER = 8
BF = jnp.bfloat16
F32 = jnp.float32

CODE_TABLE = "FFLLSSSSYYXXCCXWLLLLPPPPHHQQRRRRIIIMTTTTNNKKSSRRVVVVAAAADDEEGGGG"


def codon_tables():
    amino_acid = np.array(list(CODE_TABLE))
    codon_index = np.arange(64)
    digits = np.stack([codon_index // 16, codon_index // 4 % 4, codon_index % 4], 1)
    differ = (digits[:, None, :] != digits[None, :, :]).sum(-1)
    is_sense = amino_acid != "X"
    single = (differ == 1) & is_sense[:, None] & is_sense[None, :]
    nonsyn = single & (amino_acid[:, None] != amino_acid[None, :])
    return (is_sense.astype(np.float32), single.astype(np.float32), nonsyn.astype(np.float32))


def low_half():
    return lax.broadcasted_iota(jnp.int32, (64, 128), 1) < 64


def split(x):
    high = x.astype(BF)
    low = (x - high.astype(F32)).astype(BF)
    return high, low


def spread(x, scale=1.0):
    mask = low_half()
    low = jnp.where(mask, scale, 0.0).astype(x.dtype)
    high = jnp.where(mask, 0.0, scale).astype(x.dtype)
    return jnp.concatenate([x * low, x * high], axis=0)


def mxu(left, right):
    return jnp.dot(left, right, preferred_element_type=F32)


def mxu_nt(left, right):
    return lax.dot_general(left, right, (((1,), (1,)), ((), ())), preferred_element_type=F32)


def exact(left, right):
    return jnp.dot(left, right, preferred_element_type=F32, precision=lax.Precision.HIGHEST)


def exact_tn(left, right):
    return lax.dot_general(
        left, right, (((0,), (0,)), ((), ())), preferred_element_type=F32,
        precision=lax.Precision.HIGHEST,
    )


def pair_products(*terms):
    lefts, rights = [], []
    for left, right in terms:
        left_high, left_low = split(left)
        right_high, right_low = split(right)
        wide_high, wide_low = spread(right_high), spread(right_low)
        lefts += [left_high, left_high, left_low]
        rights += [wide_high, wide_low, wide_high]
    return mxu(jnp.concatenate(lefts, axis=1), jnp.concatenate(rights, axis=0))


def messages(matrix, high, low):
    return mxu(matrix, jnp.concatenate([high, low, high, low], axis=0))


def double(ref, p, x):
    mask = low_half()
    swapped = pltpu.roll(x, 64, 1)
    for e, both in enumerate((jnp.where(mask, x, swapped), jnp.where(mask, swapped, x))):
        high, low = split(both)
        ref[2 * p + e] = jnp.concatenate([high, low], axis=1)


def identity_twice():
    row = lax.broadcasted_iota(jnp.int32, (64, 128), 0)
    lane = lax.broadcasted_iota(jnp.int32, (64, 128), 1)
    return (row == lane % 64).astype(F32)


def frequencies(freq_ref, sense_ref):
    twice = identity_twice()
    sense2 = sense_ref[...]
    freq2 = exact(jnp.broadcast_to(freq_ref[...], (8, 64)), twice)[0:1] * sense2
    total = 0.5 * jnp.sum(freq2, axis=1, keepdims=True)
    pi_row = freq2 / total
    pi_col = 0.5 * jnp.sum(twice * pi_row, axis=1, keepdims=True)
    sense_col = 0.5 * jnp.sum(twice * sense2, axis=1, keepdims=True)
    root_row = jnp.sqrt(jnp.where(sense2 > 0, pi_row, 1.0))
    root_col = jnp.sqrt(jnp.where(sense_col > 0, pi_col, 1.0))
    return twice, pi_row, pi_col, root_row, root_col


def symmetric_table(ex_ref, single_ref, twice):
    ex = ex_ref[...]
    return 0.5 * (exact(ex, twice) + exact_tn(ex, twice)) * single_ref[...]


def class_pair(table, nonsyn, omega_ref, pair, twice, pi_row, pi_col):
    mask = low_half()
    omega = jnp.where(mask, omega_ref[2 * pair], omega_ref[2 * pair + 1])
    factor = 1.0 + nonsyn * (omega - 1.0)
    flux = table * factor
    off = flux * pi_row
    row0 = jnp.sum(jnp.where(mask, off, 0.0), axis=1, keepdims=True)
    row1 = jnp.sum(jnp.where(mask, 0.0, off), axis=1, keepdims=True)
    mean0 = jnp.sum(pi_col * row0, axis=0, keepdims=True)
    mean1 = jnp.sum(pi_col * row1, axis=0, keepdims=True)
    rows = jnp.where(mask, row0, row1)
    mean = jnp.where(mask, mean0, mean1)
    return factor, off, rows, mean


def neighbours():
    row = lax.broadcasted_iota(jnp.int32, (64, 128), 0)
    lane = lax.broadcasted_iota(jnp.int32, (64, 128), 1) % 64
    masks = [
        row % 16 == lane % 16,
        (row // 16 == lane // 16) & (row % 4 == lane % 4),
        row // 4 == lane // 4,
    ]
    codon = lax.broadcasted_iota(jnp.int32, (64, 16), 0)
    column = lax.broadcasted_iota(jnp.int32, (64, 16), 1)
    digits = [codon // 16, codon // 4 % 4, codon % 4]
    picks = [(column == 4 * p + digits[p]).astype(F32) for p in range(3)]
    return masks, picks


def coefficients(len_ref, cls_ref, slope):
    lane = lax.broadcasted_iota(jnp.int32, (PAIRS, EDGES), 1)
    row = lax.broadcasted_iota(jnp.int32, (PAIRS, EDGES), 0)
    lengths = len_ref[...] * 0.0625
    classes = cls_ref[...].astype(F32)
    place = lax.broadcasted_iota(jnp.int32, (PAIRS, 128), 1) % 64
    found = []
    for odd in range(2):
        here = lane == 2 * row + odd
        y = jnp.sum(jnp.where(here, lengths, 0.0), axis=1, keepdims=True)
        owner = jnp.sum(jnp.where(here, classes, 0.0), axis=1, keepdims=True)
        current = jnp.ones((PAIRS, 128), F32)
        series = jnp.zeros((PAIRS, 128), F32)
        for k in range(ORDER):
            following = current * y * (1.0 / (k + 1))
            series = jnp.where(place // CLASSES == k, current if slope else following, series)
            current = following
        found.append(jnp.where((place % CLASSES).astype(F32) == owner, series, 0.0))
    return found


def four_left(x):
    high, low = split(x)
    return jnp.concatenate([high, low], axis=1)


def four_right(x):
    high, low = split(x)
    return jnp.concatenate([high, low, high, low], axis=0)


def expand(coefs, dup_ref, store):
    high, low = split(coefs)
    left = jnp.concatenate(
        [jnp.concatenate([high, high], axis=1), jnp.concatenate([low, low], axis=1)], axis=0
    )

    def some(step, carry):
        for j in range(16):
            i = step * 32 + 2 * j
            parts = [split(dup_ref[rows_of(i + t, 64), :]) for t in range(2)]
            right = jnp.concatenate([
                jnp.concatenate([spread(parts[0][h]), spread(parts[1][h])], axis=1)
                for h in range(2)
            ], axis=0)
            both = mxu(left, right)
            both = both[0:64] + both[64:128]
            for t in range(2):
                store(i + t, both[:, 128 * t : 128 * t + 128])
        return carry

    lax.fori_loop(0, 2, some, 0)


def rows_of(step, width):
    return pl.ds(pl.multiple_of(step * width, width), width)


def up_kernel(
    states_ref, gap_ref, order_ref,
    ex_ref, freq_ref, omega_ref, len_ref, cls_ref, sense_ref, single_ref, nonsyn_ref,
    top_ref, chain_ref, last_ref, power_ref, dup_ref, fixed_ref,
    message_ref, high_ref, low_ref, leaf_ref, scale_ref, inverse_ref,
    first_ref, up_ref,
):
    subtree = lax.axis_index("branch")
    mask = low_half()
    twice, pi_row, pi_col, root_row, root_col = frequencies(freq_ref, sense_ref)
    table = symmetric_table(ex_ref, single_ref, twice)
    nonsyn = nonsyn_ref[...]
    for at, value in enumerate(
        (pi_row, pi_col, root_row, root_col, 1.0 / root_row, 1.0 / root_col, table)
    ):
        fixed_ref[at] = jnp.broadcast_to(value, (64, 128))

    powers = []
    for pair in range(CLASSES // 2):
        factor, off, rows, mean = class_pair(
            table, nonsyn, omega_ref, pair, twice, pi_row, pi_col
        )
        powers.append([(table * factor * root_col * root_row - twice * rows) / mean])
    for left, right in ((0, 0), (1, 0), (1, 1), (3, 0), (3, 1), (3, 2), (3, 3)):
        for pair in range(CLASSES // 2):
            powers[pair].append(pair_products((powers[pair][left], powers[pair][right])))
    for pair in range(CLASSES // 2):
        for k in range(ORDER):
            value = powers[pair][k]
            swapped = pltpu.roll(value, 64, 1)
            at = CLASSES * k + 2 * pair
            dup_ref[pl.ds(at, 64, stride=64), :] = jnp.where(mask, value, swapped)
            dup_ref[pl.ds(at + 1, 64, stride=64), :] = jnp.where(mask, swapped, value)
            if k < 4:
                power_ref[pair, k] = value

    even, odd = coefficients(len_ref, cls_ref, False)

    def store(i, value):
        first_ref[rows_of(i, 64), :] = value

    expand(jnp.where(low_half(), even, odd), dup_ref, store)

    def squarings(step, carry):
        width = 32
        held = [first_ref[pl.ds(step * width + j, 64, stride=64), :] for j in range(width)]
        for level in range(4):
            for j in range(width):
                high, low = split(held[j])
                chain_ref[level, 0, step * width + j] = high
                chain_ref[level, 1, step * width + j] = low
                wide_high, wide_low = spread(high), spread(low)
                held[j] = 2.0 * held[j] + mxu(
                    jnp.concatenate([high, high, low], axis=1),
                    jnp.concatenate([wide_high, wide_low, wide_high], axis=0),
                )
        for j in range(width):
            p = step * width + j
            last_ref[p] = held[j]
            double(up_ref, p, inverse_root_col * (held[j] + twice) * root_row)
        return carry

    inverse_root_col = 1.0 / root_col
    lax.fori_loop(0, PAIRS // 32, squarings, 0)

    def finish(p, message):
        message_ref[p] = jnp.concatenate(message, axis=0)
        raw = message[0] * message[1]
        scaling = jnp.sum(raw, axis=0, keepdims=True)
        inverse = 1.0 / scaling
        scale_ref[pl.ds(p, 1), :] = scaling
        inverse_ref[pl.ds(p, 1), :] = inverse
        high, low = split(raw * inverse)
        high_ref[p] = high
        low_ref[p] = low

    sites = states_ref.shape[1]
    codon = lax.broadcasted_iota(jnp.int32, (64, sites), 0)

    def leaf_level(step, carry):
        for j in range(8):
            p = step * 8 + j
            both = []
            for e in range(2):
                taxon = order_ref[subtree * LEAF_DEV + 2 * p + e]
                state = jnp.where(
                    gap_ref[pl.ds(taxon, 1), :] > 0, -1, states_ref[pl.ds(taxon, 1), :]
                )
                hit = (codon == state) | (state < 0)
                both.append(jnp.where(hit, 1.0, 0.0).astype(BF))
            leaf_ref[p] = jnp.concatenate(both, axis=0)
            nothing = jnp.zeros_like(both[0])
            finish(p, [messages(up_ref[2 * p + e], both[e], nothing) for e in range(2)])
        return carry

    lax.fori_loop(0, LEAF_DEV // 16, leaf_level, 0)

    def inner(p):
        child = 2 * p - 64
        return [
            messages(up_ref[2 * p + e], high_ref[child + e], low_ref[child + e]) for e in range(2)
        ]

    for p in range(32, 48):
        finish(p, inner(p))
    for p in range(48, 63):
        finish(p, inner(p))
    high_ref[63] = jnp.zeros((64, sites), BF)
    low_ref[63] = jnp.zeros((64, sites), BF)
    scale_ref[63:64, :] = jnp.ones((1, sites), F32)
    inverse_ref[63:64, :] = jnp.ones((1, sites), F32)
    top = inner(63)
    message_ref[63] = jnp.concatenate(top, axis=0)
    top_ref[...] = top[0]


def side_kernel(
    dup_ref, last_ref, len_ref, cls_ref, fixed_ref, slope_ref, matrix_ref, turned_ref,
):
    twice = identity_twice()
    even, odd = coefficients(len_ref, cls_ref, True)

    def store(i, value):
        slope_ref[rows_of(i, 64), :] = value

    expand(jnp.where(low_half(), even, odd), dup_ref, store)
    even, odd = coefficients(len_ref, cls_ref, False)
    turned_ref[...] = exact_tn(jnp.where(low_half(), even, odd), twice)
    root_col, inverse_root_row = fixed_ref[3], fixed_ref[4]

    def matrices(step, carry):
        for j in range(8):
            r = step * 8 + j
            double(matrix_ref, r, root_col * (last_ref[32 + r] + twice) * inverse_root_row)
        return carry

    lax.fori_loop(0, 4, matrices, 0)


def down_kernel(total_sites, members, *refs):
    tops = refs[:members]
    (
        matrix_ref, message_ref, high_ref, low_ref, leaf_ref, scale_ref, inverse_ref,
        chain_ref, turned_ref, slope_ref, power_ref, fixed_ref,
        weights_ref, omega_ref, single_ref, nonsyn_ref,
        out_ref,
        a_high_ref, a_low_ref, count_ref, back_ref, bins_ref,
    ) = refs[members:]
    subtree = lax.axis_index("branch")
    mask = low_half()
    twice = identity_twice()
    pi_row, pi_col, root_row, root_col, inverse_root_row, inverse_root_col = [
        fixed_ref[at] for at in range(6)
    ]
    sites = weights_ref.shape[1]
    weight = weights_ref[...].astype(F32)

    above = jnp.broadcast_to(pi_col[:, 0:1], (64, sites))
    for other in tops[1:]:
        above = above * other[...]
    own = tops[0][...]
    likelihood = jnp.sum(above * own, axis=0, keepdims=True)
    logs = jnp.sum(jnp.log(scale_ref[...]), axis=0, keepdims=True)
    logs = logs + jnp.where(subtree == 0, jnp.log(likelihood), 0.0)
    log_part = jnp.sum(weight * logs, axis=1, keepdims=True)
    high, low = split(above * (weight / (likelihood * total_sites)))
    a_high_ref[31, 0:64, :] = high
    a_low_ref[31, 0:64, :] = low
    a_high_ref[31, 64:128, :] = jnp.zeros((64, sites), BF)
    a_low_ref[31, 64:128, :] = jnp.zeros((64, sites), BF)

    def store_counts(p, square):
        counts = jnp.where(mask, square[0:64], square[64:128])
        count_ref[p] = inverse_root_col * counts * root_row

    def descend(r):
        a_high, a_low = a_high_ref[r - 32], a_low_ref[r - 32]
        child = 2 * r - 64
        u_high = jnp.concatenate([high_ref[child], high_ref[child + 1]], axis=0)
        u_low = jnp.concatenate([low_ref[child], low_ref[child + 1]], axis=0)
        first = mxu_nt(jnp.concatenate([a_high, a_low], axis=0), u_high)
        second = mxu_nt(a_high, u_low)
        store_counts(r, first[0:128] + first[128:256] + second)
        return [
            messages(
                matrix_ref[2 * (r - 32) + e], a_high[64 * e : 64 * e + 64], a_low[64 * e : 64 * e + 64]
            )
            for e in range(2)
        ]

    def children(down, e, p):
        vector = down[e]
        inverse = inverse_ref[pl.ds(p, 1), :]
        message = message_ref[p]
        pair = jnp.concatenate(
            [vector * message[64:128] * inverse, vector * message[0:64] * inverse], axis=0
        )
        return split(pair)

    def inner(r):
        down = descend(r)
        for e in range(2):
            p = 2 * r + e - 64
            if isinstance(p, int) and p == 63:
                continue
            high, low = children(down, e, p)
            a_high_ref[p - 32] = high
            a_low_ref[p - 32] = low

    for r in range(63, 47, -1):
        inner(r)

    def leaf_level(step, carry):
        for j in range(4):
            r = 32 + step * 4 + j
            down = descend(r)
            for e in range(2):
                p = 2 * r + e - 64
                high, low = children(down, e, p)
                square = mxu_nt(jnp.concatenate([high, low], axis=0), leaf_ref[p])
                store_counts(p, square[0:128] + square[128:256])
        return carry

    lax.fori_loop(0, 4, leaf_level, 0)


    def adjoint(step, carry):
        held = [count_ref[step * 16 + j] for j in range(16)]
        for level in range(3, -1, -1):
            for j in range(16):
                high, low = split(held[j])
                e_high, e_low = chain_ref[level, 0, step * 16 + j], chain_ref[level, 1, step * 16 + j]
                left = jnp.concatenate([
                    jnp.concatenate([high, e_high], axis=1),
                    jnp.concatenate([low, e_low], axis=1),
                ], axis=0)
                right = jnp.concatenate([
                    jnp.concatenate([spread(e_high), spread(e_low)], axis=1),
                    jnp.concatenate([spread(high), spread(low)], axis=1),
                ], axis=0)
                four = mxu(left, right)
                four = four[0:64] + four[64:128]
                held[j] = 2.0 * held[j] + four[:, 0:128] + four[:, 128:256]
        for j in range(16):
            back_ref[pl.ds(step * 16 + j, 64, stride=64), :] = held[j]
        return carry

    lax.fori_loop(0, PAIRS // 16, adjoint, 0)

    left = four_left(turned_ref[...])

    def sums(step, total):
        for j in range(16):
            ats = [rows_of(step * 32 + 2 * j + t, 64) for t in range(2)]
            values = [back_ref[at, :] for at in ats]
            both = mxu(left, four_right(jnp.concatenate(values, axis=1)))
            for t in range(2):
                total = total + values[t] * slope_ref[ats[t], :]
                here = both[:, 128 * t : 128 * t + 128]
                bins_ref[ats[t], :] = jnp.where(mask, here[0:64], here[64:128])
        return total

    slopes = lax.fori_loop(0, 2, sums, jnp.zeros((64, 128), F32)) * 0.0625

    table, nonsyn = fixed_ref[6], nonsyn_ref[...]
    row = lax.broadcasted_iota(jnp.int32, (64, 128), 0)
    lane = lax.broadcasted_iota(jnp.int32, (64, 128), 1)
    table_grad = jnp.zeros((64, 128), F32)
    omega_row = jnp.zeros((1, 128), F32)
    lane_row = lax.broadcasted_iota(jnp.int32, (1, 128), 1)
    for pair in range(CLASSES // 2):
        grads = []
        for k in range(ORDER):
            at = CLASSES * k + 2 * pair
            first = bins_ref[pl.ds(at, 64, stride=64), :]
            second = bins_ref[pl.ds(at + 1, 64, stride=64), :]
            first = first + pltpu.roll(first, 64, 1)
            second = second + pltpu.roll(second, 64, 1)
            grads.append(jnp.where(mask, first, second))
        g1, g2, g3, g4, g5, g6, g7, g8 = grads
        a1, a2, a3, a4 = [power_ref[pair, k] for k in range(4)]
        g4 = g4 + pair_products((g8, a4), (a4, g8), (g7, a3), (g6, a2), (g5, a1))
        g3 = g3 + pair_products((a4, g7))
        g2 = g2 + pair_products((a4, g6))
        g1 = g1 + pair_products((a4, g5))
        g2 = g2 + pair_products((g4, a2), (a2, g4), (g3, a1))
        g1 = g1 + pair_products((a2, g3))
        g1 = g1 + pair_products((g2, a1), (a1, g2))
        factor, off, rows, mean = class_pair(
            table, nonsyn, omega_ref, pair, twice, pi_row, pi_col
        )
        d_rate = root_col * g1 * inverse_root_row
        rate = (off - twice * rows) / mean
        weighted = d_rate * rate
        diagonal = d_rate * twice
        total0 = jnp.sum(jnp.where(mask, weighted, 0.0), axis=1, keepdims=True)
        total1 = jnp.sum(jnp.where(mask, 0.0, weighted), axis=1, keepdims=True)
        total0 = jnp.sum(total0, axis=0, keepdims=True)
        total1 = jnp.sum(total1, axis=0, keepdims=True)
        diag0 = jnp.sum(jnp.where(mask, diagonal, 0.0), axis=1, keepdims=True)
        diag1 = jnp.sum(jnp.where(mask, 0.0, diagonal), axis=1, keepdims=True)
        row_grad = jnp.where(mask, diag0 + pi_col * total0, diag1 + pi_col * total1)
        flux_grad = (d_rate - row_grad) * pi_row / mean
        table_grad = table_grad + flux_grad * factor * single_ref[...]
        ratio = flux_grad * table * nonsyn
        ratio0 = jnp.sum(jnp.where(mask, ratio, 0.0), axis=1, keepdims=True)
        ratio1 = jnp.sum(jnp.where(mask, 0.0, ratio), axis=1, keepdims=True)
        ratio0 = jnp.sum(ratio0, axis=0, keepdims=True)
        ratio1 = jnp.sum(ratio1, axis=0, keepdims=True)
        omega_row = jnp.where(lane_row == 2 * pair, ratio0, omega_row)
        omega_row = jnp.where(lane_row == 2 * pair + 1, ratio1, omega_row)
    table_grad = table_grad + pltpu.roll(table_grad, 64, 1)
    masks, picks = neighbours()
    packed = jnp.zeros((16, 128), F32)
    for at_position, pick in zip(masks, picks):
        some = jnp.where(at_position, 0.5 * table_grad, 0.0)
        packed = packed + exact_tn(pick, some) + exact_tn(pick, exact_tn(some[:, 0:64], twice))
    packed = jnp.where(lax.broadcasted_iota(jnp.int32, (16, 128), 1) < 64, packed, 0.0)

    even = jnp.sum(jnp.where(mask, slopes, 0.0), axis=1, keepdims=True)
    other = jnp.sum(jnp.where(mask, 0.0, slopes), axis=1, keepdims=True)
    placed = jnp.where(lane == 2 * row, even, 0.0) + jnp.where(lane == 2 * row + 1, other, 0.0)
    length_row = jnp.sum(placed, axis=0, keepdims=True)
    line = lax.broadcasted_iota(jnp.int32, out_ref.shape, 0)
    omega_row = jnp.where(lane_row == CLASSES, log_part, omega_row)
    omega_row = pltpu.roll(jnp.broadcast_to(omega_row, (8, 128)), 64, 1)[0:1]
    packed = packed + jnp.where(line == 0, omega_row, 0.0)
    out_ref[...] = packed + jnp.where(line == 12 + subtree, length_row, 0.0)


def last_kernel(total_sites, count, *refs):
    members = lax.axis_size("branch")
    subtree = lax.axis_index("branch")
    exch_ref, omega_ref, length_ref, log_ref = refs[count:]
    total = tree_sum([ref[...] for ref in refs[:count]])
    masks, picks = neighbours()
    table = jnp.zeros((64, 128), F32)
    for at_position, pick in zip(masks, picks):
        table = table + jnp.where(at_position, exact(pick, total), 0.0)
    exch_ref[...] = table[:, 0:64]
    moved = pltpu.roll(total[0:8], 64, 1)
    omega_ref[...] = moved[0:1, 0:CLASSES]
    line = lax.broadcasted_iota(jnp.int32, total.shape, 0)
    lengths = jnp.sum(jnp.where(line == 12 + subtree, total, 0.0), axis=0, keepdims=True)
    length_ref[...] = lengths[:, 0:EDGES]
    log_ref[...] = moved[0:1, CLASSES : CLASSES + 1] / total_sites / (LEAF_DEV * members)


def partners(x, axis, start, radix):
    size = lax.axis_size(axis)
    others = [
        lax.ppermute(x, axis, [(i, i ^ (step * start)) for i in range(size)])
        for step in range(1, radix)
    ]
    return [x] + others


def tree_sum(parts):
    while len(parts) > 1:
        parts = [parts[i] + parts[i + 1] for i in range(0, len(parts), 2)]
    return parts[0]


def axis_steps(axis):
    size, start, steps = lax.axis_size(axis), 1, []
    while start < size:
        radix = 2 if size // start in (2, 8) else 4
        steps.append((axis, start, radix))
        start *= radix
    return steps[::-1]


def body(
    total_sites, states, gap_mask, weights, leaf_order, exchanges, codon_freq, omega_ratio,
    lengths, classes,
):
    sites = states.shape[1]
    members = lax.axis_size("branch")
    sense, single, nonsyn = codon_tables()
    vmem = pl.BlockSpec(memory_space=pltpu.VMEM)
    smem = pl.BlockSpec(memory_space=pltpu.SMEM)
    shape = jax.ShapeDtypeStruct
    held = pltpu.VMEM
    limit = pltpu.CompilerParams(vmem_limit_bytes=20 * 2**20)

    def outside(x):
        return pltpu.with_memory_space_constraint(x, pltpu.HBM)

    def inside(xs):
        return [pltpu.with_memory_space_constraint(x, pltpu.VMEM) for x in xs]

    sense2 = outside(jnp.asarray(np.tile(sense[None, :], (1, 2))))
    single2 = outside(jnp.asarray(np.tile(single, (1, 2))))
    nonsyn2 = outside(jnp.asarray(np.tile(nonsyn, (1, 2))))
    freq = outside(codon_freq.reshape(1, 64))
    span, owner = outside(lengths.reshape(1, EDGES)), outside(classes.reshape(1, EDGES))
    table, omega = outside(exchanges), outside(omega_ratio)

    top, *kept = pl.pallas_call(
        up_kernel,
        out_shape=[
            shape((64, sites), F32),
            held((4, 2, PAIRS, 64, 128), BF),
            held((PAIRS, 64, 128), F32),
            held((CLASSES // 2, 4, 64, 128), F32),
            held((ORDER * CLASSES * 64, 128), F32),
            held((7, 64, 128), F32),
            held((PAIRS, 128, sites), F32),
            held((64, 64, sites), BF),
            held((64, 64, sites), BF),
            held((32, 128, sites), BF),
            held((64, sites), F32),
            held((64, sites), F32),
        ],
        in_specs=[vmem, vmem, smem, vmem, vmem, smem] + [vmem] * 5,
        out_specs=[vmem] * 12,
        scratch_shapes=[
            pltpu.VMEM((PAIRS * 64, 128), F32),
            pltpu.VMEM((2 * PAIRS, 64, 256), BF),
        ],
        compiler_params=limit,
        name="up",
    )(
        outside(states), outside(gap_mask), outside(leaf_order),
        table, freq, omega, span, owner, sense2, single2, nonsyn2,
    )
    (
        chain, last, powers, dup, fixed, message, high, low, leaf, scale, inverse,
    ) = inside(kept)
    tops = partners(top, "branch", 1, members)
    slope, matrix, turned = inside(pl.pallas_call(
        side_kernel,
        out_shape=[
            held((PAIRS * 64, 128), F32),
            held((64, 64, 256), BF),
            held((128, 128), F32),
        ],
        in_specs=[vmem] * 5,
        out_specs=[vmem] * 3,
        compiler_params=limit,
        name="side",
    )(dup, last, span, owner, fixed))
    part = pl.pallas_call(
        functools.partial(down_kernel, total_sites, members),
        out_shape=shape((16, 128), F32),
        in_specs=[vmem] * (13 + members) + [smem, vmem, vmem],
        out_specs=vmem,
        scratch_shapes=[
            pltpu.VMEM((32, 128, sites), BF),
            pltpu.VMEM((32, 128, sites), BF),
            pltpu.VMEM((PAIRS, 64, 128), F32),
            pltpu.VMEM((PAIRS * 64, 128), F32),
            pltpu.VMEM((64 * 64, 128), F32),
        ],
        compiler_params=limit,
        name="down",
    )(
        *tops, matrix, message, high, low, leaf, scale, inverse,
        chain, turned, slope, powers, fixed,
        outside(weights.reshape(1, sites)), omega, single2, nonsyn2,
    )
    steps = axis_steps("branch") + axis_steps("site")
    for step in steps[:-1]:
        part = tree_sum(partners(part, *step))
    parts = partners(part, *steps[-1])
    exch, ratio, length, loglik = pl.pallas_call(
        functools.partial(last_kernel, total_sites, len(parts)),
        out_shape=[shape((64, 64), F32), shape((1, CLASSES), F32), shape((1, EDGES), F32), shape((1, 1), F32)],
        in_specs=[vmem] * len(parts),
        out_specs=[vmem] * 4,
        compiler_params=limit,
        name="last",
    )(*parts)
    return (exch, ratio.reshape(CLASSES), length.reshape(EDGES), loglik.reshape(()))


def solution(mesh):
    def whole(states, *rest):
        total_sites = states.shape[1]
        return jax.shard_map(
            functools.partial(body, total_sites),
            mesh=mesh,
            in_specs=(
                P(None, "site"),
                P(None, "site"),
                P("site"),
                P(),
                P(),
                P(),
                P(),
                P("branch"),
                P("branch"),
            ),
            out_specs=(P(), P(), P("branch"), P()),
            check_vma=False,
        )(states, *rest)

    return whole
```

```python
import functools
import jax
import jax.numpy as jnp
import numpy as np
from jax import lax
from jax.experimental import pallas as pl
from jax.experimental.pallas import tpu as pltpu
from jax.sharding import PartitionSpec as P

LEAF_DEV = 64
EDGES = 127
PAIRS = 64
CLASSES = 8
ORDER = 8
BF = jnp.bfloat16
F32 = jnp.float32

CODE_TABLE = "FFLLSSSSYYXXCCXWLLLLPPPPHHQQRRRRIIIMTTTTNNKKSSRRVVVVAAAADDEEGGGG"


def codon_tables():
    amino_acid = np.array(list(CODE_TABLE))
    codon_index = np.arange(64)
    digits = np.stack([codon_index // 16, codon_index // 4 % 4, codon_index % 4], 1)
    differ = (digits[:, None, :] != digits[None, :, :]).sum(-1)
    is_sense = amino_acid != "X"
    single = (differ == 1) & is_sense[:, None] & is_sense[None, :]
    nonsyn = single & (amino_acid[:, None] != amino_acid[None, :])
    return (is_sense.astype(np.float32), single.astype(np.float32), nonsyn.astype(np.float32))


def low_half():
    return lax.broadcasted_iota(jnp.int32, (64, 128), 1) < 64


def split(x):
    high = x.astype(BF)
    low = (x - high.astype(F32)).astype(BF)
    return high, low


def spread(x, scale=1.0):
    mask = low_half()
    low = jnp.where(mask, scale, 0.0).astype(x.dtype)
    high = jnp.where(mask, 0.0, scale).astype(x.dtype)
    return jnp.concatenate([x * low, x * high], axis=0)


def mxu(left, right):
    return jnp.dot(left, right, preferred_element_type=F32)


def mxu_nt(left, right):
    return lax.dot_general(left, right, (((1,), (1,)), ((), ())), preferred_element_type=F32)


def exact(left, right):
    return jnp.dot(left, right, preferred_element_type=F32, precision=lax.Precision.HIGHEST)


def exact_tn(left, right):
    return lax.dot_general(
        left, right, (((0,), (0,)), ((), ())), preferred_element_type=F32,
        precision=lax.Precision.HIGHEST,
    )


def pair_products(*terms):
    lefts, rights = [], []
    for left, right in terms:
        left_high, left_low = split(left)
        right_high, right_low = split(right)
        wide_high, wide_low = spread(right_high), spread(right_low)
        lefts += [left_high, left_high, left_low]
        rights += [wide_high, wide_low, wide_high]
    return mxu(jnp.concatenate(lefts, axis=1), jnp.concatenate(rights, axis=0))


def messages(matrix, high, low):
    return mxu(matrix, jnp.concatenate([high, low, high, low], axis=0))


def double(ref, p, x):
    mask = low_half()
    swapped = pltpu.roll(x, 64, 1)
    for e, both in enumerate((jnp.where(mask, x, swapped), jnp.where(mask, swapped, x))):
        high, low = split(both)
        ref[2 * p + e] = jnp.concatenate([high, low], axis=1)


def identity_twice():
    row = lax.broadcasted_iota(jnp.int32, (64, 128), 0)
    lane = lax.broadcasted_iota(jnp.int32, (64, 128), 1)
    return (row == lane % 64).astype(F32)


def frequencies(freq_ref, sense_ref):
    twice = identity_twice()
    sense2 = sense_ref[...]
    freq2 = exact(jnp.broadcast_to(freq_ref[...], (8, 64)), twice)[0:1] * sense2
    total = 0.5 * jnp.sum(freq2, axis=1, keepdims=True)
    pi_row = freq2 / total
    pi_col = 0.5 * jnp.sum(twice * pi_row, axis=1, keepdims=True)
    sense_col = 0.5 * jnp.sum(twice * sense2, axis=1, keepdims=True)
    root_row = jnp.sqrt(jnp.where(sense2 > 0, pi_row, 1.0))
    root_col = jnp.sqrt(jnp.where(sense_col > 0, pi_col, 1.0))
    return twice, pi_row, pi_col, root_row, root_col


def symmetric_table(ex_ref, single_ref, twice):
    ex = ex_ref[...]
    return 0.5 * (exact(ex, twice) + exact_tn(ex, twice)) * single_ref[...]


def class_pair(table, nonsyn, omega_ref, pair, twice, pi_row, pi_col):
    mask = low_half()
    omega = jnp.where(mask, omega_ref[2 * pair], omega_ref[2 * pair + 1])
    factor = 1.0 + nonsyn * (omega - 1.0)
    flux = table * factor
    off = flux * pi_row
    row0 = jnp.sum(jnp.where(mask, off, 0.0), axis=1, keepdims=True)
    row1 = jnp.sum(jnp.where(mask, 0.0, off), axis=1, keepdims=True)
    mean0 = jnp.sum(pi_col * row0, axis=0, keepdims=True)
    mean1 = jnp.sum(pi_col * row1, axis=0, keepdims=True)
    rows = jnp.where(mask, row0, row1)
    mean = jnp.where(mask, mean0, mean1)
    return factor, off, rows, mean


def neighbours():
    row = lax.broadcasted_iota(jnp.int32, (64, 128), 0)
    lane = lax.broadcasted_iota(jnp.int32, (64, 128), 1) % 64
    masks = [
        row % 16 == lane % 16,
        (row // 16 == lane // 16) & (row % 4 == lane % 4),
        row // 4 == lane // 4,
    ]
    codon = lax.broadcasted_iota(jnp.int32, (64, 16), 0)
    column = lax.broadcasted_iota(jnp.int32, (64, 16), 1)
    digits = [codon // 16, codon // 4 % 4, codon % 4]
    picks = [(column == 4 * p + digits[p]).astype(F32) for p in range(3)]
    return masks, picks


def coefficients(len_ref, cls_ref, slope):
    lane = lax.broadcasted_iota(jnp.int32, (PAIRS, EDGES), 1)
    row = lax.broadcasted_iota(jnp.int32, (PAIRS, EDGES), 0)
    lengths = len_ref[...] * 0.0625
    classes = cls_ref[...].astype(F32)
    place = lax.broadcasted_iota(jnp.int32, (PAIRS, 128), 1) % 64
    found = []
    for odd in range(2):
        here = lane == 2 * row + odd
        y = jnp.sum(jnp.where(here, lengths, 0.0), axis=1, keepdims=True)
        owner = jnp.sum(jnp.where(here, classes, 0.0), axis=1, keepdims=True)
        current = jnp.ones((PAIRS, 128), F32)
        series = jnp.zeros((PAIRS, 128), F32)
        for k in range(ORDER):
            following = current * y * (1.0 / (k + 1))
            series = jnp.where(place // CLASSES == k, current if slope else following, series)
            current = following
        found.append(jnp.where((place % CLASSES).astype(F32) == owner, series, 0.0))
    return found


def four_left(x):
    high, low = split(x)
    return jnp.concatenate([high, low], axis=1)


def four_right(x):
    high, low = split(x)
    return jnp.concatenate([high, low, high, low], axis=0)


def expand(coefs, dup_ref, store):
    high, low = split(coefs)
    left = jnp.concatenate(
        [jnp.concatenate([high, high], axis=1), jnp.concatenate([low, low], axis=1)], axis=0
    )

    def some(step, carry):
        for j in range(16):
            i = step * 32 + 2 * j
            parts = [split(dup_ref[rows_of(i + t, 64), :]) for t in range(2)]
            right = jnp.concatenate([
                jnp.concatenate([spread(parts[0][h]), spread(parts[1][h])], axis=1)
                for h in range(2)
            ], axis=0)
            both = mxu(left, right)
            both = both[0:64] + both[64:128]
            for t in range(2):
                store(i + t, both[:, 128 * t : 128 * t + 128])
        return carry

    lax.fori_loop(0, 2, some, 0)


def rows_of(step, width):
    return pl.ds(pl.multiple_of(step * width, width), width)


def up_kernel(
    states_ref, gap_ref, order_ref,
    ex_ref, freq_ref, omega_ref, len_ref, cls_ref, sense_ref, single_ref, nonsyn_ref,
    top_ref, chain_ref, last_ref, power_ref, dup_ref, fixed_ref,
    message_ref, high_ref, low_ref, leaf_ref, scale_ref, inverse_ref,
    first_ref, up_ref,
):
    subtree = lax.axis_index("branch")
    mask = low_half()
    twice, pi_row, pi_col, root_row, root_col = frequencies(freq_ref, sense_ref)
    table = symmetric_table(ex_ref, single_ref, twice)
    nonsyn = nonsyn_ref[...]
    for at, value in enumerate(
        (pi_row, pi_col, root_row, root_col, 1.0 / root_row, 1.0 / root_col, table)
    ):
        fixed_ref[at] = jnp.broadcast_to(value, (64, 128))

    sites = states_ref.shape[1]
    codon = lax.broadcasted_iota(jnp.int32, (64, sites), 0)
    for p in range(32):
        both = []
        for e in range(2):
            taxon = order_ref[subtree * LEAF_DEV + 2 * p + e]
            state = jnp.where(gap_ref[pl.ds(taxon, 1), :] > 0, -1, states_ref[pl.ds(taxon, 1), :])
            hit = (codon == state) | (state < 0)
            both.append(jnp.where(hit, 1.0, 0.0).astype(BF))
        leaf_ref[p] = jnp.concatenate(both, axis=0)

    powers = []
    for pair in range(CLASSES // 2):
        factor, off, rows, mean = class_pair(
            table, nonsyn, omega_ref, pair, twice, pi_row, pi_col
        )
        powers.append([(table * factor * root_col * root_row - twice * rows) / mean])
    for left, right in ((0, 0), (1, 0), (1, 1), (3, 0), (3, 1), (3, 2), (3, 3)):
        for pair in range(CLASSES // 2):
            powers[pair].append(pair_products((powers[pair][left], powers[pair][right])))
    for pair in range(CLASSES // 2):
        for k in range(ORDER):
            value = powers[pair][k]
            swapped = pltpu.roll(value, 64, 1)
            at = CLASSES * k + 2 * pair
            dup_ref[pl.ds(at, 64, stride=64), :] = jnp.where(mask, value, swapped)
            dup_ref[pl.ds(at + 1, 64, stride=64), :] = jnp.where(mask, swapped, value)
            if k < 4:
                power_ref[pair, k] = value

    even, odd = coefficients(len_ref, cls_ref, False)

    def store(i, value):
        first_ref[rows_of(i, 64), :] = value

    expand(jnp.where(low_half(), even, odd), dup_ref, store)

    def squarings(step, carry):
        width = 16
        held = [first_ref[pl.ds(step * width + j, 64, stride=64), :] for j in range(width)]
        zero = jnp.zeros((128, 128), BF)
        for level in range(4):
            for j in range(0, width, 2):
                highs, lows, products = [], [], []
                for t in range(2):
                    high, low = split(held[j + t])
                    chain_ref[level, 0, step * width + j + t] = high
                    chain_ref[level, 1, step * width + j + t] = low
                    wide = spread(high)
                    highs.append(high)
                    lows.append(spread(low))
                    products.append(mxu(
                        jnp.concatenate([high, low], axis=1), jnp.concatenate([wide, wide], axis=0)
                    ))
                rest = mxu(jnp.concatenate(highs, axis=1), jnp.concatenate([
                    jnp.concatenate([lows[0], zero], axis=1),
                    jnp.concatenate([zero, lows[1]], axis=1),
                ], axis=0))
                for t in range(2):
                    held[j + t] = (
                        2.0 * held[j + t] + products[t] + rest[:, 128 * t : 128 * t + 128]
                    )
        for j in range(width):
            p = step * width + j
            last_ref[p] = held[j]
            double(up_ref, p, inverse_root_col * (held[j] + twice) * root_row)
        return carry

    inverse_root_col = 1.0 / root_col
    lax.fori_loop(0, PAIRS // 16, squarings, 0)

    def finish(p, message):
        message_ref[p] = jnp.concatenate(message, axis=0)
        raw = message[0] * message[1]
        scaling = jnp.sum(raw, axis=0, keepdims=True)
        inverse = 1.0 / scaling
        scale_ref[pl.ds(p, 1), :] = scaling
        inverse_ref[pl.ds(p, 1), :] = inverse
        high, low = split(raw * inverse)
        high_ref[p] = high
        low_ref[p] = low

    for p in range(32):
        both = [leaf_ref[p, 64 * e : 64 * e + 64, :] for e in range(2)]
        nothing = jnp.zeros_like(both[0])
        finish(p, [messages(up_ref[2 * p + e], both[e], nothing) for e in range(2)])

    def inner(p):
        child = 2 * p - 64
        return [
            messages(up_ref[2 * p + e], high_ref[child + e], low_ref[child + e]) for e in range(2)
        ]

    for p in range(32, 48):
        finish(p, inner(p))
    for p in range(48, 63):
        finish(p, inner(p))
    high_ref[63] = jnp.zeros((64, sites), BF)
    low_ref[63] = jnp.zeros((64, sites), BF)
    scale_ref[63:64, :] = jnp.ones((1, sites), F32)
    inverse_ref[63:64, :] = jnp.ones((1, sites), F32)
    top = inner(63)
    message_ref[63] = jnp.concatenate(top, axis=0)
    top_ref[...] = top[0]


def side_kernel(
    dup_ref, last_ref, len_ref, cls_ref, fixed_ref, slope_ref, matrix_ref, turned_ref,
):
    twice = identity_twice()
    even, odd = coefficients(len_ref, cls_ref, True)

    def store(i, value):
        slope_ref[rows_of(i, 64), :] = value

    expand(jnp.where(low_half(), even, odd), dup_ref, store)
    even, odd = coefficients(len_ref, cls_ref, False)
    turned_ref[...] = exact_tn(jnp.where(low_half(), even, odd), twice)
    root_col, inverse_root_row = fixed_ref[3], fixed_ref[4]

    def matrices(step, carry):
        for j in range(8):
            r = step * 8 + j
            double(matrix_ref, r, root_col * (last_ref[32 + r] + twice) * inverse_root_row)
        return carry

    lax.fori_loop(0, 4, matrices, 0)


def down_kernel(total_sites, members, *refs):
    tops = refs[:members]
    (
        matrix_ref, message_ref, high_ref, low_ref, leaf_ref, scale_ref, inverse_ref,
        chain_ref, turned_ref, slope_ref, power_ref, fixed_ref,
        weights_ref, omega_ref, single_ref, nonsyn_ref,
        out_ref,
        a_high_ref, a_low_ref, count_ref, back_ref, bins_ref,
    ) = refs[members:]
    subtree = lax.axis_index("branch")
    mask = low_half()
    twice = identity_twice()
    pi_row, pi_col, root_row, root_col, inverse_root_row, inverse_root_col = [
        fixed_ref[at] for at in range(6)
    ]
    sites = weights_ref.shape[1]
    weight = weights_ref[...].astype(F32)

    above = jnp.broadcast_to(pi_col[:, 0:1], (64, sites))
    for other in tops[1:]:
        above = above * other[...]
    own = tops[0][...]
    likelihood = jnp.sum(above * own, axis=0, keepdims=True)
    logs = jnp.sum(jnp.log(scale_ref[...]), axis=0, keepdims=True)
    logs = logs + jnp.where(subtree == 0, jnp.log(likelihood), 0.0)
    log_part = jnp.sum(weight * logs, axis=1, keepdims=True)
    high, low = split(above * (weight / (likelihood * total_sites)))
    a_high_ref[31, 0:64, :] = high
    a_low_ref[31, 0:64, :] = low
    a_high_ref[31, 64:128, :] = jnp.zeros((64, sites), BF)
    a_low_ref[31, 64:128, :] = jnp.zeros((64, sites), BF)

    def store_counts(p, square):
        counts = jnp.where(mask, square[0:64], square[64:128])
        count_ref[p] = inverse_root_col * counts * root_row

    def descend(r):
        a_high, a_low = a_high_ref[r - 32], a_low_ref[r - 32]
        child = 2 * r - 64
        u_high = jnp.concatenate([high_ref[child], high_ref[child + 1]], axis=0)
        u_low = jnp.concatenate([low_ref[child], low_ref[child + 1]], axis=0)
        first = mxu_nt(jnp.concatenate([a_high, a_low], axis=0), u_high)
        second = mxu_nt(a_high, u_low)
        store_counts(r, first[0:128] + first[128:256] + second)
        return [
            messages(
                matrix_ref[2 * (r - 32) + e], a_high[64 * e : 64 * e + 64], a_low[64 * e : 64 * e + 64]
            )
            for e in range(2)
        ]

    def children(down, e, p):
        vector = down[e]
        inverse = inverse_ref[pl.ds(p, 1), :]
        message = message_ref[p]
        pair = jnp.concatenate(
            [vector * message[64:128] * inverse, vector * message[0:64] * inverse], axis=0
        )
        return split(pair)

    def inner(r):
        down = descend(r)
        for e in range(2):
            p = 2 * r + e - 64
            if isinstance(p, int) and p == 63:
                continue
            high, low = children(down, e, p)
            a_high_ref[p - 32] = high
            a_low_ref[p - 32] = low

    for r in range(63, 47, -1):
        inner(r)

    for r in range(47, 31, -1):
        down = descend(r)
        for e in range(2):
            p = 2 * r + e - 64
            high, low = children(down, e, p)
            square = mxu_nt(jnp.concatenate([high, low], axis=0), leaf_ref[p])
            store_counts(p, square[0:128] + square[128:256])

    def adjoint(step, carry):
        held = [count_ref[step * 16 + j] for j in range(16)]
        for level in range(3, -1, -1):
            for j in range(16):
                high, low = split(held[j])
                e_high, e_low = chain_ref[level, 0, step * 16 + j], chain_ref[level, 1, step * 16 + j]
                left = jnp.concatenate([
                    jnp.concatenate([high, e_high], axis=1),
                    jnp.concatenate([low, e_low], axis=1),
                ], axis=0)
                right = jnp.concatenate([
                    jnp.concatenate([spread(e_high), spread(e_low)], axis=1),
                    jnp.concatenate([spread(high), spread(low)], axis=1),
                ], axis=0)
                four = mxu(left, right)
                held[j] = 2.0 * held[j] + (
                    four[0:64, 0:128] + four[0:64, 128:256] + four[64:128, 0:128]
                )
        for j in range(16):
            back_ref[pl.ds(step * 16 + j, 64, stride=64), :] = held[j]
        return carry

    lax.fori_loop(0, PAIRS // 16, adjoint, 0)

    left = four_left(turned_ref[...])

    def sums(step, total):
        for j in range(16):
            ats = [rows_of(step * 32 + 2 * j + t, 64) for t in range(2)]
            values = [back_ref[at, :] for at in ats]
            both = mxu(left, four_right(jnp.concatenate(values, axis=1)))
            for t in range(2):
                total = total + values[t] * slope_ref[ats[t], :]
                here = both[:, 128 * t : 128 * t + 128]
                bins_ref[ats[t], :] = jnp.where(mask, here[0:64], here[64:128])
        return total

    slopes = lax.fori_loop(0, 2, sums, jnp.zeros((64, 128), F32)) * 0.0625

    table, nonsyn = fixed_ref[6], nonsyn_ref[...]
    row = lax.broadcasted_iota(jnp.int32, (64, 128), 0)
    lane = lax.broadcasted_iota(jnp.int32, (64, 128), 1)
    table_grad = jnp.zeros((64, 128), F32)
    omega_row = jnp.zeros((1, 128), F32)
    lane_row = lax.broadcasted_iota(jnp.int32, (1, 128), 1)
    for pair in range(CLASSES // 2):
        grads = []
        for k in range(ORDER):
            at = CLASSES * k + 2 * pair
            first = bins_ref[pl.ds(at, 64, stride=64), :]
            second = bins_ref[pl.ds(at + 1, 64, stride=64), :]
            first = first + pltpu.roll(first, 64, 1)
            second = second + pltpu.roll(second, 64, 1)
            grads.append(jnp.where(mask, first, second))
        g1, g2, g3, g4, g5, g6, g7, g8 = grads
        a1, a2, a3, a4 = [power_ref[pair, k] for k in range(4)]
        g4 = g4 + pair_products((g8, a4), (a4, g8), (g7, a3), (g6, a2), (g5, a1))
        g3 = g3 + pair_products((a4, g7))
        g2 = g2 + pair_products((a4, g6))
        g1 = g1 + pair_products((a4, g5))
        g2 = g2 + pair_products((g4, a2), (a2, g4), (g3, a1))
        g1 = g1 + pair_products((a2, g3))
        g1 = g1 + pair_products((g2, a1), (a1, g2))
        factor, off, rows, mean = class_pair(
            table, nonsyn, omega_ref, pair, twice, pi_row, pi_col
        )
        d_rate = root_col * g1 * inverse_root_row
        rate = (off - twice * rows) / mean
        weighted = d_rate * rate
        diagonal = d_rate * twice
        total0 = jnp.sum(jnp.where(mask, weighted, 0.0), axis=1, keepdims=True)
        total1 = jnp.sum(jnp.where(mask, 0.0, weighted), axis=1, keepdims=True)
        total0 = jnp.sum(total0, axis=0, keepdims=True)
        total1 = jnp.sum(total1, axis=0, keepdims=True)
        diag0 = jnp.sum(jnp.where(mask, diagonal, 0.0), axis=1, keepdims=True)
        diag1 = jnp.sum(jnp.where(mask, 0.0, diagonal), axis=1, keepdims=True)
        row_grad = jnp.where(mask, diag0 + pi_col * total0, diag1 + pi_col * total1)
        flux_grad = (d_rate - row_grad) * pi_row / mean
        table_grad = table_grad + flux_grad * factor * single_ref[...]
        ratio = flux_grad * table * nonsyn
        ratio0 = jnp.sum(jnp.where(mask, ratio, 0.0), axis=1, keepdims=True)
        ratio1 = jnp.sum(jnp.where(mask, 0.0, ratio), axis=1, keepdims=True)
        ratio0 = jnp.sum(ratio0, axis=0, keepdims=True)
        ratio1 = jnp.sum(ratio1, axis=0, keepdims=True)
        omega_row = jnp.where(lane_row == 2 * pair, ratio0, omega_row)
        omega_row = jnp.where(lane_row == 2 * pair + 1, ratio1, omega_row)
    table_grad = table_grad + pltpu.roll(table_grad, 64, 1)
    masks, picks = neighbours()
    packed = jnp.zeros((16, 128), F32)
    for at_position, pick in zip(masks, picks):
        some = jnp.where(at_position, 0.5 * table_grad, 0.0)
        packed = packed + exact_tn(pick, some) + exact_tn(pick, exact_tn(some[:, 0:64], twice))
    packed = jnp.where(lax.broadcasted_iota(jnp.int32, (16, 128), 1) < 64, packed, 0.0)

    even = jnp.sum(jnp.where(mask, slopes, 0.0), axis=1, keepdims=True)
    other = jnp.sum(jnp.where(mask, 0.0, slopes), axis=1, keepdims=True)
    placed = jnp.where(lane == 2 * row, even, 0.0) + jnp.where(lane == 2 * row + 1, other, 0.0)
    length_row = jnp.sum(placed, axis=0, keepdims=True)
    line = lax.broadcasted_iota(jnp.int32, out_ref.shape, 0)
    omega_row = jnp.where(lane_row == CLASSES, log_part, omega_row)
    omega_row = pltpu.roll(jnp.broadcast_to(omega_row, (8, 128)), 64, 1)[0:1]
    packed = packed + jnp.where(line == 0, omega_row, 0.0)
    out_ref[...] = packed + jnp.where(line == 12 + subtree, length_row, 0.0)


def last_kernel(total_sites, count, *refs):
    members = lax.axis_size("branch")
    subtree = lax.axis_index("branch")
    exch_ref, omega_ref, length_ref, log_ref = refs[count:]
    total = tree_sum([ref[...] for ref in refs[:count]])
    masks, picks = neighbours()
    table = jnp.zeros((64, 128), F32)
    for at_position, pick in zip(masks, picks):
        table = table + jnp.where(at_position, exact(pick, total), 0.0)
    exch_ref[...] = table[:, 0:64]
    moved = pltpu.roll(total[0:8], 64, 1)
    omega_ref[...] = moved[0:1, 0:CLASSES]
    line = lax.broadcasted_iota(jnp.int32, total.shape, 0)
    lengths = jnp.sum(jnp.where(line == 12 + subtree, total, 0.0), axis=0, keepdims=True)
    length_ref[...] = lengths[:, 0:EDGES]
    log_ref[...] = moved[0:1, CLASSES : CLASSES + 1] / total_sites / (LEAF_DEV * members)


def partners(x, axis, start, radix):
    size = lax.axis_size(axis)
    others = [
        lax.ppermute(x, axis, [(i, i ^ (step * start)) for i in range(size)])
        for step in range(1, radix)
    ]
    return [x] + others


def tree_sum(parts):
    while len(parts) > 1:
        parts = [parts[i] + parts[i + 1] for i in range(0, len(parts), 2)]
    return parts[0]


def axis_steps(axis):
    size, start, steps = lax.axis_size(axis), 1, []
    while start < size:
        radix = 2 if size // start in (2, 8) else 4
        steps.append((axis, start, radix))
        start *= radix
    return steps[::-1]


def body(
    total_sites, states, gap_mask, weights, leaf_order, exchanges, codon_freq, omega_ratio,
    lengths, classes,
):
    sites = states.shape[1]
    members = lax.axis_size("branch")
    sense, single, nonsyn = codon_tables()
    vmem = pl.BlockSpec(memory_space=pltpu.VMEM)
    smem = pl.BlockSpec(memory_space=pltpu.SMEM)
    shape = jax.ShapeDtypeStruct
    held = pltpu.VMEM
    limit = pltpu.CompilerParams(vmem_limit_bytes=20 * 2**20)

    def outside(x):
        return pltpu.with_memory_space_constraint(x, pltpu.HBM)

    def inside(xs):
        return [pltpu.with_memory_space_constraint(x, pltpu.VMEM) for x in xs]

    sense2 = outside(jnp.asarray(np.tile(sense[None, :], (1, 2))))
    single2 = outside(jnp.asarray(np.tile(single, (1, 2))))
    nonsyn2 = outside(jnp.asarray(np.tile(nonsyn, (1, 2))))
    freq = outside(codon_freq.reshape(1, 64))
    span, owner = outside(lengths.reshape(1, EDGES)), outside(classes.reshape(1, EDGES))
    table, omega = outside(exchanges), outside(omega_ratio)

    top, *kept = pl.pallas_call(
        up_kernel,
        out_shape=[
            shape((64, sites), F32),
            held((4, 2, PAIRS, 64, 128), BF),
            held((PAIRS, 64, 128), F32),
            held((CLASSES // 2, 4, 64, 128), F32),
            held((ORDER * CLASSES * 64, 128), F32),
            held((7, 64, 128), F32),
            held((PAIRS, 128, sites), F32),
            held((64, 64, sites), BF),
            held((64, 64, sites), BF),
            held((32, 128, sites), BF),
            held((64, sites), F32),
            held((64, sites), F32),
        ],
        in_specs=[vmem, vmem, smem, vmem, vmem, smem] + [vmem] * 5,
        out_specs=[vmem] * 12,
        scratch_shapes=[
            pltpu.VMEM((PAIRS * 64, 128), F32),
            pltpu.VMEM((2 * PAIRS, 64, 256), BF),
        ],
        compiler_params=limit,
        name="up",
    )(
        outside(states), outside(gap_mask), outside(leaf_order),
        table, freq, omega, span, owner, sense2, single2, nonsyn2,
    )
    (
        chain, last, powers, dup, fixed, message, high, low, leaf, scale, inverse,
    ) = inside(kept)
    tops = partners(top, "branch", 1, members)
    slope, matrix, turned = inside(pl.pallas_call(
        side_kernel,
        out_shape=[
            held((PAIRS * 64, 128), F32),
            held((64, 64, 256), BF),
            held((128, 128), F32),
        ],
        in_specs=[vmem] * 5,
        out_specs=[vmem] * 3,
        compiler_params=limit,
        name="side",
    )(dup, last, span, owner, fixed))
    part = pl.pallas_call(
        functools.partial(down_kernel, total_sites, members),
        out_shape=shape((16, 128), F32),
        in_specs=[vmem] * (13 + members) + [smem, vmem, vmem],
        out_specs=vmem,
        scratch_shapes=[
            pltpu.VMEM((32, 128, sites), BF),
            pltpu.VMEM((32, 128, sites), BF),
            pltpu.VMEM((PAIRS, 64, 128), F32),
            pltpu.VMEM((PAIRS * 64, 128), F32),
            pltpu.VMEM((64 * 64, 128), F32),
        ],
        compiler_params=limit,
        name="down",
    )(
        *tops, matrix, message, high, low, leaf, scale, inverse,
        chain, turned, slope, powers, fixed,
        outside(weights.reshape(1, sites)), omega, single2, nonsyn2,
    )
    steps = axis_steps("branch") + axis_steps("site")
    for step in steps[:-1]:
        part = tree_sum(partners(part, *step))
    parts = partners(part, *steps[-1])
    exch, ratio, length, loglik = pl.pallas_call(
        functools.partial(last_kernel, total_sites, len(parts)),
        out_shape=[shape((64, 64), F32), shape((1, CLASSES), F32), shape((1, EDGES), F32), shape((1, 1), F32)],
        in_specs=[vmem] * len(parts),
        out_specs=[vmem] * 4,
        compiler_params=limit,
        name="last",
    )(*parts)
    return (exch, ratio.reshape(CLASSES), length.reshape(EDGES), loglik.reshape(()))


def solution(mesh):
    def whole(states, *rest):
        total_sites = states.shape[1]
        return jax.shard_map(
            functools.partial(body, total_sites),
            mesh=mesh,
            in_specs=(
                P(None, "site"),
                P(None, "site"),
                P("site"),
                P(),
                P(),
                P(),
                P(),
                P("branch"),
                P("branch"),
            ),
            out_specs=(P(), P(), P("branch"), P()),
            check_vma=False,
        )(states, *rest)

    return whole
```

```python
import functools
import jax
import jax.numpy as jnp
import numpy as np
from jax import lax
from jax.experimental import pallas as pl
from jax.experimental.pallas import tpu as pltpu
from jax.sharding import PartitionSpec as P

LEAF_DEV = 64
EDGES = 127
PAIRS = 64
CLASSES = 8
ORDER = 8
STRIDE = 65
BF = jnp.bfloat16
F32 = jnp.float32

CODE_TABLE = "FFLLSSSSYYXXCCXWLLLLPPPPHHQQRRRRIIIMTTTTNNKKSSRRVVVVAAAADDEEGGGG"


def codon_tables():
    amino_acid = np.array(list(CODE_TABLE))
    codon_index = np.arange(64)
    digits = np.stack([codon_index // 16, codon_index // 4 % 4, codon_index % 4], 1)
    differ = (digits[:, None, :] != digits[None, :, :]).sum(-1)
    is_sense = amino_acid != "X"
    single = (differ == 1) & is_sense[:, None] & is_sense[None, :]
    nonsyn = single & (amino_acid[:, None] != amino_acid[None, :])
    return (is_sense.astype(np.float32), single.astype(np.float32), nonsyn.astype(np.float32))


def low_half():
    return lax.broadcasted_iota(jnp.int32, (64, 128), 1) < 64


def split(x):
    high = x.astype(BF)
    low = (x - high.astype(F32)).astype(BF)
    return high, low


def spread(x, scale=1.0):
    mask = low_half()
    low = jnp.where(mask, scale, 0.0).astype(x.dtype)
    high = jnp.where(mask, 0.0, scale).astype(x.dtype)
    return jnp.concatenate([x * low, x * high], axis=0)


def mxu(left, right):
    return jnp.dot(left, right, preferred_element_type=F32)


def mxu_nt(left, right):
    return lax.dot_general(left, right, (((1,), (1,)), ((), ())), preferred_element_type=F32)


def exact(left, right):
    return jnp.dot(left, right, preferred_element_type=F32, precision=lax.Precision.HIGHEST)


def exact_tn(left, right):
    return lax.dot_general(
        left, right, (((0,), (0,)), ((), ())), preferred_element_type=F32,
        precision=lax.Precision.HIGHEST,
    )


def pair_products(*terms):
    lefts, rights = [], []
    for left, right in terms:
        left_high, left_low = split(left)
        right_high, right_low = split(right)
        wide_high, wide_low = spread(right_high), spread(right_low)
        lefts += [left_high, left_high, left_low]
        rights += [wide_high, wide_low, wide_high]
    return mxu(jnp.concatenate(lefts, axis=1), jnp.concatenate(rights, axis=0))


def messages(matrix, high, low):
    return mxu(matrix, jnp.concatenate([high, low, high, low], axis=0))


def double(ref, p, x):
    mask = low_half()
    swapped = pltpu.roll(x, 64, 1)
    for e, both in enumerate((jnp.where(mask, x, swapped), jnp.where(mask, swapped, x))):
        high, low = split(both)
        ref[2 * p + e] = jnp.concatenate([high, low], axis=1)


def identity_twice():
    row = lax.broadcasted_iota(jnp.int32, (64, 128), 0)
    lane = lax.broadcasted_iota(jnp.int32, (64, 128), 1)
    return (row == lane % 64).astype(F32)


def frequencies(freq_ref, sense_ref):
    twice = identity_twice()
    sense2 = sense_ref[...]
    freq2 = exact(jnp.broadcast_to(freq_ref[...], (8, 64)), twice)[0:1] * sense2
    total = 0.5 * jnp.sum(freq2, axis=1, keepdims=True)
    pi_row = freq2 / total
    pi_col = 0.5 * jnp.sum(twice * pi_row, axis=1, keepdims=True)
    sense_col = 0.5 * jnp.sum(twice * sense2, axis=1, keepdims=True)
    root_row = jnp.sqrt(jnp.where(sense2 > 0, pi_row, 1.0))
    root_col = jnp.sqrt(jnp.where(sense_col > 0, pi_col, 1.0))
    return twice, pi_row, pi_col, root_row, root_col


def symmetric_table(ex_ref, single_ref, twice):
    ex = ex_ref[...]
    return 0.5 * (exact(ex, twice) + exact_tn(ex, twice)) * single_ref[...]


def class_pair(table, nonsyn, omega_ref, pair, twice, pi_row, pi_col):
    mask = low_half()
    omega = jnp.where(mask, omega_ref[2 * pair], omega_ref[2 * pair + 1])
    factor = 1.0 + nonsyn * (omega - 1.0)
    flux = table * factor
    off = flux * pi_row
    row0 = jnp.sum(jnp.where(mask, off, 0.0), axis=1, keepdims=True)
    row1 = jnp.sum(jnp.where(mask, 0.0, off), axis=1, keepdims=True)
    mean0 = jnp.sum(pi_col * row0, axis=0, keepdims=True)
    mean1 = jnp.sum(pi_col * row1, axis=0, keepdims=True)
    rows = jnp.where(mask, row0, row1)
    mean = jnp.where(mask, mean0, mean1)
    return factor, off, rows, mean


def neighbours():
    row = lax.broadcasted_iota(jnp.int32, (64, 128), 0)
    lane = lax.broadcasted_iota(jnp.int32, (64, 128), 1) % 64
    masks = [
        row % 16 == lane % 16,
        (row // 16 == lane // 16) & (row % 4 == lane % 4),
        row // 4 == lane // 4,
    ]
    codon = lax.broadcasted_iota(jnp.int32, (64, 16), 0)
    column = lax.broadcasted_iota(jnp.int32, (64, 16), 1)
    digits = [codon // 16, codon // 4 % 4, codon % 4]
    picks = [(column == 4 * p + digits[p]).astype(F32) for p in range(3)]
    return masks, picks


def coefficients(len_ref, cls_ref, slope):
    lane = lax.broadcasted_iota(jnp.int32, (PAIRS, EDGES), 1)
    row = lax.broadcasted_iota(jnp.int32, (PAIRS, EDGES), 0)
    lengths = len_ref[...] * 0.0625
    classes = cls_ref[...].astype(F32)
    place = lax.broadcasted_iota(jnp.int32, (PAIRS, 128), 1) % 64
    found = []
    for odd in range(2):
        here = lane == 2 * row + odd
        y = jnp.sum(jnp.where(here, lengths, 0.0), axis=1, keepdims=True)
        owner = jnp.sum(jnp.where(here, classes, 0.0), axis=1, keepdims=True)
        current = jnp.ones((PAIRS, 128), F32)
        series = jnp.zeros((PAIRS, 128), F32)
        for k in range(ORDER):
            following = current * y * (1.0 / (k + 1))
            series = jnp.where(place // CLASSES == k, current if slope else following, series)
            current = following
        found.append(jnp.where((place % CLASSES).astype(F32) == owner, series, 0.0))
    return found


def four_left(x):
    high, low = split(x)
    return jnp.concatenate([high, low], axis=1)


def four_right(x):
    high, low = split(x)
    return jnp.concatenate([high, low, high, low], axis=0)


def expand(coefs, dup_ref, store):
    high, low = split(coefs)
    left = jnp.concatenate(
        [jnp.concatenate([high, high], axis=1), jnp.concatenate([low, low], axis=1)], axis=0
    )
    for i in range(0, 64, 2):
        parts = [split(dup_ref[rows_of(i + t), :]) for t in range(2)]
        right = jnp.concatenate([
            jnp.concatenate([spread(parts[0][h]), spread(parts[1][h])], axis=1) for h in range(2)
        ], axis=0)
        both = mxu(left, right)
        both = both[0:64] + both[64:128]
        for t in range(2):
            store(i + t, both[:, 128 * t : 128 * t + 128])


def rows_of(i):
    return pl.ds(STRIDE * i, 64)


def up_kernel(
    states_ref, gap_ref, order_ref,
    ex_ref, freq_ref, omega_ref, len_ref, cls_ref, sense_ref, single_ref, nonsyn_ref,
    top_ref, chain_ref, last_ref, power_ref, dup_ref, fixed_ref,
    message_ref, high_ref, low_ref, leaf_ref, scale_ref, inverse_ref,
    first_ref, up_ref,
):
    subtree = lax.axis_index("branch")
    mask = low_half()
    twice, pi_row, pi_col, root_row, root_col = frequencies(freq_ref, sense_ref)
    table = symmetric_table(ex_ref, single_ref, twice)
    nonsyn = nonsyn_ref[...]
    for at, value in enumerate(
        (pi_row, pi_col, root_row, root_col, 1.0 / root_row, 1.0 / root_col, table)
    ):
        fixed_ref[at] = jnp.broadcast_to(value, (64, 128))

    sites = states_ref.shape[1]
    codon = lax.broadcasted_iota(jnp.int32, (64, sites), 0)
    for p in range(32):
        both = []
        for e in range(2):
            taxon = order_ref[subtree * LEAF_DEV + 2 * p + e]
            state = jnp.where(gap_ref[pl.ds(taxon, 1), :] > 0, -1, states_ref[pl.ds(taxon, 1), :])
            hit = (codon == state) | (state < 0)
            both.append(jnp.where(hit, 1.0, 0.0).astype(BF))
        leaf_ref[p] = jnp.concatenate(both, axis=0)

    powers = []
    for pair in range(CLASSES // 2):
        factor, off, rows, mean = class_pair(
            table, nonsyn, omega_ref, pair, twice, pi_row, pi_col
        )
        powers.append([(table * factor * root_col * root_row - twice * rows) / mean])
    for left, right in ((0, 0), (1, 0), (1, 1), (3, 0), (3, 1), (3, 2), (3, 3)):
        for pair in range(CLASSES // 2):
            powers[pair].append(pair_products((powers[pair][left], powers[pair][right])))
    for pair in range(CLASSES // 2):
        for k in range(ORDER):
            value = powers[pair][k]
            swapped = pltpu.roll(value, 64, 1)
            at = CLASSES * k + 2 * pair
            dup_ref[pl.ds(at, 64, stride=STRIDE), :] = jnp.where(mask, value, swapped)
            dup_ref[pl.ds(at + 1, 64, stride=STRIDE), :] = jnp.where(mask, swapped, value)
            if k < 4:
                power_ref[pair, k] = value

    even, odd = coefficients(len_ref, cls_ref, False)

    def store(i, value):
        first_ref[rows_of(i), :] = value

    expand(jnp.where(low_half(), even, odd), dup_ref, store)

    def squarings(step, carry):
        width = 16
        held = [first_ref[pl.ds(step * width + j, 64, stride=STRIDE), :] for j in range(width)]
        zero = jnp.zeros((128, 128), BF)
        for level in range(4):
            for j in range(0, width, 2):
                highs, lows, products = [], [], []
                for t in range(2):
                    high, low = split(held[j + t])
                    chain_ref[level, 0, step * width + j + t] = high
                    chain_ref[level, 1, step * width + j + t] = low
                    wide = spread(high)
                    highs.append(high)
                    lows.append(spread(low))
                    products.append(mxu(
                        jnp.concatenate([high, low], axis=1), jnp.concatenate([wide, wide], axis=0)
                    ))
                rest = mxu(jnp.concatenate(highs, axis=1), jnp.concatenate([
                    jnp.concatenate([lows[0], zero], axis=1),
                    jnp.concatenate([zero, lows[1]], axis=1),
                ], axis=0))
                for t in range(2):
                    held[j + t] = (
                        2.0 * held[j + t] + products[t] + rest[:, 128 * t : 128 * t + 128]
                    )
        for j in range(width):
            p = step * width + j
            last_ref[p] = held[j]
            double(up_ref, p, inverse_root_col * (held[j] + twice) * root_row)
        return carry

    inverse_root_col = 1.0 / root_col
    lax.fori_loop(0, PAIRS // 16, squarings, 0)

    def finish(p, message):
        message_ref[p] = jnp.concatenate(message, axis=0)
        raw = message[0] * message[1]
        scaling = jnp.sum(raw, axis=0, keepdims=True)
        inverse = 1.0 / scaling
        scale_ref[pl.ds(p, 1), :] = scaling
        inverse_ref[pl.ds(p, 1), :] = inverse
        high, low = split(raw * inverse)
        high_ref[p] = high
        low_ref[p] = low

    for p in range(32):
        both = [leaf_ref[p, 64 * e : 64 * e + 64, :] for e in range(2)]
        nothing = jnp.zeros_like(both[0])
        finish(p, [messages(up_ref[2 * p + e], both[e], nothing) for e in range(2)])

    def inner(p):
        child = 2 * p - 64
        return [
            messages(up_ref[2 * p + e], high_ref[child + e], low_ref[child + e]) for e in range(2)
        ]

    for p in range(32, 48):
        finish(p, inner(p))
    for p in range(48, 63):
        finish(p, inner(p))
    high_ref[63] = jnp.zeros((64, sites), BF)
    low_ref[63] = jnp.zeros((64, sites), BF)
    scale_ref[63:64, :] = jnp.ones((1, sites), F32)
    inverse_ref[63:64, :] = jnp.ones((1, sites), F32)
    top = inner(63)
    message_ref[63] = jnp.concatenate(top, axis=0)
    top_ref[...] = top[0]


def side_kernel(
    dup_ref, last_ref, len_ref, cls_ref, fixed_ref, slope_ref, matrix_ref, turned_ref,
):
    twice = identity_twice()
    even, odd = coefficients(len_ref, cls_ref, True)

    def store(i, value):
        slope_ref[rows_of(i), :] = value

    expand(jnp.where(low_half(), even, odd), dup_ref, store)
    even, odd = coefficients(len_ref, cls_ref, False)
    turned_ref[...] = exact_tn(jnp.where(low_half(), even, odd), twice)
    root_col, inverse_root_row = fixed_ref[3], fixed_ref[4]

    def matrices(step, carry):
        for j in range(8):
            r = step * 8 + j
            double(matrix_ref, r, root_col * (last_ref[32 + r] + twice) * inverse_root_row)
        return carry

    lax.fori_loop(0, 4, matrices, 0)


def down_kernel(total_sites, members, *refs):
    tops = refs[:members]
    (
        matrix_ref, message_ref, high_ref, low_ref, leaf_ref, scale_ref, inverse_ref,
        chain_ref, turned_ref, slope_ref, power_ref, fixed_ref,
        weights_ref, omega_ref, single_ref, nonsyn_ref,
        out_ref,
        a_high_ref, a_low_ref, count_ref, back_ref, bins_ref,
    ) = refs[members:]
    subtree = lax.axis_index("branch")
    mask = low_half()
    twice = identity_twice()
    pi_row, pi_col, root_row, root_col, inverse_root_row, inverse_root_col = [
        fixed_ref[at] for at in range(6)
    ]
    sites = weights_ref.shape[1]
    weight = weights_ref[...].astype(F32)

    above = jnp.broadcast_to(pi_col[:, 0:1], (64, sites))
    for other in tops[1:]:
        above = above * other[...]
    own = tops[0][...]
    likelihood = jnp.sum(above * own, axis=0, keepdims=True)
    logs = jnp.sum(jnp.log(scale_ref[...]), axis=0, keepdims=True)
    logs = logs + jnp.where(subtree == 0, jnp.log(likelihood), 0.0)
    log_part = jnp.sum(weight * logs, axis=1, keepdims=True)
    high, low = split(above * (weight / (likelihood * total_sites)))
    a_high_ref[31, 0:64, :] = high
    a_low_ref[31, 0:64, :] = low
    a_high_ref[31, 64:128, :] = jnp.zeros((64, sites), BF)
    a_low_ref[31, 64:128, :] = jnp.zeros((64, sites), BF)

    def store_counts(p, square):
        counts = jnp.where(mask, square[0:64], square[64:128])
        count_ref[p] = inverse_root_col * counts * root_row

    def descend(r):
        a_high, a_low = a_high_ref[r - 32], a_low_ref[r - 32]
        child = 2 * r - 64
        u_high = jnp.concatenate([high_ref[child], high_ref[child + 1]], axis=0)
        u_low = jnp.concatenate([low_ref[child], low_ref[child + 1]], axis=0)
        first = mxu_nt(jnp.concatenate([a_high, a_low], axis=0), u_high)
        second = mxu_nt(a_high, u_low)
        store_counts(r, first[0:128] + first[128:256] + second)
        return [
            messages(
                matrix_ref[2 * (r - 32) + e], a_high[64 * e : 64 * e + 64], a_low[64 * e : 64 * e + 64]
            )
            for e in range(2)
        ]

    def children(down, e, p):
        vector = down[e]
        inverse = inverse_ref[pl.ds(p, 1), :]
        message = message_ref[p]
        pair = jnp.concatenate(
            [vector * message[64:128] * inverse, vector * message[0:64] * inverse], axis=0
        )
        return split(pair)

    def inner(r):
        down = descend(r)
        for e in range(2):
            p = 2 * r + e - 64
            if isinstance(p, int) and p == 63:
                continue
            high, low = children(down, e, p)
            a_high_ref[p - 32] = high
            a_low_ref[p - 32] = low

    for r in range(63, 47, -1):
        inner(r)

    for r in range(47, 31, -1):
        down = descend(r)
        for e in range(2):
            p = 2 * r + e - 64
            high, low = children(down, e, p)
            square = mxu_nt(jnp.concatenate([high, low], axis=0), leaf_ref[p])
            store_counts(p, square[0:128] + square[128:256])

    def adjoint(step, carry):
        held = [count_ref[step * 16 + j] for j in range(16)]
        for level in range(3, -1, -1):
            for j in range(16):
                high, low = split(held[j])
                e_high, e_low = chain_ref[level, 0, step * 16 + j], chain_ref[level, 1, step * 16 + j]
                left = jnp.concatenate([
                    jnp.concatenate([high, e_high], axis=1),
                    jnp.concatenate([low, e_low], axis=1),
                ], axis=0)
                right = jnp.concatenate([
                    jnp.concatenate([spread(e_high), spread(e_low)], axis=1),
                    jnp.concatenate([spread(high), spread(low)], axis=1),
                ], axis=0)
                four = mxu(left, right)
                held[j] = 2.0 * held[j] + (
                    four[0:64, 0:128] + four[0:64, 128:256] + four[64:128, 0:128]
                )
        for j in range(16):
            back_ref[pl.ds(step * 16 + j, 64, stride=STRIDE), :] = held[j]
        return carry

    lax.fori_loop(0, PAIRS // 16, adjoint, 0)

    left = four_left(turned_ref[...])

    total = jnp.zeros((64, 128), F32)
    for i in range(0, 64, 2):
        values = [back_ref[rows_of(i + t), :] for t in range(2)]
        both = mxu(left, four_right(jnp.concatenate(values, axis=1)))
        for t in range(2):
            total = total + values[t] * slope_ref[rows_of(i + t), :]
            here = both[:, 128 * t : 128 * t + 128]
            bins_ref[rows_of(i + t), :] = jnp.where(mask, here[0:64], here[64:128])
    slopes = total * 0.0625

    table, nonsyn = fixed_ref[6], nonsyn_ref[...]
    row = lax.broadcasted_iota(jnp.int32, (64, 128), 0)
    lane = lax.broadcasted_iota(jnp.int32, (64, 128), 1)
    table_grad = jnp.zeros((64, 128), F32)
    omega_row = jnp.zeros((1, 128), F32)
    lane_row = lax.broadcasted_iota(jnp.int32, (1, 128), 1)
    for pair in range(CLASSES // 2):
        grads = []
        for k in range(ORDER):
            at = CLASSES * k + 2 * pair
            first = bins_ref[pl.ds(at, 64, stride=STRIDE), :]
            second = bins_ref[pl.ds(at + 1, 64, stride=STRIDE), :]
            first = first + pltpu.roll(first, 64, 1)
            second = second + pltpu.roll(second, 64, 1)
            grads.append(jnp.where(mask, first, second))
        g1, g2, g3, g4, g5, g6, g7, g8 = grads
        a1, a2, a3, a4 = [power_ref[pair, k] for k in range(4)]
        g4 = g4 + pair_products((g8, a4), (a4, g8), (g7, a3), (g6, a2), (g5, a1))
        g3 = g3 + pair_products((a4, g7))
        g2 = g2 + pair_products((a4, g6))
        g1 = g1 + pair_products((a4, g5))
        g2 = g2 + pair_products((g4, a2), (a2, g4), (g3, a1))
        g1 = g1 + pair_products((a2, g3))
        g1 = g1 + pair_products((g2, a1), (a1, g2))
        factor, off, rows, mean = class_pair(
            table, nonsyn, omega_ref, pair, twice, pi_row, pi_col
        )
        d_rate = root_col * g1 * inverse_root_row
        rate = (off - twice * rows) / mean
        weighted = d_rate * rate
        diagonal = d_rate * twice
        total0 = jnp.sum(jnp.where(mask, weighted, 0.0), axis=1, keepdims=True)
        total1 = jnp.sum(jnp.where(mask, 0.0, weighted), axis=1, keepdims=True)
        total0 = jnp.sum(total0, axis=0, keepdims=True)
        total1 = jnp.sum(total1, axis=0, keepdims=True)
        diag0 = jnp.sum(jnp.where(mask, diagonal, 0.0), axis=1, keepdims=True)
        diag1 = jnp.sum(jnp.where(mask, 0.0, diagonal), axis=1, keepdims=True)
        row_grad = jnp.where(mask, diag0 + pi_col * total0, diag1 + pi_col * total1)
        flux_grad = (d_rate - row_grad) * pi_row / mean
        table_grad = table_grad + flux_grad * factor * single_ref[...]
        ratio = flux_grad * table * nonsyn
        ratio0 = jnp.sum(jnp.where(mask, ratio, 0.0), axis=1, keepdims=True)
        ratio1 = jnp.sum(jnp.where(mask, 0.0, ratio), axis=1, keepdims=True)
        ratio0 = jnp.sum(ratio0, axis=0, keepdims=True)
        ratio1 = jnp.sum(ratio1, axis=0, keepdims=True)
        omega_row = jnp.where(lane_row == 2 * pair, ratio0, omega_row)
        omega_row = jnp.where(lane_row == 2 * pair + 1, ratio1, omega_row)
    table_grad = table_grad + pltpu.roll(table_grad, 64, 1)
    masks, picks = neighbours()
    packed = jnp.zeros((16, 128), F32)
    for at_position, pick in zip(masks, picks):
        some = jnp.where(at_position, 0.5 * table_grad, 0.0)
        packed = packed + exact_tn(pick, some) + exact_tn(pick, exact_tn(some[:, 0:64], twice))
    packed = jnp.where(lax.broadcasted_iota(jnp.int32, (16, 128), 1) < 64, packed, 0.0)

    even = jnp.sum(jnp.where(mask, slopes, 0.0), axis=1, keepdims=True)
    other = jnp.sum(jnp.where(mask, 0.0, slopes), axis=1, keepdims=True)
    placed = jnp.where(lane == 2 * row, even, 0.0) + jnp.where(lane == 2 * row + 1, other, 0.0)
    length_row = jnp.sum(placed, axis=0, keepdims=True)
    line = lax.broadcasted_iota(jnp.int32, out_ref.shape, 0)
    omega_row = jnp.where(lane_row == CLASSES, log_part, omega_row)
    omega_row = pltpu.roll(jnp.broadcast_to(omega_row, (8, 128)), 64, 1)[0:1]
    packed = packed + jnp.where(line == 0, omega_row, 0.0)
    out_ref[...] = packed + jnp.where(line == 12 + subtree, length_row, 0.0)


def last_kernel(total_sites, count, *refs):
    members = lax.axis_size("branch")
    subtree = lax.axis_index("branch")
    exch_ref, omega_ref, length_ref, log_ref = refs[count:]
    total = tree_sum([ref[...] for ref in refs[:count]])
    masks, picks = neighbours()
    table = jnp.zeros((64, 128), F32)
    for at_position, pick in zip(masks, picks):
        table = table + jnp.where(at_position, exact(pick, total), 0.0)
    exch_ref[...] = table[:, 0:64]
    moved = pltpu.roll(total[0:8], 64, 1)
    omega_ref[...] = moved[0:1, 0:CLASSES]
    line = lax.broadcasted_iota(jnp.int32, total.shape, 0)
    lengths = jnp.sum(jnp.where(line == 12 + subtree, total, 0.0), axis=0, keepdims=True)
    length_ref[...] = lengths[:, 0:EDGES]
    log_ref[...] = moved[0:1, CLASSES : CLASSES + 1] / total_sites / (LEAF_DEV * members)


def partners(x, axis, start, radix):
    size = lax.axis_size(axis)
    others = [
        lax.ppermute(x, axis, [(i, i ^ (step * start)) for i in range(size)])
        for step in range(1, radix)
    ]
    return [x] + others


def tree_sum(parts):
    while len(parts) > 1:
        parts = [parts[i] + parts[i + 1] for i in range(0, len(parts), 2)]
    return parts[0]


def axis_steps(axis):
    size, start, steps = lax.axis_size(axis), 1, []
    while start < size:
        radix = 2 if size // start in (2, 8) else 4
        steps.append((axis, start, radix))
        start *= radix
    return steps[::-1]


def body(
    total_sites, states, gap_mask, weights, leaf_order, exchanges, codon_freq, omega_ratio,
    lengths, classes,
):
    sites = states.shape[1]
    members = lax.axis_size("branch")
    sense, single, nonsyn = codon_tables()
    vmem = pl.BlockSpec(memory_space=pltpu.VMEM)
    smem = pl.BlockSpec(memory_space=pltpu.SMEM)
    shape = jax.ShapeDtypeStruct
    held = pltpu.VMEM
    limit = pltpu.CompilerParams(vmem_limit_bytes=20 * 2**20)

    def outside(x):
        return pltpu.with_memory_space_constraint(x, pltpu.HBM)

    def inside(xs):
        return [pltpu.with_memory_space_constraint(x, pltpu.VMEM) for x in xs]

    sense2 = outside(jnp.asarray(np.tile(sense[None, :], (1, 2))))
    single2 = outside(jnp.asarray(np.tile(single, (1, 2))))
    nonsyn2 = outside(jnp.asarray(np.tile(nonsyn, (1, 2))))
    freq = outside(codon_freq.reshape(1, 64))
    span, owner = outside(lengths.reshape(1, EDGES)), outside(classes.reshape(1, EDGES))
    table, omega = outside(exchanges), outside(omega_ratio)

    top, *kept = pl.pallas_call(
        up_kernel,
        out_shape=[
            shape((64, sites), F32),
            held((4, 2, PAIRS, 64, 128), BF),
            held((PAIRS, 64, 128), F32),
            held((CLASSES // 2, 4, 64, 128), F32),
            held((STRIDE * 64, 128), F32),
            held((7, 64, 128), F32),
            held((PAIRS, 128, sites), F32),
            held((64, 64, sites), BF),
            held((64, 64, sites), BF),
            held((32, 128, sites), BF),
            held((64, sites), F32),
            held((64, sites), F32),
        ],
        in_specs=[vmem, vmem, smem, vmem, vmem, smem] + [vmem] * 5,
        out_specs=[vmem] * 12,
        scratch_shapes=[
            pltpu.VMEM((STRIDE * 64, 128), F32),
            pltpu.VMEM((2 * PAIRS, 64, 256), BF),
        ],
        compiler_params=limit,
        name="up",
    )(
        outside(states), outside(gap_mask), outside(leaf_order),
        table, freq, omega, span, owner, sense2, single2, nonsyn2,
    )
    (
        chain, last, powers, dup, fixed, message, high, low, leaf, scale, inverse,
    ) = inside(kept)
    tops = partners(top, "branch", 1, members)
    slope, matrix, turned = inside(pl.pallas_call(
        side_kernel,
        out_shape=[
            held((STRIDE * 64, 128), F32),
            held((64, 64, 256), BF),
            held((128, 128), F32),
        ],
        in_specs=[vmem] * 5,
        out_specs=[vmem] * 3,
        compiler_params=limit,
        name="side",
    )(dup, last, span, owner, fixed))
    part = pl.pallas_call(
        functools.partial(down_kernel, total_sites, members),
        out_shape=shape((16, 128), F32),
        in_specs=[vmem] * (13 + members) + [smem, vmem, vmem],
        out_specs=vmem,
        scratch_shapes=[
            pltpu.VMEM((32, 128, sites), BF),
            pltpu.VMEM((32, 128, sites), BF),
            pltpu.VMEM((PAIRS, 64, 128), F32),
            pltpu.VMEM((STRIDE * 64, 128), F32),
            pltpu.VMEM((STRIDE * 64, 128), F32),
        ],
        compiler_params=limit,
        name="down",
    )(
        *tops, matrix, message, high, low, leaf, scale, inverse,
        chain, turned, slope, powers, fixed,
        outside(weights.reshape(1, sites)), omega, single2, nonsyn2,
    )
    steps = axis_steps("branch") + axis_steps("site")
    for step in steps[:-1]:
        part = tree_sum(partners(part, *step))
    parts = partners(part, *steps[-1])
    exch, ratio, length, loglik = pl.pallas_call(
        functools.partial(last_kernel, total_sites, len(parts)),
        out_shape=[shape((64, 64), F32), shape((1, CLASSES), F32), shape((1, EDGES), F32), shape((1, 1), F32)],
        in_specs=[vmem] * len(parts),
        out_specs=[vmem] * 4,
        compiler_params=limit,
        name="last",
    )(*parts)
    return (exch, ratio.reshape(CLASSES), length.reshape(EDGES), loglik.reshape(()))


def solution(mesh):
    def whole(states, *rest):
        total_sites = states.shape[1]
        return jax.shard_map(
            functools.partial(body, total_sites),
            mesh=mesh,
            in_specs=(
                P(None, "site"),
                P(None, "site"),
                P("site"),
                P(),
                P(),
                P(),
                P(),
                P("branch"),
                P("branch"),
            ),
            out_specs=(P(), P(), P("branch"), P()),
            check_vma=False,
        )(states, *rest)

    return whole
```

```python
import functools
import jax
import jax.numpy as jnp
import numpy as np
from jax import lax
from jax.experimental import pallas as pl
from jax.experimental.pallas import tpu as pltpu
from jax.sharding import PartitionSpec as P

LEAF_DEV = 64
EDGES = 127
PAIRS = 64
CLASSES = 8
ORDER = 8
STRIDE = 65
BF = jnp.bfloat16
F32 = jnp.float32

CODE_TABLE = "FFLLSSSSYYXXCCXWLLLLPPPPHHQQRRRRIIIMTTTTNNKKSSRRVVVVAAAADDEEGGGG"


def codon_tables():
    amino_acid = np.array(list(CODE_TABLE))
    codon_index = np.arange(64)
    digits = np.stack([codon_index // 16, codon_index // 4 % 4, codon_index % 4], 1)
    differ = (digits[:, None, :] != digits[None, :, :]).sum(-1)
    is_sense = amino_acid != "X"
    single = (differ == 1) & is_sense[:, None] & is_sense[None, :]
    nonsyn = single & (amino_acid[:, None] != amino_acid[None, :])
    return (is_sense.astype(np.float32), single.astype(np.float32), nonsyn.astype(np.float32))


def low_half():
    return lax.broadcasted_iota(jnp.int32, (64, 128), 1) < 64


def split(x):
    high = x.astype(BF)
    low = (x - high.astype(F32)).astype(BF)
    return high, low


def spread(x, scale=1.0):
    mask = low_half()
    low = jnp.where(mask, scale, 0.0).astype(x.dtype)
    high = jnp.where(mask, 0.0, scale).astype(x.dtype)
    return jnp.concatenate([x * low, x * high], axis=0)


def mxu(left, right):
    return jnp.dot(left, right, preferred_element_type=F32)


def mxu_nt(left, right):
    return lax.dot_general(left, right, (((1,), (1,)), ((), ())), preferred_element_type=F32)


def exact(left, right):
    return jnp.dot(left, right, preferred_element_type=F32, precision=lax.Precision.HIGHEST)


def exact_tn(left, right):
    return lax.dot_general(
        left, right, (((0,), (0,)), ((), ())), preferred_element_type=F32,
        precision=lax.Precision.HIGHEST,
    )


def pair_products(*terms):
    lefts, rights = [], []
    for left, right in terms:
        left_high, left_low = split(left)
        right_high, right_low = split(right)
        wide_high, wide_low = spread(right_high), spread(right_low)
        lefts += [left_high, left_high, left_low]
        rights += [wide_high, wide_low, wide_high]
    return mxu(jnp.concatenate(lefts, axis=1), jnp.concatenate(rights, axis=0))


def messages(matrix, high, low):
    return mxu(matrix, jnp.concatenate([high, low, high, low], axis=0))


def double(ref, p, x):
    mask = low_half()
    swapped = pltpu.roll(x, 64, 1)
    for e, both in enumerate((jnp.where(mask, x, swapped), jnp.where(mask, swapped, x))):
        high, low = split(both)
        ref[2 * p + e] = jnp.concatenate([high, low], axis=1)


def identity_twice():
    row = lax.broadcasted_iota(jnp.int32, (64, 128), 0)
    lane = lax.broadcasted_iota(jnp.int32, (64, 128), 1)
    return (row == lane % 64).astype(F32)


def frequencies(freq_ref, sense_ref):
    twice = identity_twice()
    sense2 = sense_ref[...]
    freq2 = jnp.concatenate([freq_ref[...]] * 2, axis=1) * sense2
    total = 0.5 * jnp.sum(freq2, axis=1, keepdims=True)
    pi_row = freq2 / total
    pi_col = 0.5 * jnp.sum(twice * pi_row, axis=1, keepdims=True)
    sense_col = 0.5 * jnp.sum(twice * sense2, axis=1, keepdims=True)
    root_row = jnp.sqrt(jnp.where(sense2 > 0, pi_row, 1.0))
    root_col = jnp.sqrt(jnp.where(sense_col > 0, pi_col, 1.0))
    return twice, pi_row, pi_col, root_row, root_col


def symmetric_table(ex_ref, single_ref, twice):
    ex = ex_ref[...]
    both = ex + ex.T
    return 0.5 * jnp.concatenate([both, both], axis=1) * single_ref[...]


def class_pair(table, nonsyn, omega_ref, pair, twice, pi_row, pi_col):
    mask = low_half()
    omega = jnp.where(mask, omega_ref[2 * pair], omega_ref[2 * pair + 1])
    factor = 1.0 + nonsyn * (omega - 1.0)
    flux = table * factor
    off = flux * pi_row
    row0 = jnp.sum(jnp.where(mask, off, 0.0), axis=1, keepdims=True)
    row1 = jnp.sum(jnp.where(mask, 0.0, off), axis=1, keepdims=True)
    mean0 = jnp.sum(pi_col * row0, axis=0, keepdims=True)
    mean1 = jnp.sum(pi_col * row1, axis=0, keepdims=True)
    rows = jnp.where(mask, row0, row1)
    mean = jnp.where(mask, mean0, mean1)
    return factor, off, rows, mean


def neighbours():
    row = lax.broadcasted_iota(jnp.int32, (64, 128), 0)
    lane = lax.broadcasted_iota(jnp.int32, (64, 128), 1) % 64
    masks = [
        row % 16 == lane % 16,
        (row // 16 == lane // 16) & (row % 4 == lane % 4),
        row // 4 == lane // 4,
    ]
    codon = lax.broadcasted_iota(jnp.int32, (64, 16), 0)
    column = lax.broadcasted_iota(jnp.int32, (64, 16), 1)
    digits = [codon // 16, codon // 4 % 4, codon % 4]
    picks = [(column == 4 * p + digits[p]).astype(F32) for p in range(3)]
    return masks, picks


def coefficients(len_ref, cls_ref, slope):
    lane = lax.broadcasted_iota(jnp.int32, (PAIRS, EDGES), 1)
    row = lax.broadcasted_iota(jnp.int32, (PAIRS, EDGES), 0)
    lengths = len_ref[...] * 0.0625
    classes = cls_ref[...].astype(F32)
    place = lax.broadcasted_iota(jnp.int32, (PAIRS, 128), 1) % 64
    found = []
    for odd in range(2):
        here = lane == 2 * row + odd
        y = jnp.sum(jnp.where(here, lengths, 0.0), axis=1, keepdims=True)
        owner = jnp.sum(jnp.where(here, classes, 0.0), axis=1, keepdims=True)
        current = jnp.ones((PAIRS, 128), F32)
        series = jnp.zeros((PAIRS, 128), F32)
        for k in range(ORDER):
            following = current * y * (1.0 / (k + 1))
            series = jnp.where(place // CLASSES == k, current if slope else following, series)
            current = following
        found.append(jnp.where((place % CLASSES).astype(F32) == owner, series, 0.0))
    return found


def four_left(x):
    high, low = split(x)
    return jnp.concatenate([high, low], axis=1)


def four_right(x):
    high, low = split(x)
    return jnp.concatenate([high, low, high, low], axis=0)


def expand(coefs, dup_ref, store):
    high, low = split(coefs)
    left = jnp.concatenate(
        [jnp.concatenate([high, high], axis=1), jnp.concatenate([low, low], axis=1)], axis=0
    )
    for i in range(0, 64, 2):
        parts = [split(dup_ref[rows_of(i + t), :]) for t in range(2)]
        right = jnp.concatenate([
            jnp.concatenate([spread(parts[0][h]), spread(parts[1][h])], axis=1) for h in range(2)
        ], axis=0)
        both = mxu(left, right)
        both = both[0:64] + both[64:128]
        for t in range(2):
            store(i + t, both[:, 128 * t : 128 * t + 128])


def rows_of(i):
    return pl.ds(STRIDE * i, 64)


def up_kernel(
    states_ref, gap_ref, order_ref,
    ex_ref, freq_ref, omega_ref, len_ref, cls_ref, sense_ref, single_ref, nonsyn_ref,
    top_ref, chain_ref, last_ref, power_ref, dup_ref, fixed_ref,
    message_ref, high_ref, low_ref, leaf_ref, scale_ref, inverse_ref,
    first_ref, up_ref,
):
    subtree = lax.axis_index("branch")
    mask = low_half()
    twice, pi_row, pi_col, root_row, root_col = frequencies(freq_ref, sense_ref)
    table = symmetric_table(ex_ref, single_ref, twice)
    nonsyn = nonsyn_ref[...]
    for at, value in enumerate(
        (pi_row, pi_col, root_row, root_col, 1.0 / root_row, 1.0 / root_col, table)
    ):
        fixed_ref[at] = jnp.broadcast_to(value, (64, 128))

    sites = states_ref.shape[1]
    codon = lax.broadcasted_iota(jnp.int32, (64, sites), 0)
    for p in range(32):
        both = []
        for e in range(2):
            taxon = order_ref[subtree * LEAF_DEV + 2 * p + e]
            state = jnp.where(gap_ref[pl.ds(taxon, 1), :] > 0, -1, states_ref[pl.ds(taxon, 1), :])
            hit = (codon == state) | (state < 0)
            both.append(jnp.where(hit, 1.0, 0.0).astype(BF))
        leaf_ref[p] = jnp.concatenate(both, axis=0)

    powers = []
    for pair in range(CLASSES // 2):
        factor, off, rows, mean = class_pair(
            table, nonsyn, omega_ref, pair, twice, pi_row, pi_col
        )
        powers.append([(table * factor * root_col * root_row - twice * rows) / mean])
    for left, right in ((0, 0), (1, 0), (1, 1), (3, 0), (3, 1), (3, 2), (3, 3)):
        for pair in range(CLASSES // 2):
            powers[pair].append(pair_products((powers[pair][left], powers[pair][right])))
    for pair in range(CLASSES // 2):
        for k in range(ORDER):
            value = powers[pair][k]
            swapped = pltpu.roll(value, 64, 1)
            at = CLASSES * k + 2 * pair
            dup_ref[pl.ds(at, 64, stride=STRIDE), :] = jnp.where(mask, value, swapped)
            dup_ref[pl.ds(at + 1, 64, stride=STRIDE), :] = jnp.where(mask, swapped, value)
            if k < 4:
                power_ref[pair, k] = value

    even, odd = coefficients(len_ref, cls_ref, False)

    def store(i, value):
        first_ref[rows_of(i), :] = value

    expand(jnp.where(low_half(), even, odd), dup_ref, store)

    def squarings(step, carry):
        width = 16
        held = [first_ref[pl.ds(step * width + j, 64, stride=STRIDE), :] for j in range(width)]
        zero = jnp.zeros((128, 128), BF)
        for level in range(4):
            for j in range(0, width, 2):
                highs, lows, products = [], [], []
                for t in range(2):
                    high, low = split(held[j + t])
                    chain_ref[level, 0, step * width + j + t] = high
                    chain_ref[level, 1, step * width + j + t] = low
                    wide = spread(high)
                    highs.append(high)
                    lows.append(spread(low))
                    products.append(mxu(
                        jnp.concatenate([high, low], axis=1), jnp.concatenate([wide, wide], axis=0)
                    ))
                rest = mxu(jnp.concatenate(highs, axis=1), jnp.concatenate([
                    jnp.concatenate([lows[0], zero], axis=1),
                    jnp.concatenate([zero, lows[1]], axis=1),
                ], axis=0))
                for t in range(2):
                    held[j + t] = (
                        2.0 * held[j + t] + products[t] + rest[:, 128 * t : 128 * t + 128]
                    )
        for j in range(width):
            p = step * width + j
            last_ref[p] = held[j]
            double(up_ref, p, inverse_root_col * (held[j] + twice) * root_row)
        return carry

    inverse_root_col = 1.0 / root_col
    lax.fori_loop(0, PAIRS // 16, squarings, 0)

    def finish(p, message):
        message_ref[p] = jnp.concatenate(message, axis=0)
        raw = message[0] * message[1]
        scaling = jnp.sum(raw, axis=0, keepdims=True)
        inverse = 1.0 / scaling
        scale_ref[pl.ds(p, 1), :] = scaling
        inverse_ref[pl.ds(p, 1), :] = inverse
        high, low = split(raw * inverse)
        high_ref[p] = high
        low_ref[p] = low

    for p in range(32):
        both = [leaf_ref[p, 64 * e : 64 * e + 64, :] for e in range(2)]
        nothing = jnp.zeros_like(both[0])
        finish(p, [messages(up_ref[2 * p + e], both[e], nothing) for e in range(2)])

    def inner(p):
        child = 2 * p - 64
        return [
            messages(up_ref[2 * p + e], high_ref[child + e], low_ref[child + e]) for e in range(2)
        ]

    for p in range(32, 48):
        finish(p, inner(p))
    for p in range(48, 63):
        finish(p, inner(p))
    high_ref[63] = jnp.zeros((64, sites), BF)
    low_ref[63] = jnp.zeros((64, sites), BF)
    scale_ref[63:64, :] = jnp.ones((1, sites), F32)
    inverse_ref[63:64, :] = jnp.ones((1, sites), F32)
    top = inner(63)
    message_ref[63] = jnp.concatenate(top, axis=0)
    top_ref[...] = top[0]


def side_kernel(
    dup_ref, last_ref, len_ref, cls_ref, fixed_ref, slope_ref, matrix_ref, turned_ref,
):
    twice = identity_twice()
    even, odd = coefficients(len_ref, cls_ref, True)

    def store(i, value):
        slope_ref[rows_of(i), :] = value

    expand(jnp.where(low_half(), even, odd), dup_ref, store)
    even, odd = coefficients(len_ref, cls_ref, False)
    turned_ref[...] = exact_tn(jnp.where(low_half(), even, odd), twice)
    root_col, inverse_root_row = fixed_ref[3], fixed_ref[4]

    def matrices(step, carry):
        for j in range(8):
            r = step * 8 + j
            double(matrix_ref, r, root_col * (last_ref[32 + r] + twice) * inverse_root_row)
        return carry

    lax.fori_loop(0, 4, matrices, 0)


def down_kernel(total_sites, members, *refs):
    tops = refs[:members]
    (
        matrix_ref, message_ref, high_ref, low_ref, leaf_ref, scale_ref, inverse_ref,
        chain_ref, turned_ref, slope_ref, power_ref, fixed_ref,
        weights_ref, omega_ref, single_ref, nonsyn_ref,
        out_ref,
        a_high_ref, a_low_ref, count_ref, back_ref, bins_ref,
    ) = refs[members:]
    subtree = lax.axis_index("branch")
    mask = low_half()
    twice = identity_twice()
    pi_row, pi_col, root_row, root_col, inverse_root_row, inverse_root_col = [
        fixed_ref[at] for at in range(6)
    ]
    sites = weights_ref.shape[1]
    weight = weights_ref[...].astype(F32)

    above = jnp.broadcast_to(pi_col[:, 0:1], (64, sites))
    for other in tops[1:]:
        above = above * other[...]
    own = tops[0][...]
    likelihood = jnp.sum(above * own, axis=0, keepdims=True)
    logs = jnp.sum(jnp.log(scale_ref[...]), axis=0, keepdims=True)
    logs = logs + jnp.where(subtree == 0, jnp.log(likelihood), 0.0)
    log_part = jnp.sum(weight * logs, axis=1, keepdims=True)
    high, low = split(above * (weight / (likelihood * total_sites)))
    a_high_ref[31, 0:64, :] = high
    a_low_ref[31, 0:64, :] = low
    a_high_ref[31, 64:128, :] = jnp.zeros((64, sites), BF)
    a_low_ref[31, 64:128, :] = jnp.zeros((64, sites), BF)

    def store_counts(p, square):
        counts = jnp.where(mask, square[0:64], square[64:128])
        count_ref[p] = inverse_root_col * counts * root_row

    def descend(r):
        a_high, a_low = a_high_ref[r - 32], a_low_ref[r - 32]
        child = 2 * r - 64
        u_high = jnp.concatenate([high_ref[child], high_ref[child + 1]], axis=0)
        u_low = jnp.concatenate([low_ref[child], low_ref[child + 1]], axis=0)
        first = mxu_nt(jnp.concatenate([a_high, a_low], axis=0), u_high)
        second = mxu_nt(a_high, u_low)
        store_counts(r, first[0:128] + first[128:256] + second)
        return [
            messages(
                matrix_ref[2 * (r - 32) + e], a_high[64 * e : 64 * e + 64], a_low[64 * e : 64 * e + 64]
            )
            for e in range(2)
        ]

    def children(down, e, p):
        vector = down[e]
        inverse = inverse_ref[pl.ds(p, 1), :]
        message = message_ref[p]
        pair = jnp.concatenate(
            [vector * message[64:128] * inverse, vector * message[0:64] * inverse], axis=0
        )
        return split(pair)

    def inner(r):
        down = descend(r)
        for e in range(2):
            p = 2 * r + e - 64
            if isinstance(p, int) and p == 63:
                continue
            high, low = children(down, e, p)
            a_high_ref[p - 32] = high
            a_low_ref[p - 32] = low

    for r in range(63, 47, -1):
        inner(r)

    for r in range(47, 31, -1):
        down = descend(r)
        for e in range(2):
            p = 2 * r + e - 64
            high, low = children(down, e, p)
            square = mxu_nt(jnp.concatenate([high, low], axis=0), leaf_ref[p])
            store_counts(p, square[0:128] + square[128:256])

    def adjoint(step, carry):
        held = [count_ref[step * 16 + j] for j in range(16)]
        for level in range(3, -1, -1):
            for j in range(16):
                high, low = split(held[j])
                e_high, e_low = chain_ref[level, 0, step * 16 + j], chain_ref[level, 1, step * 16 + j]
                left = jnp.concatenate([
                    jnp.concatenate([high, e_high], axis=1),
                    jnp.concatenate([low, e_low], axis=1),
                ], axis=0)
                right = jnp.concatenate([
                    jnp.concatenate([spread(e_high), spread(e_low)], axis=1),
                    jnp.concatenate([spread(high), spread(low)], axis=1),
                ], axis=0)
                four = mxu(left, right)
                held[j] = 2.0 * held[j] + (
                    four[0:64, 0:128] + four[0:64, 128:256] + four[64:128, 0:128]
                )
        for j in range(16):
            back_ref[pl.ds(step * 16 + j, 64, stride=STRIDE), :] = held[j]
        return carry

    lax.fori_loop(0, PAIRS // 16, adjoint, 0)

    left = four_left(turned_ref[...])

    total = jnp.zeros((64, 128), F32)
    for i in range(0, 64, 2):
        values = [back_ref[rows_of(i + t), :] for t in range(2)]
        both = mxu(left, four_right(jnp.concatenate(values, axis=1)))
        for t in range(2):
            total = total + values[t] * slope_ref[rows_of(i + t), :]
            here = both[:, 128 * t : 128 * t + 128]
            bins_ref[rows_of(i + t), :] = jnp.where(mask, here[0:64], here[64:128])
    slopes = total * 0.0625

    table, nonsyn = fixed_ref[6], nonsyn_ref[...]
    row = lax.broadcasted_iota(jnp.int32, (64, 128), 0)
    lane = lax.broadcasted_iota(jnp.int32, (64, 128), 1)
    table_grad = jnp.zeros((64, 128), F32)
    omega_row = jnp.zeros((1, 128), F32)
    lane_row = lax.broadcasted_iota(jnp.int32, (1, 128), 1)
    for pair in range(CLASSES // 2):
        grads = []
        for k in range(ORDER):
            at = CLASSES * k + 2 * pair
            first = bins_ref[pl.ds(at, 64, stride=STRIDE), :]
            second = bins_ref[pl.ds(at + 1, 64, stride=STRIDE), :]
            first = first + pltpu.roll(first, 64, 1)
            second = second + pltpu.roll(second, 64, 1)
            grads.append(jnp.where(mask, first, second))
        g1, g2, g3, g4, g5, g6, g7, g8 = grads
        a1, a2, a3, a4 = [power_ref[pair, k] for k in range(4)]
        g4 = g4 + pair_products((g8, a4), (a4, g8), (g7, a3), (g6, a2), (g5, a1))
        g3 = g3 + pair_products((a4, g7))
        g2 = g2 + pair_products((a4, g6))
        g1 = g1 + pair_products((a4, g5))
        g2 = g2 + pair_products((g4, a2), (a2, g4), (g3, a1))
        g1 = g1 + pair_products((a2, g3))
        g1 = g1 + pair_products((g2, a1), (a1, g2))
        factor, off, rows, mean = class_pair(
            table, nonsyn, omega_ref, pair, twice, pi_row, pi_col
        )
        d_rate = root_col * g1 * inverse_root_row
        rate = (off - twice * rows) / mean
        weighted = d_rate * rate
        diagonal = d_rate * twice
        total0 = jnp.sum(jnp.where(mask, weighted, 0.0), axis=1, keepdims=True)
        total1 = jnp.sum(jnp.where(mask, 0.0, weighted), axis=1, keepdims=True)
        total0 = jnp.sum(total0, axis=0, keepdims=True)
        total1 = jnp.sum(total1, axis=0, keepdims=True)
        diag0 = jnp.sum(jnp.where(mask, diagonal, 0.0), axis=1, keepdims=True)
        diag1 = jnp.sum(jnp.where(mask, 0.0, diagonal), axis=1, keepdims=True)
        row_grad = jnp.where(mask, diag0 + pi_col * total0, diag1 + pi_col * total1)
        flux_grad = (d_rate - row_grad) * pi_row / mean
        table_grad = table_grad + flux_grad * factor * single_ref[...]
        ratio = flux_grad * table * nonsyn
        ratio0 = jnp.sum(jnp.where(mask, ratio, 0.0), axis=1, keepdims=True)
        ratio1 = jnp.sum(jnp.where(mask, 0.0, ratio), axis=1, keepdims=True)
        ratio0 = jnp.sum(ratio0, axis=0, keepdims=True)
        ratio1 = jnp.sum(ratio1, axis=0, keepdims=True)
        omega_row = jnp.where(lane_row == 2 * pair, ratio0, omega_row)
        omega_row = jnp.where(lane_row == 2 * pair + 1, ratio1, omega_row)
    table_grad = table_grad + pltpu.roll(table_grad, 64, 1)
    masks, picks = neighbours()
    codon = lax.broadcasted_iota(jnp.int32, (16, 128), 1)
    column = lax.broadcasted_iota(jnp.int32, (16, 128), 0)
    lefts, rights = [], []
    for p, digit in enumerate((codon // 16, codon // 4 % 4, codon % 4)):
        left = jnp.where((column == 4 * p + digit) & (codon < 64), 1.0, 0.0).astype(BF)
        for part in split(jnp.where(masks[p], 0.5 * table_grad, 0.0)):
            lefts.append(left)
            rights.append(part)
    packed = mxu(
        jnp.concatenate(lefts, axis=1),
        jnp.concatenate([jnp.concatenate([part, jnp.zeros_like(part)], axis=0) for part in rights], axis=0),
    )
    turned = mxu_nt(
        jnp.concatenate(lefts, axis=1),
        jnp.concatenate([
            jnp.concatenate([part, jnp.zeros_like(part)], axis=0) for part in rights
        ], axis=1),
    )
    packed = packed + turned
    packed = jnp.where(lax.broadcasted_iota(jnp.int32, (16, 128), 1) < 64, packed, 0.0)

    even = jnp.sum(jnp.where(mask, slopes, 0.0), axis=1, keepdims=True)
    other = jnp.sum(jnp.where(mask, 0.0, slopes), axis=1, keepdims=True)
    placed = jnp.where(lane == 2 * row, even, 0.0) + jnp.where(lane == 2 * row + 1, other, 0.0)
    length_row = jnp.sum(placed, axis=0, keepdims=True)
    line = lax.broadcasted_iota(jnp.int32, out_ref.shape, 0)
    omega_row = jnp.where(lane_row == CLASSES, log_part, omega_row)
    omega_row = pltpu.roll(jnp.broadcast_to(omega_row, (8, 128)), 64, 1)[0:1]
    packed = packed + jnp.where(line == 0, omega_row, 0.0)
    out_ref[...] = packed + jnp.where(line == 12 + subtree, length_row, 0.0)


def last_kernel(total_sites, count, *refs):
    members = lax.axis_size("branch")
    subtree = lax.axis_index("branch")
    exch_ref, omega_ref, length_ref, log_ref = refs[count:]
    total = tree_sum([ref[...] for ref in refs[:count]])
    masks, picks = neighbours()
    table = jnp.zeros((64, 128), F32)
    for at_position, pick in zip(masks, picks):
        table = table + jnp.where(at_position, exact(pick, total), 0.0)
    exch_ref[...] = table[:, 0:64]
    moved = pltpu.roll(total[0:8], 64, 1)
    omega_ref[...] = moved[0:1, 0:CLASSES]
    line = lax.broadcasted_iota(jnp.int32, total.shape, 0)
    lengths = jnp.sum(jnp.where(line == 12 + subtree, total, 0.0), axis=0, keepdims=True)
    length_ref[...] = lengths[:, 0:EDGES]
    log_ref[...] = moved[0:1, CLASSES : CLASSES + 1] / total_sites / (LEAF_DEV * members)


def partners(x, axis, start, radix):
    size = lax.axis_size(axis)
    others = [
        lax.ppermute(x, axis, [(i, i ^ (step * start)) for i in range(size)])
        for step in range(1, radix)
    ]
    return [x] + others


def tree_sum(parts):
    while len(parts) > 1:
        parts = [parts[i] + parts[i + 1] for i in range(0, len(parts), 2)]
    return parts[0]


def axis_steps(axis):
    size, start, steps = lax.axis_size(axis), 1, []
    while start < size:
        radix = 2 if size // start in (2, 8) else 4
        steps.append((axis, start, radix))
        start *= radix
    return steps[::-1]


def body(
    total_sites, states, gap_mask, weights, leaf_order, exchanges, codon_freq, omega_ratio,
    lengths, classes,
):
    sites = states.shape[1]
    members = lax.axis_size("branch")
    sense, single, nonsyn = codon_tables()
    vmem = pl.BlockSpec(memory_space=pltpu.VMEM)
    smem = pl.BlockSpec(memory_space=pltpu.SMEM)
    shape = jax.ShapeDtypeStruct
    held = pltpu.VMEM
    limit = pltpu.CompilerParams(vmem_limit_bytes=20 * 2**20)

    def outside(x):
        return pltpu.with_memory_space_constraint(x, pltpu.HBM)

    def inside(xs):
        return [pltpu.with_memory_space_constraint(x, pltpu.VMEM) for x in xs]

    sense2 = outside(jnp.asarray(np.tile(sense[None, :], (1, 2))))
    single2 = outside(jnp.asarray(np.tile(single, (1, 2))))
    nonsyn2 = outside(jnp.asarray(np.tile(nonsyn, (1, 2))))
    freq = outside(codon_freq.reshape(1, 64))
    span, owner = outside(lengths.reshape(1, EDGES)), outside(classes.reshape(1, EDGES))
    table, omega = outside(exchanges), outside(omega_ratio)

    top, *kept = pl.pallas_call(
        up_kernel,
        out_shape=[
            shape((64, sites), F32),
            held((4, 2, PAIRS, 64, 128), BF),
            held((PAIRS, 64, 128), F32),
            held((CLASSES // 2, 4, 64, 128), F32),
            held((STRIDE * 64, 128), F32),
            held((7, 64, 128), F32),
            held((PAIRS, 128, sites), F32),
            held((64, 64, sites), BF),
            held((64, 64, sites), BF),
            held((32, 128, sites), BF),
            held((64, sites), F32),
            held((64, sites), F32),
        ],
        in_specs=[vmem, vmem, smem, vmem, vmem, smem] + [vmem] * 5,
        out_specs=[vmem] * 12,
        scratch_shapes=[
            pltpu.VMEM((STRIDE * 64, 128), F32),
            pltpu.VMEM((2 * PAIRS, 64, 256), BF),
        ],
        compiler_params=limit,
        name="up",
    )(
        outside(states), outside(gap_mask), outside(leaf_order),
        table, freq, omega, span, owner, sense2, single2, nonsyn2,
    )
    (
        chain, last, powers, dup, fixed, message, high, low, leaf, scale, inverse,
    ) = inside(kept)
    tops = partners(top, "branch", 1, members)
    slope, matrix, turned = inside(pl.pallas_call(
        side_kernel,
        out_shape=[
            held((STRIDE * 64, 128), F32),
            held((64, 64, 256), BF),
            held((128, 128), F32),
        ],
        in_specs=[vmem] * 5,
        out_specs=[vmem] * 3,
        compiler_params=limit,
        name="side",
    )(dup, last, span, owner, fixed))
    part = pl.pallas_call(
        functools.partial(down_kernel, total_sites, members),
        out_shape=shape((16, 128), F32),
        in_specs=[vmem] * (13 + members) + [smem, vmem, vmem],
        out_specs=vmem,
        scratch_shapes=[
            pltpu.VMEM((32, 128, sites), BF),
            pltpu.VMEM((32, 128, sites), BF),
            pltpu.VMEM((PAIRS, 64, 128), F32),
            pltpu.VMEM((STRIDE * 64, 128), F32),
            pltpu.VMEM((STRIDE * 64, 128), F32),
        ],
        compiler_params=limit,
        name="down",
    )(
        *tops, matrix, message, high, low, leaf, scale, inverse,
        chain, turned, slope, powers, fixed,
        outside(weights.reshape(1, sites)), omega, single2, nonsyn2,
    )
    steps = axis_steps("branch") + axis_steps("site")
    for step in steps[:-1]:
        part = tree_sum(partners(part, *step))
    parts = partners(part, *steps[-1])
    exch, ratio, length, loglik = pl.pallas_call(
        functools.partial(last_kernel, total_sites, len(parts)),
        out_shape=[shape((64, 64), F32), shape((1, CLASSES), F32), shape((1, EDGES), F32), shape((1, 1), F32)],
        in_specs=[vmem] * len(parts),
        out_specs=[vmem] * 4,
        compiler_params=limit,
        name="last",
    )(*parts)
    return (exch, ratio.reshape(CLASSES), length.reshape(EDGES), loglik.reshape(()))


def solution(mesh):
    def whole(states, *rest):
        total_sites = states.shape[1]
        return jax.shard_map(
            functools.partial(body, total_sites),
            mesh=mesh,
            in_specs=(
                P(None, "site"),
                P(None, "site"),
                P("site"),
                P(),
                P(),
                P(),
                P(),
                P("branch"),
                P("branch"),
            ),
            out_specs=(P(), P(), P("branch"), P()),
            check_vma=False,
        )(states, *rest)

    return whole
```

```python
import functools
import jax
import jax.numpy as jnp
import numpy as np
from jax import lax
from jax.experimental import pallas as pl
from jax.experimental.pallas import tpu as pltpu
from jax.sharding import PartitionSpec as P

LEAF_DEV = 64
EDGES = 127
PAIRS = 64
CLASSES = 8
ORDER = 8
STRIDE = 65
BF = jnp.bfloat16
F32 = jnp.float32

CODE_TABLE = "FFLLSSSSYYXXCCXWLLLLPPPPHHQQRRRRIIIMTTTTNNKKSSRRVVVVAAAADDEEGGGG"


def codon_tables():
    amino_acid = np.array(list(CODE_TABLE))
    codon_index = np.arange(64)
    digits = np.stack([codon_index // 16, codon_index // 4 % 4, codon_index % 4], 1)
    differ = (digits[:, None, :] != digits[None, :, :]).sum(-1)
    is_sense = amino_acid != "X"
    single = (differ == 1) & is_sense[:, None] & is_sense[None, :]
    nonsyn = single & (amino_acid[:, None] != amino_acid[None, :])
    return (is_sense.astype(np.float32), single.astype(np.float32), nonsyn.astype(np.float32))


def low_half():
    return lax.broadcasted_iota(jnp.int32, (64, 128), 1) < 64


def split(x):
    high = x.astype(BF)
    low = (x - high.astype(F32)).astype(BF)
    return high, low


def spread(x, scale=1.0):
    mask = low_half()
    low = jnp.where(mask, scale, 0.0).astype(x.dtype)
    high = jnp.where(mask, 0.0, scale).astype(x.dtype)
    return jnp.concatenate([x * low, x * high], axis=0)


def mxu(left, right):
    return jnp.dot(left, right, preferred_element_type=F32)


def mxu_nt(left, right):
    return lax.dot_general(left, right, (((1,), (1,)), ((), ())), preferred_element_type=F32)


def exact(left, right):
    return jnp.dot(left, right, preferred_element_type=F32, precision=lax.Precision.HIGHEST)


def exact_tn(left, right):
    return lax.dot_general(
        left, right, (((0,), (0,)), ((), ())), preferred_element_type=F32,
        precision=lax.Precision.HIGHEST,
    )


def pair_products(*terms):
    lefts, rights = [], []
    for left, right in terms:
        left_high, left_low = split(left)
        right_high, right_low = split(right)
        wide_high, wide_low = spread(right_high), spread(right_low)
        lefts += [left_high, left_high, left_low]
        rights += [wide_high, wide_low, wide_high]
    return mxu(jnp.concatenate(lefts, axis=1), jnp.concatenate(rights, axis=0))


def messages(matrix, high, low):
    return mxu(matrix, jnp.concatenate([high, low, high, low], axis=0))


def doubled(x):
    mask = low_half()
    swapped = pltpu.roll(x, 64, 1)
    return jnp.where(mask, x, swapped), jnp.where(mask, swapped, x)


def double(ref, p, x):
    for e, both in enumerate(doubled(x)):
        high, low = split(both)
        ref[2 * p + e] = jnp.concatenate([high, low], axis=1)


def side_by_side(ref, p, x):
    for e, both in enumerate(doubled(x)):
        rest = both - both.astype(BF).astype(F32)
        ref[2 * p + e] = jnp.where(low_half(), both, rest).astype(BF)


def identity_twice():
    row = lax.broadcasted_iota(jnp.int32, (64, 128), 0)
    lane = lax.broadcasted_iota(jnp.int32, (64, 128), 1)
    return (row == lane % 64).astype(F32)


def frequencies(freq_ref, sense_ref):
    twice = identity_twice()
    sense2 = sense_ref[...]
    freq2 = jnp.concatenate([freq_ref[...]] * 2, axis=1) * sense2
    total = 0.5 * jnp.sum(freq2, axis=1, keepdims=True)
    pi_row = freq2 / total
    pi_col = 0.5 * jnp.sum(twice * pi_row, axis=1, keepdims=True)
    sense_col = 0.5 * jnp.sum(twice * sense2, axis=1, keepdims=True)
    root_row = jnp.sqrt(jnp.where(sense2 > 0, pi_row, 1.0))
    root_col = jnp.sqrt(jnp.where(sense_col > 0, pi_col, 1.0))
    return twice, pi_row, pi_col, root_row, root_col


def symmetric_table(ex_ref, single_ref, twice):
    ex = ex_ref[...]
    both = ex + ex.T
    return 0.5 * jnp.concatenate([both, both], axis=1) * single_ref[...]


def class_pair(table, nonsyn, omega_ref, pair, twice, pi_row, pi_col):
    mask = low_half()
    omega = jnp.where(mask, omega_ref[2 * pair], omega_ref[2 * pair + 1])
    factor = 1.0 + nonsyn * (omega - 1.0)
    flux = table * factor
    off = flux * pi_row
    row0 = jnp.sum(jnp.where(mask, off, 0.0), axis=1, keepdims=True)
    row1 = jnp.sum(jnp.where(mask, 0.0, off), axis=1, keepdims=True)
    mean0 = jnp.sum(pi_col * row0, axis=0, keepdims=True)
    mean1 = jnp.sum(pi_col * row1, axis=0, keepdims=True)
    rows = jnp.where(mask, row0, row1)
    mean = jnp.where(mask, mean0, mean1)
    return factor, off, rows, mean


def neighbours():
    row = lax.broadcasted_iota(jnp.int32, (64, 128), 0)
    lane = lax.broadcasted_iota(jnp.int32, (64, 128), 1) % 64
    masks = [
        row % 16 == lane % 16,
        (row // 16 == lane // 16) & (row % 4 == lane % 4),
        row // 4 == lane // 4,
    ]
    codon = lax.broadcasted_iota(jnp.int32, (64, 16), 0)
    column = lax.broadcasted_iota(jnp.int32, (64, 16), 1)
    digits = [codon // 16, codon // 4 % 4, codon % 4]
    picks = [(column == 4 * p + digits[p]).astype(F32) for p in range(3)]
    return masks, picks


def coefficients(len_ref, cls_ref, slope):
    lane = lax.broadcasted_iota(jnp.int32, (PAIRS, EDGES), 1)
    row = lax.broadcasted_iota(jnp.int32, (PAIRS, EDGES), 0)
    lengths = len_ref[...] * 0.0625
    classes = cls_ref[...].astype(F32)
    place = lax.broadcasted_iota(jnp.int32, (PAIRS, 128), 1) % 64
    found = []
    for odd in range(2):
        here = lane == 2 * row + odd
        y = jnp.sum(jnp.where(here, lengths, 0.0), axis=1, keepdims=True)
        owner = jnp.sum(jnp.where(here, classes, 0.0), axis=1, keepdims=True)
        current = jnp.ones((PAIRS, 128), F32)
        series = jnp.zeros((PAIRS, 128), F32)
        for k in range(ORDER):
            following = current * y * (1.0 / (k + 1))
            series = jnp.where(place // CLASSES == k, current if slope else following, series)
            current = following
        found.append(jnp.where((place % CLASSES).astype(F32) == owner, series, 0.0))
    return found


def four_left(x):
    high, low = split(x)
    return jnp.concatenate([high, low], axis=1)


def four_right(x):
    high, low = split(x)
    return jnp.concatenate([high, low, high, low], axis=0)


def expand(coefs, dup_ref, store):
    high, low = split(coefs)
    left = jnp.concatenate(
        [jnp.concatenate([high, high], axis=1), jnp.concatenate([low, low], axis=1)], axis=0
    )
    for i in range(0, 64, 2):
        parts = [split(dup_ref[rows_of(i + t), :]) for t in range(2)]
        right = jnp.concatenate([
            jnp.concatenate([spread(parts[0][h]), spread(parts[1][h])], axis=1) for h in range(2)
        ], axis=0)
        both = mxu(left, right)
        both = both[0:64] + both[64:128]
        for t in range(2):
            store(i + t, both[:, 128 * t : 128 * t + 128])


def rows_of(i):
    return pl.ds(STRIDE * i, 64)


def up_kernel(
    states_ref, gap_ref, order_ref,
    ex_ref, freq_ref, omega_ref, len_ref, cls_ref, sense_ref, single_ref, nonsyn_ref,
    top_ref, chain_ref, last_ref, power_ref, dup_ref, fixed_ref,
    message_ref, high_ref, low_ref, leaf_ref, scale_ref, inverse_ref,
    first_ref, up_ref, thin_ref,
):
    subtree = lax.axis_index("branch")
    mask = low_half()
    twice, pi_row, pi_col, root_row, root_col = frequencies(freq_ref, sense_ref)
    table = symmetric_table(ex_ref, single_ref, twice)
    nonsyn = nonsyn_ref[...]
    for at, value in enumerate(
        (pi_row, pi_col, root_row, root_col, 1.0 / root_row, 1.0 / root_col, table)
    ):
        fixed_ref[at] = jnp.broadcast_to(value, (64, 128))

    sites = states_ref.shape[1]
    codon = lax.broadcasted_iota(jnp.int32, (64, sites), 0)
    for p in range(32):
        both = []
        for e in range(2):
            taxon = order_ref[subtree * LEAF_DEV + 2 * p + e]
            state = jnp.where(gap_ref[pl.ds(taxon, 1), :] > 0, -1, states_ref[pl.ds(taxon, 1), :])
            hit = (codon == state) | (state < 0)
            both.append(jnp.where(hit, 1.0, 0.0).astype(BF))
        leaf_ref[p] = jnp.concatenate(both, axis=0)

    powers = []
    for pair in range(CLASSES // 2):
        factor, off, rows, mean = class_pair(
            table, nonsyn, omega_ref, pair, twice, pi_row, pi_col
        )
        powers.append([(table * factor * root_col * root_row - twice * rows) / mean])
    for left, right in ((0, 0), (1, 0), (1, 1), (3, 0), (3, 1), (3, 2), (3, 3)):
        for pair in range(CLASSES // 2):
            powers[pair].append(pair_products((powers[pair][left], powers[pair][right])))
    for pair in range(CLASSES // 2):
        for k in range(ORDER):
            value = powers[pair][k]
            swapped = pltpu.roll(value, 64, 1)
            at = CLASSES * k + 2 * pair
            dup_ref[pl.ds(at, 64, stride=STRIDE), :] = jnp.where(mask, value, swapped)
            dup_ref[pl.ds(at + 1, 64, stride=STRIDE), :] = jnp.where(mask, swapped, value)
            if k < 4:
                power_ref[pair, k] = value

    even, odd = coefficients(len_ref, cls_ref, False)

    def store(i, value):
        first_ref[rows_of(i), :] = value

    expand(jnp.where(low_half(), even, odd), dup_ref, store)

    def squarings(leaves, step, carry):
        width = 16
        held = [first_ref[pl.ds(step * width + j, 64, stride=STRIDE), :] for j in range(width)]
        zero = jnp.zeros((128, 128), BF)
        for level in range(4):
            for j in range(0, width, 2):
                highs, lows, products = [], [], []
                for t in range(2):
                    high, low = split(held[j + t])
                    chain_ref[level, 0, step * width + j + t] = high
                    chain_ref[level, 1, step * width + j + t] = low
                    wide = spread(high)
                    highs.append(high)
                    lows.append(spread(low))
                    products.append(mxu(
                        jnp.concatenate([high, low], axis=1), jnp.concatenate([wide, wide], axis=0)
                    ))
                rest = mxu(jnp.concatenate(highs, axis=1), jnp.concatenate([
                    jnp.concatenate([lows[0], zero], axis=1),
                    jnp.concatenate([zero, lows[1]], axis=1),
                ], axis=0))
                for t in range(2):
                    held[j + t] = (
                        2.0 * held[j + t] + products[t] + rest[:, 128 * t : 128 * t + 128]
                    )
        for j in range(width):
            p = step * width + j
            matrix = inverse_root_col * (held[j] + twice) * root_row
            if leaves:
                side_by_side(thin_ref, p, matrix)
            else:
                last_ref[p - 32] = held[j]
                double(up_ref, p - 32, matrix)
        return carry

    inverse_root_col = 1.0 / root_col
    lax.fori_loop(0, 2, functools.partial(squarings, True), 0)
    lax.fori_loop(2, 4, functools.partial(squarings, False), 0)

    def finish(p, message):
        message_ref[p] = jnp.concatenate(message, axis=0)
        raw = message[0] * message[1]
        scaling = jnp.sum(raw, axis=0, keepdims=True)
        inverse = 1.0 / scaling
        scale_ref[pl.ds(p, 1), :] = scaling
        inverse_ref[pl.ds(p, 1), :] = inverse
        high, low = split(raw * inverse)
        high_ref[p] = high
        low_ref[p] = low

    for p in range(32):
        both = [leaf_ref[p, 64 * e : 64 * e + 64, :] for e in range(2)]
        finish(p, [
            mxu(thin_ref[2 * p + e], jnp.concatenate([both[e], both[e]], axis=0)) for e in range(2)
        ])

    def inner(p):
        child = 2 * p - 64
        return [
            messages(up_ref[child + e], high_ref[child + e], low_ref[child + e]) for e in range(2)
        ]

    for p in range(32, 48):
        finish(p, inner(p))
    for p in range(48, 63):
        finish(p, inner(p))
    high_ref[63] = jnp.zeros((64, sites), BF)
    low_ref[63] = jnp.zeros((64, sites), BF)
    scale_ref[63:64, :] = jnp.ones((1, sites), F32)
    inverse_ref[63:64, :] = jnp.ones((1, sites), F32)
    top = inner(63)
    message_ref[63] = jnp.concatenate(top, axis=0)
    top_ref[...] = top[0]


def side_kernel(
    dup_ref, last_ref, len_ref, cls_ref, fixed_ref, slope_ref, matrix_ref, turned_ref,
):
    twice = identity_twice()
    even, odd = coefficients(len_ref, cls_ref, True)

    def store(i, value):
        slope_ref[rows_of(i), :] = value

    expand(jnp.where(low_half(), even, odd), dup_ref, store)
    even, odd = coefficients(len_ref, cls_ref, False)
    turned_ref[...] = exact_tn(jnp.where(low_half(), even, odd), twice)
    root_col, inverse_root_row = fixed_ref[3], fixed_ref[4]

    def matrices(step, carry):
        for j in range(8):
            r = step * 8 + j
            double(matrix_ref, r, root_col * (last_ref[r] + twice) * inverse_root_row)
        return carry

    lax.fori_loop(0, 4, matrices, 0)


def down_kernel(total_sites, members, *refs):
    tops = refs[:members]
    (
        matrix_ref, message_ref, high_ref, low_ref, leaf_ref, scale_ref, inverse_ref,
        chain_ref, turned_ref, slope_ref, power_ref, fixed_ref,
        weights_ref, omega_ref, single_ref, nonsyn_ref,
        out_ref,
        a_high_ref, a_low_ref, count_ref, back_ref, bins_ref,
    ) = refs[members:]
    subtree = lax.axis_index("branch")
    mask = low_half()
    twice = identity_twice()
    pi_row, pi_col, root_row, root_col, inverse_root_row, inverse_root_col = [
        fixed_ref[at] for at in range(6)
    ]
    sites = weights_ref.shape[1]
    weight = weights_ref[...].astype(F32)

    above = jnp.broadcast_to(pi_col[:, 0:1], (64, sites))
    for other in tops[1:]:
        above = above * other[...]
    own = tops[0][...]
    likelihood = jnp.sum(above * own, axis=0, keepdims=True)
    logs = jnp.sum(jnp.log(scale_ref[...]), axis=0, keepdims=True)
    logs = logs + jnp.where(subtree == 0, jnp.log(likelihood), 0.0)
    log_part = jnp.sum(weight * logs, axis=1, keepdims=True)
    high, low = split(above * (weight / (likelihood * total_sites)))
    a_high_ref[31, 0:64, :] = high
    a_low_ref[31, 0:64, :] = low
    a_high_ref[31, 64:128, :] = jnp.zeros((64, sites), BF)
    a_low_ref[31, 64:128, :] = jnp.zeros((64, sites), BF)

    def store_counts(p, square):
        counts = jnp.where(mask, square[0:64], square[64:128])
        count_ref[p] = inverse_root_col * counts * root_row

    def descend(r):
        a_high, a_low = a_high_ref[r - 32], a_low_ref[r - 32]
        child = 2 * r - 64
        u_high = jnp.concatenate([high_ref[child], high_ref[child + 1]], axis=0)
        u_low = jnp.concatenate([low_ref[child], low_ref[child + 1]], axis=0)
        first = mxu_nt(jnp.concatenate([a_high, a_low], axis=0), u_high)
        second = mxu_nt(a_high, u_low)
        store_counts(r, first[0:128] + first[128:256] + second)
        return [
            messages(
                matrix_ref[2 * (r - 32) + e], a_high[64 * e : 64 * e + 64], a_low[64 * e : 64 * e + 64]
            )
            for e in range(2)
        ]

    def children(down, e, p):
        vector = down[e]
        inverse = inverse_ref[pl.ds(p, 1), :]
        message = message_ref[p]
        pair = jnp.concatenate(
            [vector * message[64:128] * inverse, vector * message[0:64] * inverse], axis=0
        )
        return split(pair)

    def inner(r):
        down = descend(r)
        for e in range(2):
            p = 2 * r + e - 64
            if isinstance(p, int) and p == 63:
                continue
            high, low = children(down, e, p)
            a_high_ref[p - 32] = high
            a_low_ref[p - 32] = low

    for r in range(63, 47, -1):
        inner(r)

    for r in range(47, 31, -1):
        down = descend(r)
        for e in range(2):
            p = 2 * r + e - 64
            high, low = children(down, e, p)
            square = mxu_nt(jnp.concatenate([high, low], axis=0), leaf_ref[p])
            store_counts(p, square[0:128] + square[128:256])

    def adjoint(step, carry):
        held = [count_ref[step * 16 + j] for j in range(16)]
        for level in range(3, -1, -1):
            for j in range(16):
                high, low = split(held[j])
                e_high, e_low = chain_ref[level, 0, step * 16 + j], chain_ref[level, 1, step * 16 + j]
                left = jnp.concatenate([
                    jnp.concatenate([high, e_high], axis=1),
                    jnp.concatenate([low, e_low], axis=1),
                ], axis=0)
                right = jnp.concatenate([
                    jnp.concatenate([spread(e_high), spread(e_low)], axis=1),
                    jnp.concatenate([spread(high), spread(low)], axis=1),
                ], axis=0)
                four = mxu(left, right)
                held[j] = 2.0 * held[j] + (
                    four[0:64, 0:128] + four[0:64, 128:256] + four[64:128, 0:128]
                )
        for j in range(16):
            back_ref[pl.ds(step * 16 + j, 64, stride=STRIDE), :] = held[j]
        return carry

    lax.fori_loop(0, PAIRS // 16, adjoint, 0)

    left = four_left(turned_ref[...])

    total = jnp.zeros((64, 128), F32)
    for i in range(0, 64, 2):
        values = [back_ref[rows_of(i + t), :] for t in range(2)]
        both = mxu(left, four_right(jnp.concatenate(values, axis=1)))
        for t in range(2):
            total = total + values[t] * slope_ref[rows_of(i + t), :]
            here = both[:, 128 * t : 128 * t + 128]
            bins_ref[rows_of(i + t), :] = jnp.where(mask, here[0:64], here[64:128])
    slopes = total * 0.0625

    table, nonsyn = fixed_ref[6], nonsyn_ref[...]
    row = lax.broadcasted_iota(jnp.int32, (64, 128), 0)
    lane = lax.broadcasted_iota(jnp.int32, (64, 128), 1)
    table_grad = jnp.zeros((64, 128), F32)
    omega_row = jnp.zeros((1, 128), F32)
    lane_row = lax.broadcasted_iota(jnp.int32, (1, 128), 1)
    for pair in range(CLASSES // 2):
        grads = []
        for k in range(ORDER):
            at = CLASSES * k + 2 * pair
            first = bins_ref[pl.ds(at, 64, stride=STRIDE), :]
            second = bins_ref[pl.ds(at + 1, 64, stride=STRIDE), :]
            first = first + pltpu.roll(first, 64, 1)
            second = second + pltpu.roll(second, 64, 1)
            grads.append(jnp.where(mask, first, second))
        g1, g2, g3, g4, g5, g6, g7, g8 = grads
        a1, a2, a3, a4 = [power_ref[pair, k] for k in range(4)]
        g4 = g4 + pair_products((g8, a4), (a4, g8), (g7, a3), (g6, a2), (g5, a1))
        g3 = g3 + pair_products((a4, g7))
        g2 = g2 + pair_products((a4, g6))
        g1 = g1 + pair_products((a4, g5))
        g2 = g2 + pair_products((g4, a2), (a2, g4), (g3, a1))
        g1 = g1 + pair_products((a2, g3))
        g1 = g1 + pair_products((g2, a1), (a1, g2))
        factor, off, rows, mean = class_pair(
            table, nonsyn, omega_ref, pair, twice, pi_row, pi_col
        )
        d_rate = root_col * g1 * inverse_root_row
        rate = (off - twice * rows) / mean
        weighted = d_rate * rate
        diagonal = d_rate * twice
        total0 = jnp.sum(jnp.where(mask, weighted, 0.0), axis=1, keepdims=True)
        total1 = jnp.sum(jnp.where(mask, 0.0, weighted), axis=1, keepdims=True)
        total0 = jnp.sum(total0, axis=0, keepdims=True)
        total1 = jnp.sum(total1, axis=0, keepdims=True)
        diag0 = jnp.sum(jnp.where(mask, diagonal, 0.0), axis=1, keepdims=True)
        diag1 = jnp.sum(jnp.where(mask, 0.0, diagonal), axis=1, keepdims=True)
        row_grad = jnp.where(mask, diag0 + pi_col * total0, diag1 + pi_col * total1)
        flux_grad = (d_rate - row_grad) * pi_row / mean
        table_grad = table_grad + flux_grad * factor * single_ref[...]
        ratio = flux_grad * table * nonsyn
        ratio0 = jnp.sum(jnp.where(mask, ratio, 0.0), axis=1, keepdims=True)
        ratio1 = jnp.sum(jnp.where(mask, 0.0, ratio), axis=1, keepdims=True)
        ratio0 = jnp.sum(ratio0, axis=0, keepdims=True)
        ratio1 = jnp.sum(ratio1, axis=0, keepdims=True)
        omega_row = jnp.where(lane_row == 2 * pair, ratio0, omega_row)
        omega_row = jnp.where(lane_row == 2 * pair + 1, ratio1, omega_row)
    table_grad = table_grad + pltpu.roll(table_grad, 64, 1)
    masks, picks = neighbours()
    codon = lax.broadcasted_iota(jnp.int32, (16, 128), 1)
    column = lax.broadcasted_iota(jnp.int32, (16, 128), 0)
    lefts, rights = [], []
    for p, digit in enumerate((codon // 16, codon // 4 % 4, codon % 4)):
        left = jnp.where((column == 4 * p + digit) & (codon < 64), 1.0, 0.0).astype(BF)
        for part in split(jnp.where(masks[p], 0.5 * table_grad, 0.0)):
            lefts.append(left)
            rights.append(part)
    packed = mxu(
        jnp.concatenate(lefts, axis=1),
        jnp.concatenate([jnp.concatenate([part, jnp.zeros_like(part)], axis=0) for part in rights], axis=0),
    )
    turned = mxu_nt(
        jnp.concatenate(lefts, axis=1),
        jnp.concatenate([
            jnp.concatenate([part, jnp.zeros_like(part)], axis=0) for part in rights
        ], axis=1),
    )
    packed = packed + turned
    packed = jnp.where(lax.broadcasted_iota(jnp.int32, (16, 128), 1) < 64, packed, 0.0)

    even = jnp.sum(jnp.where(mask, slopes, 0.0), axis=1, keepdims=True)
    other = jnp.sum(jnp.where(mask, 0.0, slopes), axis=1, keepdims=True)
    placed = jnp.where(lane == 2 * row, even, 0.0) + jnp.where(lane == 2 * row + 1, other, 0.0)
    length_row = jnp.sum(placed, axis=0, keepdims=True)
    line = lax.broadcasted_iota(jnp.int32, out_ref.shape, 0)
    omega_row = jnp.where(lane_row == CLASSES, log_part, omega_row)
    omega_row = pltpu.roll(jnp.broadcast_to(omega_row, (8, 128)), 64, 1)[0:1]
    packed = packed + jnp.where(line == 0, omega_row, 0.0)
    out_ref[...] = packed + jnp.where(line == 12 + subtree, length_row, 0.0)


def last_kernel(total_sites, own_ref, got_ref, exch_ref, omega_ref, length_ref, log_ref):
    members = lax.axis_size("branch")
    subtree = lax.axis_index("branch")
    total = jnp.where(subtree % 2 == 1, own_ref[...], got_ref[...])
    masks, picks = neighbours()
    table = jnp.zeros((64, 128), F32)
    for at_position, pick in zip(masks, picks):
        table = table + jnp.where(at_position, exact(pick, total), 0.0)
    exch_ref[...] = table[:, 0:64]
    moved = pltpu.roll(total[0:8], 64, 1)
    omega_ref[...] = moved[0:1, 0:CLASSES]
    line = lax.broadcasted_iota(jnp.int32, total.shape, 0)
    lengths = jnp.sum(jnp.where(line == 12 + subtree, total, 0.0), axis=0, keepdims=True)
    length_ref[...] = lengths[:, 0:EDGES]
    log_ref[...] = moved[0:1, CLASSES : CLASSES + 1] / total_sites / (LEAF_DEV * members)


def partners(x, axis, start, radix):
    size = lax.axis_size(axis)
    others = [
        lax.ppermute(x, axis, [(i, i ^ (step * start)) for i in range(size)])
        for step in range(1, radix)
    ]
    return [x] + others


def tree_sum(parts):
    while len(parts) > 1:
        parts = [parts[i] + parts[i + 1] for i in range(0, len(parts), 2)]
    return parts[0]


def sum_stages(x, axes, size):
    stages, start = [(1, 2)], 2
    while start < size:
        radix = min(4, size // start)
        stages.append((start, radix))
        start *= radix
    for start, radix in stages:
        x = tree_sum([x] + [
            lax.ppermute(x, axes, [
                (i, i ^ (step * start)) for i in range(size) if start == 1 or i % 2
            ])
            for step in range(1, radix)
        ])
    return x, lax.ppermute(x, axes, [(i, i - 1) for i in range(1, size, 2)])


def body(
    total_sites, states, gap_mask, weights, leaf_order, exchanges, codon_freq, omega_ratio,
    lengths, classes,
):
    sites = states.shape[1]
    members = lax.axis_size("branch")
    sense, single, nonsyn = codon_tables()
    vmem = pl.BlockSpec(memory_space=pltpu.VMEM)
    smem = pl.BlockSpec(memory_space=pltpu.SMEM)
    shape = jax.ShapeDtypeStruct
    held = pltpu.VMEM
    limit = pltpu.CompilerParams(vmem_limit_bytes=20 * 2**20)

    def outside(x):
        return pltpu.with_memory_space_constraint(x, pltpu.HBM)

    def inside(xs):
        return [pltpu.with_memory_space_constraint(x, pltpu.VMEM) for x in xs]

    sense2 = outside(jnp.asarray(np.tile(sense[None, :], (1, 2))))
    single2 = outside(jnp.asarray(np.tile(single, (1, 2))))
    nonsyn2 = outside(jnp.asarray(np.tile(nonsyn, (1, 2))))
    freq = outside(codon_freq.reshape(1, 64))
    span, owner = outside(lengths.reshape(1, EDGES)), outside(classes.reshape(1, EDGES))
    table, omega = outside(exchanges), outside(omega_ratio)

    top, *kept = pl.pallas_call(
        up_kernel,
        out_shape=[
            shape((64, sites), F32),
            held((4, 2, PAIRS, 64, 128), BF),
            held((PAIRS // 2, 64, 128), F32),
            held((CLASSES // 2, 4, 64, 128), F32),
            held((STRIDE * 64, 128), F32),
            held((7, 64, 128), F32),
            held((PAIRS, 128, sites), F32),
            held((64, 64, sites), BF),
            held((64, 64, sites), BF),
            held((32, 128, sites), BF),
            held((64, sites), F32),
            held((64, sites), F32),
        ],
        in_specs=[vmem, vmem, smem, vmem, vmem, smem] + [vmem] * 5,
        out_specs=[vmem] * 12,
        scratch_shapes=[
            pltpu.VMEM((STRIDE * 64, 128), F32),
            pltpu.VMEM((PAIRS, 64, 256), BF),
            pltpu.VMEM((PAIRS, 64, 128), BF),
        ],
        compiler_params=limit,
        name="up",
    )(
        outside(states), outside(gap_mask), outside(leaf_order),
        table, freq, omega, span, owner, sense2, single2, nonsyn2,
    )
    (
        chain, last, powers, dup, fixed, message, high, low, leaf, scale, inverse,
    ) = inside(kept)
    tops = partners(top, "branch", 1, members)
    slope, matrix, turned = inside(pl.pallas_call(
        side_kernel,
        out_shape=[
            held((STRIDE * 64, 128), F32),
            held((64, 64, 256), BF),
            held((128, 128), F32),
        ],
        in_specs=[vmem] * 5,
        out_specs=[vmem] * 3,
        compiler_params=limit,
        name="side",
    )(dup, last, span, owner, fixed))
    part = pl.pallas_call(
        functools.partial(down_kernel, total_sites, members),
        out_shape=shape((16, 128), F32),
        in_specs=[vmem] * (13 + members) + [smem, vmem, vmem],
        out_specs=vmem,
        scratch_shapes=[
            pltpu.VMEM((32, 128, sites), BF),
            pltpu.VMEM((32, 128, sites), BF),
            pltpu.VMEM((PAIRS, 64, 128), F32),
            pltpu.VMEM((STRIDE * 64, 128), F32),
            pltpu.VMEM((STRIDE * 64, 128), F32),
        ],
        compiler_params=limit,
        name="down",
    )(
        *tops, matrix, message, high, low, leaf, scale, inverse,
        chain, turned, slope, powers, fixed,
        outside(weights.reshape(1, sites)), omega, single2, nonsyn2,
    )
    parts = sum_stages(part, ("site", "branch"), members * lax.axis_size("site"))
    exch, ratio, length, loglik = pl.pallas_call(
        functools.partial(last_kernel, total_sites),
        out_shape=[shape((64, 64), F32), shape((1, CLASSES), F32), shape((1, EDGES), F32), shape((1, 1), F32)],
        in_specs=[vmem] * len(parts),
        out_specs=[vmem] * 4,
        compiler_params=limit,
        name="last",
    )(*parts)
    return (exch, ratio.reshape(CLASSES), length.reshape(EDGES), loglik.reshape(()))


def solution(mesh):
    def whole(states, *rest):
        total_sites = states.shape[1]
        return jax.shard_map(
            functools.partial(body, total_sites),
            mesh=mesh,
            in_specs=(
                P(None, "site"),
                P(None, "site"),
                P("site"),
                P(),
                P(),
                P(),
                P(),
                P("branch"),
                P("branch"),
            ),
            out_specs=(P(), P(), P("branch"), P()),
            check_vma=False,
        )(states, *rest)

    return whole
```

```python
import functools
import jax
import jax.numpy as jnp
import numpy as np
from jax import lax
from jax.experimental import pallas as pl
from jax.experimental.pallas import tpu as pltpu
from jax.sharding import PartitionSpec as P

LEAF_DEV = 64
EDGES = 127
PAIRS = 64
CLASSES = 8
ORDER = 8
STRIDE = 65
SPACED = 72
BF = jnp.bfloat16
F32 = jnp.float32

CODE_TABLE = "FFLLSSSSYYXXCCXWLLLLPPPPHHQQRRRRIIIMTTTTNNKKSSRRVVVVAAAADDEEGGGG"


def codon_tables():
    amino_acid = np.array(list(CODE_TABLE))
    codon_index = np.arange(64)
    digits = np.stack([codon_index // 16, codon_index // 4 % 4, codon_index % 4], 1)
    differ = (digits[:, None, :] != digits[None, :, :]).sum(-1)
    is_sense = amino_acid != "X"
    single = (differ == 1) & is_sense[:, None] & is_sense[None, :]
    nonsyn = single & (amino_acid[:, None] != amino_acid[None, :])
    return (is_sense.astype(np.float32), single.astype(np.float32), nonsyn.astype(np.float32))


def low_half():
    return lax.broadcasted_iota(jnp.int32, (64, 128), 1) < 64


def split(x):
    high = x.astype(BF)
    low = (x - high.astype(F32)).astype(BF)
    return high, low


def spread(x, scale=1.0):
    mask = low_half()
    low = jnp.where(mask, scale, 0.0).astype(x.dtype)
    high = jnp.where(mask, 0.0, scale).astype(x.dtype)
    return jnp.concatenate([x * low, x * high], axis=0)


def mxu(left, right):
    return jnp.dot(left, right, preferred_element_type=F32)


def mxu_nt(left, right):
    return lax.dot_general(left, right, (((1,), (1,)), ((), ())), preferred_element_type=F32)


def exact(left, right):
    return jnp.dot(left, right, preferred_element_type=F32, precision=lax.Precision.HIGHEST)


def exact_tn(left, right):
    return lax.dot_general(
        left, right, (((0,), (0,)), ((), ())), preferred_element_type=F32,
        precision=lax.Precision.HIGHEST,
    )


def pair_products(*terms):
    lefts, rights = [], []
    for left, right in terms:
        left_high, left_low = split(left)
        right_high, right_low = split(right)
        wide_high, wide_low = spread(right_high), spread(right_low)
        lefts += [left_high, left_high, left_low]
        rights += [wide_high, wide_low, wide_high]
    return mxu(jnp.concatenate(lefts, axis=1), jnp.concatenate(rights, axis=0))


def messages(matrix, high, low):
    return mxu(matrix, jnp.concatenate([high, low, high, low], axis=0))


def doubled(x):
    mask = low_half()
    swapped = pltpu.roll(x, 64, 1)
    return jnp.where(mask, x, swapped), jnp.where(mask, swapped, x)


def double(ref, p, x):
    for e, both in enumerate(doubled(x)):
        high, low = split(both)
        ref[2 * p + e] = jnp.concatenate([high, low], axis=1)


def side_by_side(ref, p, x):
    for e, both in enumerate(doubled(x)):
        rest = both - both.astype(BF).astype(F32)
        ref[2 * p + e] = jnp.where(low_half(), both, rest).astype(BF)


def identity_twice():
    row = lax.broadcasted_iota(jnp.int32, (64, 128), 0)
    lane = lax.broadcasted_iota(jnp.int32, (64, 128), 1)
    return (row == lane % 64).astype(F32)


def frequencies(freq_ref, sense_ref):
    twice = identity_twice()
    sense2 = sense_ref[...]
    freq2 = jnp.concatenate([freq_ref[...]] * 2, axis=1) * sense2
    total = 0.5 * jnp.sum(freq2, axis=1, keepdims=True)
    pi_row = freq2 / total
    pi_col = 0.5 * jnp.sum(twice * pi_row, axis=1, keepdims=True)
    sense_col = 0.5 * jnp.sum(twice * sense2, axis=1, keepdims=True)
    root_row = jnp.sqrt(jnp.where(sense2 > 0, pi_row, 1.0))
    root_col = jnp.sqrt(jnp.where(sense_col > 0, pi_col, 1.0))
    return twice, pi_row, pi_col, root_row, root_col


def symmetric_table(ex_ref, single_ref, twice):
    ex = ex_ref[...]
    both = ex + ex.T
    return 0.5 * jnp.concatenate([both, both], axis=1) * single_ref[...]


def class_pair(table, nonsyn, omega_ref, pair, twice, pi_row, pi_col):
    mask = low_half()
    omega = jnp.where(mask, omega_ref[2 * pair], omega_ref[2 * pair + 1])
    factor = 1.0 + nonsyn * (omega - 1.0)
    flux = table * factor
    off = flux * pi_row
    row0 = jnp.sum(jnp.where(mask, off, 0.0), axis=1, keepdims=True)
    row1 = jnp.sum(jnp.where(mask, 0.0, off), axis=1, keepdims=True)
    mean0 = jnp.sum(pi_col * row0, axis=0, keepdims=True)
    mean1 = jnp.sum(pi_col * row1, axis=0, keepdims=True)
    rows = jnp.where(mask, row0, row1)
    mean = jnp.where(mask, mean0, mean1)
    return factor, off, rows, mean


def neighbours():
    row = lax.broadcasted_iota(jnp.int32, (64, 128), 0)
    lane = lax.broadcasted_iota(jnp.int32, (64, 128), 1) % 64
    masks = [
        row % 16 == lane % 16,
        (row // 16 == lane // 16) & (row % 4 == lane % 4),
        row // 4 == lane // 4,
    ]
    codon = lax.broadcasted_iota(jnp.int32, (64, 16), 0)
    column = lax.broadcasted_iota(jnp.int32, (64, 16), 1)
    digits = [codon // 16, codon // 4 % 4, codon % 4]
    picks = [(column == 4 * p + digits[p]).astype(F32) for p in range(3)]
    return masks, picks


def coefficients(len_ref, cls_ref, slope):
    lane = lax.broadcasted_iota(jnp.int32, (PAIRS, EDGES), 1)
    row = lax.broadcasted_iota(jnp.int32, (PAIRS, EDGES), 0)
    lengths = len_ref[...] * 0.0625
    classes = cls_ref[...].astype(F32)
    place = lax.broadcasted_iota(jnp.int32, (PAIRS, 128), 1) % 64
    found = []
    for odd in range(2):
        here = lane == 2 * row + odd
        y = jnp.sum(jnp.where(here, lengths, 0.0), axis=1, keepdims=True)
        owner = jnp.sum(jnp.where(here, classes, 0.0), axis=1, keepdims=True)
        current = jnp.ones((PAIRS, 128), F32)
        series = jnp.zeros((PAIRS, 128), F32)
        for k in range(ORDER):
            following = current * y * (1.0 / (k + 1))
            series = jnp.where(place // CLASSES == k, current if slope else following, series)
            current = following
        found.append(jnp.where((place % CLASSES).astype(F32) == owner, series, 0.0))
    return found


def four_left(x):
    high, low = split(x)
    return jnp.concatenate([high, low], axis=1)


def four_right(x):
    high, low = split(x)
    return jnp.concatenate([high, low, high, low], axis=0)


def expand(coefs, dup_ref, store):
    high, low = split(coefs)
    left = jnp.concatenate(
        [jnp.concatenate([high, high], axis=1), jnp.concatenate([low, low], axis=1)], axis=0
    )
    for i in range(0, 64, 2):
        parts = [split(dup_ref[SPACED * (i + t) : SPACED * (i + t) + 64, :]) for t in range(2)]
        right = jnp.concatenate([
            jnp.concatenate([spread(parts[0][h]), spread(parts[1][h])], axis=1) for h in range(2)
        ], axis=0)
        both = mxu(left, right)
        both = both[0:64] + both[64:128]
        for t in range(2):
            store(i + t, both[:, 128 * t : 128 * t + 128])


def rows_of(i):
    return pl.ds(STRIDE * i, 64)


def up_kernel(
    states_ref, gap_ref, order_ref,
    ex_ref, freq_ref, omega_ref, len_ref, cls_ref, sense_ref, single_ref, nonsyn_ref,
    top_ref, chain_ref, last_ref, power_ref, dup_ref, fixed_ref,
    message_ref, high_ref, low_ref, leaf_ref, scale_ref, inverse_ref,
    first_ref, up_ref, thin_ref,
):
    subtree = lax.axis_index("branch")
    mask = low_half()
    twice, pi_row, pi_col, root_row, root_col = frequencies(freq_ref, sense_ref)
    table = symmetric_table(ex_ref, single_ref, twice)
    nonsyn = nonsyn_ref[...]
    for at, value in enumerate(
        (pi_row, pi_col, root_row, root_col, 1.0 / root_row, 1.0 / root_col, table)
    ):
        fixed_ref[at] = jnp.broadcast_to(value, (64, 128))

    sites = states_ref.shape[1]
    codon = lax.broadcasted_iota(jnp.int32, (64, sites), 0)
    for p in range(32):
        both = []
        for e in range(2):
            taxon = order_ref[subtree * LEAF_DEV + 2 * p + e]
            state = jnp.where(gap_ref[pl.ds(taxon, 1), :] > 0, -1, states_ref[pl.ds(taxon, 1), :])
            hit = (codon == state) | (state < 0)
            both.append(jnp.where(hit, 1.0, 0.0).astype(BF))
        leaf_ref[p] = jnp.concatenate(both, axis=0)

    powers = []
    for pair in range(CLASSES // 2):
        factor, off, rows, mean = class_pair(
            table, nonsyn, omega_ref, pair, twice, pi_row, pi_col
        )
        powers.append([(table * factor * root_col * root_row - twice * rows) / mean])
    for left, right in ((0, 0), (1, 0), (1, 1), (3, 0), (3, 1), (3, 2), (3, 3)):
        for pair in range(CLASSES // 2):
            powers[pair].append(pair_products((powers[pair][left], powers[pair][right])))
    for pair in range(CLASSES // 2):
        for k in range(ORDER):
            value = powers[pair][k]
            swapped = pltpu.roll(value, 64, 1)
            at = CLASSES * k + 2 * pair
            dup_ref[pl.ds(at, 64, stride=SPACED), :] = jnp.where(mask, value, swapped)
            dup_ref[pl.ds(at + 1, 64, stride=SPACED), :] = jnp.where(mask, swapped, value)
            if k < 4:
                power_ref[pair, k] = value

    even, odd = coefficients(len_ref, cls_ref, False)

    def store(i, value):
        first_ref[SPACED * i : SPACED * i + 64, :] = value

    expand(jnp.where(low_half(), even, odd), dup_ref, store)

    def squarings(leaves, step, carry):
        width = 16
        held = [first_ref[pl.ds(step * width + j, 64, stride=SPACED), :] for j in range(width)]
        zero = jnp.zeros((128, 128), BF)
        for level in range(4):
            for j in range(0, width, 2):
                highs, lows, products = [], [], []
                for t in range(2):
                    high, low = split(held[j + t])
                    chain_ref[level, 0, step * width + j + t] = high
                    chain_ref[level, 1, step * width + j + t] = low
                    wide = spread(high)
                    highs.append(high)
                    lows.append(spread(low))
                    products.append(mxu(
                        jnp.concatenate([high, low], axis=1), jnp.concatenate([wide, wide], axis=0)
                    ))
                rest = mxu(jnp.concatenate(highs, axis=1), jnp.concatenate([
                    jnp.concatenate([lows[0], zero], axis=1),
                    jnp.concatenate([zero, lows[1]], axis=1),
                ], axis=0))
                for t in range(2):
                    held[j + t] = (
                        2.0 * held[j + t] + products[t] + rest[:, 128 * t : 128 * t + 128]
                    )
        for j in range(width):
            p = step * width + j
            matrix = inverse_root_col * (held[j] + twice) * root_row
            if leaves:
                side_by_side(thin_ref, p, matrix)
            else:
                last_ref[p - 32] = held[j]
                double(up_ref, p - 32, matrix)
        return carry

    inverse_root_col = 1.0 / root_col
    lax.fori_loop(0, 2, functools.partial(squarings, True), 0)
    lax.fori_loop(2, 4, functools.partial(squarings, False), 0)

    def finish(p, message):
        message_ref[p] = jnp.concatenate(message, axis=0)
        raw = message[0] * message[1]
        scaling = jnp.sum(raw, axis=0, keepdims=True)
        inverse = 1.0 / scaling
        scale_ref[pl.ds(p, 1), :] = scaling
        inverse_ref[pl.ds(p, 1), :] = inverse
        high, low = split(raw * inverse)
        high_ref[p] = high
        low_ref[p] = low

    for p in range(32):
        both = [leaf_ref[p, 64 * e : 64 * e + 64, :] for e in range(2)]
        finish(p, [
            mxu(thin_ref[2 * p + e], jnp.concatenate([both[e], both[e]], axis=0)) for e in range(2)
        ])

    def inner(p):
        child = 2 * p - 64
        return [
            messages(up_ref[child + e], high_ref[child + e], low_ref[child + e]) for e in range(2)
        ]

    for p in range(32, 48):
        finish(p, inner(p))
    for p in range(48, 63):
        finish(p, inner(p))
    high_ref[63] = jnp.zeros((64, sites), BF)
    low_ref[63] = jnp.zeros((64, sites), BF)
    scale_ref[63:64, :] = jnp.ones((1, sites), F32)
    inverse_ref[63:64, :] = jnp.ones((1, sites), F32)
    top = inner(63)
    message_ref[63] = jnp.concatenate(top, axis=0)
    top_ref[...] = top[0]


def side_kernel(
    dup_ref, last_ref, len_ref, cls_ref, fixed_ref, slope_ref, matrix_ref, turned_ref,
):
    twice = identity_twice()
    even, odd = coefficients(len_ref, cls_ref, True)

    def store(i, value):
        slope_ref[64 * i : 64 * i + 64, :] = value

    expand(jnp.where(low_half(), even, odd), dup_ref, store)
    even, odd = coefficients(len_ref, cls_ref, False)
    turned_ref[...] = exact_tn(jnp.where(low_half(), even, odd), twice)
    root_col, inverse_root_row = fixed_ref[3], fixed_ref[4]

    def matrices(step, carry):
        for j in range(8):
            r = step * 8 + j
            double(matrix_ref, r, root_col * (last_ref[r] + twice) * inverse_root_row)
        return carry

    lax.fori_loop(0, 4, matrices, 0)


def down_kernel(total_sites, members, *refs):
    tops = refs[:members]
    (
        matrix_ref, message_ref, high_ref, low_ref, leaf_ref, scale_ref, inverse_ref,
        chain_ref, turned_ref, slope_ref, power_ref, fixed_ref,
        weights_ref, omega_ref, single_ref, nonsyn_ref,
        out_ref,
        a_high_ref, a_low_ref, count_ref, back_ref, bins_ref,
    ) = refs[members:]
    subtree = lax.axis_index("branch")
    mask = low_half()
    twice = identity_twice()
    pi_row, pi_col, root_row, root_col, inverse_root_row, inverse_root_col = [
        fixed_ref[at] for at in range(6)
    ]
    sites = weights_ref.shape[1]
    weight = weights_ref[...].astype(F32)

    above = jnp.broadcast_to(pi_col[:, 0:1], (64, sites))
    for other in tops[1:]:
        above = above * other[...]
    own = tops[0][...]
    likelihood = jnp.sum(above * own, axis=0, keepdims=True)
    logs = jnp.sum(jnp.log(scale_ref[...]), axis=0, keepdims=True)
    logs = logs + jnp.where(subtree == 0, jnp.log(likelihood), 0.0)
    log_part = jnp.sum(weight * logs, axis=1, keepdims=True)
    high, low = split(above * (weight / (likelihood * total_sites)))
    a_high_ref[31, 0:64, :] = high
    a_low_ref[31, 0:64, :] = low
    a_high_ref[31, 64:128, :] = jnp.zeros((64, sites), BF)
    a_low_ref[31, 64:128, :] = jnp.zeros((64, sites), BF)

    def store_counts(p, square):
        counts = jnp.where(mask, square[0:64], square[64:128])
        count_ref[p] = inverse_root_col * counts * root_row

    def descend(r):
        a_high, a_low = a_high_ref[r - 32], a_low_ref[r - 32]
        child = 2 * r - 64
        u_high = jnp.concatenate([high_ref[child], high_ref[child + 1]], axis=0)
        u_low = jnp.concatenate([low_ref[child], low_ref[child + 1]], axis=0)
        first = mxu_nt(jnp.concatenate([a_high, a_low], axis=0), u_high)
        second = mxu_nt(a_high, u_low)
        store_counts(r, first[0:128] + first[128:256] + second)
        return [
            messages(
                matrix_ref[2 * (r - 32) + e], a_high[64 * e : 64 * e + 64], a_low[64 * e : 64 * e + 64]
            )
            for e in range(2)
        ]

    def children(down, e, p):
        vector = down[e]
        inverse = inverse_ref[pl.ds(p, 1), :]
        message = message_ref[p]
        pair = jnp.concatenate(
            [vector * message[64:128] * inverse, vector * message[0:64] * inverse], axis=0
        )
        return split(pair)

    def inner(r):
        down = descend(r)
        for e in range(2):
            p = 2 * r + e - 64
            if isinstance(p, int) and p == 63:
                continue
            high, low = children(down, e, p)
            a_high_ref[p - 32] = high
            a_low_ref[p - 32] = low

    for r in range(63, 47, -1):
        inner(r)

    for r in range(47, 31, -1):
        down = descend(r)
        for e in range(2):
            p = 2 * r + e - 64
            high, low = children(down, e, p)
            square = mxu_nt(jnp.concatenate([high, low], axis=0), leaf_ref[p])
            store_counts(p, square[0:128] + square[128:256])

    def adjoint(step, carry):
        held = [count_ref[step * 16 + j] for j in range(16)]
        for level in range(3, -1, -1):
            for j in range(16):
                high, low = split(held[j])
                e_high, e_low = chain_ref[level, 0, step * 16 + j], chain_ref[level, 1, step * 16 + j]
                left = jnp.concatenate([
                    jnp.concatenate([high, e_high], axis=1),
                    jnp.concatenate([low, e_low], axis=1),
                ], axis=0)
                right = jnp.concatenate([
                    jnp.concatenate([spread(e_high), spread(e_low)], axis=1),
                    jnp.concatenate([spread(high), spread(low)], axis=1),
                ], axis=0)
                four = mxu(left, right)
                held[j] = 2.0 * held[j] + (
                    four[0:64, 0:128] + four[0:64, 128:256] + four[64:128, 0:128]
                )
        for j in range(16):
            back_ref[pl.ds(step * 16 + j, 64, stride=STRIDE), :] = held[j]
        return carry

    lax.fori_loop(0, PAIRS // 16, adjoint, 0)

    left = four_left(turned_ref[...])

    total = jnp.zeros((64, 128), F32)
    for i in range(0, 64, 2):
        values = [back_ref[rows_of(i + t), :] for t in range(2)]
        both = mxu(left, four_right(jnp.concatenate(values, axis=1)))
        for t in range(2):
            total = total + values[t] * slope_ref[64 * (i + t) : 64 * (i + t) + 64, :]
            here = both[:, 128 * t : 128 * t + 128]
            bins_ref[rows_of(i + t), :] = jnp.where(mask, here[0:64], here[64:128])
    slopes = total * 0.0625

    table, nonsyn = fixed_ref[6], nonsyn_ref[...]
    row = lax.broadcasted_iota(jnp.int32, (64, 128), 0)
    lane = lax.broadcasted_iota(jnp.int32, (64, 128), 1)
    table_grad = jnp.zeros((64, 128), F32)
    omega_row = jnp.zeros((1, 128), F32)
    lane_row = lax.broadcasted_iota(jnp.int32, (1, 128), 1)
    for pair in range(CLASSES // 2):
        grads = []
        for k in range(ORDER):
            at = CLASSES * k + 2 * pair
            first = bins_ref[pl.ds(at, 64, stride=STRIDE), :]
            second = bins_ref[pl.ds(at + 1, 64, stride=STRIDE), :]
            first = first + pltpu.roll(first, 64, 1)
            second = second + pltpu.roll(second, 64, 1)
            grads.append(jnp.where(mask, first, second))
        g1, g2, g3, g4, g5, g6, g7, g8 = grads
        a1, a2, a3, a4 = [power_ref[pair, k] for k in range(4)]
        g4 = g4 + pair_products((g8, a4), (a4, g8), (g7, a3), (g6, a2), (g5, a1))
        g3 = g3 + pair_products((a4, g7))
        g2 = g2 + pair_products((a4, g6))
        g1 = g1 + pair_products((a4, g5))
        g2 = g2 + pair_products((g4, a2), (a2, g4), (g3, a1))
        g1 = g1 + pair_products((a2, g3))
        g1 = g1 + pair_products((g2, a1), (a1, g2))
        factor, off, rows, mean = class_pair(
            table, nonsyn, omega_ref, pair, twice, pi_row, pi_col
        )
        d_rate = root_col * g1 * inverse_root_row
        rate = (off - twice * rows) / mean
        weighted = d_rate * rate
        diagonal = d_rate * twice
        total0 = jnp.sum(jnp.where(mask, weighted, 0.0), axis=1, keepdims=True)
        total1 = jnp.sum(jnp.where(mask, 0.0, weighted), axis=1, keepdims=True)
        total0 = jnp.sum(total0, axis=0, keepdims=True)
        total1 = jnp.sum(total1, axis=0, keepdims=True)
        diag0 = jnp.sum(jnp.where(mask, diagonal, 0.0), axis=1, keepdims=True)
        diag1 = jnp.sum(jnp.where(mask, 0.0, diagonal), axis=1, keepdims=True)
        row_grad = jnp.where(mask, diag0 + pi_col * total0, diag1 + pi_col * total1)
        flux_grad = (d_rate - row_grad) * pi_row / mean
        table_grad = table_grad + flux_grad * factor * single_ref[...]
        ratio = flux_grad * table * nonsyn
        ratio0 = jnp.sum(jnp.where(mask, ratio, 0.0), axis=1, keepdims=True)
        ratio1 = jnp.sum(jnp.where(mask, 0.0, ratio), axis=1, keepdims=True)
        ratio0 = jnp.sum(ratio0, axis=0, keepdims=True)
        ratio1 = jnp.sum(ratio1, axis=0, keepdims=True)
        omega_row = jnp.where(lane_row == 2 * pair, ratio0, omega_row)
        omega_row = jnp.where(lane_row == 2 * pair + 1, ratio1, omega_row)
    table_grad = table_grad + pltpu.roll(table_grad, 64, 1)
    masks, picks = neighbours()
    codon = lax.broadcasted_iota(jnp.int32, (16, 128), 1)
    column = lax.broadcasted_iota(jnp.int32, (16, 128), 0)
    lefts, rights = [], []
    for p, digit in enumerate((codon // 16, codon // 4 % 4, codon % 4)):
        left = jnp.where((column == 4 * p + digit) & (codon < 64), 1.0, 0.0).astype(BF)
        for part in split(jnp.where(masks[p], 0.5 * table_grad, 0.0)):
            lefts.append(left)
            rights.append(part)
    packed = mxu(
        jnp.concatenate(lefts, axis=1),
        jnp.concatenate([jnp.concatenate([part, jnp.zeros_like(part)], axis=0) for part in rights], axis=0),
    )
    turned = mxu_nt(
        jnp.concatenate(lefts, axis=1),
        jnp.concatenate([
            jnp.concatenate([part, jnp.zeros_like(part)], axis=0) for part in rights
        ], axis=1),
    )
    packed = packed + turned
    packed = jnp.where(lax.broadcasted_iota(jnp.int32, (16, 128), 1) < 64, packed, 0.0)

    even = jnp.sum(jnp.where(mask, slopes, 0.0), axis=1, keepdims=True)
    other = jnp.sum(jnp.where(mask, 0.0, slopes), axis=1, keepdims=True)
    placed = jnp.where(lane == 2 * row, even, 0.0) + jnp.where(lane == 2 * row + 1, other, 0.0)
    length_row = jnp.sum(placed, axis=0, keepdims=True)
    line = lax.broadcasted_iota(jnp.int32, out_ref.shape, 0)
    omega_row = jnp.where(lane_row == CLASSES, log_part, omega_row)
    omega_row = pltpu.roll(jnp.broadcast_to(omega_row, (8, 128)), 64, 1)[0:1]
    packed = packed + jnp.where(line == 0, omega_row, 0.0)
    out_ref[...] = packed + jnp.where(line == 12 + subtree, length_row, 0.0)


def last_kernel(total_sites, count, *refs):
    members = lax.axis_size("branch")
    subtree = lax.axis_index("branch")
    exch_ref, omega_ref, length_ref, log_ref = refs[count:]
    total = tree_sum([ref[...] for ref in refs[:count]])
    masks, picks = neighbours()
    table = jnp.zeros((64, 128), F32)
    for at_position, pick in zip(masks, picks):
        table = table + jnp.where(at_position, exact(pick, total), 0.0)
    exch_ref[...] = table[:, 0:64]
    moved = pltpu.roll(total[0:8], 64, 1)
    omega_ref[...] = moved[0:1, 0:CLASSES]
    line = lax.broadcasted_iota(jnp.int32, total.shape, 0)
    lengths = jnp.sum(jnp.where(line == 12 + subtree, total, 0.0), axis=0, keepdims=True)
    length_ref[...] = lengths[:, 0:EDGES]
    log_ref[...] = moved[0:1, CLASSES : CLASSES + 1] / total_sites / (LEAF_DEV * members)


def partners(x, axis, start, radix):
    size = lax.axis_size(axis)
    others = [
        lax.ppermute(x, axis, [(i, i ^ (step * start)) for i in range(size)])
        for step in range(1, radix)
    ]
    return [x] + others


def tree_sum(parts):
    while len(parts) > 1:
        parts = [parts[i] + parts[i + 1] for i in range(0, len(parts), 2)]
    return parts[0]


def sum_stages(x, members, sites):
    stages, start = [], 1
    while start < sites:
        radix = 2 if sites // start in (2, 8) else 4
        stages.append((members * start, radix, 1))
        start *= radix
    stages.append((1, members, 0))
    parts = [x]
    for start, radix, flip in stages[::-1]:
        x = tree_sum(parts)
        parts = [x] + [
            lax.ppermute(x, ("site", "branch"), [
                (i, i ^ (step * start + flip)) for i in range(sites * members)
            ])
            for step in range(1, radix)
        ]
    return parts


def body(
    total_sites, states, gap_mask, weights, leaf_order, exchanges, codon_freq, omega_ratio,
    lengths, classes,
):
    sites = states.shape[1]
    members = lax.axis_size("branch")
    sense, single, nonsyn = codon_tables()
    vmem = pl.BlockSpec(memory_space=pltpu.VMEM)
    smem = pl.BlockSpec(memory_space=pltpu.SMEM)
    shape = jax.ShapeDtypeStruct
    held = pltpu.VMEM
    limit = pltpu.CompilerParams(vmem_limit_bytes=20 * 2**20)

    def outside(x):
        return pltpu.with_memory_space_constraint(x, pltpu.HBM)

    def inside(xs):
        return [pltpu.with_memory_space_constraint(x, pltpu.VMEM) for x in xs]

    sense2 = outside(jnp.asarray(np.tile(sense[None, :], (1, 2))))
    single2 = outside(jnp.asarray(np.tile(single, (1, 2))))
    nonsyn2 = outside(jnp.asarray(np.tile(nonsyn, (1, 2))))
    freq = outside(codon_freq.reshape(1, 64))
    span, owner = outside(lengths.reshape(1, EDGES)), outside(classes.reshape(1, EDGES))
    table, omega = outside(exchanges), outside(omega_ratio)

    top, *kept = pl.pallas_call(
        up_kernel,
        out_shape=[
            shape((64, sites), F32),
            held((4, 2, PAIRS, 64, 128), BF),
            held((PAIRS // 2, 64, 128), F32),
            held((CLASSES // 2, 4, 64, 128), F32),
            held((SPACED * 64, 128), F32),
            held((7, 64, 128), F32),
            held((PAIRS, 128, sites), F32),
            held((64, 64, sites), BF),
            held((64, 64, sites), BF),
            held((32, 128, sites), BF),
            held((64, sites), F32),
            held((64, sites), F32),
        ],
        in_specs=[vmem, vmem, smem, vmem, vmem, smem] + [vmem] * 5,
        out_specs=[vmem] * 12,
        scratch_shapes=[
            pltpu.VMEM((SPACED * 64, 128), F32),
            pltpu.VMEM((PAIRS, 64, 256), BF),
            pltpu.VMEM((PAIRS, 64, 128), BF),
        ],
        compiler_params=limit,
        name="up",
    )(
        outside(states), outside(gap_mask), outside(leaf_order),
        table, freq, omega, span, owner, sense2, single2, nonsyn2,
    )
    (
        chain, last, powers, dup, fixed, message, high, low, leaf, scale, inverse,
    ) = inside(kept)
    tops = partners(top, "branch", 1, members)
    slope, matrix, turned = inside(pl.pallas_call(
        side_kernel,
        out_shape=[
            held((PAIRS * 64, 128), F32),
            held((64, 64, 256), BF),
            held((128, 128), F32),
        ],
        in_specs=[vmem] * 5,
        out_specs=[vmem] * 3,
        compiler_params=limit,
        name="side",
    )(dup, last, span, owner, fixed))
    part = pl.pallas_call(
        functools.partial(down_kernel, total_sites, members),
        out_shape=shape((16, 128), F32),
        in_specs=[vmem] * (13 + members) + [smem, vmem, vmem],
        out_specs=vmem,
        scratch_shapes=[
            pltpu.VMEM((32, 128, sites), BF),
            pltpu.VMEM((32, 128, sites), BF),
            pltpu.VMEM((PAIRS, 64, 128), F32),
            pltpu.VMEM((STRIDE * 64, 128), F32),
            pltpu.VMEM((STRIDE * 64, 128), F32),
        ],
        compiler_params=limit,
        name="down",
    )(
        *tops, matrix, message, high, low, leaf, scale, inverse,
        chain, turned, slope, powers, fixed,
        outside(weights.reshape(1, sites)), omega, single2, nonsyn2,
    )
    parts = sum_stages(part, members, lax.axis_size("site"))
    exch, ratio, length, loglik = pl.pallas_call(
        functools.partial(last_kernel, total_sites, len(parts)),
        out_shape=[shape((64, 64), F32), shape((1, CLASSES), F32), shape((1, EDGES), F32), shape((1, 1), F32)],
        in_specs=[vmem] * len(parts),
        out_specs=[vmem] * 4,
        compiler_params=limit,
        name="last",
    )(*parts)
    return (exch, ratio.reshape(CLASSES), length.reshape(EDGES), loglik.reshape(()))


def solution(mesh):
    def whole(states, *rest):
        total_sites = states.shape[1]
        return jax.shard_map(
            functools.partial(body, total_sites),
            mesh=mesh,
            in_specs=(
                P(None, "site"),
                P(None, "site"),
                P("site"),
                P(),
                P(),
                P(),
                P(),
                P("branch"),
                P("branch"),
            ),
            out_specs=(P(), P(), P("branch"), P()),
            check_vma=False,
        )(states, *rest)

    return whole
```

```python
import functools
import jax
import jax.numpy as jnp
import numpy as np
from jax import lax
from jax.experimental import pallas as pl
from jax.experimental.pallas import tpu as pltpu
from jax.sharding import PartitionSpec as P

LEAF_DEV = 64
EDGES = 127
PAIRS = 64
CLASSES = 8
ORDER = 8
STRIDE = 65
BF = jnp.bfloat16
F32 = jnp.float32

CODE_TABLE = "FFLLSSSSYYXXCCXWLLLLPPPPHHQQRRRRIIIMTTTTNNKKSSRRVVVVAAAADDEEGGGG"


def codon_tables():
    amino_acid = np.array(list(CODE_TABLE))
    codon_index = np.arange(64)
    digits = np.stack([codon_index // 16, codon_index // 4 % 4, codon_index % 4], 1)
    differ = (digits[:, None, :] != digits[None, :, :]).sum(-1)
    is_sense = amino_acid != "X"
    single = (differ == 1) & is_sense[:, None] & is_sense[None, :]
    nonsyn = single & (amino_acid[:, None] != amino_acid[None, :])
    return (is_sense.astype(np.float32), single.astype(np.float32), nonsyn.astype(np.float32))


def low_half():
    return lax.broadcasted_iota(jnp.int32, (64, 128), 1) < 64


def split(x):
    high = x.astype(BF)
    low = (x - high.astype(F32)).astype(BF)
    return high, low


def spread(x, scale=1.0):
    mask = low_half()
    low = jnp.where(mask, scale, 0.0).astype(x.dtype)
    high = jnp.where(mask, 0.0, scale).astype(x.dtype)
    return jnp.concatenate([x * low, x * high], axis=0)


def mxu(left, right):
    return jnp.dot(left, right, preferred_element_type=F32)


def mxu_nt(left, right):
    return lax.dot_general(left, right, (((1,), (1,)), ((), ())), preferred_element_type=F32)


def exact(left, right):
    return jnp.dot(left, right, preferred_element_type=F32, precision=lax.Precision.HIGHEST)


def exact_tn(left, right):
    return lax.dot_general(
        left, right, (((0,), (0,)), ((), ())), preferred_element_type=F32,
        precision=lax.Precision.HIGHEST,
    )


def pair_products(*terms):
    lefts, rights = [], []
    for left, right in terms:
        left_high, left_low = split(left)
        right_high, right_low = split(right)
        wide_high, wide_low = spread(right_high), spread(right_low)
        lefts += [left_high, left_high, left_low]
        rights += [wide_high, wide_low, wide_high]
    return mxu(jnp.concatenate(lefts, axis=1), jnp.concatenate(rights, axis=0))


def messages(matrix, high, low):
    return mxu(matrix, jnp.concatenate([high, low, high, low], axis=0))


def leaf_messages(thin_ref, leaf_ref, p):
    found = []
    for e in range(2):
        vector = leaf_ref[p, 64 * e : 64 * e + 64, :]
        found.append(mxu(thin_ref[2 * p + e], jnp.concatenate([vector, vector], axis=0)))
    return found


def doubled(x):
    mask = low_half()
    swapped = pltpu.roll(x, 64, 1)
    return jnp.where(mask, x, swapped), jnp.where(mask, swapped, x)


def double(ref, p, x):
    for e, both in enumerate(doubled(x)):
        high, low = split(both)
        ref[2 * p + e] = jnp.concatenate([high, low], axis=1)


def side_by_side(ref, p, x):
    for e, both in enumerate(doubled(x)):
        rest = both - both.astype(BF).astype(F32)
        ref[2 * p + e] = jnp.where(low_half(), both, rest).astype(BF)


def identity_twice():
    row = lax.broadcasted_iota(jnp.int32, (64, 128), 0)
    lane = lax.broadcasted_iota(jnp.int32, (64, 128), 1)
    return (row == lane % 64).astype(F32)


def frequencies(freq_ref, sense_ref):
    twice = identity_twice()
    sense2 = sense_ref[...]
    freq2 = jnp.concatenate([freq_ref[...]] * 2, axis=1) * sense2
    total = 0.5 * jnp.sum(freq2, axis=1, keepdims=True)
    pi_row = freq2 / total
    pi_col = 0.5 * jnp.sum(twice * pi_row, axis=1, keepdims=True)
    sense_col = 0.5 * jnp.sum(twice * sense2, axis=1, keepdims=True)
    root_row = jnp.sqrt(jnp.where(sense2 > 0, pi_row, 1.0))
    root_col = jnp.sqrt(jnp.where(sense_col > 0, pi_col, 1.0))
    return twice, pi_row, pi_col, root_row, root_col


def symmetric_table(ex_ref, single_ref, twice):
    ex = ex_ref[...]
    both = ex + ex.T
    return 0.5 * jnp.concatenate([both, both], axis=1) * single_ref[...]


def class_pair(table, nonsyn, omega_ref, pair, twice, pi_row, pi_col):
    mask = low_half()
    omega = jnp.where(mask, omega_ref[2 * pair], omega_ref[2 * pair + 1])
    factor = 1.0 + nonsyn * (omega - 1.0)
    flux = table * factor
    off = flux * pi_row
    row0 = jnp.sum(jnp.where(mask, off, 0.0), axis=1, keepdims=True)
    row1 = jnp.sum(jnp.where(mask, 0.0, off), axis=1, keepdims=True)
    mean0 = jnp.sum(pi_col * row0, axis=0, keepdims=True)
    mean1 = jnp.sum(pi_col * row1, axis=0, keepdims=True)
    rows = jnp.where(mask, row0, row1)
    mean = jnp.where(mask, mean0, mean1)
    return factor, off, rows, mean


def neighbours():
    row = lax.broadcasted_iota(jnp.int32, (64, 128), 0)
    lane = lax.broadcasted_iota(jnp.int32, (64, 128), 1) % 64
    masks = [
        row % 16 == lane % 16,
        (row // 16 == lane // 16) & (row % 4 == lane % 4),
        row // 4 == lane // 4,
    ]
    codon = lax.broadcasted_iota(jnp.int32, (64, 16), 0)
    column = lax.broadcasted_iota(jnp.int32, (64, 16), 1)
    digits = [codon // 16, codon // 4 % 4, codon % 4]
    picks = [(column == 4 * p + digits[p]).astype(F32) for p in range(3)]
    return masks, picks


def coefficients(len_ref, cls_ref, slope):
    lane = lax.broadcasted_iota(jnp.int32, (PAIRS, EDGES), 1)
    row = lax.broadcasted_iota(jnp.int32, (PAIRS, EDGES), 0)
    lengths = len_ref[...] * 0.0625
    classes = cls_ref[...].astype(F32)
    place = lax.broadcasted_iota(jnp.int32, (PAIRS, 128), 1) % 64
    found = []
    for odd in range(2):
        here = lane == 2 * row + odd
        y = jnp.sum(jnp.where(here, lengths, 0.0), axis=1, keepdims=True)
        owner = jnp.sum(jnp.where(here, classes, 0.0), axis=1, keepdims=True)
        current = jnp.ones((PAIRS, 128), F32)
        series = jnp.zeros((PAIRS, 128), F32)
        for k in range(ORDER):
            following = current * y * (1.0 / (k + 1))
            series = jnp.where(place // CLASSES == k, current if slope else following, series)
            current = following
        found.append(jnp.where((place % CLASSES).astype(F32) == owner, series, 0.0))
    return found


def four_left(x):
    high, low = split(x)
    return jnp.concatenate([high, low], axis=1)


def four_right(x):
    high, low = split(x)
    return jnp.concatenate([high, low, high, low], axis=0)


def expand(coefs, dup_ref, store):
    high, low = split(coefs)
    left = jnp.concatenate(
        [jnp.concatenate([high, high], axis=1), jnp.concatenate([low, low], axis=1)], axis=0
    )
    for i in range(0, 64, 2):
        parts = [split(dup_ref[rows_of(i + t), :]) for t in range(2)]
        right = jnp.concatenate([
            jnp.concatenate([spread(parts[0][h]), spread(parts[1][h])], axis=1) for h in range(2)
        ], axis=0)
        both = mxu(left, right)
        both = both[0:64] + both[64:128]
        for t in range(2):
            store(i + t, both[:, 128 * t : 128 * t + 128])


def rows_of(i):
    return pl.ds(STRIDE * i, 64)


def up_kernel(
    states_ref, gap_ref, order_ref,
    ex_ref, freq_ref, omega_ref, len_ref, cls_ref, sense_ref, single_ref, nonsyn_ref,
    top_ref, chain_ref, last_ref, power_ref, dup_ref, fixed_ref,
    message_ref, high_ref, low_ref, leaf_ref, scale_ref, inverse_ref, thin_ref,
    first_ref, up_ref,
):
    subtree = lax.axis_index("branch")
    mask = low_half()
    twice, pi_row, pi_col, root_row, root_col = frequencies(freq_ref, sense_ref)
    table = symmetric_table(ex_ref, single_ref, twice)
    nonsyn = nonsyn_ref[...]
    for at, value in enumerate(
        (pi_row, pi_col, root_row, root_col, 1.0 / root_row, 1.0 / root_col, table)
    ):
        fixed_ref[at] = jnp.broadcast_to(value, (64, 128))

    sites = states_ref.shape[1]
    codon = lax.broadcasted_iota(jnp.int32, (64, sites), 0)
    for p in range(32):
        both = []
        for e in range(2):
            taxon = order_ref[subtree * LEAF_DEV + 2 * p + e]
            state = jnp.where(gap_ref[pl.ds(taxon, 1), :] > 0, -1, states_ref[pl.ds(taxon, 1), :])
            hit = (codon == state) | (state < 0)
            both.append(jnp.where(hit, 1.0, 0.0).astype(BF))
        leaf_ref[p] = jnp.concatenate(both, axis=0)

    powers = []
    for pair in range(CLASSES // 2):
        factor, off, rows, mean = class_pair(
            table, nonsyn, omega_ref, pair, twice, pi_row, pi_col
        )
        powers.append([(table * factor * root_col * root_row - twice * rows) / mean])
    for left, right in ((0, 0), (1, 0), (1, 1), (3, 0), (3, 1), (3, 2), (3, 3)):
        for pair in range(CLASSES // 2):
            powers[pair].append(pair_products((powers[pair][left], powers[pair][right])))
    for pair in range(CLASSES // 2):
        for k in range(ORDER):
            value = powers[pair][k]
            swapped = pltpu.roll(value, 64, 1)
            at = CLASSES * k + 2 * pair
            dup_ref[pl.ds(at, 64, stride=STRIDE), :] = jnp.where(mask, value, swapped)
            dup_ref[pl.ds(at + 1, 64, stride=STRIDE), :] = jnp.where(mask, swapped, value)
            if k < 4:
                power_ref[pair, k] = value

    even, odd = coefficients(len_ref, cls_ref, False)

    def store(i, value):
        first_ref[rows_of(i), :] = value

    expand(jnp.where(low_half(), even, odd), dup_ref, store)

    def squarings(leaves, step, carry):
        width = 16
        held = [first_ref[pl.ds(step * width + j, 64, stride=STRIDE), :] for j in range(width)]
        for level in range(4):
            for j in range(width):
                high, low = split(held[j])
                chain_ref[level, 0, step * width + j] = high
                chain_ref[level, 1, step * width + j] = low
                wide_high, wide_low = spread(high), spread(low)
                held[j] = 2.0 * held[j] + mxu(
                    jnp.concatenate([high, high, low], axis=1),
                    jnp.concatenate([wide_high, wide_low, wide_high], axis=0),
                )
        for j in range(width):
            p = step * width + j
            matrix = inverse_root_col * (held[j] + twice) * root_row
            if leaves:
                side_by_side(thin_ref, p, matrix)
            else:
                last_ref[p - 32] = held[j]
                double(up_ref, p - 32, matrix)
        return carry

    inverse_root_col = 1.0 / root_col
    lax.fori_loop(0, 2, functools.partial(squarings, True), 0)
    lax.fori_loop(2, 4, functools.partial(squarings, False), 0)

    def finish(p, message):
        if p >= 32:
            message_ref[p - 32] = jnp.concatenate(message, axis=0)
        raw = message[0] * message[1]
        scaling = jnp.sum(raw, axis=0, keepdims=True)
        inverse = 1.0 / scaling
        scale_ref[pl.ds(p, 1), :] = scaling
        inverse_ref[pl.ds(p, 1), :] = inverse
        high, low = split(raw * inverse)
        high_ref[p] = high
        low_ref[p] = low

    for p in range(32):
        finish(p, leaf_messages(thin_ref, leaf_ref, p))

    def inner(p):
        child = 2 * p - 64
        return [
            messages(up_ref[child + e], high_ref[child + e], low_ref[child + e]) for e in range(2)
        ]

    for p in range(32, 48):
        finish(p, inner(p))
    for p in range(48, 63):
        finish(p, inner(p))
    high_ref[63] = jnp.zeros((64, sites), BF)
    low_ref[63] = jnp.zeros((64, sites), BF)
    scale_ref[63:64, :] = jnp.ones((1, sites), F32)
    inverse_ref[63:64, :] = jnp.ones((1, sites), F32)
    top = inner(63)
    top_ref[...] = top[0]


def side_kernel(
    dup_ref, last_ref, len_ref, cls_ref, fixed_ref, thin_ref, leaf_ref,
    slope_ref, matrix_ref, turned_ref, given_ref,
):
    twice = identity_twice()
    even, odd = coefficients(len_ref, cls_ref, True)

    def store(i, value):
        slope_ref[64 * i : 64 * i + 64, :] = value

    expand(jnp.where(low_half(), even, odd), dup_ref, store)
    even, odd = coefficients(len_ref, cls_ref, False)
    turned_ref[...] = exact_tn(jnp.where(low_half(), even, odd), twice)
    root_col, inverse_root_row = fixed_ref[3], fixed_ref[4]

    def matrices(step, carry):
        for j in range(8):
            r = step * 8 + j
            double(matrix_ref, r, root_col * (last_ref[r] + twice) * inverse_root_row)
        return carry

    lax.fori_loop(0, 4, matrices, 0)
    for p in range(32):
        given_ref[p] = jnp.concatenate(leaf_messages(thin_ref, leaf_ref, p), axis=0)


def down_kernel(total_sites, members, *refs):
    tops = refs[:members]
    (
        matrix_ref, given_ref, message_ref, high_ref, low_ref, leaf_ref, scale_ref, inverse_ref,
        chain_ref, turned_ref, slope_ref, power_ref, fixed_ref,
        weights_ref, omega_ref, single_ref, nonsyn_ref,
        out_ref,
        a_high_ref, a_low_ref, count_ref, back_ref, bins_ref,
    ) = refs[members:]
    subtree = lax.axis_index("branch")
    mask = low_half()
    twice = identity_twice()
    pi_row, pi_col, root_row, root_col, inverse_root_row, inverse_root_col = [
        fixed_ref[at] for at in range(6)
    ]
    sites = weights_ref.shape[1]
    weight = weights_ref[...].astype(F32)

    above = jnp.broadcast_to(pi_col[:, 0:1], (64, sites))
    for other in tops[1:]:
        above = above * other[...]
    own = tops[0][...]
    likelihood = jnp.sum(above * own, axis=0, keepdims=True)
    logs = jnp.sum(jnp.log(scale_ref[...]), axis=0, keepdims=True)
    logs = logs + jnp.where(subtree == 0, jnp.log(likelihood), 0.0)
    log_part = jnp.sum(weight * logs, axis=1, keepdims=True)
    high, low = split(above * (weight / (likelihood * total_sites)))
    a_high_ref[31, 0:64, :] = high
    a_low_ref[31, 0:64, :] = low
    a_high_ref[31, 64:128, :] = jnp.zeros((64, sites), BF)
    a_low_ref[31, 64:128, :] = jnp.zeros((64, sites), BF)

    def store_counts(p, square):
        counts = jnp.where(mask, square[0:64], square[64:128])
        count_ref[p] = inverse_root_col * counts * root_row

    def descend(r):
        a_high, a_low = a_high_ref[r - 32], a_low_ref[r - 32]
        child = 2 * r - 64
        u_high = jnp.concatenate([high_ref[child], high_ref[child + 1]], axis=0)
        u_low = jnp.concatenate([low_ref[child], low_ref[child + 1]], axis=0)
        first = mxu_nt(jnp.concatenate([a_high, a_low], axis=0), u_high)
        second = mxu_nt(a_high, u_low)
        store_counts(r, first[0:128] + first[128:256] + second)
        return [
            messages(
                matrix_ref[2 * (r - 32) + e], a_high[64 * e : 64 * e + 64], a_low[64 * e : 64 * e + 64]
            )
            for e in range(2)
        ]

    def children(down, e, p):
        vector = down[e]
        inverse = inverse_ref[pl.ds(p, 1), :]
        message = message_ref[p - 32] if p >= 32 else given_ref[p]
        pair = jnp.concatenate(
            [vector * message[64:128] * inverse, vector * message[0:64] * inverse], axis=0
        )
        return split(pair)

    def inner(r):
        down = descend(r)
        for e in range(2):
            p = 2 * r + e - 64
            if isinstance(p, int) and p == 63:
                continue
            high, low = children(down, e, p)
            a_high_ref[p - 32] = high
            a_low_ref[p - 32] = low

    for r in range(63, 47, -1):
        inner(r)

    for r in range(47, 31, -1):
        down = descend(r)
        for e in range(2):
            p = 2 * r + e - 64
            high, low = children(down, e, p)
            square = mxu_nt(jnp.concatenate([high, low], axis=0), leaf_ref[p])
            store_counts(p, square[0:128] + square[128:256])

    def adjoint(step, carry):
        held = [count_ref[step * 16 + j] for j in range(16)]
        for level in range(3, -1, -1):
            for j in range(16):
                high, low = split(held[j])
                e_high, e_low = chain_ref[level, 0, step * 16 + j], chain_ref[level, 1, step * 16 + j]
                left = jnp.concatenate([
                    jnp.concatenate([high, e_high], axis=1),
                    jnp.concatenate([low, e_low], axis=1),
                ], axis=0)
                right = jnp.concatenate([
                    jnp.concatenate([spread(e_high), spread(e_low)], axis=1),
                    jnp.concatenate([spread(high), spread(low)], axis=1),
                ], axis=0)
                four = mxu(left, right)
                held[j] = 2.0 * held[j] + (
                    four[0:64, 0:128] + four[0:64, 128:256] + four[64:128, 0:128]
                )
        for j in range(16):
            back_ref[pl.ds(step * 16 + j, 64, stride=STRIDE), :] = held[j]
        return carry

    lax.fori_loop(0, PAIRS // 16, adjoint, 0)

    left = four_left(turned_ref[...])

    total = jnp.zeros((64, 128), F32)
    for i in range(0, 64, 2):
        values = [back_ref[rows_of(i + t), :] for t in range(2)]
        both = mxu(left, four_right(jnp.concatenate(values, axis=1)))
        for t in range(2):
            total = total + values[t] * slope_ref[64 * (i + t) : 64 * (i + t) + 64, :]
            here = both[:, 128 * t : 128 * t + 128]
            bins_ref[rows_of(i + t), :] = jnp.where(mask, here[0:64], here[64:128])
    slopes = total * 0.0625

    table, nonsyn = fixed_ref[6], nonsyn_ref[...]
    row = lax.broadcasted_iota(jnp.int32, (64, 128), 0)
    lane = lax.broadcasted_iota(jnp.int32, (64, 128), 1)
    table_grad = jnp.zeros((64, 128), F32)
    omega_row = jnp.zeros((1, 128), F32)
    lane_row = lax.broadcasted_iota(jnp.int32, (1, 128), 1)
    for pair in range(CLASSES // 2):
        grads = []
        for k in range(ORDER):
            at = CLASSES * k + 2 * pair
            first = bins_ref[pl.ds(at, 64, stride=STRIDE), :]
            second = bins_ref[pl.ds(at + 1, 64, stride=STRIDE), :]
            first = first + pltpu.roll(first, 64, 1)
            second = second + pltpu.roll(second, 64, 1)
            grads.append(jnp.where(mask, first, second))
        g1, g2, g3, g4, g5, g6, g7, g8 = grads
        a1, a2, a3, a4 = [power_ref[pair, k] for k in range(4)]
        g4 = g4 + pair_products((g8, a4), (a4, g8), (g7, a3), (g6, a2), (g5, a1))
        g3 = g3 + pair_products((a4, g7))
        g2 = g2 + pair_products((a4, g6))
        g1 = g1 + pair_products((a4, g5))
        g2 = g2 + pair_products((g4, a2), (a2, g4), (g3, a1))
        g1 = g1 + pair_products((a2, g3))
        g1 = g1 + pair_products((g2, a1), (a1, g2))
        factor, off, rows, mean = class_pair(
            table, nonsyn, omega_ref, pair, twice, pi_row, pi_col
        )
        d_rate = root_col * g1 * inverse_root_row
        rate = (off - twice * rows) / mean
        weighted = d_rate * rate
        diagonal = d_rate * twice
        total0 = jnp.sum(jnp.where(mask, weighted, 0.0), axis=1, keepdims=True)
        total1 = jnp.sum(jnp.where(mask, 0.0, weighted), axis=1, keepdims=True)
        total0 = jnp.sum(total0, axis=0, keepdims=True)
        total1 = jnp.sum(total1, axis=0, keepdims=True)
        diag0 = jnp.sum(jnp.where(mask, diagonal, 0.0), axis=1, keepdims=True)
        diag1 = jnp.sum(jnp.where(mask, 0.0, diagonal), axis=1, keepdims=True)
        row_grad = jnp.where(mask, diag0 + pi_col * total0, diag1 + pi_col * total1)
        flux_grad = (d_rate - row_grad) * pi_row / mean
        table_grad = table_grad + flux_grad * factor * single_ref[...]
        ratio = flux_grad * table * nonsyn
        ratio0 = jnp.sum(jnp.where(mask, ratio, 0.0), axis=1, keepdims=True)
        ratio1 = jnp.sum(jnp.where(mask, 0.0, ratio), axis=1, keepdims=True)
        ratio0 = jnp.sum(ratio0, axis=0, keepdims=True)
        ratio1 = jnp.sum(ratio1, axis=0, keepdims=True)
        omega_row = jnp.where(lane_row == 2 * pair, ratio0, omega_row)
        omega_row = jnp.where(lane_row == 2 * pair + 1, ratio1, omega_row)
    table_grad = table_grad + pltpu.roll(table_grad, 64, 1)
    masks, picks = neighbours()
    codon = lax.broadcasted_iota(jnp.int32, (16, 128), 1)
    column = lax.broadcasted_iota(jnp.int32, (16, 128), 0)
    lefts, rights = [], []
    for p, digit in enumerate((codon // 16, codon // 4 % 4, codon % 4)):
        left = jnp.where((column == 4 * p + digit) & (codon < 64), 1.0, 0.0).astype(BF)
        for part in split(jnp.where(masks[p], 0.5 * table_grad, 0.0)):
            lefts.append(left)
            rights.append(part)
    packed = mxu(
        jnp.concatenate(lefts, axis=1),
        jnp.concatenate([jnp.concatenate([part, jnp.zeros_like(part)], axis=0) for part in rights], axis=0),
    )
    turned = mxu_nt(
        jnp.concatenate(lefts, axis=1),
        jnp.concatenate([
            jnp.concatenate([part, jnp.zeros_like(part)], axis=0) for part in rights
        ], axis=1),
    )
    packed = packed + turned
    packed = jnp.where(lax.broadcasted_iota(jnp.int32, (16, 128), 1) < 64, packed, 0.0)

    even = jnp.sum(jnp.where(mask, slopes, 0.0), axis=1, keepdims=True)
    other = jnp.sum(jnp.where(mask, 0.0, slopes), axis=1, keepdims=True)
    placed = jnp.where(lane == 2 * row, even, 0.0) + jnp.where(lane == 2 * row + 1, other, 0.0)
    length_row = jnp.sum(placed, axis=0, keepdims=True)
    line = lax.broadcasted_iota(jnp.int32, out_ref.shape, 0)
    omega_row = jnp.where(lane_row == CLASSES, log_part, omega_row)
    omega_row = pltpu.roll(jnp.broadcast_to(omega_row, (8, 128)), 64, 1)[0:1]
    packed = packed + jnp.where(line == 0, omega_row, 0.0)
    out_ref[...] = packed + jnp.where(line == 12 + subtree, length_row, 0.0)


def last_kernel(total_sites, count, *refs):
    members = lax.axis_size("branch")
    subtree = lax.axis_index("branch")
    exch_ref, omega_ref, length_ref, log_ref = refs[count:]
    total = tree_sum([ref[...] for ref in refs[:count]])
    masks, picks = neighbours()
    table = jnp.zeros((64, 128), F32)
    for at_position, pick in zip(masks, picks):
        table = table + jnp.where(at_position, exact(pick, total), 0.0)
    exch_ref[...] = table[:, 0:64]
    moved = pltpu.roll(total[0:8], 64, 1)
    omega_ref[...] = moved[0:1, 0:CLASSES]
    line = lax.broadcasted_iota(jnp.int32, total.shape, 0)
    lengths = jnp.sum(jnp.where(line == 12 + subtree, total, 0.0), axis=0, keepdims=True)
    length_ref[...] = lengths[:, 0:EDGES]
    log_ref[...] = moved[0:1, CLASSES : CLASSES + 1] / total_sites / (LEAF_DEV * members)


def partners(x, axis, start, radix):
    size = lax.axis_size(axis)
    others = [
        lax.ppermute(x, axis, [(i, i ^ (step * start)) for i in range(size)])
        for step in range(1, radix)
    ]
    return [x] + others


def tree_sum(parts):
    while len(parts) > 1:
        parts = [parts[i] + parts[i + 1] for i in range(0, len(parts), 2)]
    return parts[0]


def sum_stages(x, members, sites):
    stages, start = [], 1
    while start < sites:
        radix = 2 if sites // start in (2, 8) else 4
        stages.append((members * start, radix, 1))
        start *= radix
    stages.append((1, members, 0))
    parts = [x]
    for start, radix, flip in stages[::-1]:
        x = tree_sum(parts)
        parts = [x] + [
            lax.ppermute(x, ("site", "branch"), [
                (i, i ^ (step * start + flip)) for i in range(sites * members)
            ])
            for step in range(1, radix)
        ]
    return parts


def body(
    total_sites, states, gap_mask, weights, leaf_order, exchanges, codon_freq, omega_ratio,
    lengths, classes,
):
    sites = states.shape[1]
    members = lax.axis_size("branch")
    sense, single, nonsyn = codon_tables()
    vmem = pl.BlockSpec(memory_space=pltpu.VMEM)
    smem = pl.BlockSpec(memory_space=pltpu.SMEM)
    shape = jax.ShapeDtypeStruct
    held = pltpu.VMEM
    limit = pltpu.CompilerParams(vmem_limit_bytes=20 * 2**20)

    def outside(x):
        return pltpu.with_memory_space_constraint(x, pltpu.HBM)

    def inside(xs):
        return [pltpu.with_memory_space_constraint(x, pltpu.VMEM) for x in xs]

    sense2 = outside(jnp.asarray(np.tile(sense[None, :], (1, 2))))
    single2 = outside(jnp.asarray(np.tile(single, (1, 2))))
    nonsyn2 = outside(jnp.asarray(np.tile(nonsyn, (1, 2))))
    freq = outside(codon_freq.reshape(1, 64))
    span, owner = outside(lengths.reshape(1, EDGES)), outside(classes.reshape(1, EDGES))
    table, omega = outside(exchanges), outside(omega_ratio)

    top, *kept = pl.pallas_call(
        up_kernel,
        out_shape=[
            shape((64, sites), F32),
            held((4, 2, PAIRS, 64, 128), BF),
            held((PAIRS // 2, 64, 128), F32),
            held((CLASSES // 2, 4, 64, 128), F32),
            held((STRIDE * 64, 128), F32),
            held((7, 64, 128), F32),
            held((PAIRS // 2, 128, sites), F32),
            held((64, 64, sites), BF),
            held((64, 64, sites), BF),
            held((32, 128, sites), BF),
            held((64, sites), F32),
            held((64, sites), F32),
            held((PAIRS, 64, 128), BF),
        ],
        in_specs=[vmem, vmem, smem, vmem, vmem, smem] + [vmem] * 5,
        out_specs=[vmem] * 13,
        scratch_shapes=[
            pltpu.VMEM((STRIDE * 64, 128), F32),
            pltpu.VMEM((PAIRS, 64, 256), BF),
        ],
        compiler_params=limit,
        name="up",
    )(
        outside(states), outside(gap_mask), outside(leaf_order),
        table, freq, omega, span, owner, sense2, single2, nonsyn2,
    )
    (
        chain, last, powers, dup, fixed, message, high, low, leaf, scale, inverse, thin,
    ) = inside(kept)
    tops = partners(top, "branch", 1, members)
    slope, matrix, turned, given = inside(pl.pallas_call(
        side_kernel,
        out_shape=[
            held((PAIRS * 64, 128), F32),
            held((64, 64, 256), BF),
            held((128, 128), F32),
            held((PAIRS // 2, 128, sites), F32),
        ],
        in_specs=[vmem] * 7,
        out_specs=[vmem] * 4,
        compiler_params=limit,
        name="side",
    )(dup, last, span, owner, fixed, thin, leaf))
    part = pl.pallas_call(
        functools.partial(down_kernel, total_sites, members),
        out_shape=shape((16, 128), F32),
        in_specs=[vmem] * (14 + members) + [smem, vmem, vmem],
        out_specs=vmem,
        scratch_shapes=[
            pltpu.VMEM((32, 128, sites), BF),
            pltpu.VMEM((32, 128, sites), BF),
            pltpu.VMEM((PAIRS, 64, 128), F32),
            pltpu.VMEM((STRIDE * 64, 128), F32),
            pltpu.VMEM((STRIDE * 64, 128), F32),
        ],
        compiler_params=limit,
        name="down",
    )(
        *tops, matrix, given, message, high, low, leaf, scale, inverse,
        chain, turned, slope, powers, fixed,
        outside(weights.reshape(1, sites)), omega, single2, nonsyn2,
    )
    parts = sum_stages(part, members, lax.axis_size("site"))
    exch, ratio, length, loglik = pl.pallas_call(
        functools.partial(last_kernel, total_sites, len(parts)),
        out_shape=[shape((64, 64), F32), shape((1, CLASSES), F32), shape((1, EDGES), F32), shape((1, 1), F32)],
        in_specs=[vmem] * len(parts),
        out_specs=[vmem] * 4,
        compiler_params=limit,
        name="last",
    )(*parts)
    return (exch, ratio.reshape(CLASSES), length.reshape(EDGES), loglik.reshape(()))


def solution(mesh):
    def whole(states, *rest):
        total_sites = states.shape[1]
        return jax.shard_map(
            functools.partial(body, total_sites),
            mesh=mesh,
            in_specs=(
                P(None, "site"),
                P(None, "site"),
                P("site"),
                P(),
                P(),
                P(),
                P(),
                P("branch"),
                P("branch"),
            ),
            out_specs=(P(), P(), P("branch"), P()),
            check_vma=False,
        )(states, *rest)

    return whole
```

```python
import functools
import jax
import jax.numpy as jnp
import numpy as np
from jax import lax
from jax.experimental import pallas as pl
from jax.experimental.pallas import tpu as pltpu
from jax.sharding import PartitionSpec as P

LEAF_DEV = 64
EDGES = 127
PAIRS = 64
CLASSES = 8
ORDER = 8
STRIDE = 65
BF = jnp.bfloat16
F32 = jnp.float32

CODE_TABLE = "FFLLSSSSYYXXCCXWLLLLPPPPHHQQRRRRIIIMTTTTNNKKSSRRVVVVAAAADDEEGGGG"


def codon_tables():
    amino_acid = np.array(list(CODE_TABLE))
    codon_index = np.arange(64)
    digits = np.stack([codon_index // 16, codon_index // 4 % 4, codon_index % 4], 1)
    differ = (digits[:, None, :] != digits[None, :, :]).sum(-1)
    is_sense = amino_acid != "X"
    single = (differ == 1) & is_sense[:, None] & is_sense[None, :]
    nonsyn = single & (amino_acid[:, None] != amino_acid[None, :])
    return (is_sense.astype(np.float32), single.astype(np.float32), nonsyn.astype(np.float32))


def low_half():
    return lax.broadcasted_iota(jnp.int32, (64, 128), 1) < 64


def split(x):
    high = x.astype(BF)
    low = (x - high.astype(F32)).astype(BF)
    return high, low


def spread(x, scale=1.0):
    mask = low_half()
    low = jnp.where(mask, scale, 0.0).astype(x.dtype)
    high = jnp.where(mask, 0.0, scale).astype(x.dtype)
    return jnp.concatenate([x * low, x * high], axis=0)


def mxu(left, right):
    return jnp.dot(left, right, preferred_element_type=F32)


def mxu_nt(left, right):
    return lax.dot_general(left, right, (((1,), (1,)), ((), ())), preferred_element_type=F32)


def exact(left, right):
    return jnp.dot(left, right, preferred_element_type=F32, precision=lax.Precision.HIGHEST)


def exact_tn(left, right):
    return lax.dot_general(
        left, right, (((0,), (0,)), ((), ())), preferred_element_type=F32,
        precision=lax.Precision.HIGHEST,
    )


def pair_products(*terms):
    lefts, rights = [], []
    for left, right in terms:
        left_high, left_low = split(left)
        right_high, right_low = split(right)
        wide_high, wide_low = spread(right_high), spread(right_low)
        lefts += [left_high, left_high, left_low]
        rights += [wide_high, wide_low, wide_high]
    return mxu(jnp.concatenate(lefts, axis=1), jnp.concatenate(rights, axis=0))


def messages(matrix, high, low):
    return mxu(matrix, jnp.concatenate([high, low, high, low], axis=0))


def leaf_messages(thin_ref, leaf_ref, p):
    found = []
    for e in range(2):
        vector = leaf_ref[p, 64 * e : 64 * e + 64, :]
        found.append(mxu(thin_ref[2 * p + e], jnp.concatenate([vector, vector], axis=0)))
    return found


def doubled(x):
    mask = low_half()
    swapped = pltpu.roll(x, 64, 1)
    return jnp.where(mask, x, swapped), jnp.where(mask, swapped, x)


def double(ref, p, x):
    for e, both in enumerate(doubled(x)):
        high, low = split(both)
        ref[2 * p + e] = jnp.concatenate([high, low], axis=1)


def side_by_side(ref, p, x):
    for e, both in enumerate(doubled(x)):
        rest = both - both.astype(BF).astype(F32)
        ref[2 * p + e] = jnp.where(low_half(), both, rest).astype(BF)


def identity_twice():
    row = lax.broadcasted_iota(jnp.int32, (64, 128), 0)
    lane = lax.broadcasted_iota(jnp.int32, (64, 128), 1)
    return (row == lane % 64).astype(F32)


def frequencies(freq_ref, sense_ref):
    twice = identity_twice()
    sense2 = sense_ref[...]
    freq2 = jnp.concatenate([freq_ref[...]] * 2, axis=1) * sense2
    total = 0.5 * jnp.sum(freq2, axis=1, keepdims=True)
    pi_row = freq2 / total
    pi_col = 0.5 * jnp.sum(twice * pi_row, axis=1, keepdims=True)
    sense_col = 0.5 * jnp.sum(twice * sense2, axis=1, keepdims=True)
    root_row = jnp.sqrt(jnp.where(sense2 > 0, pi_row, 1.0))
    root_col = jnp.sqrt(jnp.where(sense_col > 0, pi_col, 1.0))
    return twice, pi_row, pi_col, root_row, root_col


def symmetric_table(ex_ref, single_ref, twice):
    ex = ex_ref[...]
    both = ex + ex.T
    return 0.5 * jnp.concatenate([both, both], axis=1) * single_ref[...]


def class_pair(table, nonsyn, omega_ref, pair, twice, pi_row, pi_col):
    mask = low_half()
    omega = jnp.where(mask, omega_ref[2 * pair], omega_ref[2 * pair + 1])
    factor = 1.0 + nonsyn * (omega - 1.0)
    flux = table * factor
    off = flux * pi_row
    row0 = jnp.sum(jnp.where(mask, off, 0.0), axis=1, keepdims=True)
    row1 = jnp.sum(jnp.where(mask, 0.0, off), axis=1, keepdims=True)
    mean0 = jnp.sum(pi_col * row0, axis=0, keepdims=True)
    mean1 = jnp.sum(pi_col * row1, axis=0, keepdims=True)
    rows = jnp.where(mask, row0, row1)
    mean = jnp.where(mask, mean0, mean1)
    return factor, off, rows, mean


def neighbours():
    row = lax.broadcasted_iota(jnp.int32, (64, 128), 0)
    lane = lax.broadcasted_iota(jnp.int32, (64, 128), 1) % 64
    masks = [
        row % 16 == lane % 16,
        (row // 16 == lane // 16) & (row % 4 == lane % 4),
        row // 4 == lane // 4,
    ]
    codon = lax.broadcasted_iota(jnp.int32, (64, 16), 0)
    column = lax.broadcasted_iota(jnp.int32, (64, 16), 1)
    digits = [codon // 16, codon // 4 % 4, codon % 4]
    picks = [(column == 4 * p + digits[p]).astype(F32) for p in range(3)]
    return masks, picks


def coefficients(len_ref, cls_ref, slope):
    lane = lax.broadcasted_iota(jnp.int32, (PAIRS, EDGES), 1)
    row = lax.broadcasted_iota(jnp.int32, (PAIRS, EDGES), 0)
    lengths = len_ref[...] * 0.0625
    classes = cls_ref[...].astype(F32)
    place = lax.broadcasted_iota(jnp.int32, (PAIRS, 128), 1) % 64
    found = []
    for odd in range(2):
        here = lane == 2 * row + odd
        y = jnp.sum(jnp.where(here, lengths, 0.0), axis=1, keepdims=True)
        owner = jnp.sum(jnp.where(here, classes, 0.0), axis=1, keepdims=True)
        current = jnp.ones((PAIRS, 128), F32)
        series = jnp.zeros((PAIRS, 128), F32)
        for k in range(ORDER):
            following = current * y * (1.0 / (k + 1))
            series = jnp.where(place // CLASSES == k, current if slope else following, series)
            current = following
        found.append(jnp.where((place % CLASSES).astype(F32) == owner, series, 0.0))
    return found


def four_left(x):
    high, low = split(x)
    return jnp.concatenate([high, low], axis=1)


def four_right(x):
    high, low = split(x)
    return jnp.concatenate([high, low, high, low], axis=0)


def expand(coefs, dup_ref, store):
    high, low = split(coefs)
    left = jnp.concatenate(
        [jnp.concatenate([high, high], axis=1), jnp.concatenate([low, low], axis=1)], axis=0
    )
    for i in range(0, 64, 2):
        parts = [split(dup_ref[rows_of(i + t), :]) for t in range(2)]
        right = jnp.concatenate([
            jnp.concatenate([spread(parts[0][h]), spread(parts[1][h])], axis=1) for h in range(2)
        ], axis=0)
        both = mxu(left, right)
        both = both[0:64] + both[64:128]
        for t in range(2):
            store(i + t, both[:, 128 * t : 128 * t + 128])


def rows_of(i):
    return pl.ds(STRIDE * i, 64)


def up_kernel(
    states_ref, gap_ref, order_ref,
    ex_ref, freq_ref, omega_ref, len_ref, cls_ref, sense_ref, single_ref, nonsyn_ref,
    top_ref, chain_ref, last_ref, power_ref, dup_ref, fixed_ref,
    message_ref, high_ref, low_ref, leaf_ref, scale_ref, inverse_ref, thin_ref,
    first_ref, up_ref,
):
    subtree = lax.axis_index("branch")
    mask = low_half()
    twice, pi_row, pi_col, root_row, root_col = frequencies(freq_ref, sense_ref)
    table = symmetric_table(ex_ref, single_ref, twice)
    nonsyn = nonsyn_ref[...]
    for at, value in enumerate(
        (pi_row, pi_col, root_row, root_col, 1.0 / root_row, 1.0 / root_col, table)
    ):
        fixed_ref[at] = jnp.broadcast_to(value, (64, 128))

    sites = states_ref.shape[1]
    codon = lax.broadcasted_iota(jnp.int32, (64, sites), 0)
    for p in range(32):
        both = []
        for e in range(2):
            taxon = order_ref[subtree * LEAF_DEV + 2 * p + e]
            state = jnp.where(gap_ref[pl.ds(taxon, 1), :] > 0, -1, states_ref[pl.ds(taxon, 1), :])
            hit = (codon == state) | (state < 0)
            both.append(jnp.where(hit, 1.0, 0.0).astype(BF))
        leaf_ref[p] = jnp.concatenate(both, axis=0)

    powers = []
    for pair in range(CLASSES // 2):
        factor, off, rows, mean = class_pair(
            table, nonsyn, omega_ref, pair, twice, pi_row, pi_col
        )
        powers.append([(table * factor * root_col * root_row - twice * rows) / mean])
    for left, right in ((0, 0), (1, 0), (1, 1), (3, 0), (3, 1), (3, 2), (3, 3)):
        for pair in range(CLASSES // 2):
            powers[pair].append(pair_products((powers[pair][left], powers[pair][right])))
    for pair in range(CLASSES // 2):
        for k in range(ORDER):
            value = powers[pair][k]
            swapped = pltpu.roll(value, 64, 1)
            at = CLASSES * k + 2 * pair
            dup_ref[pl.ds(at, 64, stride=STRIDE), :] = jnp.where(mask, value, swapped)
            dup_ref[pl.ds(at + 1, 64, stride=STRIDE), :] = jnp.where(mask, swapped, value)
            if k < 4:
                power_ref[pair, k] = value

    even, odd = coefficients(len_ref, cls_ref, False)

    def store(i, value):
        first_ref[rows_of(i), :] = value

    expand(jnp.where(low_half(), even, odd), dup_ref, store)

    def squarings(leaves, step, carry):
        width = 16
        held = [first_ref[pl.ds(step * width + j, 64, stride=STRIDE), :] for j in range(width)]
        for level in range(4):
            for j in range(width):
                high, low = split(held[j])
                chain_ref[level, 0, step * width + j] = high
                chain_ref[level, 1, step * width + j] = low
                wide_high, wide_low = spread(high), spread(low)
                held[j] = 2.0 * held[j] + mxu(
                    jnp.concatenate([high, high, low], axis=1),
                    jnp.concatenate([wide_high, wide_low, wide_high], axis=0),
                )
        for j in range(width):
            p = step * width + j
            matrix = inverse_root_col * (held[j] + twice) * root_row
            if leaves:
                side_by_side(thin_ref, p, matrix)
            else:
                last_ref[p - 32] = held[j]
                double(up_ref, p - 32, matrix)
        return carry

    inverse_root_col = 1.0 / root_col
    lax.fori_loop(0, 2, functools.partial(squarings, True), 0)
    lax.fori_loop(2, 4, functools.partial(squarings, False), 0)

    def finish(p, message):
        if p >= 32:
            message_ref[p - 32] = jnp.concatenate(message, axis=0)
        raw = message[0] * message[1]
        scaling = jnp.sum(raw, axis=0, keepdims=True)
        inverse = 1.0 / scaling
        scale_ref[pl.ds(p, 1), :] = scaling
        inverse_ref[pl.ds(p, 1), :] = inverse
        high, low = split(raw * inverse)
        high_ref[p] = high
        low_ref[p] = low

    for p in range(32):
        finish(p, leaf_messages(thin_ref, leaf_ref, p))

    def inner(p):
        child = 2 * p - 64
        return [
            messages(up_ref[child + e], high_ref[child + e], low_ref[child + e]) for e in range(2)
        ]

    for p in range(32, 48):
        finish(p, inner(p))
    for p in range(48, 63):
        finish(p, inner(p))
    high_ref[63] = jnp.zeros((64, sites), BF)
    low_ref[63] = jnp.zeros((64, sites), BF)
    scale_ref[63:64, :] = jnp.ones((1, sites), F32)
    inverse_ref[63:64, :] = jnp.ones((1, sites), F32)
    top = inner(63)
    top_ref[...] = top[0]


def side_kernel(
    dup_ref, last_ref, len_ref, cls_ref, fixed_ref, thin_ref, leaf_ref, omega_ref, single_ref,
    nonsyn_ref,
    slope_ref, matrix_ref, turned_ref, given_ref, class_ref,
):
    twice = identity_twice()
    even, odd = coefficients(len_ref, cls_ref, True)

    def store(i, value):
        slope_ref[64 * i : 64 * i + 64, :] = value

    expand(jnp.where(low_half(), even, odd), dup_ref, store)
    even, odd = coefficients(len_ref, cls_ref, False)
    turned_ref[...] = exact_tn(jnp.where(low_half(), even, odd), twice)
    root_col, inverse_root_row = fixed_ref[3], fixed_ref[4]

    def matrices(step, carry):
        for j in range(8):
            r = step * 8 + j
            double(matrix_ref, r, root_col * (last_ref[r] + twice) * inverse_root_row)
        return carry

    lax.fori_loop(0, 4, matrices, 0)
    pi_row, pi_col, table, single = fixed_ref[0], fixed_ref[1], fixed_ref[6], single_ref[...]
    for pair in range(CLASSES // 2):
        factor, off, rows, mean = class_pair(
            table, nonsyn_ref[...], omega_ref, pair, twice, pi_row, pi_col
        )
        class_ref[pair, 0] = (off - twice * rows) / mean
        class_ref[pair, 1] = pi_row / mean
        class_ref[pair, 2] = factor * single
    for p in range(32):
        given_ref[p] = jnp.concatenate(leaf_messages(thin_ref, leaf_ref, p), axis=0)


def down_kernel(total_sites, members, *refs):
    tops = refs[:members]
    (
        matrix_ref, given_ref, message_ref, high_ref, low_ref, leaf_ref, scale_ref, inverse_ref,
        chain_ref, turned_ref, slope_ref, power_ref, fixed_ref,
        class_ref, weights_ref, nonsyn_ref,
        out_ref,
        a_high_ref, a_low_ref, count_ref, back_ref, bins_ref,
    ) = refs[members:]
    subtree = lax.axis_index("branch")
    mask = low_half()
    twice = identity_twice()
    pi_row, pi_col, root_row, root_col, inverse_root_row, inverse_root_col = [
        fixed_ref[at] for at in range(6)
    ]
    sites = weights_ref.shape[1]
    weight = weights_ref[...].astype(F32)

    above = jnp.broadcast_to(pi_col[:, 0:1], (64, sites))
    for other in tops[1:]:
        above = above * other[...]
    own = tops[0][...]
    likelihood = jnp.sum(above * own, axis=0, keepdims=True)
    logs = jnp.sum(jnp.log(scale_ref[...]), axis=0, keepdims=True)
    logs = logs + jnp.where(subtree == 0, jnp.log(likelihood), 0.0)
    log_part = jnp.sum(weight * logs, axis=1, keepdims=True)
    high, low = split(above * (weight / (likelihood * total_sites)))
    a_high_ref[31, 0:64, :] = high
    a_low_ref[31, 0:64, :] = low
    a_high_ref[31, 64:128, :] = jnp.zeros((64, sites), BF)
    a_low_ref[31, 64:128, :] = jnp.zeros((64, sites), BF)

    def store_counts(p, square):
        counts = jnp.where(mask, square[0:64], square[64:128])
        count_ref[p] = inverse_root_col * counts * root_row

    def descend(r):
        a_high, a_low = a_high_ref[r - 32], a_low_ref[r - 32]
        child = 2 * r - 64
        u_high = jnp.concatenate([high_ref[child], high_ref[child + 1]], axis=0)
        u_low = jnp.concatenate([low_ref[child], low_ref[child + 1]], axis=0)
        first = mxu_nt(jnp.concatenate([a_high, a_low], axis=0), u_high)
        second = mxu_nt(a_high, u_low)
        store_counts(r, first[0:128] + first[128:256] + second)
        return [
            messages(
                matrix_ref[2 * (r - 32) + e], a_high[64 * e : 64 * e + 64], a_low[64 * e : 64 * e + 64]
            )
            for e in range(2)
        ]

    def children(down, e, p):
        vector = down[e]
        inverse = inverse_ref[pl.ds(p, 1), :]
        message = message_ref[p - 32] if p >= 32 else given_ref[p]
        pair = jnp.concatenate(
            [vector * message[64:128] * inverse, vector * message[0:64] * inverse], axis=0
        )
        return split(pair)

    def inner(r):
        down = descend(r)
        for e in range(2):
            p = 2 * r + e - 64
            if isinstance(p, int) and p == 63:
                continue
            high, low = children(down, e, p)
            a_high_ref[p - 32] = high
            a_low_ref[p - 32] = low

    for r in range(63, 47, -1):
        inner(r)

    for r in range(47, 31, -1):
        down = descend(r)
        for e in range(2):
            p = 2 * r + e - 64
            high, low = children(down, e, p)
            square = mxu_nt(jnp.concatenate([high, low], axis=0), leaf_ref[p])
            store_counts(p, square[0:128] + square[128:256])

    def adjoint(step, carry):
        held = [count_ref[step * 16 + j] for j in range(16)]
        for level in range(3, -1, -1):
            for j in range(16):
                high, low = split(held[j])
                e_high, e_low = chain_ref[level, 0, step * 16 + j], chain_ref[level, 1, step * 16 + j]
                wide_high, wide_e_high = spread(high), spread(e_high)
                held[j] = 2.0 * held[j] + mxu(
                    jnp.concatenate([high, e_high, high, e_high, low, e_low], axis=1),
                    jnp.concatenate([
                        wide_e_high, wide_high, spread(e_low), spread(low), wide_e_high, wide_high
                    ], axis=0),
                )
        for j in range(16):
            back_ref[pl.ds(step * 16 + j, 64, stride=STRIDE), :] = held[j]
        return carry

    lax.fori_loop(0, PAIRS // 16, adjoint, 0)

    left = four_left(turned_ref[...])

    total = jnp.zeros((64, 128), F32)
    for i in range(0, 64, 2):
        values = [back_ref[rows_of(i + t), :] for t in range(2)]
        both = mxu(left, four_right(jnp.concatenate(values, axis=1)))
        for t in range(2):
            total = total + values[t] * slope_ref[64 * (i + t) : 64 * (i + t) + 64, :]
            here = both[:, 128 * t : 128 * t + 128]
            bins_ref[rows_of(i + t), :] = jnp.where(mask, here[0:64], here[64:128])
    slopes = total * 0.0625

    ratio_table = fixed_ref[6] * nonsyn_ref[...]
    half = lax.broadcasted_iota(jnp.int32, (1, 128), 1) < 64
    row = lax.broadcasted_iota(jnp.int32, (64, 128), 0)
    lane = lax.broadcasted_iota(jnp.int32, (64, 128), 1)
    table_grad = jnp.zeros((64, 128), F32)
    omega_row = jnp.zeros((1, 128), F32)
    lane_row = lax.broadcasted_iota(jnp.int32, (1, 128), 1)
    for pair in range(CLASSES // 2):
        grads = []
        for k in range(ORDER):
            at = CLASSES * k + 2 * pair
            first = bins_ref[pl.ds(at, 64, stride=STRIDE), :]
            second = bins_ref[pl.ds(at + 1, 64, stride=STRIDE), :]
            first = first + pltpu.roll(first, 64, 1)
            second = second + pltpu.roll(second, 64, 1)
            grads.append(jnp.where(mask, first, second))
        g1, g2, g3, g4, g5, g6, g7, g8 = grads
        a1, a2, a3, a4 = [power_ref[pair, k] for k in range(4)]
        g4 = g4 + pair_products((g8, a4), (a4, g8), (g7, a3), (g6, a2), (g5, a1))
        g3 = g3 + pair_products((a4, g7))
        g2 = g2 + pair_products((a4, g6))
        g1 = g1 + pair_products((a4, g5))
        g2 = g2 + pair_products((g4, a2), (a2, g4), (g3, a1))
        g1 = g1 + pair_products((a2, g3))
        g1 = g1 + pair_products((g2, a1), (a1, g2))
        rate, pi_mean, factor = [class_ref[pair, at] for at in range(3)]
        d_rate = root_col * g1 * inverse_root_row
        weighted = jnp.sum(d_rate * rate, axis=0, keepdims=True)
        total0 = jnp.sum(jnp.where(half, weighted, 0.0), axis=1, keepdims=True)
        total1 = jnp.sum(jnp.where(half, 0.0, weighted), axis=1, keepdims=True)
        diagonal = d_rate * twice
        diag0 = jnp.sum(jnp.where(mask, diagonal, 0.0), axis=1, keepdims=True)
        diag1 = jnp.sum(jnp.where(mask, 0.0, diagonal), axis=1, keepdims=True)
        row_grad = jnp.where(mask, diag0, diag1) + pi_col * jnp.where(half, total0, total1)
        flux_grad = (d_rate - row_grad) * pi_mean
        table_grad = table_grad + flux_grad * factor
        ratio = jnp.sum(flux_grad * ratio_table, axis=0, keepdims=True)
        ratio0 = jnp.sum(jnp.where(half, ratio, 0.0), axis=1, keepdims=True)
        ratio1 = jnp.sum(jnp.where(half, 0.0, ratio), axis=1, keepdims=True)
        omega_row = jnp.where(lane_row == 2 * pair, ratio0, omega_row)
        omega_row = jnp.where(lane_row == 2 * pair + 1, ratio1, omega_row)
    table_grad = table_grad + pltpu.roll(table_grad, 64, 1)
    masks, picks = neighbours()
    codon = lax.broadcasted_iota(jnp.int32, (16, 128), 1)
    column = lax.broadcasted_iota(jnp.int32, (16, 128), 0)
    lefts, rights = [], []
    for p, digit in enumerate((codon // 16, codon // 4 % 4, codon % 4)):
        left = jnp.where((column == 4 * p + digit) & (codon < 64), 1.0, 0.0).astype(BF)
        for part in split(jnp.where(masks[p], 0.5 * table_grad, 0.0)):
            lefts.append(left)
            rights.append(part)
    packed = mxu(
        jnp.concatenate(lefts, axis=1),
        jnp.concatenate([jnp.concatenate([part, jnp.zeros_like(part)], axis=0) for part in rights], axis=0),
    )
    turned = mxu_nt(
        jnp.concatenate(lefts, axis=1),
        jnp.concatenate([
            jnp.concatenate([part, jnp.zeros_like(part)], axis=0) for part in rights
        ], axis=1),
    )
    packed = packed + turned
    packed = jnp.where(lax.broadcasted_iota(jnp.int32, (16, 128), 1) < 64, packed, 0.0)

    even = jnp.sum(jnp.where(mask, slopes, 0.0), axis=1, keepdims=True)
    other = jnp.sum(jnp.where(mask, 0.0, slopes), axis=1, keepdims=True)
    placed = jnp.where(lane == 2 * row, even, 0.0) + jnp.where(lane == 2 * row + 1, other, 0.0)
    length_row = jnp.sum(placed, axis=0, keepdims=True)
    line = lax.broadcasted_iota(jnp.int32, out_ref.shape, 0)
    omega_row = jnp.where(lane_row == CLASSES, log_part, omega_row)
    omega_row = pltpu.roll(jnp.broadcast_to(omega_row, (8, 128)), 64, 1)[0:1]
    packed = packed + jnp.where(line == 0, omega_row, 0.0)
    out_ref[...] = packed + jnp.where(line == 12 + subtree, length_row, 0.0)


def last_kernel(total_sites, count, *refs):
    members = lax.axis_size("branch")
    subtree = lax.axis_index("branch")
    exch_ref, omega_ref, length_ref, log_ref = refs[count:]
    total = tree_sum([ref[...] for ref in refs[:count]])
    masks, picks = neighbours()
    table = jnp.zeros((64, 128), F32)
    for at_position, pick in zip(masks, picks):
        table = table + jnp.where(at_position, exact(pick, total), 0.0)
    exch_ref[...] = table[:, 0:64]
    moved = pltpu.roll(total[0:8], 64, 1)
    omega_ref[...] = moved[0:1, 0:CLASSES]
    line = lax.broadcasted_iota(jnp.int32, total.shape, 0)
    lengths = jnp.sum(jnp.where(line == 12 + subtree, total, 0.0), axis=0, keepdims=True)
    length_ref[...] = lengths[:, 0:EDGES]
    log_ref[...] = moved[0:1, CLASSES : CLASSES + 1] / total_sites / (LEAF_DEV * members)


def partners(x, axis, start, radix):
    size = lax.axis_size(axis)
    others = [
        lax.ppermute(x, axis, [(i, i ^ (step * start)) for i in range(size)])
        for step in range(1, radix)
    ]
    return [x] + others


def tree_sum(parts):
    while len(parts) > 1:
        parts = [parts[i] + parts[i + 1] for i in range(0, len(parts), 2)]
    return parts[0]


def sum_stages(x, members, sites):
    stages, start = [], 1
    while start < sites:
        radix = 2 if sites // start in (2, 8) else 4
        stages.append((members * start, radix, 1))
        start *= radix
    stages.append((1, members, 0))
    parts = [x]
    for start, radix, flip in stages[::-1]:
        x = tree_sum(parts)
        parts = [x] + [
            lax.ppermute(x, ("site", "branch"), [
                (i, i ^ (step * start + flip)) for i in range(sites * members)
            ])
            for step in range(1, radix)
        ]
    return parts


def body(
    total_sites, states, gap_mask, weights, leaf_order, exchanges, codon_freq, omega_ratio,
    lengths, classes,
):
    sites = states.shape[1]
    members = lax.axis_size("branch")
    sense, single, nonsyn = codon_tables()
    vmem = pl.BlockSpec(memory_space=pltpu.VMEM)
    smem = pl.BlockSpec(memory_space=pltpu.SMEM)
    shape = jax.ShapeDtypeStruct
    held = pltpu.VMEM
    limit = pltpu.CompilerParams(vmem_limit_bytes=20 * 2**20)

    def outside(x):
        return pltpu.with_memory_space_constraint(x, pltpu.HBM)

    def inside(xs):
        return [pltpu.with_memory_space_constraint(x, pltpu.VMEM) for x in xs]

    sense2 = outside(jnp.asarray(np.tile(sense[None, :], (1, 2))))
    single2 = outside(jnp.asarray(np.tile(single, (1, 2))))
    nonsyn2 = outside(jnp.asarray(np.tile(nonsyn, (1, 2))))
    freq = outside(codon_freq.reshape(1, 64))
    span, owner = outside(lengths.reshape(1, EDGES)), outside(classes.reshape(1, EDGES))
    table, omega = outside(exchanges), outside(omega_ratio)

    top, *kept = pl.pallas_call(
        up_kernel,
        out_shape=[
            shape((64, sites), F32),
            held((4, 2, PAIRS, 64, 128), BF),
            held((PAIRS // 2, 64, 128), F32),
            held((CLASSES // 2, 4, 64, 128), F32),
            held((STRIDE * 64, 128), F32),
            held((7, 64, 128), F32),
            held((PAIRS // 2, 128, sites), F32),
            held((64, 64, sites), BF),
            held((64, 64, sites), BF),
            held((32, 128, sites), BF),
            held((64, sites), F32),
            held((64, sites), F32),
            held((PAIRS, 64, 128), BF),
        ],
        in_specs=[vmem, vmem, smem, vmem, vmem, smem] + [vmem] * 5,
        out_specs=[vmem] * 13,
        scratch_shapes=[
            pltpu.VMEM((STRIDE * 64, 128), F32),
            pltpu.VMEM((PAIRS, 64, 256), BF),
        ],
        compiler_params=limit,
        name="up",
    )(
        outside(states), outside(gap_mask), outside(leaf_order),
        table, freq, omega, span, owner, sense2, single2, nonsyn2,
    )
    (
        chain, last, powers, dup, fixed, message, high, low, leaf, scale, inverse, thin,
    ) = inside(kept)
    tops = partners(top, "branch", 1, members)
    slope, matrix, turned, given, table_of = inside(pl.pallas_call(
        side_kernel,
        out_shape=[
            held((PAIRS * 64, 128), F32),
            held((64, 64, 256), BF),
            held((128, 128), F32),
            held((PAIRS // 2, 128, sites), F32),
            held((CLASSES // 2, 3, 64, 128), F32),
        ],
        in_specs=[vmem] * 7 + [smem, vmem, vmem],
        out_specs=[vmem] * 5,
        compiler_params=limit,
        name="side",
    )(dup, last, span, owner, fixed, thin, leaf, omega, single2, nonsyn2))
    part = pl.pallas_call(
        functools.partial(down_kernel, total_sites, members),
        out_shape=shape((16, 128), F32),
        in_specs=[vmem] * (16 + members),
        out_specs=vmem,
        scratch_shapes=[
            pltpu.VMEM((32, 128, sites), BF),
            pltpu.VMEM((32, 128, sites), BF),
            pltpu.VMEM((PAIRS, 64, 128), F32),
            pltpu.VMEM((STRIDE * 64, 128), F32),
            pltpu.VMEM((STRIDE * 64, 128), F32),
        ],
        compiler_params=limit,
        name="down",
    )(
        *tops, matrix, given, message, high, low, leaf, scale, inverse,
        chain, turned, slope, powers, fixed,
        table_of, outside(weights.reshape(1, sites)), nonsyn2,
    )
    parts = sum_stages(part, members, lax.axis_size("site"))
    exch, ratio, length, loglik = pl.pallas_call(
        functools.partial(last_kernel, total_sites, len(parts)),
        out_shape=[shape((64, 64), F32), shape((1, CLASSES), F32), shape((1, EDGES), F32), shape((1, 1), F32)],
        in_specs=[vmem] * len(parts),
        out_specs=[vmem] * 4,
        compiler_params=limit,
        name="last",
    )(*parts)
    return (exch, ratio.reshape(CLASSES), length.reshape(EDGES), loglik.reshape(()))


def solution(mesh):
    def whole(states, *rest):
        total_sites = states.shape[1]
        return jax.shard_map(
            functools.partial(body, total_sites),
            mesh=mesh,
            in_specs=(
                P(None, "site"),
                P(None, "site"),
                P("site"),
                P(),
                P(),
                P(),
                P(),
                P("branch"),
                P("branch"),
            ),
            out_specs=(P(), P(), P("branch"), P()),
            check_vma=False,
        )(states, *rest)

    return whole
```

```python
import functools
import jax
import jax.numpy as jnp
import numpy as np
from jax import lax
from jax.experimental import pallas as pl
from jax.experimental.pallas import tpu as pltpu
from jax.sharding import PartitionSpec as P

LEAF_DEV = 64
EDGES = 127
PAIRS = 64
CLASSES = 8
ORDER = 8
STRIDE = 65
BF = jnp.bfloat16
F32 = jnp.float32

CODE_TABLE = "FFLLSSSSYYXXCCXWLLLLPPPPHHQQRRRRIIIMTTTTNNKKSSRRVVVVAAAADDEEGGGG"


def codon_tables():
    amino_acid = np.array(list(CODE_TABLE))
    codon_index = np.arange(64)
    digits = np.stack([codon_index // 16, codon_index // 4 % 4, codon_index % 4], 1)
    differ = (digits[:, None, :] != digits[None, :, :]).sum(-1)
    is_sense = amino_acid != "X"
    single = (differ == 1) & is_sense[:, None] & is_sense[None, :]
    nonsyn = single & (amino_acid[:, None] != amino_acid[None, :])
    return (is_sense.astype(np.float32), single.astype(np.float32), nonsyn.astype(np.float32))


def low_half():
    return lax.broadcasted_iota(jnp.int32, (64, 128), 1) < 64


def split(x):
    high = x.astype(BF)
    low = (x - high.astype(F32)).astype(BF)
    return high, low


def spread(x, scale=1.0):
    mask = low_half()
    low = jnp.where(mask, scale, 0.0).astype(x.dtype)
    high = jnp.where(mask, 0.0, scale).astype(x.dtype)
    return jnp.concatenate([x * low, x * high], axis=0)


def mxu(left, right):
    return jnp.dot(left, right, preferred_element_type=F32)


def mxu_nt(left, right):
    return lax.dot_general(left, right, (((1,), (1,)), ((), ())), preferred_element_type=F32)


def exact(left, right):
    return jnp.dot(left, right, preferred_element_type=F32, precision=lax.Precision.HIGHEST)


def exact_tn(left, right):
    return lax.dot_general(
        left, right, (((0,), (0,)), ((), ())), preferred_element_type=F32,
        precision=lax.Precision.HIGHEST,
    )


def pair_products(*terms):
    lefts, rights = [], []
    for left, right in terms:
        left_high, left_low = split(left)
        right_high, right_low = split(right)
        wide_high, wide_low = spread(right_high), spread(right_low)
        lefts += [left_high, left_high, left_low]
        rights += [wide_high, wide_low, wide_high]
    return mxu(jnp.concatenate(lefts, axis=1), jnp.concatenate(rights, axis=0))


def messages(matrix, high, low):
    return mxu(matrix, jnp.concatenate([high, low, high, low], axis=0))


def leaf_messages(thin_ref, leaf_ref, p):
    found = []
    for e in range(2):
        vector = leaf_ref[p, 64 * e : 64 * e + 64, :]
        found.append(mxu(thin_ref[2 * p + e], jnp.concatenate([vector, vector], axis=0)))
    return found


def doubled(x):
    mask = low_half()
    swapped = pltpu.roll(x, 64, 1)
    return jnp.where(mask, x, swapped), jnp.where(mask, swapped, x)


def double(ref, p, x):
    for e, both in enumerate(doubled(x)):
        high, low = split(both)
        ref[2 * p + e] = jnp.concatenate([high, low], axis=1)


def side_by_side(ref, p, x):
    for e, both in enumerate(doubled(x)):
        rest = both - both.astype(BF).astype(F32)
        ref[2 * p + e] = jnp.where(low_half(), both, rest).astype(BF)


def identity_twice():
    row = lax.broadcasted_iota(jnp.int32, (64, 128), 0)
    lane = lax.broadcasted_iota(jnp.int32, (64, 128), 1)
    return (row == lane % 64).astype(F32)


def frequencies(freq_ref, sense_ref):
    twice = identity_twice()
    sense2 = sense_ref[...]
    freq2 = jnp.concatenate([freq_ref[...]] * 2, axis=1) * sense2
    total = 0.5 * jnp.sum(freq2, axis=1, keepdims=True)
    pi_row = freq2 / total
    pi_col = 0.5 * jnp.sum(twice * pi_row, axis=1, keepdims=True)
    sense_col = 0.5 * jnp.sum(twice * sense2, axis=1, keepdims=True)
    root_row = jnp.sqrt(jnp.where(sense2 > 0, pi_row, 1.0))
    root_col = jnp.sqrt(jnp.where(sense_col > 0, pi_col, 1.0))
    return twice, pi_row, pi_col, root_row, root_col


def symmetric_table(ex_ref, single_ref, twice):
    ex = ex_ref[...]
    both = ex + ex.T
    return 0.5 * jnp.concatenate([both, both], axis=1) * single_ref[...]


def class_pair(table, nonsyn, omega_ref, pair, twice, pi_row, pi_col):
    mask = low_half()
    omega = jnp.where(mask, omega_ref[2 * pair], omega_ref[2 * pair + 1])
    factor = 1.0 + nonsyn * (omega - 1.0)
    flux = table * factor
    off = flux * pi_row
    row0 = jnp.sum(jnp.where(mask, off, 0.0), axis=1, keepdims=True)
    row1 = jnp.sum(jnp.where(mask, 0.0, off), axis=1, keepdims=True)
    mean0 = jnp.sum(pi_col * row0, axis=0, keepdims=True)
    mean1 = jnp.sum(pi_col * row1, axis=0, keepdims=True)
    rows = jnp.where(mask, row0, row1)
    mean = jnp.where(mask, mean0, mean1)
    return factor, off, rows, mean


def neighbours():
    row = lax.broadcasted_iota(jnp.int32, (64, 128), 0)
    lane = lax.broadcasted_iota(jnp.int32, (64, 128), 1) % 64
    masks = [
        row % 16 == lane % 16,
        (row // 16 == lane // 16) & (row % 4 == lane % 4),
        row // 4 == lane // 4,
    ]
    codon = lax.broadcasted_iota(jnp.int32, (64, 16), 0)
    column = lax.broadcasted_iota(jnp.int32, (64, 16), 1)
    digits = [codon // 16, codon // 4 % 4, codon % 4]
    picks = [(column == 4 * p + digits[p]).astype(F32) for p in range(3)]
    return masks, picks


def coefficients(len_ref, cls_ref, slope):
    lane = lax.broadcasted_iota(jnp.int32, (PAIRS, EDGES), 1)
    row = lax.broadcasted_iota(jnp.int32, (PAIRS, EDGES), 0)
    lengths = len_ref[...] * 0.0625
    classes = cls_ref[...].astype(F32)
    place = lax.broadcasted_iota(jnp.int32, (PAIRS, 128), 1) % 64
    found = []
    for odd in range(2):
        here = lane == 2 * row + odd
        y = jnp.sum(jnp.where(here, lengths, 0.0), axis=1, keepdims=True)
        owner = jnp.sum(jnp.where(here, classes, 0.0), axis=1, keepdims=True)
        current = jnp.ones((PAIRS, 128), F32)
        series = jnp.zeros((PAIRS, 128), F32)
        for k in range(ORDER):
            following = current * y * (1.0 / (k + 1))
            series = jnp.where(place // CLASSES == k, current if slope else following, series)
            current = following
        found.append(jnp.where((place % CLASSES).astype(F32) == owner, series, 0.0))
    return found


def four_left(x):
    high, low = split(x)
    return jnp.concatenate([high, low], axis=1)


def four_right(x):
    high, low = split(x)
    return jnp.concatenate([high, low, high, low], axis=0)


def expand(coefs, dup_ref, store):
    high, low = split(coefs)
    left = jnp.concatenate(
        [jnp.concatenate([high, high], axis=1), jnp.concatenate([low, low], axis=1)], axis=0
    )
    for i in range(0, 64, 2):
        parts = [split(dup_ref[rows_of(i + t), :]) for t in range(2)]
        right = jnp.concatenate([
            jnp.concatenate([spread(parts[0][h]), spread(parts[1][h])], axis=1) for h in range(2)
        ], axis=0)
        both = mxu(left, right)
        both = both[0:64] + both[64:128]
        for t in range(2):
            store(i + t, both[:, 128 * t : 128 * t + 128])


def rows_of(i):
    return pl.ds(STRIDE * i, 64)


def up_kernel(
    states_ref, gap_ref, order_ref,
    ex_ref, freq_ref, omega_ref, len_ref, cls_ref, sense_ref, single_ref, nonsyn_ref,
    top_ref, chain_ref, last_ref, power_ref, dup_ref, fixed_ref,
    message_ref, high_ref, low_ref, leaf_ref, scale_ref, inverse_ref, thin_ref,
    first_ref, up_ref,
):
    subtree = lax.axis_index("branch")
    mask = low_half()
    twice, pi_row, pi_col, root_row, root_col = frequencies(freq_ref, sense_ref)
    table = symmetric_table(ex_ref, single_ref, twice)
    nonsyn = nonsyn_ref[...]
    for at, value in enumerate(
        (pi_row, pi_col, root_row, root_col, 1.0 / root_row, 1.0 / root_col, table)
    ):
        fixed_ref[at] = jnp.broadcast_to(value, (64, 128))

    sites = states_ref.shape[1]
    codon = lax.broadcasted_iota(jnp.int32, (64, sites), 0)
    for p in range(32):
        both = []
        for e in range(2):
            taxon = order_ref[subtree * LEAF_DEV + 2 * p + e]
            state = jnp.where(gap_ref[pl.ds(taxon, 1), :] > 0, -1, states_ref[pl.ds(taxon, 1), :])
            hit = (codon == state) | (state < 0)
            both.append(jnp.where(hit, 1.0, 0.0).astype(BF))
        leaf_ref[p] = jnp.concatenate(both, axis=0)

    powers = []
    for pair in range(CLASSES // 2):
        factor, off, rows, mean = class_pair(
            table, nonsyn, omega_ref, pair, twice, pi_row, pi_col
        )
        powers.append([(table * factor * root_col * root_row - twice * rows) / mean])
    for left, right in ((0, 0), (1, 0), (1, 1), (3, 0), (3, 1), (3, 2), (3, 3)):
        for pair in range(CLASSES // 2):
            powers[pair].append(pair_products((powers[pair][left], powers[pair][right])))
    for pair in range(CLASSES // 2):
        for k in range(ORDER):
            value = powers[pair][k]
            swapped = pltpu.roll(value, 64, 1)
            at = CLASSES * k + 2 * pair
            dup_ref[pl.ds(at, 64, stride=STRIDE), :] = jnp.where(mask, value, swapped)
            dup_ref[pl.ds(at + 1, 64, stride=STRIDE), :] = jnp.where(mask, swapped, value)
            if k < 4:
                power_ref[pair, k] = value

    even, odd = coefficients(len_ref, cls_ref, False)

    def store(i, value):
        first_ref[rows_of(i), :] = value

    expand(jnp.where(low_half(), even, odd), dup_ref, store)

    def squarings(leaves, step, carry):
        width = 16
        held = [first_ref[pl.ds(step * width + j, 64, stride=STRIDE), :] for j in range(width)]
        for level in range(4):
            for j in range(width):
                high, low = split(held[j])
                chain_ref[level, 0, step * width + j] = high
                chain_ref[level, 1, step * width + j] = low
                wide_high, wide_low = spread(high), spread(low)
                held[j] = 2.0 * held[j] + mxu(
                    jnp.concatenate([high, high, low], axis=1),
                    jnp.concatenate([wide_high, wide_low, wide_high], axis=0),
                )
        for j in range(width):
            p = step * width + j
            matrix = inverse_root_col * (held[j] + twice) * root_row
            if leaves:
                side_by_side(thin_ref, p, matrix)
            else:
                last_ref[p - 32] = held[j]
                double(up_ref, p - 32, matrix)
        return carry

    inverse_root_col = 1.0 / root_col
    lax.fori_loop(0, 2, functools.partial(squarings, True), 0)
    lax.fori_loop(2, 4, functools.partial(squarings, False), 0)

    def finish(p, message):
        if p >= 32:
            message_ref[p - 32] = jnp.concatenate(message, axis=0)
        raw = message[0] * message[1]
        scaling = jnp.sum(raw, axis=0, keepdims=True)
        inverse = 1.0 / scaling
        scale_ref[pl.ds(p, 1), :] = scaling
        inverse_ref[pl.ds(p, 1), :] = inverse
        high, low = split(raw * inverse)
        high_ref[p] = high
        low_ref[p] = low

    for p in range(32):
        finish(p, leaf_messages(thin_ref, leaf_ref, p))

    def inner(p):
        child = 2 * p - 64
        return [
            messages(up_ref[child + e], high_ref[child + e], low_ref[child + e]) for e in range(2)
        ]

    for p in range(32, 48):
        finish(p, inner(p))
    for p in range(48, 63):
        finish(p, inner(p))
    high_ref[63] = jnp.zeros((64, sites), BF)
    low_ref[63] = jnp.zeros((64, sites), BF)
    scale_ref[63:64, :] = jnp.ones((1, sites), F32)
    inverse_ref[63:64, :] = jnp.ones((1, sites), F32)
    top = inner(63)
    top_ref[...] = top[0]


def side_kernel(
    dup_ref, last_ref, len_ref, cls_ref, fixed_ref, thin_ref, leaf_ref, omega_ref, single_ref,
    nonsyn_ref,
    slope_ref, matrix_ref, turned_ref, given_ref, class_ref,
):
    twice = identity_twice()
    even, odd = coefficients(len_ref, cls_ref, True)

    def store(i, value):
        slope_ref[64 * i : 64 * i + 64, :] = value

    expand(jnp.where(low_half(), even, odd), dup_ref, store)
    even, odd = coefficients(len_ref, cls_ref, False)
    turned_ref[...] = exact_tn(jnp.where(low_half(), even, odd), twice)
    root_col, inverse_root_row = fixed_ref[3], fixed_ref[4]

    def matrices(step, carry):
        for j in range(8):
            r = step * 8 + j
            double(matrix_ref, r, root_col * (last_ref[r] + twice) * inverse_root_row)
        return carry

    lax.fori_loop(0, 4, matrices, 0)
    pi_row, pi_col, table, single = fixed_ref[0], fixed_ref[1], fixed_ref[6], single_ref[...]
    for pair in range(CLASSES // 2):
        factor, off, rows, mean = class_pair(
            table, nonsyn_ref[...], omega_ref, pair, twice, pi_row, pi_col
        )
        class_ref[pair, 0] = (off - twice * rows) / mean
        class_ref[pair, 1] = pi_row / mean
        class_ref[pair, 2] = factor * single
    for p in range(32):
        given_ref[p] = jnp.concatenate(leaf_messages(thin_ref, leaf_ref, p), axis=0)


def down_kernel(total_sites, members, *refs):
    tops = refs[:members]
    (
        matrix_ref, given_ref, message_ref, high_ref, low_ref, leaf_ref, scale_ref, inverse_ref,
        chain_ref, turned_ref, slope_ref, power_ref, fixed_ref,
        class_ref, weights_ref, nonsyn_ref,
        out_ref,
        a_high_ref, a_low_ref, count_ref, back_ref, bins_ref,
    ) = refs[members:]
    subtree = lax.axis_index("branch")
    mask = low_half()
    twice = identity_twice()
    pi_row, pi_col, root_row, root_col, inverse_root_row, inverse_root_col = [
        fixed_ref[at] for at in range(6)
    ]
    sites = weights_ref.shape[1]
    weight = weights_ref[...].astype(F32)

    above = jnp.broadcast_to(pi_col[:, 0:1], (64, sites))
    for other in tops[1:]:
        above = above * other[...]
    own = tops[0][...]
    likelihood = jnp.sum(above * own, axis=0, keepdims=True)
    logs = jnp.sum(jnp.log(scale_ref[...]), axis=0, keepdims=True)
    logs = logs + jnp.where(subtree == 0, jnp.log(likelihood), 0.0)
    log_part = jnp.sum(weight * logs, axis=1, keepdims=True)
    high, low = split(above * (weight / (likelihood * total_sites)))
    a_high_ref[31, 0:64, :] = high
    a_low_ref[31, 0:64, :] = low
    a_high_ref[31, 64:128, :] = jnp.zeros((64, sites), BF)
    a_low_ref[31, 64:128, :] = jnp.zeros((64, sites), BF)

    def store_counts(p, square):
        counts = jnp.where(mask, square[0:64], square[64:128])
        count_ref[p] = inverse_root_col * counts * root_row

    def descend(r):
        a_high, a_low = a_high_ref[r - 32], a_low_ref[r - 32]
        child = 2 * r - 64
        u_high = jnp.concatenate([high_ref[child], high_ref[child + 1]], axis=0)
        u_low = jnp.concatenate([low_ref[child], low_ref[child + 1]], axis=0)
        four = mxu_nt(
            jnp.concatenate([a_high, a_low], axis=0), jnp.concatenate([u_high, u_low], axis=0)
        )
        store_counts(r, four[0:128, 0:128] + four[0:128, 128:256] + four[128:256, 0:128])
        return [
            messages(
                matrix_ref[2 * (r - 32) + e], a_high[64 * e : 64 * e + 64], a_low[64 * e : 64 * e + 64]
            )
            for e in range(2)
        ]

    def children(down, e, p):
        vector = down[e]
        inverse = inverse_ref[pl.ds(p, 1), :]
        message = message_ref[p - 32] if p >= 32 else given_ref[p]
        pair = jnp.concatenate(
            [vector * message[64:128] * inverse, vector * message[0:64] * inverse], axis=0
        )
        return split(pair)

    def inner(r):
        down = descend(r)
        for e in range(2):
            p = 2 * r + e - 64
            if isinstance(p, int) and p == 63:
                continue
            high, low = children(down, e, p)
            a_high_ref[p - 32] = high
            a_low_ref[p - 32] = low

    for r in range(63, 47, -1):
        inner(r)

    for r in range(47, 31, -1):
        down = descend(r)
        for e in range(2):
            p = 2 * r + e - 64
            high, low = children(down, e, p)
            square = mxu_nt(jnp.concatenate([high, low], axis=0), leaf_ref[p])
            store_counts(p, square[0:128] + square[128:256])

    def adjoint(step, carry):
        held = [count_ref[step * 16 + j] for j in range(16)]
        for level in range(3, -1, -1):
            for j in range(16):
                high, low = split(held[j])
                e_high, e_low = chain_ref[level, 0, step * 16 + j], chain_ref[level, 1, step * 16 + j]
                left = jnp.concatenate([
                    jnp.concatenate([high, e_high], axis=1),
                    jnp.concatenate([low, e_low], axis=1),
                ], axis=0)
                right = jnp.concatenate([
                    jnp.concatenate([spread(e_high), spread(e_low)], axis=1),
                    jnp.concatenate([spread(high), spread(low)], axis=1),
                ], axis=0)
                four = mxu(left, right)
                held[j] = 2.0 * held[j] + (
                    four[0:64, 0:128] + four[0:64, 128:256] + four[64:128, 0:128]
                )
        for j in range(16):
            back_ref[pl.ds(step * 16 + j, 64, stride=STRIDE), :] = held[j]
        return carry

    lax.fori_loop(0, PAIRS // 16, adjoint, 0)

    left = four_left(turned_ref[...])

    total = jnp.zeros((64, 128), F32)
    for i in range(0, 64, 2):
        values = [back_ref[rows_of(i + t), :] for t in range(2)]
        both = mxu(left, four_right(jnp.concatenate(values, axis=1)))
        for t in range(2):
            total = total + values[t] * slope_ref[64 * (i + t) : 64 * (i + t) + 64, :]
            here = both[:, 128 * t : 128 * t + 128]
            bins_ref[rows_of(i + t), :] = jnp.where(mask, here[0:64], here[64:128])
    slopes = total * 0.0625

    ratio_table = fixed_ref[6] * nonsyn_ref[...]
    half = lax.broadcasted_iota(jnp.int32, (1, 128), 1) < 64
    row = lax.broadcasted_iota(jnp.int32, (64, 128), 0)
    lane = lax.broadcasted_iota(jnp.int32, (64, 128), 1)
    table_grad = jnp.zeros((64, 128), F32)
    omega_row = jnp.zeros((1, 128), F32)
    lane_row = lax.broadcasted_iota(jnp.int32, (1, 128), 1)
    for pair in range(CLASSES // 2):
        grads = []
        for k in range(ORDER):
            at = CLASSES * k + 2 * pair
            first = bins_ref[pl.ds(at, 64, stride=STRIDE), :]
            second = bins_ref[pl.ds(at + 1, 64, stride=STRIDE), :]
            first = first + pltpu.roll(first, 64, 1)
            second = second + pltpu.roll(second, 64, 1)
            grads.append(jnp.where(mask, first, second))
        g1, g2, g3, g4, g5, g6, g7, g8 = grads
        a1, a2, a3, a4 = [power_ref[pair, k] for k in range(4)]
        g4 = g4 + pair_products((g8, a4), (a4, g8), (g7, a3), (g6, a2), (g5, a1))
        g3 = g3 + pair_products((a4, g7))
        g2 = g2 + pair_products((a4, g6))
        g1 = g1 + pair_products((a4, g5))
        g2 = g2 + pair_products((g4, a2), (a2, g4), (g3, a1))
        g1 = g1 + pair_products((a2, g3))
        g1 = g1 + pair_products((g2, a1), (a1, g2))
        rate, pi_mean, factor = [class_ref[pair, at] for at in range(3)]
        d_rate = root_col * g1 * inverse_root_row
        weighted = jnp.sum(d_rate * rate, axis=0, keepdims=True)
        total0 = jnp.sum(jnp.where(half, weighted, 0.0), axis=1, keepdims=True)
        total1 = jnp.sum(jnp.where(half, 0.0, weighted), axis=1, keepdims=True)
        diagonal = d_rate * twice
        diag0 = jnp.sum(jnp.where(mask, diagonal, 0.0), axis=1, keepdims=True)
        diag1 = jnp.sum(jnp.where(mask, 0.0, diagonal), axis=1, keepdims=True)
        row_grad = jnp.where(mask, diag0, diag1) + pi_col * jnp.where(half, total0, total1)
        flux_grad = (d_rate - row_grad) * pi_mean
        table_grad = table_grad + flux_grad * factor
        ratio = jnp.sum(flux_grad * ratio_table, axis=0, keepdims=True)
        ratio0 = jnp.sum(jnp.where(half, ratio, 0.0), axis=1, keepdims=True)
        ratio1 = jnp.sum(jnp.where(half, 0.0, ratio), axis=1, keepdims=True)
        omega_row = jnp.where(lane_row == 2 * pair, ratio0, omega_row)
        omega_row = jnp.where(lane_row == 2 * pair + 1, ratio1, omega_row)
    table_grad = table_grad + pltpu.roll(table_grad, 64, 1)
    masks, picks = neighbours()
    codon = lax.broadcasted_iota(jnp.int32, (16, 128), 1)
    column = lax.broadcasted_iota(jnp.int32, (16, 128), 0)
    lefts, rights = [], []
    for p, digit in enumerate((codon // 16, codon // 4 % 4, codon % 4)):
        left = jnp.where((column == 4 * p + digit) & (codon < 64), 1.0, 0.0).astype(BF)
        for part in split(jnp.where(masks[p], 0.5 * table_grad, 0.0)):
            lefts.append(left)
            rights.append(part)
    packed = mxu(
        jnp.concatenate(lefts, axis=1),
        jnp.concatenate([jnp.concatenate([part, jnp.zeros_like(part)], axis=0) for part in rights], axis=0),
    )
    turned = mxu_nt(
        jnp.concatenate(lefts, axis=1),
        jnp.concatenate([
            jnp.concatenate([part, jnp.zeros_like(part)], axis=0) for part in rights
        ], axis=1),
    )
    packed = packed + turned
    packed = jnp.where(lax.broadcasted_iota(jnp.int32, (16, 128), 1) < 64, packed, 0.0)

    even = jnp.sum(jnp.where(mask, slopes, 0.0), axis=1, keepdims=True)
    other = jnp.sum(jnp.where(mask, 0.0, slopes), axis=1, keepdims=True)
    placed = jnp.where(lane == 2 * row, even, 0.0) + jnp.where(lane == 2 * row + 1, other, 0.0)
    length_row = jnp.sum(placed, axis=0, keepdims=True)
    line = lax.broadcasted_iota(jnp.int32, out_ref.shape, 0)
    omega_row = jnp.where(lane_row == CLASSES, log_part, omega_row)
    omega_row = pltpu.roll(jnp.broadcast_to(omega_row, (8, 128)), 64, 1)[0:1]
    packed = packed + jnp.where(line == 0, omega_row, 0.0)
    out_ref[...] = packed + jnp.where(line == 12 + subtree, length_row, 0.0)


def last_kernel(total_sites, count, *refs):
    members = lax.axis_size("branch")
    subtree = lax.axis_index("branch")
    exch_ref, omega_ref, length_ref, log_ref = refs[count:]
    total = tree_sum([ref[...] for ref in refs[:count]])
    masks, picks = neighbours()
    table = jnp.zeros((64, 128), F32)
    for at_position, pick in zip(masks, picks):
        table = table + jnp.where(at_position, exact(pick, total), 0.0)
    exch_ref[...] = table[:, 0:64]
    moved = pltpu.roll(total[0:8], 64, 1)
    omega_ref[...] = moved[0:1, 0:CLASSES]
    line = lax.broadcasted_iota(jnp.int32, total.shape, 0)
    lengths = jnp.sum(jnp.where(line == 12 + subtree, total, 0.0), axis=0, keepdims=True)
    length_ref[...] = lengths[:, 0:EDGES]
    log_ref[...] = moved[0:1, CLASSES : CLASSES + 1] / total_sites / (LEAF_DEV * members)


def partners(x, axis, start, radix):
    size = lax.axis_size(axis)
    others = [
        lax.ppermute(x, axis, [(i, i ^ (step * start)) for i in range(size)])
        for step in range(1, radix)
    ]
    return [x] + others


def tree_sum(parts):
    while len(parts) > 1:
        parts = [parts[i] + parts[i + 1] for i in range(0, len(parts), 2)]
    return parts[0]


def sum_stages(x, members, sites):
    stages, start = [], 1
    while start < sites:
        radix = 2 if sites // start in (2, 8) else 4
        stages.append((members * start, radix, 1))
        start *= radix
    stages.append((1, members, 0))
    parts = [x]
    for start, radix, flip in stages[::-1]:
        x = tree_sum(parts)
        parts = [x] + [
            lax.ppermute(x, ("site", "branch"), [
                (i, i ^ (step * start + flip)) for i in range(sites * members)
            ])
            for step in range(1, radix)
        ]
    return parts


def body(
    total_sites, states, gap_mask, weights, leaf_order, exchanges, codon_freq, omega_ratio,
    lengths, classes,
):
    sites = states.shape[1]
    members = lax.axis_size("branch")
    sense, single, nonsyn = codon_tables()
    vmem = pl.BlockSpec(memory_space=pltpu.VMEM)
    smem = pl.BlockSpec(memory_space=pltpu.SMEM)
    shape = jax.ShapeDtypeStruct
    held = pltpu.VMEM
    limit = pltpu.CompilerParams(vmem_limit_bytes=20 * 2**20)

    def outside(x):
        return pltpu.with_memory_space_constraint(x, pltpu.HBM)

    def inside(xs):
        return [pltpu.with_memory_space_constraint(x, pltpu.VMEM) for x in xs]

    sense2 = outside(jnp.asarray(np.tile(sense[None, :], (1, 2))))
    single2 = outside(jnp.asarray(np.tile(single, (1, 2))))
    nonsyn2 = outside(jnp.asarray(np.tile(nonsyn, (1, 2))))
    freq = outside(codon_freq.reshape(1, 64))
    span, owner = outside(lengths.reshape(1, EDGES)), outside(classes.reshape(1, EDGES))
    table, omega = outside(exchanges), outside(omega_ratio)

    top, *kept = pl.pallas_call(
        up_kernel,
        out_shape=[
            shape((64, sites), F32),
            held((4, 2, PAIRS, 64, 128), BF),
            held((PAIRS // 2, 64, 128), F32),
            held((CLASSES // 2, 4, 64, 128), F32),
            held((STRIDE * 64, 128), F32),
            held((7, 64, 128), F32),
            held((PAIRS // 2, 128, sites), F32),
            held((64, 64, sites), BF),
            held((64, 64, sites), BF),
            held((32, 128, sites), BF),
            held((64, sites), F32),
            held((64, sites), F32),
            held((PAIRS, 64, 128), BF),
        ],
        in_specs=[vmem, vmem, smem, vmem, vmem, smem] + [vmem] * 5,
        out_specs=[vmem] * 13,
        scratch_shapes=[
            pltpu.VMEM((STRIDE * 64, 128), F32),
            pltpu.VMEM((PAIRS, 64, 256), BF),
        ],
        compiler_params=limit,
        name="up",
    )(
        outside(states), outside(gap_mask), outside(leaf_order),
        table, freq, omega, span, owner, sense2, single2, nonsyn2,
    )
    (
        chain, last, powers, dup, fixed, message, high, low, leaf, scale, inverse, thin,
    ) = inside(kept)
    tops = partners(top, "branch", 1, members)
    slope, matrix, turned, given, table_of = inside(pl.pallas_call(
        side_kernel,
        out_shape=[
            held((PAIRS * 64, 128), F32),
            held((64, 64, 256), BF),
            held((128, 128), F32),
            held((PAIRS // 2, 128, sites), F32),
            held((CLASSES // 2, 3, 64, 128), F32),
        ],
        in_specs=[vmem] * 7 + [smem, vmem, vmem],
        out_specs=[vmem] * 5,
        compiler_params=limit,
        name="side",
    )(dup, last, span, owner, fixed, thin, leaf, omega, single2, nonsyn2))
    part = pl.pallas_call(
        functools.partial(down_kernel, total_sites, members),
        out_shape=shape((16, 128), F32),
        in_specs=[vmem] * (16 + members),
        out_specs=vmem,
        scratch_shapes=[
            pltpu.VMEM((32, 128, sites), BF),
            pltpu.VMEM((32, 128, sites), BF),
            pltpu.VMEM((PAIRS, 64, 128), F32),
            pltpu.VMEM((STRIDE * 64, 128), F32),
            pltpu.VMEM((STRIDE * 64, 128), F32),
        ],
        compiler_params=limit,
        name="down",
    )(
        *tops, matrix, given, message, high, low, leaf, scale, inverse,
        chain, turned, slope, powers, fixed,
        table_of, outside(weights.reshape(1, sites)), nonsyn2,
    )
    parts = sum_stages(part, members, lax.axis_size("site"))
    exch, ratio, length, loglik = pl.pallas_call(
        functools.partial(last_kernel, total_sites, len(parts)),
        out_shape=[shape((64, 64), F32), shape((1, CLASSES), F32), shape((1, EDGES), F32), shape((1, 1), F32)],
        in_specs=[vmem] * len(parts),
        out_specs=[vmem] * 4,
        compiler_params=limit,
        name="last",
    )(*parts)
    return (exch, ratio.reshape(CLASSES), length.reshape(EDGES), loglik.reshape(()))


def solution(mesh):
    def whole(states, *rest):
        total_sites = states.shape[1]
        return jax.shard_map(
            functools.partial(body, total_sites),
            mesh=mesh,
            in_specs=(
                P(None, "site"),
                P(None, "site"),
                P("site"),
                P(),
                P(),
                P(),
                P(),
                P("branch"),
                P("branch"),
            ),
            out_specs=(P(), P(), P("branch"), P()),
            check_vma=False,
        )(states, *rest)

    return whole
```

```python
import functools
import jax
import jax.numpy as jnp
import numpy as np
from jax import lax
from jax.experimental import pallas as pl
from jax.experimental.pallas import tpu as pltpu
from jax.sharding import PartitionSpec as P

LEAF_DEV = 64
EDGES = 127
PAIRS = 64
CLASSES = 8
ORDER = 8
STRIDE = 65
BF = jnp.bfloat16
F32 = jnp.float32

CODE_TABLE = "FFLLSSSSYYXXCCXWLLLLPPPPHHQQRRRRIIIMTTTTNNKKSSRRVVVVAAAADDEEGGGG"


def codon_tables():
    amino_acid = np.array(list(CODE_TABLE))
    codon_index = np.arange(64)
    digits = np.stack([codon_index // 16, codon_index // 4 % 4, codon_index % 4], 1)
    differ = (digits[:, None, :] != digits[None, :, :]).sum(-1)
    is_sense = amino_acid != "X"
    single = (differ == 1) & is_sense[:, None] & is_sense[None, :]
    nonsyn = single & (amino_acid[:, None] != amino_acid[None, :])
    return (is_sense.astype(np.float32), single.astype(np.float32), nonsyn.astype(np.float32))


def low_half():
    return lax.broadcasted_iota(jnp.int32, (64, 128), 1) < 64


def split(x):
    high = x.astype(BF)
    low = (x - high.astype(F32)).astype(BF)
    return high, low


def spread(x, scale=1.0):
    mask = low_half()
    low = jnp.where(mask, scale, 0.0).astype(x.dtype)
    high = jnp.where(mask, 0.0, scale).astype(x.dtype)
    return jnp.concatenate([x * low, x * high], axis=0)


def mxu(left, right):
    return jnp.dot(left, right, preferred_element_type=F32)


def mxu_nt(left, right):
    return lax.dot_general(left, right, (((1,), (1,)), ((), ())), preferred_element_type=F32)


def exact(left, right):
    return jnp.dot(left, right, preferred_element_type=F32, precision=lax.Precision.HIGHEST)


def exact_tn(left, right):
    return lax.dot_general(
        left, right, (((0,), (0,)), ((), ())), preferred_element_type=F32,
        precision=lax.Precision.HIGHEST,
    )


def pair_products(*terms):
    lefts, rights = [], []
    for left, right in terms:
        left_high, left_low = split(left)
        right_high, right_low = split(right)
        wide_high, wide_low = spread(right_high), spread(right_low)
        lefts += [left_high, left_high, left_low]
        rights += [wide_high, wide_low, wide_high]
    return mxu(jnp.concatenate(lefts, axis=1), jnp.concatenate(rights, axis=0))


def messages(matrix, high, low):
    return mxu(matrix, jnp.concatenate([high, low, high, low], axis=0))


def leaf_messages(thin_ref, leaf_ref, p):
    found = []
    for e in range(2):
        vector = leaf_ref[p, 64 * e : 64 * e + 64, :]
        found.append(mxu(thin_ref[2 * p + e], jnp.concatenate([vector, vector], axis=0)))
    return found


def doubled(x):
    mask = low_half()
    swapped = pltpu.roll(x, 64, 1)
    return jnp.where(mask, x, swapped), jnp.where(mask, swapped, x)


def double(ref, p, x):
    for e, both in enumerate(doubled(x)):
        high, low = split(both)
        ref[2 * p + e] = jnp.concatenate([high, low], axis=1)


def side_by_side(ref, p, x):
    for e, both in enumerate(doubled(x)):
        rest = both - both.astype(BF).astype(F32)
        ref[2 * p + e] = jnp.where(low_half(), both, rest).astype(BF)


def identity_twice():
    row = lax.broadcasted_iota(jnp.int32, (64, 128), 0)
    lane = lax.broadcasted_iota(jnp.int32, (64, 128), 1)
    return (row == lane % 64).astype(F32)


def frequencies(freq_ref, sense_ref):
    twice = identity_twice()
    sense2 = sense_ref[...]
    freq2 = jnp.concatenate([freq_ref[...]] * 2, axis=1) * sense2
    total = 0.5 * jnp.sum(freq2, axis=1, keepdims=True)
    pi_row = freq2 / total
    pi_col = 0.5 * jnp.sum(twice * pi_row, axis=1, keepdims=True)
    sense_col = 0.5 * jnp.sum(twice * sense2, axis=1, keepdims=True)
    root_row = jnp.sqrt(jnp.where(sense2 > 0, pi_row, 1.0))
    root_col = jnp.sqrt(jnp.where(sense_col > 0, pi_col, 1.0))
    return twice, pi_row, pi_col, root_row, root_col


def symmetric_table(ex_ref, single_ref, twice):
    ex = ex_ref[...]
    both = ex + ex.T
    return 0.5 * jnp.concatenate([both, both], axis=1) * single_ref[...]


def class_pair(table, nonsyn, omega_ref, pair, twice, pi_row, pi_col):
    mask = low_half()
    omega = jnp.where(mask, omega_ref[2 * pair], omega_ref[2 * pair + 1])
    factor = 1.0 + nonsyn * (omega - 1.0)
    flux = table * factor
    off = flux * pi_row
    row0 = jnp.sum(jnp.where(mask, off, 0.0), axis=1, keepdims=True)
    row1 = jnp.sum(jnp.where(mask, 0.0, off), axis=1, keepdims=True)
    mean0 = jnp.sum(pi_col * row0, axis=0, keepdims=True)
    mean1 = jnp.sum(pi_col * row1, axis=0, keepdims=True)
    rows = jnp.where(mask, row0, row1)
    mean = jnp.where(mask, mean0, mean1)
    return factor, off, rows, mean


def neighbours():
    row = lax.broadcasted_iota(jnp.int32, (64, 128), 0)
    lane = lax.broadcasted_iota(jnp.int32, (64, 128), 1) % 64
    masks = [
        row % 16 == lane % 16,
        (row // 16 == lane // 16) & (row % 4 == lane % 4),
        row // 4 == lane // 4,
    ]
    codon = lax.broadcasted_iota(jnp.int32, (64, 16), 0)
    column = lax.broadcasted_iota(jnp.int32, (64, 16), 1)
    digits = [codon // 16, codon // 4 % 4, codon % 4]
    picks = [(column == 4 * p + digits[p]).astype(F32) for p in range(3)]
    return masks, picks


def coefficients(len_ref, cls_ref, slope):
    lane = lax.broadcasted_iota(jnp.int32, (PAIRS, EDGES), 1)
    row = lax.broadcasted_iota(jnp.int32, (PAIRS, EDGES), 0)
    lengths = len_ref[...] * 0.0625
    classes = cls_ref[...].astype(F32)
    place = lax.broadcasted_iota(jnp.int32, (PAIRS, 128), 1) % 64
    found = []
    for odd in range(2):
        here = lane == 2 * row + odd
        y = jnp.sum(jnp.where(here, lengths, 0.0), axis=1, keepdims=True)
        owner = jnp.sum(jnp.where(here, classes, 0.0), axis=1, keepdims=True)
        current = jnp.ones((PAIRS, 128), F32)
        series = jnp.zeros((PAIRS, 128), F32)
        for k in range(ORDER):
            following = current * y * (1.0 / (k + 1))
            series = jnp.where(place // CLASSES == k, current if slope else following, series)
            current = following
        found.append(jnp.where((place % CLASSES).astype(F32) == owner, series, 0.0))
    return found


def four_left(x):
    high, low = split(x)
    return jnp.concatenate([high, low], axis=1)


def four_right(x):
    high, low = split(x)
    return jnp.concatenate([high, low, high, low], axis=0)


def expand(coefs, dup_ref, store):
    high, low = split(coefs)
    left = jnp.concatenate(
        [jnp.concatenate([high, high], axis=1), jnp.concatenate([low, low], axis=1)], axis=0
    )
    for i in range(0, 64, 2):
        parts = [split(dup_ref[rows_of(i + t), :]) for t in range(2)]
        right = jnp.concatenate([
            jnp.concatenate([spread(parts[0][h]), spread(parts[1][h])], axis=1) for h in range(2)
        ], axis=0)
        both = mxu(left, right)
        both = both[0:64] + both[64:128]
        for t in range(2):
            store(i + t, both[:, 128 * t : 128 * t + 128])


def rows_of(i):
    return pl.ds(STRIDE * i, 64)


def up_kernel(
    states_ref, gap_ref, order_ref,
    ex_ref, freq_ref, omega_ref, len_ref, cls_ref, sense_ref, single_ref, nonsyn_ref,
    top_ref, chain_ref, last_ref, power_ref, dup_ref, fixed_ref,
    message_ref, high_ref, low_ref, leaf_ref, scale_ref, inverse_ref, thin_ref,
    first_ref, up_ref,
):
    subtree = lax.axis_index("branch")
    mask = low_half()
    twice, pi_row, pi_col, root_row, root_col = frequencies(freq_ref, sense_ref)
    table = symmetric_table(ex_ref, single_ref, twice)
    nonsyn = nonsyn_ref[...]
    for at, value in enumerate(
        (pi_row, pi_col, root_row, root_col, 1.0 / root_row, 1.0 / root_col, table)
    ):
        fixed_ref[at] = jnp.broadcast_to(value, (64, 128))

    sites = states_ref.shape[1]
    codon = lax.broadcasted_iota(jnp.int32, (64, sites), 0)
    for p in range(32):
        both = []
        for e in range(2):
            taxon = order_ref[subtree * LEAF_DEV + 2 * p + e]
            state = jnp.where(gap_ref[pl.ds(taxon, 1), :] > 0, -1, states_ref[pl.ds(taxon, 1), :])
            hit = (codon == state) | (state < 0)
            both.append(jnp.where(hit, 1.0, 0.0).astype(BF))
        leaf_ref[p] = jnp.concatenate(both, axis=0)

    powers = []
    for pair in range(CLASSES // 2):
        factor, off, rows, mean = class_pair(
            table, nonsyn, omega_ref, pair, twice, pi_row, pi_col
        )
        powers.append([(table * factor * root_col * root_row - twice * rows) / mean])
    for left, right in ((0, 0), (1, 0), (1, 1), (3, 0), (3, 1), (3, 2), (3, 3)):
        for pair in range(CLASSES // 2):
            powers[pair].append(pair_products((powers[pair][left], powers[pair][right])))
    for pair in range(CLASSES // 2):
        for k in range(ORDER):
            value = powers[pair][k]
            swapped = pltpu.roll(value, 64, 1)
            at = CLASSES * k + 2 * pair
            dup_ref[pl.ds(at, 64, stride=STRIDE), :] = jnp.where(mask, value, swapped)
            dup_ref[pl.ds(at + 1, 64, stride=STRIDE), :] = jnp.where(mask, swapped, value)
            if k < 4:
                power_ref[pair, k] = value

    even, odd = coefficients(len_ref, cls_ref, False)

    def store(i, value):
        first_ref[rows_of(i), :] = value

    expand(jnp.where(low_half(), even, odd), dup_ref, store)

    def squarings(step):
        leaves = step < 2
        width = 16
        held = [first_ref[pl.ds(step * width + j, 64, stride=STRIDE), :] for j in range(width)]
        for level in range(4):
            for j in range(width):
                high, low = split(held[j])
                chain_ref[level, 0, step * width + j] = high
                chain_ref[level, 1, step * width + j] = low
                wide_high, wide_low = spread(high), spread(low)
                held[j] = 2.0 * held[j] + mxu(
                    jnp.concatenate([high, high, low], axis=1),
                    jnp.concatenate([wide_high, wide_low, wide_high], axis=0),
                )
        for j in range(width):
            p = step * width + j
            matrix = inverse_root_col * (held[j] + twice) * root_row
            if leaves:
                side_by_side(thin_ref, p, matrix)
            else:
                last_ref[p - 32] = held[j]
                double(up_ref, p - 32, matrix)

    inverse_root_col = 1.0 / root_col
    squarings(0)
    squarings(1)

    def finish(p, message):
        if p >= 32:
            message_ref[p - 32] = jnp.concatenate(message, axis=0)
        raw = message[0] * message[1]
        scaling = jnp.sum(raw, axis=0, keepdims=True)
        inverse = 1.0 / scaling
        scale_ref[pl.ds(p, 1), :] = scaling
        inverse_ref[pl.ds(p, 1), :] = inverse
        high, low = split(raw * inverse)
        high_ref[p] = high
        low_ref[p] = low

    for p in range(16):
        finish(p, leaf_messages(thin_ref, leaf_ref, p))
    squarings(2)
    for p in range(16, 32):
        finish(p, leaf_messages(thin_ref, leaf_ref, p))
    squarings(3)

    def inner(p):
        child = 2 * p - 64
        return [
            messages(up_ref[child + e], high_ref[child + e], low_ref[child + e]) for e in range(2)
        ]

    for p in range(32, 48):
        finish(p, inner(p))
    for p in range(48, 63):
        finish(p, inner(p))
    high_ref[63] = jnp.zeros((64, sites), BF)
    low_ref[63] = jnp.zeros((64, sites), BF)
    scale_ref[63:64, :] = jnp.ones((1, sites), F32)
    inverse_ref[63:64, :] = jnp.ones((1, sites), F32)
    top = inner(63)
    top_ref[...] = top[0]


def side_kernel(
    dup_ref, last_ref, len_ref, cls_ref, fixed_ref, thin_ref, leaf_ref, omega_ref, single_ref,
    nonsyn_ref,
    slope_ref, matrix_ref, turned_ref, given_ref, class_ref,
):
    twice = identity_twice()
    even, odd = coefficients(len_ref, cls_ref, True)

    def store(i, value):
        slope_ref[64 * i : 64 * i + 64, :] = value

    expand(jnp.where(low_half(), even, odd), dup_ref, store)
    even, odd = coefficients(len_ref, cls_ref, False)
    turned_ref[...] = exact_tn(jnp.where(low_half(), even, odd), twice)
    root_col, inverse_root_row = fixed_ref[3], fixed_ref[4]

    def matrices(step, carry):
        for j in range(8):
            r = step * 8 + j
            double(matrix_ref, r, root_col * (last_ref[r] + twice) * inverse_root_row)
        return carry

    lax.fori_loop(0, 4, matrices, 0)
    pi_row, pi_col, table, single = fixed_ref[0], fixed_ref[1], fixed_ref[6], single_ref[...]
    for pair in range(CLASSES // 2):
        factor, off, rows, mean = class_pair(
            table, nonsyn_ref[...], omega_ref, pair, twice, pi_row, pi_col
        )
        class_ref[pair, 0] = (off - twice * rows) / mean
        class_ref[pair, 1] = pi_row / mean
        class_ref[pair, 2] = factor * single
    for p in range(32):
        given_ref[p] = jnp.concatenate(leaf_messages(thin_ref, leaf_ref, p), axis=0)


def down_kernel(total_sites, members, *refs):
    tops = refs[:members]
    (
        matrix_ref, given_ref, message_ref, high_ref, low_ref, leaf_ref, scale_ref, inverse_ref,
        chain_ref, turned_ref, slope_ref, power_ref, fixed_ref,
        class_ref, weights_ref, nonsyn_ref,
        out_ref,
        a_high_ref, a_low_ref, count_ref, back_ref, bins_ref,
    ) = refs[members:]
    subtree = lax.axis_index("branch")
    mask = low_half()
    twice = identity_twice()
    pi_row, pi_col, root_row, root_col, inverse_root_row, inverse_root_col = [
        fixed_ref[at] for at in range(6)
    ]
    sites = weights_ref.shape[1]
    weight = weights_ref[...].astype(F32)

    above = jnp.broadcast_to(pi_col[:, 0:1], (64, sites))
    for other in tops[1:]:
        above = above * other[...]
    own = tops[0][...]
    likelihood = jnp.sum(above * own, axis=0, keepdims=True)
    logs = jnp.sum(jnp.log(scale_ref[...]), axis=0, keepdims=True)
    logs = logs + jnp.where(subtree == 0, jnp.log(likelihood), 0.0)
    log_part = jnp.sum(weight * logs, axis=1, keepdims=True)
    high, low = split(above * (weight / (likelihood * total_sites)))
    a_high_ref[31, 0:64, :] = high
    a_low_ref[31, 0:64, :] = low
    a_high_ref[31, 64:128, :] = jnp.zeros((64, sites), BF)
    a_low_ref[31, 64:128, :] = jnp.zeros((64, sites), BF)

    def store_counts(p, square):
        counts = jnp.where(mask, square[0:64], square[64:128])
        count_ref[p] = inverse_root_col * counts * root_row

    def descend(r):
        a_high, a_low = a_high_ref[r - 32], a_low_ref[r - 32]
        child = 2 * r - 64
        u_high = jnp.concatenate([high_ref[child], high_ref[child + 1]], axis=0)
        u_low = jnp.concatenate([low_ref[child], low_ref[child + 1]], axis=0)
        four = mxu_nt(
            jnp.concatenate([a_high, a_low], axis=0), jnp.concatenate([u_high, u_low], axis=0)
        )
        store_counts(r, four[0:128, 0:128] + four[0:128, 128:256] + four[128:256, 0:128])
        return [
            messages(
                matrix_ref[2 * (r - 32) + e], a_high[64 * e : 64 * e + 64], a_low[64 * e : 64 * e + 64]
            )
            for e in range(2)
        ]

    def children(down, e, p):
        vector = down[e]
        inverse = inverse_ref[pl.ds(p, 1), :]
        message = message_ref[p - 32] if p >= 32 else given_ref[p]
        pair = jnp.concatenate(
            [vector * message[64:128] * inverse, vector * message[0:64] * inverse], axis=0
        )
        return split(pair)

    def inner(r):
        down = descend(r)
        for e in range(2):
            p = 2 * r + e - 64
            if isinstance(p, int) and p == 63:
                continue
            high, low = children(down, e, p)
            a_high_ref[p - 32] = high
            a_low_ref[p - 32] = low

    def adjoint(step):
        held = [count_ref[step * 16 + j] for j in range(16)]
        for level in range(3, -1, -1):
            for j in range(16):
                high, low = split(held[j])
                e_high, e_low = chain_ref[level, 0, step * 16 + j], chain_ref[level, 1, step * 16 + j]
                left = jnp.concatenate([
                    jnp.concatenate([high, e_high], axis=1),
                    jnp.concatenate([low, e_low], axis=1),
                ], axis=0)
                right = jnp.concatenate([
                    jnp.concatenate([spread(e_high), spread(e_low)], axis=1),
                    jnp.concatenate([spread(high), spread(low)], axis=1),
                ], axis=0)
                four = mxu(left, right)
                held[j] = 2.0 * held[j] + (
                    four[0:64, 0:128] + four[0:64, 128:256] + four[64:128, 0:128]
                )
        for j in range(16):
            back_ref[pl.ds(step * 16 + j, 64, stride=STRIDE), :] = held[j]

    def outer(r):
        down = descend(r)
        for e in range(2):
            p = 2 * r + e - 64
            high, low = children(down, e, p)
            square = mxu_nt(jnp.concatenate([high, low], axis=0), leaf_ref[p])
            store_counts(p, square[0:128] + square[128:256])

    for r in range(63, 47, -1):
        inner(r)
    for r in range(47, 39, -1):
        outer(r)
    adjoint(3)
    for r in range(39, 31, -1):
        outer(r)
    for step in (1, 2, 0):
        adjoint(step)

    left = four_left(turned_ref[...])

    total = jnp.zeros((64, 128), F32)
    for i in range(0, 64, 2):
        values = [back_ref[rows_of(i + t), :] for t in range(2)]
        both = mxu(left, four_right(jnp.concatenate(values, axis=1)))
        for t in range(2):
            total = total + values[t] * slope_ref[64 * (i + t) : 64 * (i + t) + 64, :]
            here = both[:, 128 * t : 128 * t + 128]
            bins_ref[rows_of(i + t), :] = jnp.where(mask, here[0:64], here[64:128])
    slopes = total * 0.0625

    ratio_table = fixed_ref[6] * nonsyn_ref[...]
    half = lax.broadcasted_iota(jnp.int32, (1, 128), 1) < 64
    row = lax.broadcasted_iota(jnp.int32, (64, 128), 0)
    lane = lax.broadcasted_iota(jnp.int32, (64, 128), 1)
    table_grad = jnp.zeros((64, 128), F32)
    omega_row = jnp.zeros((1, 128), F32)
    lane_row = lax.broadcasted_iota(jnp.int32, (1, 128), 1)
    for pair in range(CLASSES // 2):
        grads = []
        for k in range(ORDER):
            at = CLASSES * k + 2 * pair
            first = bins_ref[pl.ds(at, 64, stride=STRIDE), :]
            second = bins_ref[pl.ds(at + 1, 64, stride=STRIDE), :]
            first = first + pltpu.roll(first, 64, 1)
            second = second + pltpu.roll(second, 64, 1)
            grads.append(jnp.where(mask, first, second))
        g1, g2, g3, g4, g5, g6, g7, g8 = grads
        a1, a2, a3, a4 = [power_ref[pair, k] for k in range(4)]
        g4 = g4 + pair_products((g8, a4), (a4, g8), (g7, a3), (g6, a2), (g5, a1))
        g3 = g3 + pair_products((a4, g7))
        g2 = g2 + pair_products((a4, g6))
        g1 = g1 + pair_products((a4, g5))
        g2 = g2 + pair_products((g4, a2), (a2, g4), (g3, a1))
        g1 = g1 + pair_products((a2, g3))
        g1 = g1 + pair_products((g2, a1), (a1, g2))
        rate, pi_mean, factor = [class_ref[pair, at] for at in range(3)]
        d_rate = root_col * g1 * inverse_root_row
        weighted = jnp.sum(d_rate * rate, axis=0, keepdims=True)
        total0 = jnp.sum(jnp.where(half, weighted, 0.0), axis=1, keepdims=True)
        total1 = jnp.sum(jnp.where(half, 0.0, weighted), axis=1, keepdims=True)
        diagonal = d_rate * twice
        diag0 = jnp.sum(jnp.where(mask, diagonal, 0.0), axis=1, keepdims=True)
        diag1 = jnp.sum(jnp.where(mask, 0.0, diagonal), axis=1, keepdims=True)
        row_grad = jnp.where(mask, diag0, diag1) + pi_col * jnp.where(half, total0, total1)
        flux_grad = (d_rate - row_grad) * pi_mean
        table_grad = table_grad + flux_grad * factor
        ratio = jnp.sum(flux_grad * ratio_table, axis=0, keepdims=True)
        ratio0 = jnp.sum(jnp.where(half, ratio, 0.0), axis=1, keepdims=True)
        ratio1 = jnp.sum(jnp.where(half, 0.0, ratio), axis=1, keepdims=True)
        omega_row = jnp.where(lane_row == 2 * pair, ratio0, omega_row)
        omega_row = jnp.where(lane_row == 2 * pair + 1, ratio1, omega_row)
    table_grad = table_grad + pltpu.roll(table_grad, 64, 1)
    masks, picks = neighbours()
    codon = lax.broadcasted_iota(jnp.int32, (16, 128), 1)
    column = lax.broadcasted_iota(jnp.int32, (16, 128), 0)
    lefts, rights = [], []
    for p, digit in enumerate((codon // 16, codon // 4 % 4, codon % 4)):
        left = jnp.where((column == 4 * p + digit) & (codon < 64), 1.0, 0.0).astype(BF)
        for part in split(jnp.where(masks[p], 0.5 * table_grad, 0.0)):
            lefts.append(left)
            rights.append(part)
    packed = mxu(
        jnp.concatenate(lefts, axis=1),
        jnp.concatenate([jnp.concatenate([part, jnp.zeros_like(part)], axis=0) for part in rights], axis=0),
    )
    turned = mxu_nt(
        jnp.concatenate(lefts, axis=1),
        jnp.concatenate([
            jnp.concatenate([part, jnp.zeros_like(part)], axis=0) for part in rights
        ], axis=1),
    )
    packed = packed + turned
    packed = jnp.where(lax.broadcasted_iota(jnp.int32, (16, 128), 1) < 64, packed, 0.0)

    even = jnp.sum(jnp.where(mask, slopes, 0.0), axis=1, keepdims=True)
    other = jnp.sum(jnp.where(mask, 0.0, slopes), axis=1, keepdims=True)
    placed = jnp.where(lane == 2 * row, even, 0.0) + jnp.where(lane == 2 * row + 1, other, 0.0)
    length_row = jnp.sum(placed, axis=0, keepdims=True)
    line = lax.broadcasted_iota(jnp.int32, out_ref.shape, 0)
    omega_row = jnp.where(lane_row == CLASSES, log_part, omega_row)
    omega_row = pltpu.roll(jnp.broadcast_to(omega_row, (8, 128)), 64, 1)[0:1]
    packed = packed + jnp.where(line == 0, omega_row, 0.0)
    out_ref[...] = packed + jnp.where(line == 12 + subtree, length_row, 0.0)


def last_kernel(total_sites, count, *refs):
    members = lax.axis_size("branch")
    subtree = lax.axis_index("branch")
    exch_ref, omega_ref, length_ref, log_ref = refs[count:]
    total = tree_sum([ref[...] for ref in refs[:count]])
    masks, picks = neighbours()
    table = jnp.zeros((64, 128), F32)
    for at_position, pick in zip(masks, picks):
        table = table + jnp.where(at_position, exact(pick, total), 0.0)
    exch_ref[...] = table[:, 0:64]
    moved = pltpu.roll(total[0:8], 64, 1)
    omega_ref[...] = moved[0:1, 0:CLASSES]
    line = lax.broadcasted_iota(jnp.int32, total.shape, 0)
    lengths = jnp.sum(jnp.where(line == 12 + subtree, total, 0.0), axis=0, keepdims=True)
    length_ref[...] = lengths[:, 0:EDGES]
    log_ref[...] = moved[0:1, CLASSES : CLASSES + 1] / total_sites / (LEAF_DEV * members)


def partners(x, axis, start, radix):
    size = lax.axis_size(axis)
    others = [
        lax.ppermute(x, axis, [(i, i ^ (step * start)) for i in range(size)])
        for step in range(1, radix)
    ]
    return [x] + others


def tree_sum(parts):
    while len(parts) > 1:
        parts = [parts[i] + parts[i + 1] for i in range(0, len(parts), 2)]
    return parts[0]


def sum_stages(x, members, sites):
    stages, start = [], 1
    while start < sites:
        radix = 2 if sites // start in (2, 8) else 4
        stages.append((members * start, radix, 1))
        start *= radix
    stages.append((1, members, 0))
    parts = [x]
    for start, radix, flip in stages[::-1]:
        x = tree_sum(parts)
        parts = [x] + [
            lax.ppermute(x, ("site", "branch"), [
                (i, i ^ (step * start + flip)) for i in range(sites * members)
            ])
            for step in range(1, radix)
        ]
    return parts


def body(
    total_sites, states, gap_mask, weights, leaf_order, exchanges, codon_freq, omega_ratio,
    lengths, classes,
):
    sites = states.shape[1]
    members = lax.axis_size("branch")
    sense, single, nonsyn = codon_tables()
    vmem = pl.BlockSpec(memory_space=pltpu.VMEM)
    smem = pl.BlockSpec(memory_space=pltpu.SMEM)
    shape = jax.ShapeDtypeStruct
    held = pltpu.VMEM
    limit = pltpu.CompilerParams(vmem_limit_bytes=20 * 2**20)

    def outside(x):
        return pltpu.with_memory_space_constraint(x, pltpu.HBM)

    def inside(xs):
        return [pltpu.with_memory_space_constraint(x, pltpu.VMEM) for x in xs]

    sense2 = outside(jnp.asarray(np.tile(sense[None, :], (1, 2))))
    single2 = outside(jnp.asarray(np.tile(single, (1, 2))))
    nonsyn2 = outside(jnp.asarray(np.tile(nonsyn, (1, 2))))
    freq = outside(codon_freq.reshape(1, 64))
    span, owner = outside(lengths.reshape(1, EDGES)), outside(classes.reshape(1, EDGES))
    table, omega = outside(exchanges), outside(omega_ratio)

    top, *kept = pl.pallas_call(
        up_kernel,
        out_shape=[
            shape((64, sites), F32),
            held((4, 2, PAIRS, 64, 128), BF),
            held((PAIRS // 2, 64, 128), F32),
            held((CLASSES // 2, 4, 64, 128), F32),
            held((STRIDE * 64, 128), F32),
            held((7, 64, 128), F32),
            held((PAIRS // 2, 128, sites), F32),
            held((64, 64, sites), BF),
            held((64, 64, sites), BF),
            held((32, 128, sites), BF),
            held((64, sites), F32),
            held((64, sites), F32),
            held((PAIRS, 64, 128), BF),
        ],
        in_specs=[vmem, vmem, smem, vmem, vmem, smem] + [vmem] * 5,
        out_specs=[vmem] * 13,
        scratch_shapes=[
            pltpu.VMEM((STRIDE * 64, 128), F32),
            pltpu.VMEM((PAIRS, 64, 256), BF),
        ],
        compiler_params=limit,
        name="up",
    )(
        outside(states), outside(gap_mask), outside(leaf_order),
        table, freq, omega, span, owner, sense2, single2, nonsyn2,
    )
    (
        chain, last, powers, dup, fixed, message, high, low, leaf, scale, inverse, thin,
    ) = inside(kept)
    tops = partners(top, "branch", 1, members)
    slope, matrix, turned, given, table_of = inside(pl.pallas_call(
        side_kernel,
        out_shape=[
            held((PAIRS * 64, 128), F32),
            held((64, 64, 256), BF),
            held((128, 128), F32),
            held((PAIRS // 2, 128, sites), F32),
            held((CLASSES // 2, 3, 64, 128), F32),
        ],
        in_specs=[vmem] * 7 + [smem, vmem, vmem],
        out_specs=[vmem] * 5,
        compiler_params=limit,
        name="side",
    )(dup, last, span, owner, fixed, thin, leaf, omega, single2, nonsyn2))
    part = pl.pallas_call(
        functools.partial(down_kernel, total_sites, members),
        out_shape=shape((16, 128), F32),
        in_specs=[vmem] * (16 + members),
        out_specs=vmem,
        scratch_shapes=[
            pltpu.VMEM((32, 128, sites), BF),
            pltpu.VMEM((32, 128, sites), BF),
            pltpu.VMEM((PAIRS, 64, 128), F32),
            pltpu.VMEM((STRIDE * 64, 128), F32),
            pltpu.VMEM((STRIDE * 64, 128), F32),
        ],
        compiler_params=limit,
        name="down",
    )(
        *tops, matrix, given, message, high, low, leaf, scale, inverse,
        chain, turned, slope, powers, fixed,
        table_of, outside(weights.reshape(1, sites)), nonsyn2,
    )
    parts = sum_stages(part, members, lax.axis_size("site"))
    exch, ratio, length, loglik = pl.pallas_call(
        functools.partial(last_kernel, total_sites, len(parts)),
        out_shape=[shape((64, 64), F32), shape((1, CLASSES), F32), shape((1, EDGES), F32), shape((1, 1), F32)],
        in_specs=[vmem] * len(parts),
        out_specs=[vmem] * 4,
        compiler_params=limit,
        name="last",
    )(*parts)
    return (exch, ratio.reshape(CLASSES), length.reshape(EDGES), loglik.reshape(()))


def solution(mesh):
    def whole(states, *rest):
        total_sites = states.shape[1]
        return jax.shard_map(
            functools.partial(body, total_sites),
            mesh=mesh,
            in_specs=(
                P(None, "site"),
                P(None, "site"),
                P("site"),
                P(),
                P(),
                P(),
                P(),
                P("branch"),
                P("branch"),
            ),
            out_specs=(P(), P(), P("branch"), P()),
            check_vma=False,
        )(states, *rest)

    return whole
```

```python
import functools
import jax
import jax.numpy as jnp
import numpy as np
from jax import lax
from jax.experimental import pallas as pl
from jax.experimental.pallas import tpu as pltpu
from jax.sharding import PartitionSpec as P

LEAF_DEV = 64
EDGES = 127
PAIRS = 64
CLASSES = 8
ORDER = 8
STRIDE = 65
BF = jnp.bfloat16
F32 = jnp.float32

CODE_TABLE = "FFLLSSSSYYXXCCXWLLLLPPPPHHQQRRRRIIIMTTTTNNKKSSRRVVVVAAAADDEEGGGG"


def codon_tables():
    amino_acid = np.array(list(CODE_TABLE))
    codon_index = np.arange(64)
    digits = np.stack([codon_index // 16, codon_index // 4 % 4, codon_index % 4], 1)
    differ = (digits[:, None, :] != digits[None, :, :]).sum(-1)
    is_sense = amino_acid != "X"
    single = (differ == 1) & is_sense[:, None] & is_sense[None, :]
    nonsyn = single & (amino_acid[:, None] != amino_acid[None, :])
    return (is_sense.astype(np.float32), single.astype(np.float32), nonsyn.astype(np.float32))


def low_half():
    return lax.broadcasted_iota(jnp.int32, (64, 128), 1) < 64


def split(x):
    high = x.astype(BF)
    low = (x - high.astype(F32)).astype(BF)
    return high, low


def spread(x, scale=1.0):
    mask = low_half()
    low = jnp.where(mask, scale, 0.0).astype(x.dtype)
    high = jnp.where(mask, 0.0, scale).astype(x.dtype)
    return jnp.concatenate([x * low, x * high], axis=0)


def mxu(left, right):
    return jnp.dot(left, right, preferred_element_type=F32)


def mxu_nt(left, right):
    return lax.dot_general(left, right, (((1,), (1,)), ((), ())), preferred_element_type=F32)


def exact(left, right):
    return jnp.dot(left, right, preferred_element_type=F32, precision=lax.Precision.HIGHEST)


def exact_tn(left, right):
    return lax.dot_general(
        left, right, (((0,), (0,)), ((), ())), preferred_element_type=F32,
        precision=lax.Precision.HIGHEST,
    )


def pair_products(*terms):
    lefts, rights = [], []
    for left, right in terms:
        left_high, left_low = split(left)
        right_high, right_low = split(right)
        wide_high, wide_low = spread(right_high), spread(right_low)
        lefts += [left_high, left_high, left_low]
        rights += [wide_high, wide_low, wide_high]
    return mxu(jnp.concatenate(lefts, axis=1), jnp.concatenate(rights, axis=0))


def messages(matrix, high, low):
    return mxu(matrix, jnp.concatenate([high, low, high, low], axis=0))


def leaf_messages(thin_ref, leaf_ref, p):
    found = []
    for e in range(2):
        vector = leaf_ref[p, 64 * e : 64 * e + 64, :]
        found.append(mxu(thin_ref[2 * p + e], jnp.concatenate([vector, vector], axis=0)))
    return found


def doubled(x):
    mask = low_half()
    swapped = pltpu.roll(x, 64, 1)
    return jnp.where(mask, x, swapped), jnp.where(mask, swapped, x)


def double(ref, p, x):
    for e, both in enumerate(doubled(x)):
        high, low = split(both)
        ref[2 * p + e] = jnp.concatenate([high, low], axis=1)


def side_by_side(ref, p, x):
    for e, both in enumerate(doubled(x)):
        rest = both - both.astype(BF).astype(F32)
        ref[2 * p + e] = jnp.where(low_half(), both, rest).astype(BF)


def identity_twice():
    row = lax.broadcasted_iota(jnp.int32, (64, 128), 0)
    lane = lax.broadcasted_iota(jnp.int32, (64, 128), 1)
    return (row == lane % 64).astype(F32)


def frequencies(freq_ref, sense_ref):
    twice = identity_twice()
    sense2 = sense_ref[...]
    freq2 = jnp.concatenate([freq_ref[...]] * 2, axis=1) * sense2
    total = 0.5 * jnp.sum(freq2, axis=1, keepdims=True)
    pi_row = freq2 / total
    pi_col = 0.5 * jnp.sum(twice * pi_row, axis=1, keepdims=True)
    sense_col = 0.5 * jnp.sum(twice * sense2, axis=1, keepdims=True)
    root_row = jnp.sqrt(jnp.where(sense2 > 0, pi_row, 1.0))
    root_col = jnp.sqrt(jnp.where(sense_col > 0, pi_col, 1.0))
    return twice, pi_row, pi_col, root_row, root_col


def symmetric_table(ex_ref, single_ref, twice):
    ex = ex_ref[...]
    both = ex + ex.T
    return 0.5 * jnp.concatenate([both, both], axis=1) * single_ref[...]


def class_pair(table, nonsyn, omega_ref, pair, twice, pi_row, pi_col):
    mask = low_half()
    omega = jnp.where(mask, omega_ref[2 * pair], omega_ref[2 * pair + 1])
    factor = 1.0 + nonsyn * (omega - 1.0)
    flux = table * factor
    off = flux * pi_row
    row0 = jnp.sum(jnp.where(mask, off, 0.0), axis=1, keepdims=True)
    row1 = jnp.sum(jnp.where(mask, 0.0, off), axis=1, keepdims=True)
    mean0 = jnp.sum(pi_col * row0, axis=0, keepdims=True)
    mean1 = jnp.sum(pi_col * row1, axis=0, keepdims=True)
    rows = jnp.where(mask, row0, row1)
    mean = jnp.where(mask, mean0, mean1)
    return factor, off, rows, mean


def neighbours():
    row = lax.broadcasted_iota(jnp.int32, (64, 128), 0)
    lane = lax.broadcasted_iota(jnp.int32, (64, 128), 1) % 64
    masks = [
        row % 16 == lane % 16,
        (row // 16 == lane // 16) & (row % 4 == lane % 4),
        row // 4 == lane // 4,
    ]
    codon = lax.broadcasted_iota(jnp.int32, (64, 16), 0)
    column = lax.broadcasted_iota(jnp.int32, (64, 16), 1)
    digits = [codon // 16, codon // 4 % 4, codon % 4]
    picks = [(column == 4 * p + digits[p]).astype(F32) for p in range(3)]
    return masks, picks


def coefficients(len_ref, cls_ref, slope):
    lane = lax.broadcasted_iota(jnp.int32, (PAIRS, EDGES), 1)
    row = lax.broadcasted_iota(jnp.int32, (PAIRS, EDGES), 0)
    lengths = len_ref[...] * 0.0625
    classes = cls_ref[...].astype(F32)
    place = lax.broadcasted_iota(jnp.int32, (PAIRS, 128), 1) % 64
    found = []
    for odd in range(2):
        here = lane == 2 * row + odd
        y = jnp.sum(jnp.where(here, lengths, 0.0), axis=1, keepdims=True)
        owner = jnp.sum(jnp.where(here, classes, 0.0), axis=1, keepdims=True)
        current = jnp.ones((PAIRS, 128), F32)
        series = jnp.zeros((PAIRS, 128), F32)
        for k in range(ORDER):
            following = current * y * (1.0 / (k + 1))
            series = jnp.where(place // CLASSES == k, current if slope else following, series)
            current = following
        found.append(jnp.where((place % CLASSES).astype(F32) == owner, series, 0.0))
    return found


def four_left(x):
    high, low = split(x)
    return jnp.concatenate([high, low], axis=1)


def four_right(x):
    high, low = split(x)
    return jnp.concatenate([high, low, high, low], axis=0)


def expand(coefs, dup_ref, store):
    high, low = split(coefs)
    left = jnp.concatenate(
        [jnp.concatenate([high, high], axis=1), jnp.concatenate([low, low], axis=1)], axis=0
    )
    for i in range(0, 64, 2):
        parts = [split(dup_ref[rows_of(i + t), :]) for t in range(2)]
        right = jnp.concatenate([
            jnp.concatenate([spread(parts[0][h]), spread(parts[1][h])], axis=1) for h in range(2)
        ], axis=0)
        both = mxu(left, right)
        both = both[0:64] + both[64:128]
        for t in range(2):
            store(i + t, both[:, 128 * t : 128 * t + 128])


def rows_of(i):
    return pl.ds(STRIDE * i, 64)


def up_kernel(
    states_ref, gap_ref, order_ref,
    ex_ref, freq_ref, omega_ref, len_ref, cls_ref, sense_ref, single_ref, nonsyn_ref,
    top_ref, chain_ref, last_ref, power_ref, dup_ref, fixed_ref,
    message_ref, high_ref, low_ref, leaf_ref, scale_ref, inverse_ref, thin_ref,
    first_ref, up_ref,
):
    subtree = lax.axis_index("branch")
    mask = low_half()
    twice, pi_row, pi_col, root_row, root_col = frequencies(freq_ref, sense_ref)
    table = symmetric_table(ex_ref, single_ref, twice)
    nonsyn = nonsyn_ref[...]
    for at, value in enumerate(
        (pi_row, pi_col, root_row, root_col, 1.0 / root_row, 1.0 / root_col, table)
    ):
        fixed_ref[at] = jnp.broadcast_to(value, (64, 128))

    sites = states_ref.shape[1]
    codon = lax.broadcasted_iota(jnp.int32, (64, sites), 0)
    for p in range(32):
        both = []
        for e in range(2):
            taxon = order_ref[subtree * LEAF_DEV + 2 * p + e]
            state = jnp.where(gap_ref[pl.ds(taxon, 1), :] > 0, -1, states_ref[pl.ds(taxon, 1), :])
            hit = (codon == state) | (state < 0)
            both.append(jnp.where(hit, 1.0, 0.0).astype(BF))
        leaf_ref[p] = jnp.concatenate(both, axis=0)

    powers = []
    for pair in range(CLASSES // 2):
        factor, off, rows, mean = class_pair(
            table, nonsyn, omega_ref, pair, twice, pi_row, pi_col
        )
        powers.append([(table * factor * root_col * root_row - twice * rows) / mean])
    for left, right in ((0, 0), (1, 0), (1, 1), (3, 0), (3, 1), (3, 2), (3, 3)):
        for pair in range(CLASSES // 2):
            powers[pair].append(pair_products((powers[pair][left], powers[pair][right])))
    for pair in range(CLASSES // 2):
        for k in range(ORDER):
            value = powers[pair][k]
            swapped = pltpu.roll(value, 64, 1)
            at = CLASSES * k + 2 * pair
            dup_ref[pl.ds(at, 64, stride=STRIDE), :] = jnp.where(mask, value, swapped)
            dup_ref[pl.ds(at + 1, 64, stride=STRIDE), :] = jnp.where(mask, swapped, value)
            if k < 4:
                power_ref[pair, k] = value

    even, odd = coefficients(len_ref, cls_ref, False)

    def store(i, value):
        first_ref[rows_of(i), :] = value

    expand(jnp.where(low_half(), even, odd), dup_ref, store)

    def squarings(step):
        leaves = step < 2
        width = 16
        held = [first_ref[pl.ds(step * width + j, 64, stride=STRIDE), :] for j in range(width)]
        for level in range(4):
            for j in range(width):
                high, low = split(held[j])
                chain_ref[level, 0, step * width + j] = high
                chain_ref[level, 1, step * width + j] = low
                wide_high, wide_low = spread(high), spread(low)
                held[j] = 2.0 * held[j] + mxu(
                    jnp.concatenate([high, high, low], axis=1),
                    jnp.concatenate([wide_high, wide_low, wide_high], axis=0),
                )
        for j in range(width):
            p = step * width + j
            matrix = inverse_root_col * (held[j] + twice) * root_row
            if leaves:
                side_by_side(thin_ref, p, matrix)
            else:
                last_ref[p - 32] = held[j]
                double(up_ref, p - 32, matrix)

    inverse_root_col = 1.0 / root_col
    squarings(0)
    squarings(1)

    def finish(p, message):
        if p >= 32:
            message_ref[p - 32] = jnp.concatenate(message, axis=0)
        raw = message[0] * message[1]
        scaling = jnp.sum(raw, axis=0, keepdims=True)
        inverse = 1.0 / scaling
        scale_ref[pl.ds(p, 1), :] = scaling
        inverse_ref[pl.ds(p, 1), :] = inverse
        high, low = split(raw * inverse)
        high_ref[p] = high
        low_ref[p] = low

    for p in range(16):
        finish(p, leaf_messages(thin_ref, leaf_ref, p))
    squarings(2)
    for p in range(16, 32):
        finish(p, leaf_messages(thin_ref, leaf_ref, p))
    squarings(3)

    def inner(p):
        child = 2 * p - 64
        return [
            messages(up_ref[child + e], high_ref[child + e], low_ref[child + e]) for e in range(2)
        ]

    for p in range(32, 48):
        finish(p, inner(p))
    for p in range(48, 63):
        finish(p, inner(p))
    high_ref[63] = jnp.zeros((64, sites), BF)
    low_ref[63] = jnp.zeros((64, sites), BF)
    scale_ref[63:64, :] = jnp.ones((1, sites), F32)
    inverse_ref[63:64, :] = jnp.ones((1, sites), F32)
    top = inner(63)
    top_ref[...] = top[0]


def side_kernel(
    dup_ref, last_ref, len_ref, cls_ref, fixed_ref, thin_ref, leaf_ref, omega_ref, single_ref,
    nonsyn_ref,
    slope_ref, matrix_ref, turned_ref, given_ref, class_ref,
):
    twice = identity_twice()
    even, odd = coefficients(len_ref, cls_ref, True)

    def store(i, value):
        slope_ref[64 * i : 64 * i + 64, :] = value

    expand(jnp.where(low_half(), even, odd), dup_ref, store)
    even, odd = coefficients(len_ref, cls_ref, False)
    turned_ref[...] = exact_tn(jnp.where(low_half(), even, odd), twice)
    root_col, inverse_root_row = fixed_ref[3], fixed_ref[4]

    def matrices(step, carry):
        for j in range(8):
            r = step * 8 + j
            double(matrix_ref, r, root_col * (last_ref[r] + twice) * inverse_root_row)
        return carry

    lax.fori_loop(0, 4, matrices, 0)
    pi_row, pi_col, table, single = fixed_ref[0], fixed_ref[1], fixed_ref[6], single_ref[...]
    for pair in range(CLASSES // 2):
        factor, off, rows, mean = class_pair(
            table, nonsyn_ref[...], omega_ref, pair, twice, pi_row, pi_col
        )
        class_ref[pair, 0] = (off - twice * rows) / mean
        class_ref[pair, 1] = pi_row / mean
        class_ref[pair, 2] = factor * single
    for p in range(32):
        given_ref[p] = jnp.concatenate(leaf_messages(thin_ref, leaf_ref, p), axis=0)


def down_kernel(total_sites, members, *refs):
    tops = refs[:members]
    (
        matrix_ref, given_ref, message_ref, high_ref, low_ref, leaf_ref, scale_ref, inverse_ref,
        chain_ref, turned_ref, slope_ref, power_ref, fixed_ref,
        class_ref, weights_ref, nonsyn_ref,
        out_ref,
        a_high_ref, a_low_ref, count_ref, back_ref, bins_ref,
    ) = refs[members:]
    subtree = lax.axis_index("branch")
    mask = low_half()
    twice = identity_twice()
    pi_row, pi_col, root_row, root_col, inverse_root_row, inverse_root_col = [
        fixed_ref[at] for at in range(6)
    ]
    sites = weights_ref.shape[1]
    weight = weights_ref[...].astype(F32)

    above = jnp.broadcast_to(pi_col[:, 0:1], (64, sites))
    for other in tops[1:]:
        above = above * other[...]
    own = tops[0][...]
    likelihood = jnp.sum(above * own, axis=0, keepdims=True)
    logs = jnp.sum(jnp.log(scale_ref[...]), axis=0, keepdims=True)
    logs = logs + jnp.where(subtree == 0, jnp.log(likelihood), 0.0)
    log_part = jnp.sum(weight * logs, axis=1, keepdims=True)
    high, low = split(above * (weight / (likelihood * total_sites)))
    a_high_ref[31, 0:64, :] = high
    a_low_ref[31, 0:64, :] = low
    a_high_ref[31, 64:128, :] = jnp.zeros((64, sites), BF)
    a_low_ref[31, 64:128, :] = jnp.zeros((64, sites), BF)

    def store_counts(p, square):
        counts = jnp.where(mask, square[0:64], square[64:128])
        count_ref[p] = inverse_root_col * counts * root_row

    def descend(r):
        a_high, a_low = a_high_ref[r - 32], a_low_ref[r - 32]
        child = 2 * r - 64
        u_high = jnp.concatenate([high_ref[child], high_ref[child + 1]], axis=0)
        u_low = jnp.concatenate([low_ref[child], low_ref[child + 1]], axis=0)
        four = mxu_nt(
            jnp.concatenate([a_high, a_low], axis=0), jnp.concatenate([u_high, u_low], axis=0)
        )
        store_counts(r, four[0:128, 0:128] + four[0:128, 128:256] + four[128:256, 0:128])
        return [
            messages(
                matrix_ref[2 * (r - 32) + e], a_high[64 * e : 64 * e + 64], a_low[64 * e : 64 * e + 64]
            )
            for e in range(2)
        ]

    def children(down, e, p):
        vector = down[e]
        inverse = inverse_ref[pl.ds(p, 1), :]
        message = message_ref[p - 32] if p >= 32 else given_ref[p]
        pair = jnp.concatenate(
            [vector * message[64:128] * inverse, vector * message[0:64] * inverse], axis=0
        )
        return split(pair)

    def inner(r):
        down = descend(r)
        for e in range(2):
            p = 2 * r + e - 64
            if isinstance(p, int) and p == 63:
                continue
            high, low = children(down, e, p)
            a_high_ref[p - 32] = high
            a_low_ref[p - 32] = low

    def adjoint(first, width):
        held = [count_ref[first + j] for j in range(width)]
        for level in range(3, -1, -1):
            for j in range(width):
                high, low = split(held[j])
                e_high, e_low = chain_ref[level, 0, first + j], chain_ref[level, 1, first + j]
                left = jnp.concatenate([
                    jnp.concatenate([high, e_high], axis=1),
                    jnp.concatenate([low, e_low], axis=1),
                ], axis=0)
                right = jnp.concatenate([
                    jnp.concatenate([spread(e_high), spread(e_low)], axis=1),
                    jnp.concatenate([spread(high), spread(low)], axis=1),
                ], axis=0)
                four = mxu(left, right)
                held[j] = 2.0 * held[j] + (
                    four[0:64, 0:128] + four[0:64, 128:256] + four[64:128, 0:128]
                )
        for j in range(width):
            back_ref[pl.ds(first + j, 64, stride=STRIDE), :] = held[j]

    def outer(r):
        down = descend(r)
        for e in range(2):
            p = 2 * r + e - 64
            high, low = children(down, e, p)
            square = mxu_nt(jnp.concatenate([high, low], axis=0), leaf_ref[p])
            store_counts(p, square[0:128] + square[128:256])

    for r in range(63, 47, -1):
        inner(r)
    adjoint(56, 8)
    for block, first in enumerate((48, 24, 40, 16)):
        for r in range(47 - 4 * block, 43 - 4 * block, -1):
            outer(r)
        adjoint(first, 8)
    adjoint(0, 16)
    adjoint(32, 8)

    left = four_left(turned_ref[...])

    total = jnp.zeros((64, 128), F32)
    for i in range(0, 64, 2):
        values = [back_ref[rows_of(i + t), :] for t in range(2)]
        both = mxu(left, four_right(jnp.concatenate(values, axis=1)))
        for t in range(2):
            total = total + values[t] * slope_ref[64 * (i + t) : 64 * (i + t) + 64, :]
            here = both[:, 128 * t : 128 * t + 128]
            bins_ref[rows_of(i + t), :] = jnp.where(mask, here[0:64], here[64:128])
    slopes = total * 0.0625

    ratio_table = fixed_ref[6] * nonsyn_ref[...]
    half = lax.broadcasted_iota(jnp.int32, (1, 128), 1) < 64
    row = lax.broadcasted_iota(jnp.int32, (64, 128), 0)
    lane = lax.broadcasted_iota(jnp.int32, (64, 128), 1)
    table_grad = jnp.zeros((64, 128), F32)
    omega_row = jnp.zeros((1, 128), F32)
    lane_row = lax.broadcasted_iota(jnp.int32, (1, 128), 1)
    for pair in range(CLASSES // 2):
        grads = []
        for k in range(ORDER):
            at = CLASSES * k + 2 * pair
            first = bins_ref[pl.ds(at, 64, stride=STRIDE), :]
            second = bins_ref[pl.ds(at + 1, 64, stride=STRIDE), :]
            first = first + pltpu.roll(first, 64, 1)
            second = second + pltpu.roll(second, 64, 1)
            grads.append(jnp.where(mask, first, second))
        g1, g2, g3, g4, g5, g6, g7, g8 = grads
        a1, a2, a3, a4 = [power_ref[pair, k] for k in range(4)]
        g4 = g4 + pair_products((g8, a4), (a4, g8), (g7, a3), (g6, a2), (g5, a1))
        g3 = g3 + pair_products((a4, g7))
        g2 = g2 + pair_products((a4, g6))
        g1 = g1 + pair_products((a4, g5))
        g2 = g2 + pair_products((g4, a2), (a2, g4), (g3, a1))
        g1 = g1 + pair_products((a2, g3))
        g1 = g1 + pair_products((g2, a1), (a1, g2))
        rate, pi_mean, factor = [class_ref[pair, at] for at in range(3)]
        d_rate = root_col * g1 * inverse_root_row
        weighted = jnp.sum(d_rate * rate, axis=0, keepdims=True)
        total0 = jnp.sum(jnp.where(half, weighted, 0.0), axis=1, keepdims=True)
        total1 = jnp.sum(jnp.where(half, 0.0, weighted), axis=1, keepdims=True)
        diagonal = d_rate * twice
        diag0 = jnp.sum(jnp.where(mask, diagonal, 0.0), axis=1, keepdims=True)
        diag1 = jnp.sum(jnp.where(mask, 0.0, diagonal), axis=1, keepdims=True)
        row_grad = jnp.where(mask, diag0, diag1) + pi_col * jnp.where(half, total0, total1)
        flux_grad = (d_rate - row_grad) * pi_mean
        table_grad = table_grad + flux_grad * factor
        ratio = jnp.sum(flux_grad * ratio_table, axis=0, keepdims=True)
        ratio0 = jnp.sum(jnp.where(half, ratio, 0.0), axis=1, keepdims=True)
        ratio1 = jnp.sum(jnp.where(half, 0.0, ratio), axis=1, keepdims=True)
        omega_row = jnp.where(lane_row == 2 * pair, ratio0, omega_row)
        omega_row = jnp.where(lane_row == 2 * pair + 1, ratio1, omega_row)
    table_grad = table_grad + pltpu.roll(table_grad, 64, 1)
    masks, picks = neighbours()
    codon = lax.broadcasted_iota(jnp.int32, (16, 128), 1)
    column = lax.broadcasted_iota(jnp.int32, (16, 128), 0)
    lefts, rights = [], []
    for p, digit in enumerate((codon // 16, codon // 4 % 4, codon % 4)):
        left = jnp.where((column == 4 * p + digit) & (codon < 64), 1.0, 0.0).astype(BF)
        for part in split(jnp.where(masks[p], 0.5 * table_grad, 0.0)):
            lefts.append(left)
            rights.append(part)
    packed = mxu(
        jnp.concatenate(lefts, axis=1),
        jnp.concatenate([jnp.concatenate([part, jnp.zeros_like(part)], axis=0) for part in rights], axis=0),
    )
    turned = mxu_nt(
        jnp.concatenate(lefts, axis=1),
        jnp.concatenate([
            jnp.concatenate([part, jnp.zeros_like(part)], axis=0) for part in rights
        ], axis=1),
    )
    packed = packed + turned
    packed = jnp.where(lax.broadcasted_iota(jnp.int32, (16, 128), 1) < 64, packed, 0.0)

    even = jnp.sum(jnp.where(mask, slopes, 0.0), axis=1, keepdims=True)
    other = jnp.sum(jnp.where(mask, 0.0, slopes), axis=1, keepdims=True)
    placed = jnp.where(lane == 2 * row, even, 0.0) + jnp.where(lane == 2 * row + 1, other, 0.0)
    length_row = jnp.sum(placed, axis=0, keepdims=True)
    line = lax.broadcasted_iota(jnp.int32, out_ref.shape, 0)
    omega_row = jnp.where(lane_row == CLASSES, log_part, omega_row)
    omega_row = pltpu.roll(jnp.broadcast_to(omega_row, (8, 128)), 64, 1)[0:1]
    packed = packed + jnp.where(line == 0, omega_row, 0.0)
    out_ref[...] = packed + jnp.where(line == 12 + subtree, length_row, 0.0)


def last_kernel(total_sites, count, *refs):
    members = lax.axis_size("branch")
    subtree = lax.axis_index("branch")
    exch_ref, omega_ref, length_ref, log_ref = refs[count:]
    total = tree_sum([ref[...] for ref in refs[:count]])
    masks, picks = neighbours()
    table = jnp.zeros((64, 128), F32)
    for at_position, pick in zip(masks, picks):
        table = table + jnp.where(at_position, exact(pick, total), 0.0)
    exch_ref[...] = table[:, 0:64]
    moved = pltpu.roll(total[0:8], 64, 1)
    omega_ref[...] = moved[0:1, 0:CLASSES]
    line = lax.broadcasted_iota(jnp.int32, total.shape, 0)
    lengths = jnp.sum(jnp.where(line == 12 + subtree, total, 0.0), axis=0, keepdims=True)
    length_ref[...] = lengths[:, 0:EDGES]
    log_ref[...] = moved[0:1, CLASSES : CLASSES + 1] / total_sites / (LEAF_DEV * members)


def partners(x, axis, start, radix):
    size = lax.axis_size(axis)
    others = [
        lax.ppermute(x, axis, [(i, i ^ (step * start)) for i in range(size)])
        for step in range(1, radix)
    ]
    return [x] + others


def tree_sum(parts):
    while len(parts) > 1:
        parts = [parts[i] + parts[i + 1] for i in range(0, len(parts), 2)]
    return parts[0]


def sum_stages(x, members, sites):
    stages, start = [], 1
    while start < sites:
        radix = 2 if sites // start in (2, 8) else 4
        stages.append((members * start, radix, 1))
        start *= radix
    stages.append((1, members, 0))
    parts = [x]
    for start, radix, flip in stages[::-1]:
        x = tree_sum(parts)
        parts = [x] + [
            lax.ppermute(x, ("site", "branch"), [
                (i, i ^ (step * start + flip)) for i in range(sites * members)
            ])
            for step in range(1, radix)
        ]
    return parts


def body(
    total_sites, states, gap_mask, weights, leaf_order, exchanges, codon_freq, omega_ratio,
    lengths, classes,
):
    sites = states.shape[1]
    members = lax.axis_size("branch")
    sense, single, nonsyn = codon_tables()
    vmem = pl.BlockSpec(memory_space=pltpu.VMEM)
    smem = pl.BlockSpec(memory_space=pltpu.SMEM)
    shape = jax.ShapeDtypeStruct
    held = pltpu.VMEM
    limit = pltpu.CompilerParams(vmem_limit_bytes=20 * 2**20)

    def outside(x):
        return pltpu.with_memory_space_constraint(x, pltpu.HBM)

    def inside(xs):
        return [pltpu.with_memory_space_constraint(x, pltpu.VMEM) for x in xs]

    sense2 = outside(jnp.asarray(np.tile(sense[None, :], (1, 2))))
    single2 = outside(jnp.asarray(np.tile(single, (1, 2))))
    nonsyn2 = outside(jnp.asarray(np.tile(nonsyn, (1, 2))))
    freq = outside(codon_freq.reshape(1, 64))
    span, owner = outside(lengths.reshape(1, EDGES)), outside(classes.reshape(1, EDGES))
    table, omega = outside(exchanges), outside(omega_ratio)

    top, *kept = pl.pallas_call(
        up_kernel,
        out_shape=[
            shape((64, sites), F32),
            held((4, 2, PAIRS, 64, 128), BF),
            held((PAIRS // 2, 64, 128), F32),
            held((CLASSES // 2, 4, 64, 128), F32),
            held((STRIDE * 64, 128), F32),
            held((7, 64, 128), F32),
            held((PAIRS // 2, 128, sites), F32),
            held((64, 64, sites), BF),
            held((64, 64, sites), BF),
            held((32, 128, sites), BF),
            held((64, sites), F32),
            held((64, sites), F32),
            held((PAIRS, 64, 128), BF),
        ],
        in_specs=[vmem, vmem, smem, vmem, vmem, smem] + [vmem] * 5,
        out_specs=[vmem] * 13,
        scratch_shapes=[
            pltpu.VMEM((STRIDE * 64, 128), F32),
            pltpu.VMEM((PAIRS, 64, 256), BF),
        ],
        compiler_params=limit,
        name="up",
    )(
        outside(states), outside(gap_mask), outside(leaf_order),
        table, freq, omega, span, owner, sense2, single2, nonsyn2,
    )
    (
        chain, last, powers, dup, fixed, message, high, low, leaf, scale, inverse, thin,
    ) = inside(kept)
    tops = partners(top, "branch", 1, members)
    slope, matrix, turned, given, table_of = inside(pl.pallas_call(
        side_kernel,
        out_shape=[
            held((PAIRS * 64, 128), F32),
            held((64, 64, 256), BF),
            held((128, 128), F32),
            held((PAIRS // 2, 128, sites), F32),
            held((CLASSES // 2, 3, 64, 128), F32),
        ],
        in_specs=[vmem] * 7 + [smem, vmem, vmem],
        out_specs=[vmem] * 5,
        compiler_params=limit,
        name="side",
    )(dup, last, span, owner, fixed, thin, leaf, omega, single2, nonsyn2))
    part = pl.pallas_call(
        functools.partial(down_kernel, total_sites, members),
        out_shape=shape((16, 128), F32),
        in_specs=[vmem] * (16 + members),
        out_specs=vmem,
        scratch_shapes=[
            pltpu.VMEM((32, 128, sites), BF),
            pltpu.VMEM((32, 128, sites), BF),
            pltpu.VMEM((PAIRS, 64, 128), F32),
            pltpu.VMEM((STRIDE * 64, 128), F32),
            pltpu.VMEM((STRIDE * 64, 128), F32),
        ],
        compiler_params=limit,
        name="down",
    )(
        *tops, matrix, given, message, high, low, leaf, scale, inverse,
        chain, turned, slope, powers, fixed,
        table_of, outside(weights.reshape(1, sites)), nonsyn2,
    )
    parts = sum_stages(part, members, lax.axis_size("site"))
    exch, ratio, length, loglik = pl.pallas_call(
        functools.partial(last_kernel, total_sites, len(parts)),
        out_shape=[shape((64, 64), F32), shape((1, CLASSES), F32), shape((1, EDGES), F32), shape((1, 1), F32)],
        in_specs=[vmem] * len(parts),
        out_specs=[vmem] * 4,
        compiler_params=limit,
        name="last",
    )(*parts)
    return (exch, ratio.reshape(CLASSES), length.reshape(EDGES), loglik.reshape(()))


def solution(mesh):
    def whole(states, *rest):
        total_sites = states.shape[1]
        return jax.shard_map(
            functools.partial(body, total_sites),
            mesh=mesh,
            in_specs=(
                P(None, "site"),
                P(None, "site"),
                P("site"),
                P(),
                P(),
                P(),
                P(),
                P("branch"),
                P("branch"),
            ),
            out_specs=(P(), P(), P("branch"), P()),
            check_vma=False,
        )(states, *rest)

    return whole
```
